32 devices in a mesh: section: 2 (over core), dp: 4 (over z), tensor: 4 (over y, x).
Axes of the slice: x: 2, y: 2, z: 4, core: 2. Of those that a mesh axis runs over, the one named last changes fastest.
Arguments:
- patches: bfloat16 [2, 4336, 768], P(None, ('dp', 'tensor')), may hold values from -6 to 6
- cotangent: bfloat16 [2, 4336, 768], P(None, ('dp', 'tensor')), may hold values from -6 to 6
- crop_lengths: int32 [2, 8, 6], P(None, 'dp'), may hold values from 18 to 197, as said below
- route_mask: int32 [2, 4336], P(None, 'dp'), may hold values from 0 to 1, as said below
- w_qkv: bfloat16 [2, 768, 3, 768], P('section', None, None, 'tensor'), may hold values from -0.21875 to 0.21875
- w_out: bfloat16 [2, 768, 768], P('section', 'tensor'), may hold values from -1.75 to 1.75
- w_up: bfloat16 [2, 768, 3072], P('section', None, 'tensor'), may hold values from -0.21875 to 0.21875
- w_down: bfloat16 [2, 3072, 768], P('section', 'tensor'), may hold values from -0.109375 to 0.109375
- ln1_gain: float32 [2, 768], P('section'), may hold values from 0.5 to 1.5
- ln2_gain: float32 [2, 768], P('section'), may hold values from 0.5 to 1.5
- router: bfloat16 [768], replicated, may hold values from -0.21875 to 0.21875
Outputs:
- activations: bfloat16 [2, 2, 4336, 768], P('section', None, ('dp', 'tensor'))
- input_grads: float32 [2, 2, 4336, 768], P('section', None, ('dp', 'tensor'))
- qkv_grad: float32 [2, 768, 3, 768], P('section', 'dp', None, 'tensor')
- out_grad: float32 [2, 768, 768], P('section', 'tensor', 'dp')
- up_grad: float32 [2, 768, 3072], P('section', 'dp', 'tensor')
- down_grad: float32 [2, 3072, 768], P('section', 'tensor', 'dp')
- ln1_grad: float32 [2, 768], P('section', ('dp', 'tensor'))
- ln2_grad: float32 [2, 768], P('section', ('dp', 'tensor'))
- router_grad: float32 [768], P(('section', 'dp', 'tensor'))
The draws below stay inside these ranges and needn't reach their ends.
Inputs may be any that keep to these rules, and one draw needn't show every extreme that they name: `crop_lengths`: each image's 6 crop lengths sum to 542; the first crop of every image has 197 tokens. `route_mask`: in a crop of L tokens exactly (L + 1) // 2 tokens are 1.
All inputs are finite; a program needn't handle non-finite values.
Results may differ from the reference program's by a relative error of at most 0.028.
Values may be sent and summed in bfloat16 or wider, within the bound.
A program may use at most 192 MiB of HBM per device.

```python
import jax
import jax.numpy as jnp
from jax import lax

D = 768
HEADS = 12
HEAD_DIM = 64
FF = 3072
GLOBAL = 197
LOCAL = 37
CROPS = 6
MICRO = 2
IMG_MB = 2
SLOT = 542
TOK_MB = 4336
N_DP = 4
N_TENSOR = 4


def crop_plan(key):
    images = MICRO * N_DP * IMG_MB
    slot_len = 2 * GLOBAL + 4 * LOCAL
    first_key, second_key, third_key = jax.random.split(key, 3)
    second = jax.random.randint(first_key, (images, 1), 3 * GLOBAL // 4, GLOBAL + 1)
    smalls = jax.random.randint(second_key, (images, 3), LOCAL // 2, LOCAL + 1)
    leading = jnp.full((images, 1), GLOBAL, jnp.int32)
    tail_len = slot_len - GLOBAL - second - jnp.sum(smalls, axis=1, keepdims=True)
    lengths = jnp.concatenate([leading, second, smalls, tail_len], axis=1).astype(jnp.int32)
    crop_ends = jnp.cumsum(lengths, axis=1)
    positions = jnp.arange(slot_len, dtype=jnp.int32)
    crop_of = jnp.sum((positions[None, :, None] >= crop_ends[:, None, :]).astype(jnp.int32), axis=2)
    priority = jax.vmap(lambda single: jax.random.permutation(single, slot_len))(jax.random.split(third_key, images))
    same_crop = crop_of[:, :, None] == crop_of[:, None, :]
    before = jnp.sum((same_crop & (priority[:, None, :] < priority[:, :, None])).astype(jnp.int32), axis=2)
    crop_index = jnp.arange(CROPS, dtype=jnp.int32)
    crop_size = jnp.sum(jnp.where(crop_of[:, :, None] == crop_index[None, None, :], lengths[:, None, :], 0), axis=2)
    chosen = (before < (crop_size + 1) // 2).astype(jnp.int32)
    return (lengths.reshape(MICRO, N_DP * IMG_MB, CROPS), chosen.reshape(MICRO, N_DP * IMG_MB * slot_len))


def draw_crop_lengths(key, part):
    return crop_plan(key)[0]


def draw_route_mask(key, part):
    return crop_plan(key)[1]


def shard_levels(rng, dims, shards, least, high):
    factor_of, own = 1.0, jax.random.fold_in(rng, 6)
    for dim, parts in shards:
        draws = jnp.exp(jax.random.uniform(jax.random.fold_in(own, dim), (parts,), jnp.float32, least / len(shards), high / len(shards)))
        factor_of = factor_of * jnp.repeat(draws, dims[dim] // parts).reshape([-1 if axis == dim else 1 for axis in range(len(dims))])
    return factor_of


def bell_draw(own_key, shape, deviation, limit, cuts=(), kind=jnp.bfloat16):
    result = jax.random.normal(own_key, shape, jnp.float32) * deviation
    if len(cuts) > 0:
        result = shard_levels(own_key, shape, cuts, -0.22, 0.18) * result
    return jnp.clip(result, min=-limit, max=limit).astype(kind)


def setup_inputs(seed: int = 0) -> dict:
    key_of = jax.random.split(jax.random.key(seed), 12)
    patches = bell_draw(key_of[0], (MICRO, TOK_MB, D), 1.0, 6.0, ((1, 16),))
    cotangent = bell_draw(key_of[1], (MICRO, TOK_MB, D), 1.0, 6.0, ((1, 16),))
    crop_lengths = draw_crop_lengths(jax.random.fold_in(key_of[11], 71), 0)
    route_mask = draw_route_mask(jax.random.fold_in(key_of[11], 71), 0)
    w_qkv = bell_draw(key_of[4], (2, D, 3, D), D ** -0.5, 0.21875, ((0, 2), (3, 4)))
    w_out = bell_draw(key_of[5], (2, D, D), (D // 64) ** -0.5, 1.75, ((0, 2), (1, 4)))
    w_up = bell_draw(key_of[6], (2, D, FF), D ** -0.5, 0.21875, ((0, 2), (2, 4)))
    w_down = bell_draw(key_of[7], (2, FF, D), FF ** -0.5, 0.109375, ((0, 2), (1, 4)))
    ln1_gain = jnp.clip(1.0 + 0.1 * jax.random.normal(key_of[8], (2, D), jnp.float32), 0.5, 1.5)
    ln2_gain = jnp.clip(1.0 + 0.1 * jax.random.normal(key_of[9], (2, D), jnp.float32), 0.5, 1.5)
    router = bell_draw(key_of[10], (D,), D ** -0.5, 0.21875)
    return {"patches": patches, "cotangent": cotangent, "crop_lengths": crop_lengths, "route_mask": route_mask, "w_qkv": w_qkv, "w_out": w_out, "w_up": w_up, "w_down": w_down, "ln1_gain": ln1_gain, "ln2_gain": ln2_gain, "router": router}


@jax.custom_vjp
def low(v):
    return lax.optimization_barrier(v.astype(jnp.bfloat16)).astype(jnp.float32)

@jax.custom_vjp
def low_back(v):
    return v

def low_keep(v):
    return (low(v), None)

def low_pass(kept, grad):
    return (grad,)

def back_keep(v):
    return (v, None)

def back_low(kept, grad):
    return (low(grad),)
low.defvjp(low_keep, low_pass)
low_back.defvjp(back_keep, back_low)
HIGH = lax.Precision.HIGHEST
EPS = 1e-06
NEG = -1000000000.0

def norm_rows(values, gain):
    centre = values - lax.optimization_barrier(jnp.mean(values, axis=-1, keepdims=True))
    spread = lax.optimization_barrier(jnp.mean(centre * centre, axis=-1, keepdims=True))
    return centre * lax.rsqrt(spread + EPS) * gain

def crop_ids(lengths):
    crop_ends = jnp.cumsum(lengths, axis=-1)
    positions = jnp.arange(SLOT, dtype=jnp.int32)
    return lax.optimization_barrier(jnp.sum((positions[:, None] >= crop_ends[..., None, :]).astype(jnp.int32), axis=-1))

def image_layer(inputs, keys_ok, crop_row, keep_row, params, routed):
    w_qkv, w_out, w_up, w_down, gain_one, gain_two, router = params
    head_cols = D // N_TENSOR
    unit_cols = FF // N_TENSOR
    normed = low(norm_rows(inputs, gain_one))
    qkv_parts = []
    for group in range(N_TENSOR):
        cols = w_qkv[:, :, group * head_cols:(group + 1) * head_cols]
        part = jnp.einsum('sd,dke->kse', low_back(normed), cols, precision=HIGH)
        qkv_parts.append(low(low_back(part)))
    qkv_all = jnp.concatenate(qkv_parts, axis=2)
    heads = qkv_all.reshape(3, SLOT, HEADS, HEAD_DIM)
    scores = jnp.einsum('qhe,khe->hqk', heads[0], heads[1], precision=HIGH) * HEAD_DIM ** (-0.5)
    allowed = (crop_row[:, None] == crop_row[None, :]) & keys_ok[None, :]
    scores = low_back(jnp.where(allowed[None], scores, NEG))
    row_max = lax.optimization_barrier(jnp.max(scores, axis=-1, keepdims=True))
    expo = jnp.exp(scores - row_max)
    probs = expo / lax.optimization_barrier(jnp.sum(expo, axis=-1, keepdims=True))
    mixed = jnp.einsum('hqk,khe->qhe', low(probs), heads[2], precision=HIGH).reshape(SLOT, D)
    mixed = low(low_back(mixed))
    attended = jnp.zeros((SLOT, D), jnp.float32)
    for group in range(N_TENSOR):
        piece = mixed[:, group * head_cols:(group + 1) * head_cols]
        rows = w_out[group * head_cols:(group + 1) * head_cols, :]
        attended = attended + low(jnp.dot(piece, rows, precision=HIGH))
    attended = low_back(attended)
    second = low(norm_rows(inputs + attended, gain_two))
    fed_back = jnp.zeros((SLOT, D), jnp.float32)
    for group in range(N_TENSOR):
        up_cols = w_up[:, group * unit_cols:(group + 1) * unit_cols]
        upper = low_back(jnp.dot(low_back(second), up_cols, precision=HIGH))
        active = low(jax.nn.gelu(upper, approximate=False))
        down_rows = w_down[group * unit_cols:(group + 1) * unit_cols, :]
        fed_back = fed_back + low(jnp.dot(active, down_rows, precision=HIGH))
    fed_back = low_back(fed_back)
    branch = attended + fed_back
    if routed:
        scale_row = jax.nn.sigmoid(jnp.dot(inputs, router, precision=HIGH)) * keep_row
        return inputs + scale_row[:, None] * branch
    return inputs + branch

def reference(patches, cotangent, crop_lengths, route_mask, w_qkv, w_out, w_up, w_down, ln1_gain, ln2_gain, router):
    images = MICRO * N_DP * IMG_MB
    inputs = patches.astype(jnp.float32).reshape(images, SLOT, D)
    crop_all = crop_ids(crop_lengths.reshape(images, CROPS))
    keep_all = route_mask.reshape(images, SLOT).astype(jnp.float32)
    picked = route_mask.reshape(images, SLOT) > 0
    everyone = jnp.ones_like(picked)

    def forward(inputs, gap, q_weight, o_weight, u_weight, d_weight, gain_first, gain_second, r_weight):

        def first_layer(item):
            rows_in, keys_ok, crop_row, keep_row = item
            return image_layer(rows_in, keys_ok, crop_row, keep_row, (q_weight[0], o_weight[0], u_weight[0], d_weight[0], gain_first[0], gain_second[0], r_weight), True)

        def second_layer(item):
            rows_in, keys_ok, crop_row, keep_row = item
            return image_layer(rows_in, keys_ok, crop_row, keep_row, (q_weight[1], o_weight[1], u_weight[1], d_weight[1], gain_first[1], gain_second[1], r_weight), False)
        first_out = lax.map(jax.checkpoint(first_layer), (inputs, picked, crop_all, keep_all))
        passed = low(low_back(first_out)) + gap
        second_out = lax.map(jax.checkpoint(second_layer), (passed, everyone, crop_all, keep_all))
        return (first_out, second_out)
    params = tuple((w.astype(jnp.float32) for w in (w_qkv, w_out, w_up, w_down, ln1_gain, ln2_gain, router)))
    gap = jnp.zeros((images, SLOT, D), jnp.float32)
    (first_out, second_out), pull = jax.vjp(forward, inputs, gap, *params)
    grads = pull((jnp.zeros_like(first_out), cotangent.astype(jnp.float32).reshape(images, SLOT, D)))
    grad_x, grad_gap, grad_q, grad_o, grad_u, grad_d, grad_one, grad_two, grad_r = grads
    shape = (MICRO, N_DP * IMG_MB * SLOT, D)
    activations = jnp.stack([first_out.reshape(shape), second_out.reshape(shape)]).astype(jnp.bfloat16)
    input_grads = jnp.stack([grad_x.reshape(shape), grad_gap.reshape(shape)])
    return (activations, input_grads, grad_q, grad_o, grad_u, grad_d, grad_one, grad_two, grad_r)
```

```python
import functools

import jax
import jax.numpy as jnp
from jax import lax
from jax.experimental import pallas as pl
from jax.experimental.pallas import tpu as pltpu
from jax.sharding import PartitionSpec as P

HEAD_DIM = 64
LANES = 128
CUT = 197
EPS = 1e-06
NEG = -1000000000.0
ROWS = 384
TILE = 64
QROWS = 128
MESH = pl.DeviceIdType.MESH
NT = (((1,), (1,)), ((), ()))
TN = (((0,), (0,)), ((), ()))
NN = (((1,), (0,)), ((), ()))
VMEM_BYTES = 62 * 1024 * 1024
F32, BF16 = jnp.float32, jnp.bfloat16


def dot(left, right, dims=NN):
    return lax.dot_general(left, right, dims, preferred_element_type=F32)


def tiles(body, rows=ROWS, tile=TILE):
    def step(index, carry):
        body(pl.ds(pl.multiple_of(index * tile, tile), tile))
        return carry

    lax.fori_loop(0, rows // tile, step, 0)


def standardize(values):
    centre = values - jnp.mean(values, axis=-1, keepdims=True)
    spread = jnp.mean(centre * centre, axis=-1, keepdims=True)
    rstd = lax.rsqrt(spread + EPS)
    return centre * rstd, rstd


def norm_pull(xhat, rstd, gain, grad):
    grad_hat = grad * gain
    mean_grad = jnp.mean(grad_hat, axis=-1, keepdims=True)
    mean_both = jnp.mean(grad_hat * xhat, axis=-1, keepdims=True)
    return rstd * (grad_hat - mean_grad - xhat * mean_both)


def fold_rows(values):
    return jnp.sum(values.reshape(values.shape[0] // 8, 8, values.shape[1]), axis=0)


def half_masks():
    lane = lax.broadcasted_iota(jnp.int32, (1, LANES), 1)
    return [lane < HEAD_DIM, lane >= HEAD_DIM]


def softmax_rows(scores):
    expo = jnp.exp(scores - jnp.max(scores, axis=-1, keepdims=True))
    return expo * (1.0 / jnp.sum(expo, axis=-1, keepdims=True))


def only(mask, values):
    return jnp.where(mask, values, jnp.zeros_like(values))


class Place:
    def __init__(self):
        self.s = lax.axis_index("section")
        self.d = lax.axis_index("dp")
        self.t = lax.axis_index("tensor")
        self.x = self.t % 2
        self.y = self.t // 2
        self.near = self.t + (1 - self.s) * (1 - 2 * self.x) + self.s * (2 - 4 * self.y)
        self.far = self.t + self.s * (1 - 2 * self.x) + (1 - self.s) * (2 - 4 * self.y)
        self.cross = 3 - self.t
        self.sibling = (1 - self.s, self.d, self.t)

    def at(self, tensor):
        return (self.s, self.d, tensor)


def remote(src, dst, send, recv, device):
    return pltpu.make_async_remote_copy(
        src_ref=src, dst_ref=dst, send_sem=send, recv_sem=recv, device_id=device, device_id_type=MESH
    )


def greet(peers):
    barrier = pltpu.get_barrier_semaphore()
    for peer in peers:
        pl.semaphore_signal(barrier, inc=1, device_id=peer, device_id_type=MESH)
    pl.semaphore_wait(barrier, len(peers))


KINDS = 4
CHUNKS = [(0, 0), (1, 0), (2, 0), (2, 1), (3, 0), (3, 1)]
WINDOW = 3


def forward_kernel(
    x_ref, keep_ref, bias_ref, gain_ref, router_ref, wq_ref, wo_ref, wu_ref, wd_ref,
    y_ref, gq_out, go_out, gu_out, gd_out, norm_out, qkv_out, mixed_out, hidden_out,
    second_out, active_out, slope_out, branch_out,
    gq, go, gu, gd, normed, qkv, mixed, hidden, second, active, slope, branch, work,
    own_sem, lend_send, lend_recv, a_send, a_recv, b_send, b_recv, c_send, c_recv,
    e_send, e_recv, out_sem, save_sem,
):
    here = Place()
    part = wo_ref.shape[0]
    unit = wu_ref.shape[0] // 4
    shards = (wq_ref, wo_ref, wu_ref, wd_ref)

    def block(kind, layer, quarter):
        rows = pl.ds(pl.multiple_of(quarter * part, part), part)
        if kind == 0:
            return gq.at[layer, :, rows, :]
        if kind == 1:
            return go.at[layer, rows, :]
        return (gu if kind == 2 else gd).at[layer, quarter]

    def chunk(layer, index, quarter, half):
        kind, piece = CHUNKS[index]
        if kind < 2:
            rows = pl.ds(pl.multiple_of(quarter * part + half * (part // 2), part // 2), part // 2)
            return gq.at[layer, :, rows, :] if kind == 0 else go.at[layer, rows, :]
        rows = pl.ds(pl.multiple_of((2 * half + piece) * unit, unit), unit)
        return (gu if kind == 2 else gd).at[layer, quarter, rows, :]

    def own_copy(kind):
        return pltpu.make_async_copy(shards[kind], block(kind, here.s, here.t), own_sem.at[kind])

    def lend(kind, layer):
        return remote(
            shards[kind], block(kind, layer, here.t), lend_send.at[kind], lend_recv.at[kind], here.sibling
        )

    def along(which, step, quarter, peer, sems):
        piece = chunk(step // 6, step % 6, quarter, here.s)
        return remote(piece, piece, sems[0].at[step], sems[1].at[step], peer)

    def send_a(step):
        return along("a", step, here.t, here.at(here.near), (a_send, a_recv))

    def send_b(step):
        return along("b", step, here.t, here.at(here.far), (b_send, b_recv))

    def send_c(step):
        return along("c", step, here.near, here.at(here.far), (c_send, c_recv))

    def send_e(step, which, quarter):
        piece = chunk(step // 6, step % 6, quarter, here.s)
        return remote(piece, piece, e_send.at[step, which], e_recv.at[step, which], here.sibling)

    def landed_e(step, which, quarter):
        piece = chunk(step // 6, step % 6, quarter, 1 - here.s)
        return remote(piece, piece, e_send.at[step, which], e_recv.at[step, which], here.sibling)

    greet([here.sibling, here.at(here.near), here.at(here.far)])
    for kind in range(KINDS):
        lend(kind, here.s).start()
        own_copy(kind).start()

    def issue(step):
        if step >= 12:
            return
        layer, (kind, piece) = step // 6, CHUNKS[step % 6]
        if piece == 0:
            pl.when(here.s == layer)(lambda: own_copy(kind).wait())
            pl.when(here.s != layer)(lambda: lend(kind, layer).wait_recv())
        send_a(step).start()
        send_b(step).start()

    def pump(step):
        send_a(step).wait_recv()
        send_c(step).start()
        send_e(step, 0, here.near).start()
        issue(step + WINDOW)
        send_b(step).wait_recv()
        send_e(step, 1, here.far).start()
        send_c(step).wait_recv()
        send_e(step, 2, here.cross).start()
        for which in range(3):
            landed_e(step, which, here.cross).wait_recv()

    for step in range(WINDOW):
        issue(step)

    masks = half_masks()
    saves = []

    def save(index, layer, src, dst):
        copy = pltpu.make_async_copy(src, dst.at[layer], save_sem.at[index])
        copy.start()
        return copy

    for layer in range(2):
        x_now = x_ref if layer == 0 else y_ref.at[0]

        def first_norm(rows):
            xhat, _ = standardize(x_now[rows, :].astype(F32))
            normed[rows, :] = (xhat * gain_ref[pl.ds(2 * layer, 1), :]).astype(BF16)

        for copy in saves:
            copy.wait()
        saves = []
        tiles(first_norm)
        saves.append(save(0, layer, normed, norm_out))
        pump(6 * layer)

        def project(j, carry):
            qkv[j] = dot(normed[...], gq[layer, j], NT).astype(BF16)
            return carry

        lax.fori_loop(0, 3, project, 0)
        saves.append(save(1, layer, qkv, qkv_out))

        def attend(pair, carry):
            cols = pl.ds(pl.multiple_of(pair * LANES, LANES), LANES)
            key, value = qkv[1, :, cols], qkv[2, :, cols]

            def query_rows(rows):
                query = qkv[0, rows, cols] * BF16(0.125)
                outs = []
                for mask in masks:
                    scores = dot(only(mask, query), key, NT) + bias_ref[layer, rows, :]
                    outs.append(dot(softmax_rows(scores).astype(BF16), value))
                mixed[rows, cols] = jnp.where(masks[0], outs[0], outs[1]).astype(BF16)

            tiles(query_rows, tile=QROWS)
            return carry

        lax.fori_loop(0, mixed.shape[1] // LANES, attend, 0)
        saves.append(save(2, layer, mixed, mixed_out))
        pump(6 * layer + 1)
        branch[...] = dot(mixed[...], go[layer])

        def second_norm(rows):
            value = x_now[rows, :].astype(F32) + branch[rows, :]
            hidden[rows, :] = value
            xhat, _ = standardize(value)
            second[rows, :] = (xhat * gain_ref[pl.ds(2 * layer + 1, 1), :]).astype(BF16)

        tiles(second_norm)
        saves.append(save(3, layer, hidden, hidden_out))
        saves.append(save(4, layer, second, second_out))
        pump(6 * layer + 2)
        pump(6 * layer + 3)

        def widen(g, carry):
            work[...] = dot(second[...], gu[layer, g])

            def bend(rows):
                upper = work[rows, :]
                phi = 0.5 * (1.0 + lax.erf(upper * 0.7071067811865476))
                bell = jnp.exp(-0.5 * upper * upper) * 0.3989422804014327
                active[g, rows, :] = (upper * phi).astype(BF16)
                slope[g, rows, :] = (phi + upper * bell).astype(BF16)

            tiles(bend, tile=32)
            return carry

        lax.fori_loop(0, 4, widen, 0)
        saves.append(save(5, layer, active, active_out))
        saves.append(save(6, layer, slope, slope_out))
        pump(6 * layer + 4)
        pump(6 * layer + 5)

        def narrow(g, carry):
            branch[...] += dot(active[g], gd[layer, g])
            return carry

        lax.fori_loop(0, 4, narrow, 0)
        saves.append(save(7, layer, branch, branch_out))

        def finish(rows):
            value = x_now[rows, :].astype(F32)
            change = branch[rows, :]
            if layer == 0:
                logit = jnp.sum(value * router_ref[...], axis=-1, keepdims=True)
                change = change * (keep_ref[rows, :] / (1.0 + jnp.exp(-logit)))
            y_ref[layer, rows, :] = (value + change).astype(BF16)

        tiles(finish)
        for index, (src, dst) in enumerate(((gq, gq_out), (go, go_out), (gu, gu_out), (gd, gd_out))):
            pltpu.make_async_copy(src.at[layer], dst.at[layer], out_sem.at[layer, index]).start()

    for copy in saves:
        copy.wait()
    for layer in range(2):
        for index, (src, dst) in enumerate(((gq, gq_out), (go, go_out), (gu, gu_out), (gd, gd_out))):
            pltpu.make_async_copy(src.at[layer], dst.at[layer], out_sem.at[layer, index]).wait()
    for kind in range(KINDS):
        lend(kind, here.s).wait_send()
    for step in range(12):
        send_a(step).wait_send()
        send_b(step).wait_send()
        send_c(step).wait_send()
        for which in range(3):
            send_e(step, which, here.cross).wait_send()


def forward(x, keep, bias, gains, router, wq, wo, wu, wd):
    width = x.shape[1]
    ff = 4 * width
    any_spec = pl.BlockSpec(memory_space=pl.ANY)
    vmem = pl.BlockSpec(memory_space=pltpu.VMEM)

    def pair(*shape, dtype=BF16):
        return jax.ShapeDtypeStruct((2, *shape), dtype)

    shapes = [
        pair(ROWS, width),
        pair(3, width, width), pair(width, width), pair(4, width, width), pair(4, width, width),
        pair(ROWS, width), pair(3, ROWS, width), pair(ROWS, width), pair(ROWS, width, dtype=F32),
        pair(ROWS, width), pair(4, ROWS, width), pair(4, ROWS, width), pair(ROWS, width, dtype=F32),
    ]
    dma = pltpu.SemaphoreType.DMA
    scratch = [
        pltpu.VMEM((2, 3, width, width), BF16), pltpu.VMEM((2, width, width), BF16),
        pltpu.VMEM((2, 4, width, width), BF16), pltpu.VMEM((2, 4, width, width), BF16),
        pltpu.VMEM((ROWS, width), BF16), pltpu.VMEM((3, ROWS, width), BF16),
        pltpu.VMEM((ROWS, width), BF16), pltpu.VMEM((ROWS, width), F32),
        pltpu.VMEM((ROWS, width), BF16), pltpu.VMEM((4, ROWS, width), BF16),
        pltpu.VMEM((4, ROWS, width), BF16), pltpu.VMEM((ROWS, width), F32),
        pltpu.VMEM((ROWS, width), F32),
        dma((KINDS,)), dma((KINDS,)), dma((KINDS,)),
        dma((12,)), dma((12,)), dma((12,)), dma((12,)), dma((12,)), dma((12,)),
        dma((12, 3)), dma((12, 3)), dma((2, KINDS)), dma((8,)),
    ]
    return pl.pallas_call(
        forward_kernel,
        out_shape=shapes,
        in_specs=[vmem] * 5 + [any_spec] * 4,
        out_specs=[vmem] + [any_spec] * 12,
        scratch_shapes=scratch,
        compiler_params=pltpu.CompilerParams(
            collective_id=0, has_side_effects=True, vmem_limit_bytes=VMEM_BYTES
        ),
        cost_estimate=pl.CostEstimate(flops=24 * ROWS * width * width * 2, bytes_accessed=60_000_000, transcendentals=0),
        name="forward_layers",
    )(x, keep, bias, gains, router, wq, wo, wu, wd)


UNITS = 12
RING = 6


def backward_kernel(
    layer, in_kernel_z,
    grad_ref, x_ref, keep_ref, bias_ref, gain_ref, router_ref,
    gq, go, gu, gd, norm_in, qkv_in, mixed_in, hidden_in, second_in, active_in, slope_in, branch_in,
    dx_ref, small_ref, mlp_out, att_out,
    wq, wo, wu, wd, normed, qkv, mixed, hidden, second, active, slope, branch,
    dbranch, dfed, dfed_t, work, dup, dsecond, datt, dmixed, dqkv, dkv_sum, stage, sib, near_in, far_in, plane,
    load_sem, wu_sem, wd_sem, slope_sem,
    sib_send, sib_recv, near_send, near_recv, far_send, far_recv,
    mlp_send, mlp_recv, att_send, att_recv, local_sem,
):
    here = Place()
    s, d, t = here.s, here.d, here.t
    quarter_rows = stage.shape[2]
    half_rows = quarter_rows // 2
    my_rows = pl.ds(pl.multiple_of(s * half_rows, half_rows), half_rows)
    their_rows = pl.ds(pl.multiple_of((1 - s) * half_rows, half_rows), half_rows)
    n_dp = lax.axis_size("dp")

    loads = {}

    def load(name, src, dst):
        loads[name] = pltpu.make_async_copy(src, dst, load_sem.at[len(loads)])
        loads[name].start()

    def quarter_load(src, dst, sems, g):
        return pltpu.make_async_copy(src.at[layer, g], dst.at[g % 2], sems.at[g % 2])

    load("active", active_in.at[layer], active)
    if layer == 0:
        load("branch", branch_in.at[layer], branch)
    streams = ((gd, wd, wd_sem), (slope_in, slope, slope_sem), (gu, wu, wu_sem))
    for g in range(2):
        for stream in streams:
            quarter_load(*stream, g).start()
    load("second", second_in.at[layer], second)
    load("hidden", hidden_in.at[layer], hidden)
    load("mixed", mixed_in.at[layer], mixed)
    load("wo", go.at[layer], wo)
    load("qkv", qkv_in.at[layer], qkv)
    load("normed", norm_in.at[layer], normed)
    load("wq", gq.at[layer], wq)

    peers = [here.sibling, here.at(here.near), here.at(here.far)]
    if in_kernel_z:
        for shift in range(1, n_dp):
            for section in range(2):
                peers.append((section, (d + shift) % n_dp, t))
    greet(peers)

    near_sent = [s * (2 * (1 - here.y) + i) + (1 - s) * (2 * i + 1 - here.x) for i in range(2)]
    own_slot = s * here.x + (1 - s) * here.y

    def to_sibling(u):
        return remote(
            stage.at[u % RING, :, their_rows, :], sib.at[u], sib_send.at[u], sib_recv.at[u], here.sibling
        )

    def to_near(u, i):
        return remote(
            stage.at[u % RING, near_sent[i], my_rows, :], near_in.at[u, i],
            near_send.at[u, i], near_recv.at[u, i], here.at(here.near),
        )

    def to_far(u):
        return remote(
            stage.at[u % RING, here.far, my_rows, :], far_in.at[u],
            far_send.at[u], far_recv.at[u], here.at(here.far),
        )

    def give(u):
        to_sibling(u).start()

    def first(u):
        to_sibling(u).wait_recv()

        def add(q, carry):
            stage[u % RING, q, my_rows, :] = (
                stage[u % RING, q, my_rows, :].astype(F32) + sib[u, q].astype(F32)
            ).astype(BF16)
            return carry

        lax.fori_loop(0, 4, add, 0)
        for i in range(2):
            to_near(u, i).start()

    def second_step(u):
        for i in range(2):
            to_near(u, i).wait_recv()
        stage[u % RING, here.far, my_rows, :] = (
            stage[u % RING, here.far, my_rows, :].astype(F32) + near_in[u, 1 - own_slot].astype(F32)
        ).astype(BF16)
        to_far(u).start()

    def z_moves(u):
        moves = []
        if not in_kernel_z:
            target = mlp_out.at[u, my_rows, :]
            mine = s == layer
            moves.append((mine, pltpu.make_async_copy(plane.at[u], target, local_sem.at[u, 0]), remote(
                plane.at[u], target, mlp_send.at[u], mlp_recv.at[u, 0, s], (layer, d, t))))
        elif u < 8:
            target = mlp_out.at[u // 4, d, my_rows, :]
            mine = (s == layer) & (d == u % 4)
            moves.append((mine, pltpu.make_async_copy(plane.at[u], target, local_sem.at[u, 0]), remote(
                plane.at[u], target, mlp_send.at[u], mlp_recv.at[u // 4, d, s], (layer, u % 4, t))))
        else:
            for other in range(4):
                lanes = plane.shape[2] // 4 * other // LANES * LANES
                piece = plane.at[u, :, pl.ds(lanes, 2 * LANES)]
                target = att_out.at[u - 8, d, my_rows, :]
                mine = (s == layer) & (d == other)
                moves.append((mine, pltpu.make_async_copy(piece, target, local_sem.at[u, other]), remote(
                    piece, target, att_send.at[u - 8, other], att_recv.at[u - 8, d, s], (layer, other, t))))
        return moves

    def third(u):
        to_far(u).wait_recv()
        plane[u] = (
            stage[u % RING, t, my_rows, :].astype(F32)
            + near_in[u, own_slot].astype(F32) + far_in[u].astype(F32)
        ).astype(BF16)
        for mine, local, away in z_moves(u):
            pl.when(mine)(local.start)
            pl.when(jnp.logical_not(mine))(away.start)
        to_sibling(u).wait_send()
        for i in range(2):
            to_near(u, i).wait_send()
        to_far(u).wait_send()

    done = [0, 0, 0]

    def progress(*upto):
        for which, (step, limit) in enumerate(zip((first, second_step, third), upto)):
            while done[which] < min(limit, UNITS):
                step(done[which])
                done[which] += 1

    def slot(u):
        give(u)
        progress(u, u - 2, u - 4)

    def prepare(rows):
        grad = grad_ref[rows, :].astype(BF16).astype(F32)
        if layer == 0:
            value = x_ref[rows, :].astype(F32)
            logit = jnp.sum(value * router_ref[...], axis=-1, keepdims=True)
            sigma = 1.0 / (1.0 + jnp.exp(-logit))
            keep = keep_ref[rows, :]
            dlogit = jnp.sum(grad * branch[rows, :], axis=-1, keepdims=True) * keep * sigma * (1.0 - sigma)
            small_ref[2] += fold_rows(value * dlogit)
            dx_ref[rows, :] = grad + dlogit * router_ref[...]
            grad = grad * (sigma * keep)
        else:
            dx_ref[rows, :] = grad
        dbranch[rows, :] = grad
        dfed[rows, :] = grad.astype(BF16)

    small_ref[...] = jnp.zeros_like(small_ref)
    if layer == 0:
        loads["branch"].wait()
    tiles(prepare)

    def transpose(src, dst):
        def step(index, carry):
            cols = pl.ds(pl.multiple_of(index * LANES, LANES), LANES)
            dst[cols, :] = src[:, cols].astype(F32).T.astype(BF16)
            return carry

        lax.fori_loop(0, dst.shape[0] // LANES, step, 0)

    def rows_unit(u, k, left, right):
        rows = pl.ds(k * quarter_rows, quarter_rows)

        def step(g, carry):
            stage[u % RING, g] = dot(left[rows, :], right[g]).astype(BF16)
            return carry

        lax.fori_loop(0, 4, step, 0)

    transpose(dfed, dfed_t)
    loads["active"].wait()
    for k in range(4):
        g = k
        rows_unit(k, k, dfed_t, active)
        slot(k)
        for stream in streams:
            quarter_load(*stream, g).wait()
        work[...] = dot(dfed[...], wd[g % 2], NT)

        def bend(rows):
            dup[g, rows, :] = (work[rows, :] * slope[g % 2, rows, :].astype(F32)).astype(BF16)

        tiles(bend)
        part = dot(dup[g], wu[g % 2], NT)
        if g == 0:
            dsecond[...] = part
        else:
            dsecond[...] += part
        if g < 2:
            for stream in streams:
                quarter_load(*stream, g + 2).start()

    loads["second"].wait()
    transpose(second, dfed_t)
    for k in range(4):
        rows_unit(4 + k, k, dfed_t, dup)
        slot(4 + k)

    loads["hidden"].wait()

    def second_pull(rows):
        xhat, rstd = standardize(hidden[rows, :])
        grad = dsecond[rows, :]
        small_ref[1] += fold_rows(grad * xhat)
        dhidden = norm_pull(xhat, rstd, gain_ref[pl.ds(2 * layer + 1, 1), :], grad)
        dx_ref[rows, :] += dhidden
        datt[rows, :] = (dbranch[rows, :] + dhidden).astype(BF16)

    tiles(second_pull)

    def square_unit(u, left, right):
        width = left.shape[1] // 2

        def step(c, carry):
            cols = pl.ds(pl.multiple_of(c * width, width), width)
            product = dot(left[:, cols], right[...], TN).astype(BF16)
            stage[u % RING, pl.ds(2 * c, 2)] = product.reshape(2, quarter_rows, product.shape[1])
            return carry

        lax.fori_loop(0, 2, step, 0)

    loads["mixed"].wait()
    square_unit(8, mixed, datt)
    slot(8)
    loads["wo"].wait()
    dmixed[...] = dot(datt[...], wo[...], NT).astype(BF16)
    loads["qkv"].wait()
    masks = half_masks()

    def attend(pair, carry):
        cols = pl.ds(pl.multiple_of(pair * LANES, LANES), LANES)
        key, value = qkv[1, :, cols], qkv[2, :, cols]
        scaled = key * BF16(0.125)
        dkv_sum[...] = jnp.zeros_like(dkv_sum)

        def query_rows(rows):
            query = qkv[0, rows, cols] * BF16(0.125)
            grad = dmixed[rows, cols]
            dquery = jnp.zeros((QROWS, LANES), F32)
            for mask in masks:
                query_head, grad_head = only(mask, query), only(mask, grad)
                probs = softmax_rows(dot(query_head, key, NT) + bias_ref[layer, rows, :])
                dprobs = dot(grad_head, value, NT)
                dscores = probs * (dprobs - jnp.sum(probs * dprobs, axis=-1, keepdims=True))
                dscores = dscores.astype(BF16)
                dquery += dot(dscores, only(mask, scaled))
                dkv_sum[0] += dot(dscores, query_head, TN)
                dkv_sum[1] += dot(probs.astype(BF16), grad_head, TN)
            dqkv[0, rows, cols] = dquery.astype(BF16)

        tiles(query_rows, tile=QROWS)
        dqkv[1, :, cols] = dkv_sum[0].astype(BF16)
        dqkv[2, :, cols] = dkv_sum[1].astype(BF16)
        return carry

    pairs = dmixed.shape[1] // LANES
    for third_part in range(3):
        lax.fori_loop(pairs * third_part // 3, pairs * (third_part + 1) // 3, attend, 0)
        progress(9, 7 + third_part, 5 + third_part)

    loads["normed"].wait()
    for j in range(3):
        square_unit(9 + j, dqkv.at[j], normed)
        give(9 + j)
        progress(9 + j, 9, 7 + j)
    loads["wq"].wait()
    work[...] = dot(dqkv[0], wq[0])
    work[...] += dot(dqkv[1], wq[1])
    progress(12, 10, 9)
    work[...] += dot(dqkv[2], wq[2])

    def first_pull(rows):
        xhat, rstd = standardize(x_ref[rows, :].astype(F32))
        grad = work[rows, :]
        small_ref[0] += fold_rows(grad * xhat)
        dx_ref[rows, :] += norm_pull(xhat, rstd, gain_ref[pl.ds(2 * layer, 1), :], grad)

    tiles(first_pull)
    progress(12, 11, 10)
    progress(12, 12, 11)
    progress(12, 12, 12)

    for u in range(UNITS):
        for mine, local, away in z_moves(u):
            pl.when(mine)(local.wait)
            pl.when(jnp.logical_not(mine))(away.wait_send)

    @pl.when(s == layer)
    def _():
        if not in_kernel_z:
            for u in range(UNITS):
                remote(
                    plane.at[u], mlp_out.at[u, their_rows, :], mlp_send.at[u], mlp_recv.at[u, 0, 1 - layer],
                    here.sibling,
                ).wait_recv()
            return
        for source in range(4):
            for half in range(2):
                rows = pl.ds(half * half_rows, half_rows)

                def arrive():
                    for kind in range(2):
                        target = mlp_out.at[kind, source, rows, :]
                        remote(
                            target, target, mlp_send.at[0], mlp_recv.at[kind, source, half], here.sibling
                        ).wait_recv()
                    for b in range(4):
                        target = att_out.at[b, source, rows, :]
                        remote(
                            target, target, att_send.at[0, 0], att_recv.at[b, source, half], here.sibling
                        ).wait_recv()

                if half == layer:
                    pl.when(d != source)(arrive)
                else:
                    arrive()


def backward(layer, n_dp, grad, x, keep, bias, gains, router, saved):
    width = x.shape[1]
    quarter_rows = width // 4
    half_rows = quarter_rows // 2
    in_kernel_z = n_dp == 4
    any_spec = pl.BlockSpec(memory_space=pl.ANY)
    vmem = pl.BlockSpec(memory_space=pltpu.VMEM)
    dma = pltpu.SemaphoreType.DMA

    def low(*shape):
        return pltpu.VMEM(shape, BF16)

    def wide(*shape):
        return pltpu.VMEM(shape, F32)

    mlp_shape = (2, 4, quarter_rows, width) if in_kernel_z else (UNITS, quarter_rows, width)
    scratch = [
        low(3, width, width), low(width, width), low(2, width, width), low(2, width, width),
        low(ROWS, width), low(3, ROWS, width), low(ROWS, width), wide(ROWS, width), low(ROWS, width),
        low(4, ROWS, width), low(2, ROWS, width), wide(ROWS, width) if layer == 0 else wide(8, LANES),
        wide(ROWS, width), low(ROWS, width), low(width, ROWS), wide(ROWS, width), low(4, ROWS, width),
        wide(ROWS, width), low(ROWS, width), low(ROWS, width), low(3, ROWS, width), wide(2, ROWS, LANES),
        low(RING, 4, quarter_rows, width), low(UNITS, 4, half_rows, width), low(UNITS, 2, half_rows, width),
        low(UNITS, half_rows, width), low(UNITS, half_rows, width),
        dma((9,)), dma((2,)), dma((2,)), dma((2,)),
        dma((UNITS,)), dma((UNITS,)), dma((UNITS, 2)), dma((UNITS, 2)), dma((UNITS,)), dma((UNITS,)),
        dma((UNITS,)), dma((UNITS, 4, 2)), dma((4, 4)), dma((4, 4, 2)), dma((UNITS, 4)),
    ]
    return pl.pallas_call(
        functools.partial(backward_kernel, layer, in_kernel_z),
        out_shape=[
            jax.ShapeDtypeStruct((ROWS, width), F32),
            jax.ShapeDtypeStruct((3, 8, width), F32),
            jax.ShapeDtypeStruct(mlp_shape, BF16),
            jax.ShapeDtypeStruct((4, 4, quarter_rows, 2 * LANES), BF16),
        ],
        in_specs=[vmem] * 6 + [any_spec] * 12,
        out_specs=[vmem, vmem, any_spec, any_spec],
        scratch_shapes=scratch,
        compiler_params=pltpu.CompilerParams(
            collective_id=2 - layer, has_side_effects=True, vmem_limit_bytes=VMEM_BYTES
        ),
        cost_estimate=pl.CostEstimate(flops=48 * ROWS * width * width, bytes_accessed=60_000_000, transcendentals=0),
        name="backward_layer",
    )(grad, x, keep, bias, gains, router, *saved)


def on_device(
    patches, cotangent, crop_lengths, route_mask, w_qkv, w_out, w_up, w_down, ln1_gain, ln2_gain, router
):
    micro, tok_rows, width = patches.shape
    images = crop_lengths.shape[1]
    slot_len = route_mask.shape[1] // images
    s = lax.axis_index("section")
    t = lax.axis_index("tensor")
    x_half, image = t % 2, t // 2
    held = -(-tok_rows // 16) * 16
    low = CUT // 16 * 16
    spare = held - low
    quarters = lax.axis_size("tensor")
    swap = [(0, 1), (1, 0)]
    to_rest = [(q, q + 1) for q in range(0, quarters, 2)]
    to_first = [(q + 1, q) for q in range(0, quarters, 2)]

    both = jnp.stack([patches[:, :, :], cotangent[:, :, :]])
    mine = lax.dynamic_index_in_dim(both, s, 1, keepdims=False)
    mine = jnp.pad(mine, ((0, 0), (0, held - tok_rows), (0, 0)))
    extra = lax.ppermute(mine[:, low:], "tensor", to_rest)
    row = jnp.arange(ROWS, dtype=jnp.int32)
    position = jnp.where(
        x_half == 0, row, jnp.where(row < held, tok_rows + row, low + row - held)
    )
    valid = jnp.where(
        x_half == 0,
        row < CUT,
        jnp.where(
            row < held,
            row < tok_rows,
            (position >= CUT) & (position < tok_rows) & (row < held + spare),
        ),
    )
    tail = jnp.zeros((2, ROWS - held - spare, width), BF16)
    block = jnp.where(valid[None, :, None], jnp.concatenate([mine, extra, tail], axis=1), 0)
    lengths = crop_lengths[s, image]
    crop = jnp.sum((position[:, None] >= jnp.cumsum(lengths)[None, :]).astype(jnp.int32), axis=1)
    crop = jnp.where(valid, crop, -1)
    routes = lax.dynamic_slice(route_mask, (s, image * slot_len), (1, slot_len))[0]
    routes = jnp.pad(routes, (0, ROWS))
    routed = jnp.where(
        x_half == 0,
        routes[:ROWS],
        jnp.concatenate(
            [routes[tok_rows : tok_rows + held], routes[low:held], jnp.zeros((ROWS - held - spare,), jnp.int32)]
        ),
    )
    keep = jnp.where(valid, routed, 1)
    same = crop[:, None] == crop[None, :]
    bias = jnp.stack(
        [jnp.where(same & (keep > 0)[None, :], 0.0, NEG), jnp.where(same, 0.0, NEG)]
    ).astype(F32)
    keep_rows = jnp.where(valid, routed, 0).astype(F32)[:, None]

    gains = jnp.concatenate([ln1_gain, ln2_gain], axis=0)
    other = lax.ppermute(gains, "section", swap)
    gains = jnp.where(s == 0, jnp.concatenate([gains, other]), jnp.concatenate([other, gains]))
    gains = jnp.pad(gains, ((0, 4), (0, 0)))
    router_row = router.astype(F32)[None, :]

    wq = jnp.transpose(w_qkv[0], (1, 2, 0))
    outs = forward(block[0], keep_rows, bias, gains, router_row, wq, w_out[0], w_up[0], w_down[0])
    y = outs[0]

    saved = outs[1:]
    n_dp = lax.axis_size("dp")
    d = lax.axis_index("dp")
    common = (keep_rows, bias, gains, router_row, saved)
    late = backward(1, n_dp, block[1], y[0], *common)
    early = backward(0, n_dp, late[0], block[0], *common)

    def hand_back(rows, kind):
        back = lax.ppermute(rows[:, held : held + spare].astype(BF16), "tensor", to_first).astype(kind)
        back = jnp.concatenate([rows[:, :low], back], axis=1)[:, :tok_rows]
        is_back = (x_half == 0) & (jnp.arange(tok_rows) >= CUT)
        full = jnp.where(is_back[None, :, None], back, rows[:, :tok_rows])
        keep_here = lax.dynamic_index_in_dim(full, s, 0, keepdims=False)
        give = lax.dynamic_index_in_dim(full, 1 - s, 0, keepdims=False)
        take = lax.ppermute(give.astype(BF16), "section", swap).astype(kind)
        return jnp.where(s == 0, jnp.stack([keep_here, take]), jnp.stack([take, keep_here]))

    outputs = hand_back(y, BF16)
    input_grads = hand_back(jnp.stack([early[0], late[0]]), F32)

    share = width // n_dp
    if n_dp == 4:
        mlp = jnp.where(s == 0, early[2], late[2]).astype(F32).sum(axis=1)
        att = jnp.where(s == 0, early[3], late[3]).astype(F32).sum(axis=1)
        att = jnp.where(d % 2 == 0, att[:, :, :share], att[:, :, -share:])
        down, up = mlp[0].T, mlp[1]
        out, qkv = att[0], att[1:]
        qkv = jnp.transpose(qkv, (2, 0, 1))
    else:
        plane = jnp.where(s == 0, early[2], late[2])

        def scatter(value, dim):
            return lax.psum_scatter(value, "dp", scatter_dimension=dim, tiled=True).astype(F32)

        down = scatter(plane[:4].reshape(width, width), 0).T
        up = scatter(plane[4:8].reshape(width, width), 0)
        out = scatter(plane[8], 1)
        qkv = jnp.transpose(scatter(plane[9:], 2), (2, 0, 1))

    small = jnp.concatenate([early[1].sum(axis=1), late[1].sum(axis=1)[:2]])
    small = lax.psum(small, ("section", "dp", "tensor"))
    ones = jnp.where(s == 0, small[0], small[3])
    twos = jnp.where(s == 0, small[1], small[4])
    place = d * quarters + t
    span = width // (n_dp * quarters)
    ones = lax.dynamic_slice_in_dim(ones, place * span, span)
    twos = lax.dynamic_slice_in_dim(twos, place * span, span)
    routers = lax.dynamic_slice_in_dim(small[2], (s * n_dp * quarters + place) * (span // 2), span // 2)
    return (
        outputs[None], input_grads[None], qkv[None], out[None], up[None], down[None],
        ones[None], twos[None], routers,
    )


def solution(mesh):
    return jax.shard_map(
        on_device,
        mesh=mesh,
        in_specs=(
            P(None, ("dp", "tensor"), None),
            P(None, ("dp", "tensor"), None),
            P(None, "dp", None),
            P(None, "dp"),
            P("section", None, None, "tensor"),
            P("section", "tensor", None),
            P("section", None, "tensor"),
            P("section", "tensor", None),
            P("section", None),
            P("section", None),
            P(),
        ),
        out_specs=(
            P("section", None, ("dp", "tensor"), None),
            P("section", None, ("dp", "tensor"), None),
            P("section", "dp", None, "tensor"),
            P("section", "tensor", "dp"),
            P("section", "dp", "tensor"),
            P("section", "tensor", "dp"),
            P("section", ("dp", "tensor")),
            P("section", ("dp", "tensor")),
            P(("section", "dp", "tensor")),
        ),
        check_vma=False,
    )
```

```python
import functools

import jax
import jax.numpy as jnp
from jax import lax
from jax.experimental import pallas as pl
from jax.experimental.pallas import tpu as pltpu
from jax.sharding import PartitionSpec as P

HEAD_DIM = 64
LANES = 128
CUT = 197
EPS = 1e-06
NEG = -1000000000.0
ROWS = 384
TILE = 64
MESH = pl.DeviceIdType.MESH
NT = (((1,), (1,)), ((), ()))
TN = (((0,), (0,)), ((), ()))
NN = (((1,), (0,)), ((), ()))
VMEM_BYTES = 62 * 1024 * 1024
F32, BF16 = jnp.float32, jnp.bfloat16


def dot(left, right, dims=NN):
    return lax.dot_general(left, right, dims, preferred_element_type=F32)


def tiles(body, rows=ROWS, tile=TILE):
    def step(index, carry):
        body(pl.ds(pl.multiple_of(index * tile, tile), tile))
        return carry

    lax.fori_loop(0, rows // tile, step, 0)


def standardize(values):
    centre = values - jnp.mean(values, axis=-1, keepdims=True)
    spread = jnp.mean(centre * centre, axis=-1, keepdims=True)
    rstd = lax.rsqrt(spread + EPS)
    return centre * rstd, rstd


def norm_pull(xhat, rstd, gain, grad):
    grad_hat = grad * gain
    mean_grad = jnp.mean(grad_hat, axis=-1, keepdims=True)
    mean_both = jnp.mean(grad_hat * xhat, axis=-1, keepdims=True)
    return rstd * (grad_hat - mean_grad - xhat * mean_both)


def fold_rows(values):
    return jnp.sum(values.reshape(values.shape[0] // 8, 8, values.shape[1]), axis=0)


def half_masks():
    lane = lax.broadcasted_iota(jnp.int32, (1, LANES), 1)
    return [lane < HEAD_DIM, lane >= HEAD_DIM]


def softmax_parts(scores):
    expo = jnp.exp(scores - jnp.max(scores, axis=-1, keepdims=True))
    return expo, 1.0 / jnp.sum(expo, axis=-1, keepdims=True)


def valid_rows(x_half, tok_rows, row):
    held, low, _ = token_layout(tok_rows)
    rest = (row < tok_rows) | ((row >= held + CUT - low) & (row < held + tok_rows - low))
    return ((x_half == 0) & (row < CUT)) | ((x_half == 1) & rest)


def only(mask, values):
    return jnp.where(mask, values, jnp.zeros_like(values))


def token_layout(tok_rows):
    held = -(-tok_rows // 16) * 16
    low = CUT // 16 * 16
    return held, low, held - low


class Place:
    def __init__(self):
        self.s = lax.axis_index("section")
        self.d = lax.axis_index("dp")
        self.t = lax.axis_index("tensor")
        self.x = self.t % 2
        self.y = self.t // 2
        self.near = self.t + (1 - self.s) * (1 - 2 * self.x) + self.s * (2 - 4 * self.y)
        self.far = self.t + self.s * (1 - 2 * self.x) + (1 - self.s) * (2 - 4 * self.y)
        self.cross = 3 - self.t
        self.beside = self.t + 1 - 2 * self.x
        self.sibling = (1 - self.s, self.d, self.t)
        self.diagonal = (1 - self.s, self.d, self.beside)

    def at(self, tensor):
        return (self.s, self.d, tensor)


def remote(src, dst, send, recv, device):
    return pltpu.make_async_remote_copy(
        src_ref=src, dst_ref=dst, send_sem=send, recv_sem=recv, device_id=device, device_id_type=MESH
    )


def greet(peers):
    barrier = pltpu.get_barrier_semaphore()
    for peer in peers:
        pl.semaphore_signal(barrier, inc=1, device_id=peer, device_id_type=MESH)
    pl.semaphore_wait(barrier, len(peers))


class HandBack:
    def __init__(self, here, layer, tok_rows, rows_ref, main_out, back_out, sems):
        held, _, spare = token_layout(tok_rows)
        main_send, main_recv, back_send, back_recv, own = sems
        self.here, self.layer = here, layer
        main, back = rows_ref.at[pl.ds(0, held)], rows_ref.at[pl.ds(held, spare)]
        s = here.s
        self.local = pltpu.make_async_copy(main, main_out.at[s], own)
        self.away = remote(main, main_out.at[s], main_send, main_recv, here.sibling)
        self.backs = [
            remote(back, back_out.at[s], back_send, back_recv.at[s], (layer, here.d, here.beside)),
        ]
        self.landing = [
            remote(back, back_out.at[i], back_send, back_recv.at[i], here.sibling) for i in range(2)
        ]

    def start(self):
        mine = self.here.s == self.layer
        pl.when(mine)(self.local.start)
        pl.when(jnp.logical_not(mine))(self.away.start)
        pl.when(self.here.x == 1)(self.backs[0].start)

    def wait(self):
        mine = self.here.s == self.layer

        @pl.when(mine)
        def _():
            self.local.wait()
            self.away.wait_recv()

            @pl.when(self.here.x == 0)
            def _():
                for landing in self.landing:
                    landing.wait_recv()

        pl.when(jnp.logical_not(mine))(self.away.wait_send)
        pl.when(self.here.x == 1)(self.backs[0].wait_send)


def hand_back_sems():
    dma = pltpu.SemaphoreType.DMA
    return [dma, dma, dma, dma((2,)), dma]


KINDS = 4
CHUNKS = [(0, 0), (1, 0), (2, 0), (2, 1), (3, 0), (3, 1)]
WINDOW = 3


def forward_kernel(
    tok_rows,
    keep_ref, bias_ref, my_gain, router_ref, tok_ref, wq_ref, wo_ref, wu_ref, wd_ref,
    x_out, gain_out, main_out, back_out, grad_out,
    gq_out, go_out, gu_out, gd_out, norm_out, qkv_out, mixed_out, hidden_out,
    second_out, active_out, slope_out, branch_out,
    x_own, gain_ref,
    gq, go, gu, gd, normed, qkv, mixed, hidden, second, active, slope, branch, work,
    own_sem, lend_send, lend_recv, a_send, a_recv, b_send, b_recv, c_send, c_recv,
    e_send, e_recv, out_sem, save_sem, tok_sem, tok_send, tok_recv, gain_sem, gain_send, gain_recv, x_sem,
    *back_sems,
):
    here = Place()
    held, low, spare = token_layout(tok_rows)
    part = wo_ref.shape[0]
    unit = wu_ref.shape[0] // 4
    shards = (wq_ref, wo_ref, wu_ref, wd_ref)

    def block(kind, layer, quarter):
        rows = pl.ds(pl.multiple_of(quarter * part, part), part)
        if kind == 0:
            return gq.at[layer, :, rows, :]
        if kind == 1:
            return go.at[layer, rows, :]
        return (gu if kind == 2 else gd).at[layer, quarter]

    def chunk(layer, index, quarter, half):
        kind, piece = CHUNKS[index]
        if kind < 2:
            rows = pl.ds(pl.multiple_of(quarter * part + half * (part // 2), part // 2), part // 2)
            return gq.at[layer, :, rows, :] if kind == 0 else go.at[layer, rows, :]
        rows = pl.ds(pl.multiple_of((2 * half + piece) * unit, unit), unit)
        return (gu if kind == 2 else gd).at[layer, quarter, rows, :]

    def own_copy(kind):
        return pltpu.make_async_copy(shards[kind], block(kind, here.s, here.t), own_sem.at[kind])

    def lend(kind, layer):
        return remote(
            shards[kind], block(kind, layer, here.t), lend_send.at[kind], lend_recv.at[kind], here.sibling
        )

    def along(which, step, quarter, peer, sems):
        piece = chunk(step // 6, step % 6, quarter, here.s)
        return remote(piece, piece, sems[0].at[step], sems[1].at[step], peer)

    def send_a(step):
        return along("a", step, here.t, here.at(here.near), (a_send, a_recv))

    def send_b(step):
        return along("b", step, here.t, here.at(here.far), (b_send, b_recv))

    def send_c(step):
        return along("c", step, here.near, here.at(here.far), (c_send, c_recv))

    def send_e(step, which, quarter):
        piece = chunk(step // 6, step % 6, quarter, here.s)
        return remote(piece, piece, e_send.at[step, which], e_recv.at[step, which], here.sibling)

    def landed_e(step, which, quarter):
        piece = chunk(step // 6, step % 6, quarter, 1 - here.s)
        return remote(piece, piece, e_send.at[step, which], e_recv.at[step, which], here.sibling)

    greet([here.sibling, here.at(here.near), here.at(here.far), here.diagonal])

    gain_own = pltpu.make_async_copy(my_gain, gain_ref.at[here.s], gain_sem)
    gain_away = remote(my_gain, gain_ref.at[here.s], gain_send, gain_recv, here.sibling)
    tok_own, tok_away = [], []
    for which, target in enumerate((x_own.at[0], grad_out)):
        tok_own.append(
            pltpu.make_async_copy(tok_ref.at[which], target.at[pl.ds(0, held)], tok_sem.at[which])
        )
        tok_away.append(
            remote(
                tok_ref.at[which, pl.ds(low, spare)], target.at[pl.ds(held, spare)],
                tok_send.at[which], tok_recv.at[which], here.at(here.beside),
            )
        )
    tok_own[0].start()
    pl.when(here.x == 0)(tok_away[0].start)
    gain_own.start()
    gain_away.start()
    for kind in range(KINDS):
        lend(kind, here.s).start()
        own_copy(kind).start()

    def issue(step):
        if step >= 12:
            return
        layer, (kind, piece) = step // 6, CHUNKS[step % 6]
        if piece == 0:
            pl.when(here.s == layer)(lambda: own_copy(kind).wait())
            pl.when(here.s != layer)(lambda: lend(kind, layer).wait_recv())
        send_a(step).start()
        send_b(step).start()

    def relay(step):
        if step >= 12:
            return
        send_a(step).wait_recv()
        send_c(step).start()
        send_e(step, 0, here.near).start()
        issue(step + WINDOW)

    def pump(step):
        relay(step + 1)
        send_b(step).wait_recv()
        send_e(step, 1, here.far).start()
        send_c(step).wait_recv()
        send_e(step, 2, here.cross).start()
        for which in range(3):
            landed_e(step, which, here.cross).wait_recv()

    for step in range(WINDOW):
        issue(step)
    tok_own[1].start()
    pl.when(here.x == 0)(tok_away[1].start)

    tok_own[0].wait()
    pl.when(here.x == 1)(tok_away[0].wait_recv)

    def clear(rows):
        row = lax.broadcasted_iota(jnp.int32, (TILE, 1), 0) + rows.start
        valid = valid_rows(here.x, tok_rows, row)
        x_own[0, rows, :] = only(valid, x_own[0, rows, :])

    tiles(clear)
    x_save = pltpu.make_async_copy(x_own.at[0], x_out.at[0], x_sem.at[0])
    x_save.start()
    gain_own.wait()
    gain_away.wait_recv()
    gain_out[...] = gain_ref[...]
    relay(0)
    masks = half_masks()
    saves = []
    backs = []

    def save(index, layer, src, dst):
        copy = pltpu.make_async_copy(src, dst.at[layer], save_sem.at[index])
        copy.start()
        return copy

    for layer in range(2):
        x_now = x_own.at[layer]

        def first_norm(rows):
            xhat, _ = standardize(x_now[rows, :].astype(F32))
            normed[rows, :] = (xhat * gain_ref[layer, 0:1, :]).astype(BF16)

        for copy in saves:
            copy.wait()
        saves = []
        tiles(first_norm)
        saves.append(save(0, layer, normed, norm_out))
        pump(6 * layer)

        def project(j, carry):
            qkv[j] = dot(normed[...], gq[layer, j], NT).astype(BF16)
            return carry

        lax.fori_loop(0, 3, project, 0)
        saves.append(save(1, layer, qkv, qkv_out))

        def attend(pair, carry):
            cols = pl.ds(pl.multiple_of(pair * LANES, LANES), LANES)
            key, value = qkv[1, :, cols], qkv[2, :, cols]
            query = qkv[0, :, cols] * BF16(0.125)
            outs = []
            for mask in masks:
                expo, inverse = softmax_parts(dot(only(mask, query), key, NT) + bias_ref[layer])
                outs.append(dot(expo.astype(BF16), value) * inverse)
            mixed[:, cols] = jnp.where(masks[0], outs[0], outs[1]).astype(BF16)
            return carry

        lax.fori_loop(0, mixed.shape[1] // LANES, attend, 0)
        saves.append(save(2, layer, mixed, mixed_out))
        pump(6 * layer + 1)
        branch[...] = dot(mixed[...], go[layer])

        def second_norm(rows):
            value = x_now[rows, :].astype(F32) + branch[rows, :]
            hidden[rows, :] = value
            xhat, _ = standardize(value)
            second[rows, :] = (xhat * gain_ref[layer, 1:2, :]).astype(BF16)

        tiles(second_norm)
        saves.append(save(3, layer, hidden, hidden_out))
        saves.append(save(4, layer, second, second_out))
        pump(6 * layer + 2)
        pump(6 * layer + 3)

        def widen(g, carry):
            work[...] = dot(second[...], gu[layer, g])

            def bend(rows):
                upper = work[rows, :]
                phi = 0.5 * (1.0 + lax.erf(upper * 0.7071067811865476))
                bell = jnp.exp(-0.5 * upper * upper) * 0.3989422804014327
                active[g, rows, :] = (upper * phi).astype(BF16)
                slope[g, rows, :] = (phi + upper * bell).astype(BF16)

            tiles(bend, tile=32)
            return carry

        lax.fori_loop(0, 4, widen, 0)
        saves.append(save(5, layer, active, active_out))
        saves.append(save(6, layer, slope, slope_out))
        pump(6 * layer + 4)
        pump(6 * layer + 5)

        def narrow(g, carry):
            branch[...] += dot(active[g], gd[layer, g])
            return carry

        lax.fori_loop(0, 4, narrow, 0)
        saves.append(save(7, layer, branch, branch_out))

        def finish(rows):
            value = x_now[rows, :].astype(F32)
            change = branch[rows, :]
            if layer == 0:
                logit = jnp.sum(value * router_ref[...], axis=-1, keepdims=True)
                change = change * (keep_ref[rows, :] / (1.0 + jnp.exp(-logit)))
            x_own[layer + 1, rows, :] = (value + change).astype(BF16)

        tiles(finish)
        sems = back_sems[5 * layer : 5 * layer + 5]
        backs.append(HandBack(here, layer, tok_rows, x_own.at[layer + 1], main_out, back_out, sems))
        backs[layer].start()
        if layer == 0:
            y_save = pltpu.make_async_copy(x_own.at[1], x_out.at[1], x_sem.at[1])
            y_save.start()
        for index, (src, dst) in enumerate(((gq, gq_out), (go, go_out), (gu, gu_out), (gd, gd_out))):
            pltpu.make_async_copy(src.at[layer], dst.at[layer], out_sem.at[layer, index]).start()

    for copy in [*saves, x_save, y_save, tok_own[1]]:
        copy.wait()
    for back in backs:
        back.wait()
    gain_away.wait_send()

    @pl.when(here.x == 0)
    def _():
        for away in tok_away:
            away.wait_send()

    pl.when(here.x == 1)(tok_away[1].wait_recv)
    for layer in range(2):
        for index, (src, dst) in enumerate(((gq, gq_out), (go, go_out), (gu, gu_out), (gd, gd_out))):
            pltpu.make_async_copy(src.at[layer], dst.at[layer], out_sem.at[layer, index]).wait()
    for kind in range(KINDS):
        lend(kind, here.s).wait_send()
    for step in range(12):
        send_a(step).wait_send()
        send_b(step).wait_send()
        send_c(step).wait_send()
        for which in range(3):
            send_e(step, which, here.cross).wait_send()


def forward(tok_rows, keep, bias, gains, router, tokens, wq, wo, wu, wd):
    width = tokens.shape[2]
    held, _, spare = token_layout(tok_rows)
    any_spec = pl.BlockSpec(memory_space=pl.ANY)
    vmem = pl.BlockSpec(memory_space=pltpu.VMEM)

    def pair(*shape, dtype=BF16):
        return jax.ShapeDtypeStruct((2, *shape), dtype)

    shapes = [
        pair(ROWS, width), pair(8, width, dtype=F32), pair(held, width), pair(spare, width),
        jax.ShapeDtypeStruct((ROWS, width), BF16),
        pair(3, width, width), pair(width, width), pair(4, width, width), pair(4, width, width),
        pair(ROWS, width), pair(3, ROWS, width), pair(ROWS, width), pair(ROWS, width, dtype=F32),
        pair(ROWS, width), pair(4, ROWS, width), pair(4, ROWS, width), pair(ROWS, width, dtype=F32),
    ]
    dma = pltpu.SemaphoreType.DMA
    scratch = [
        pltpu.VMEM((3, ROWS, width), BF16), pltpu.VMEM((2, 8, width), F32),
        pltpu.VMEM((2, 3, width, width), BF16), pltpu.VMEM((2, width, width), BF16),
        pltpu.VMEM((2, 4, width, width), BF16), pltpu.VMEM((2, 4, width, width), BF16),
        pltpu.VMEM((ROWS, width), BF16), pltpu.VMEM((3, ROWS, width), BF16),
        pltpu.VMEM((ROWS, width), BF16), pltpu.VMEM((ROWS, width), F32),
        pltpu.VMEM((ROWS, width), BF16), pltpu.VMEM((4, ROWS, width), BF16),
        pltpu.VMEM((4, ROWS, width), BF16), pltpu.VMEM((ROWS, width), F32),
        pltpu.VMEM((ROWS, width), F32),
        dma((KINDS,)), dma((KINDS,)), dma((KINDS,)),
        dma((12,)), dma((12,)), dma((12,)), dma((12,)), dma((12,)), dma((12,)),
        dma((12, 3)), dma((12, 3)), dma((2, KINDS)), dma((8,)),
        dma((2,)), dma((2,)), dma((2,)), dma, dma, dma, dma((2,)),
        *hand_back_sems(), *hand_back_sems(),
    ]
    return pl.pallas_call(
        functools.partial(forward_kernel, tok_rows),
        out_shape=shapes,
        in_specs=[vmem] * 4 + [any_spec] * 5,
        out_specs=[any_spec, vmem] + [any_spec] * 15,
        scratch_shapes=scratch,
        compiler_params=pltpu.CompilerParams(
            collective_id=0, has_side_effects=True, vmem_limit_bytes=VMEM_BYTES
        ),
        cost_estimate=pl.CostEstimate(flops=24 * ROWS * width * width * 2, bytes_accessed=60_000_000, transcendentals=0),
        name="forward_layers",
    )(keep, bias, gains, router, tokens, wq, wo, wu, wd)


UNITS = 12
RING = 6


def backward_kernel(
    layer, in_kernel_z, tok_rows,
    keep_ref, bias_ref, gain_ref, router_ref, small_in, grad_in, x_in,
    gq, go, gu, gd, norm_in, qkv_in, mixed_in, hidden_in, second_in, active_in, slope_in, branch_in,
    dx_out, small_out, main_out, back_out, mlp_out, att_out,
    grad_ref, x_ref, dx_ref, dx_low, small_ref, tot, got,
    wq, wo, wu, wd, normed, qkv, mixed, hidden, second, active, slope, branch,
    dbranch, dfed, dfed_t, work, dup, dsecond, datt, dmixed, dqkv, stage, sib, near_in, far_in, plane,
    load_sem, wu_sem, wd_sem, slope_sem,
    sib_send, sib_recv, near_send, near_recv, far_send, far_recv,
    mlp_send, mlp_recv, att_send, att_recv, local_sem, tot_send, tot_recv, dx_sem, *back_sems,
):
    here = Place()
    s, d, t = here.s, here.d, here.t
    quarter_rows = stage.shape[2]
    half_rows = quarter_rows // 2
    my_rows = pl.ds(pl.multiple_of(s * half_rows, half_rows), half_rows)
    their_rows = pl.ds(pl.multiple_of((1 - s) * half_rows, half_rows), half_rows)
    n_dp = lax.axis_size("dp")

    loads = {}

    def load(name, src, dst):
        loads[name] = pltpu.make_async_copy(src, dst, load_sem.at[len(loads)])
        loads[name].start()

    def quarter_load(src, dst, sems, g):
        return pltpu.make_async_copy(src.at[layer, g], dst.at[g % 2], sems.at[g % 2])

    load("grad", grad_in, grad_ref)
    load("x", x_in.at[layer], x_ref)
    load("active", active_in.at[layer], active)
    if layer == 0:
        load("branch", branch_in.at[layer], branch)
    streams = ((gd, wd, wd_sem), (slope_in, slope, slope_sem), (gu, wu, wu_sem))
    for g in range(2):
        for stream in streams:
            quarter_load(*stream, g).start()
    load("second", second_in.at[layer], second)
    load("hidden", hidden_in.at[layer], hidden)
    load("mixed", mixed_in.at[layer], mixed)
    load("wo", go.at[layer], wo)
    load("qkv", qkv_in.at[layer], qkv)
    load("normed", norm_in.at[layer], normed)
    load("wq", gq.at[layer], wq)

    peers = [here.sibling, here.at(here.near), here.at(here.far), here.diagonal]
    doubled = [here.sibling, here.at(here.near), here.at(here.far)]
    bit = 1
    while bit < n_dp:
        doubled.append((s, d + bit * (1 - 2 * (d // bit % 2)), t))
        bit *= 2
    if in_kernel_z:
        for shift in range(1, n_dp):
            for section in range(2):
                peers.append((section, (d + shift) % n_dp, t))
    elif layer == 0:
        peers += doubled[3:]
    greet(peers)

    def total_move(step):
        return remote(tot.at[step], got.at[step], tot_send.at[step], tot_recv.at[step], doubled[step])

    def add_total(step):
        if layer != 0 or step >= len(doubled):
            return
        total_move(step).wait_recv()
        tot[step + 1] = tot[step] + got[step]
        if step + 1 < len(doubled):
            total_move(step + 1).start()

    near_sent = [s * (2 * (1 - here.y) + i) + (1 - s) * (2 * i + 1 - here.x) for i in range(2)]
    own_slot = s * here.x + (1 - s) * here.y

    def to_sibling(u):
        return remote(
            stage.at[u % RING, :, their_rows, :], sib.at[u], sib_send.at[u], sib_recv.at[u], here.sibling
        )

    def to_near(u, i):
        return remote(
            stage.at[u % RING, near_sent[i], my_rows, :], near_in.at[u, i],
            near_send.at[u, i], near_recv.at[u, i], here.at(here.near),
        )

    def to_far(u):
        return remote(
            stage.at[u % RING, here.far, my_rows, :], far_in.at[u],
            far_send.at[u], far_recv.at[u], here.at(here.far),
        )

    def give(u):
        to_sibling(u).start()

    def first(u):
        to_sibling(u).wait_recv()

        def add(q, carry):
            stage[u % RING, q, my_rows, :] = (
                stage[u % RING, q, my_rows, :].astype(F32) + sib[u, q].astype(F32)
            ).astype(BF16)
            return carry

        lax.fori_loop(0, 4, add, 0)
        for i in range(2):
            to_near(u, i).start()

    def second_step(u):
        for i in range(2):
            to_near(u, i).wait_recv()
        stage[u % RING, here.far, my_rows, :] = (
            stage[u % RING, here.far, my_rows, :].astype(F32) + near_in[u, 1 - own_slot].astype(F32)
        ).astype(BF16)
        to_far(u).start()

    def z_moves(u):
        moves = []
        if not in_kernel_z:
            target = mlp_out.at[u, my_rows, :]
            mine = s == layer
            moves.append((mine, pltpu.make_async_copy(plane.at[u], target, local_sem.at[u, 0]), remote(
                plane.at[u], target, mlp_send.at[u], mlp_recv.at[u, 0, s], (layer, d, t))))
        elif u < 8:
            target = mlp_out.at[u // 4, d, my_rows, :]
            mine = (s == layer) & (d == u % 4)
            moves.append((mine, pltpu.make_async_copy(plane.at[u], target, local_sem.at[u, 0]), remote(
                plane.at[u], target, mlp_send.at[u], mlp_recv.at[u // 4, d, s], (layer, u % 4, t))))
        else:
            for other in range(4):
                lanes = plane.shape[2] // 4 * other // LANES * LANES
                piece = plane.at[u, :, pl.ds(lanes, 2 * LANES)]
                target = att_out.at[u - 8, d, my_rows, :]
                mine = (s == layer) & (d == other)
                moves.append((mine, pltpu.make_async_copy(piece, target, local_sem.at[u, other]), remote(
                    piece, target, att_send.at[u - 8, other], att_recv.at[u - 8, d, s], (layer, other, t))))
        return moves

    def third(u):
        to_far(u).wait_recv()
        plane[u] = (
            stage[u % RING, t, my_rows, :].astype(F32)
            + near_in[u, own_slot].astype(F32) + far_in[u].astype(F32)
        ).astype(BF16)
        for mine, local, away in z_moves(u):
            pl.when(mine)(local.start)
            pl.when(jnp.logical_not(mine))(away.start)
        to_sibling(u).wait_send()
        for i in range(2):
            to_near(u, i).wait_send()
        to_far(u).wait_send()

    done = [0, 0, 0]

    def progress(*upto):
        for which, (step, limit) in enumerate(zip((first, second_step, third), upto)):
            while done[which] < min(limit, UNITS):
                step(done[which])
                done[which] += 1

    def slot(u):
        give(u)
        progress(u, u - 2, u - 4)

    def prepare(rows):
        row = lax.broadcasted_iota(jnp.int32, (TILE, 1), 0) + rows.start
        grad = only(valid_rows(here.x, tok_rows, row), grad_ref[rows, :]).astype(F32)
        if layer == 0:
            value = x_ref[rows, :].astype(F32)
            logit = jnp.sum(value * router_ref[...], axis=-1, keepdims=True)
            sigma = 1.0 / (1.0 + jnp.exp(-logit))
            keep = keep_ref[rows, :]
            dlogit = jnp.sum(grad * branch[rows, :], axis=-1, keepdims=True) * keep * sigma * (1.0 - sigma)
            small_ref[2] += fold_rows(value * dlogit)
            dx_ref[rows, :] = grad + dlogit * router_ref[...]
            grad = grad * (sigma * keep)
        else:
            dx_ref[rows, :] = grad
        dbranch[rows, :] = grad
        dfed[rows, :] = grad.astype(BF16)

    small_ref[...] = jnp.zeros_like(small_ref)
    loads["grad"].wait()
    loads["x"].wait()
    if layer == 0:
        loads["branch"].wait()
    tiles(prepare)

    def transpose(src, dst):
        def step(index, carry):
            cols = pl.ds(pl.multiple_of(index * LANES, LANES), LANES)
            dst[cols, :] = src[:, cols].astype(F32).T.astype(BF16)
            return carry

        lax.fori_loop(0, dst.shape[0] // LANES, step, 0)

    def rows_unit(u, k, left, right):
        rows = pl.ds(k * quarter_rows, quarter_rows)

        def step(g, carry):
            stage[u % RING, g] = dot(left[rows, :], right[g]).astype(BF16)
            return carry

        lax.fori_loop(0, 4, step, 0)

    transpose(dfed, dfed_t)
    loads["active"].wait()
    for k in range(4):
        g = k
        rows_unit(k, k, dfed_t, active)
        slot(k)
        for stream in streams:
            quarter_load(*stream, g).wait()
        work[...] = dot(dfed[...], wd[g % 2], NT)

        def bend(rows):
            dup[g, rows, :] = (work[rows, :] * slope[g % 2, rows, :].astype(F32)).astype(BF16)

        tiles(bend)
        part = dot(dup[g], wu[g % 2], NT)
        if g == 0:
            dsecond[...] = part
        else:
            dsecond[...] += part
        if g < 2:
            for stream in streams:
                quarter_load(*stream, g + 2).start()

    loads["second"].wait()
    transpose(second, dfed_t)
    for k in range(4):
        rows_unit(4 + k, k, dfed_t, dup)
        slot(4 + k)

    loads["hidden"].wait()

    def second_pull(rows):
        xhat, rstd = standardize(hidden[rows, :])
        grad = dsecond[rows, :]
        small_ref[1] += fold_rows(grad * xhat)
        dhidden = norm_pull(xhat, rstd, gain_ref[layer, 1:2, :], grad)
        dx_ref[rows, :] += dhidden
        datt[rows, :] = (dbranch[rows, :] + dhidden).astype(BF16)

    tiles(second_pull)

    def square_unit(u, left, right):
        width = left.shape[1] // 2

        def step(c, carry):
            cols = pl.ds(pl.multiple_of(c * width, width), width)
            product = dot(left[:, cols], right[...], TN).astype(BF16)
            stage[u % RING, pl.ds(2 * c, 2)] = product.reshape(2, quarter_rows, product.shape[1])
            return carry

        lax.fori_loop(0, 2, step, 0)

    loads["mixed"].wait()
    square_unit(8, mixed, datt)
    slot(8)
    loads["wo"].wait()
    dmixed[...] = dot(datt[...], wo[...], NT).astype(BF16)
    loads["qkv"].wait()
    masks = half_masks()

    def attend(pair, carry):
        cols = pl.ds(pl.multiple_of(pair * LANES, LANES), LANES)
        key, value = qkv[1, :, cols], qkv[2, :, cols]
        scaled = key * BF16(0.125)
        query = qkv[0, :, cols] * BF16(0.125)
        grad = dmixed[:, cols]
        sums = None
        for mask in masks:
            query_head, grad_head = only(mask, query), only(mask, grad)
            expo, inverse = softmax_parts(dot(query_head, key, NT) + bias_ref[layer])
            probs = expo * inverse
            dprobs = dot(grad_head, value, NT)
            dscores = probs * (dprobs - jnp.sum(probs * dprobs, axis=-1, keepdims=True))
            dscores = dscores.astype(BF16)
            parts = [
                dot(dscores, only(mask, scaled)),
                dot(dscores, query_head, TN),
                dot(probs.astype(BF16), grad_head, TN),
            ]
            sums = parts if sums is None else [left + right for left, right in zip(sums, parts)]
        for j in range(3):
            dqkv[j, :, cols] = sums[j].astype(BF16)
        return carry

    pairs = dmixed.shape[1] // LANES
    for third_part in range(3):
        lax.fori_loop(pairs * third_part // 3, pairs * (third_part + 1) // 3, attend, 0)
        progress(9, 7 + third_part, 5 + third_part)

    loads["normed"].wait()
    for j in range(3):
        square_unit(9 + j, dqkv.at[j], normed)
        give(9 + j)
        progress(9 + j, 9, 7 + j)
    loads["wq"].wait()
    work[...] = dot(dqkv[0], wq[0])
    work[...] += dot(dqkv[1], wq[1])
    progress(12, 10, 9)
    work[...] += dot(dqkv[2], wq[2])

    def first_pull(rows):
        xhat, rstd = standardize(x_ref[rows, :].astype(F32))
        grad = work[rows, :]
        small_ref[0] += fold_rows(grad * xhat)
        total = dx_ref[rows, :] + norm_pull(xhat, rstd, gain_ref[layer, 0:1, :], grad)
        dx_low[rows, :] = total.astype(BF16)

    tiles(first_pull)
    back = HandBack(here, layer, tok_rows, dx_low, main_out, back_out, back_sems)
    back.start()
    dx_save = pltpu.make_async_copy(dx_low, dx_out, dx_sem)
    dx_save.start()
    sums = jnp.sum(small_ref[...], axis=1)
    if layer == 0:
        tot[0] = small_in[...]
        tot[0, 0:3, :] = sums
        total_move(0).start()
    else:
        small_out[...] = jnp.zeros_like(small_out)
        small_out[3:5, :] = sums[0:2]
    progress(12, 11, 10)
    add_total(0)
    progress(12, 12, 10)
    add_total(1)
    progress(12, 12, 11)
    add_total(2)
    progress(12, 12, 12)
    for step in range(3, len(doubled)):
        add_total(step)
    if layer == 0:
        small_out[...] = tot[len(doubled)]
        for step in range(len(doubled)):
            total_move(step).wait_send()
    back.wait()
    dx_save.wait()

    for u in range(UNITS):
        for mine, local, away in z_moves(u):
            pl.when(mine)(local.wait)
            pl.when(jnp.logical_not(mine))(away.wait_send)

    @pl.when(s == layer)
    def _():
        if not in_kernel_z:
            for u in range(UNITS):
                remote(
                    plane.at[u], mlp_out.at[u, their_rows, :], mlp_send.at[u], mlp_recv.at[u, 0, 1 - layer],
                    here.sibling,
                ).wait_recv()
            return
        for source in range(4):
            for half in range(2):
                rows = pl.ds(half * half_rows, half_rows)

                def arrive():
                    for kind in range(2):
                        target = mlp_out.at[kind, source, rows, :]
                        remote(
                            target, target, mlp_send.at[0], mlp_recv.at[kind, source, half], here.sibling
                        ).wait_recv()
                    for b in range(4):
                        target = att_out.at[b, source, rows, :]
                        remote(
                            target, target, att_send.at[0, 0], att_recv.at[b, source, half], here.sibling
                        ).wait_recv()

                if half == layer:
                    pl.when(d != source)(arrive)
                else:
                    arrive()


def backward(layer, n_dp, tok_rows, keep, bias, gains, router, small, grad, x, saved):
    width = x.shape[2]
    held, _, spare = token_layout(tok_rows)
    steps = 3
    while 2 ** (steps - 3) < n_dp:
        steps += 1
    quarter_rows = width // 4
    half_rows = quarter_rows // 2
    in_kernel_z = n_dp == 4
    any_spec = pl.BlockSpec(memory_space=pl.ANY)
    vmem = pl.BlockSpec(memory_space=pltpu.VMEM)
    dma = pltpu.SemaphoreType.DMA

    def low(*shape):
        return pltpu.VMEM(shape, BF16)

    def wide(*shape):
        return pltpu.VMEM(shape, F32)

    mlp_shape = (2, 4, quarter_rows, width) if in_kernel_z else (UNITS, quarter_rows, width)
    scratch = [
        low(ROWS, width), low(ROWS, width), wide(ROWS, width), low(ROWS, width), wide(3, 8, width),
        wide(steps + 1, 8, width), wide(steps, 8, width),
        low(3, width, width), low(width, width), low(2, width, width), low(2, width, width),
        low(ROWS, width), low(3, ROWS, width), low(ROWS, width), wide(ROWS, width), low(ROWS, width),
        low(4, ROWS, width), low(2, ROWS, width), wide(ROWS, width) if layer == 0 else wide(8, LANES),
        wide(ROWS, width), low(ROWS, width), low(width, ROWS), wide(ROWS, width), low(4, ROWS, width),
        wide(ROWS, width), low(ROWS, width), low(ROWS, width), low(3, ROWS, width),
        low(RING, 4, quarter_rows, width), low(UNITS, 4, half_rows, width), low(UNITS, 2, half_rows, width),
        low(UNITS, half_rows, width), low(UNITS, half_rows, width),
        dma((11,)), dma((2,)), dma((2,)), dma((2,)),
        dma((UNITS,)), dma((UNITS,)), dma((UNITS, 2)), dma((UNITS, 2)), dma((UNITS,)), dma((UNITS,)),
        dma((UNITS,)), dma((UNITS, 4, 2)), dma((4, 4)), dma((4, 4, 2)), dma((UNITS, 4)),
        dma((steps,)), dma((steps,)), dma, *hand_back_sems(),
    ]
    return pl.pallas_call(
        functools.partial(backward_kernel, layer, in_kernel_z, tok_rows),
        out_shape=[
            jax.ShapeDtypeStruct((ROWS, width), BF16),
            jax.ShapeDtypeStruct((8, width), F32),
            jax.ShapeDtypeStruct((2, held, width), BF16),
            jax.ShapeDtypeStruct((2, spare, width), BF16),
            jax.ShapeDtypeStruct(mlp_shape, BF16),
            jax.ShapeDtypeStruct((4, 4, quarter_rows, 2 * LANES), BF16),
        ],
        in_specs=[vmem] * 5 + [any_spec] * 14,
        out_specs=[any_spec, vmem] + [any_spec] * 4,
        scratch_shapes=scratch,
        compiler_params=pltpu.CompilerParams(
            collective_id=2 - layer, has_side_effects=True, vmem_limit_bytes=VMEM_BYTES
        ),
        cost_estimate=pl.CostEstimate(flops=48 * ROWS * width * width, bytes_accessed=60_000_000, transcendentals=0),
        name="backward_layer",
    )(keep, bias, gains, router, small, grad, x, *saved)


def on_device(
    patches, cotangent, crop_lengths, route_mask, w_qkv, w_out, w_up, w_down, ln1_gain, ln2_gain, router
):
    micro, tok_rows, width = patches.shape
    images = crop_lengths.shape[1]
    slot_len = route_mask.shape[1] // images
    s = lax.axis_index("section")
    d = lax.axis_index("dp")
    t = lax.axis_index("tensor")
    n_dp, quarters = lax.axis_size("dp"), lax.axis_size("tensor")
    x_half, image = t % 2, t // 2
    held, low, spare = token_layout(tok_rows)

    tokens = jnp.stack([patches, cotangent])
    tokens = lax.dynamic_index_in_dim(tokens, s, 1, keepdims=False)
    tokens = jnp.pad(tokens, ((0, 0), (0, held - tok_rows), (0, 0)))
    row = jnp.arange(ROWS, dtype=jnp.int32)
    valid = valid_rows(x_half, tok_rows, row)
    position = jnp.where(
        x_half == 0, row, jnp.where(row < held, tok_rows + row, low + row - held)
    )
    lengths = crop_lengths[s, image]
    crop = jnp.sum((position[:, None] >= jnp.cumsum(lengths)[None, :]).astype(jnp.int32), axis=1)
    crop = jnp.where(valid, crop, -1)
    routes = lax.dynamic_slice(route_mask, (s, image * slot_len), (1, slot_len))[0]
    routes = jnp.pad(routes, (0, ROWS))
    routed = jnp.where(
        x_half == 0,
        routes[:ROWS],
        jnp.concatenate(
            [routes[tok_rows : tok_rows + held], routes[low:held], jnp.zeros((ROWS - held - spare,), jnp.int32)]
        ),
    )
    keep = jnp.where(valid, routed, 1)
    same = crop[:, None] == crop[None, :]
    bias = jnp.stack(
        [jnp.where(same & (keep > 0)[None, :], 0.0, NEG), jnp.where(same, 0.0, NEG)]
    ).astype(F32)
    keep_rows = jnp.where(valid, routed, 0).astype(F32)[:, None]
    my_gains = jnp.concatenate([ln1_gain, ln2_gain, jnp.zeros((6, width), F32)])
    router_row = router.astype(F32)[None, :]

    wq = jnp.transpose(w_qkv[0], (1, 2, 0))
    x, gains, y_main, y_back, grad, *saved = forward(
        tok_rows, keep_rows, bias, my_gains, router_row, tokens, wq, w_out[0], w_up[0], w_down[0]
    )
    no_small = jnp.zeros((8, width), F32)
    common = (keep_rows, bias, gains, router_row)
    late = backward(1, n_dp, tok_rows, *common, no_small, grad, x, saved)
    early = backward(0, n_dp, tok_rows, *common, late[1], late[0], x, saved)

    def joined(main, back):
        back = jnp.pad(back, ((0, 0), (low, 0), (0, 0)))[:, :tok_rows]
        is_back = (x_half == 0) & (jnp.arange(tok_rows) >= CUT)
        return jnp.where(is_back[None, :, None], back, main[:, :tok_rows])

    outputs = joined(y_main, y_back)
    input_grads = joined(
        jnp.where(s == 0, early[2], late[2]), jnp.where(s == 0, early[3], late[3])
    ).astype(F32)

    share = width // n_dp
    if n_dp == 4:
        mlp = jnp.where(s == 0, early[4], late[4]).astype(F32).sum(axis=1)
        att = jnp.where(s == 0, early[5], late[5]).astype(F32).sum(axis=1)
        att = jnp.where(d % 2 == 0, att[:, :, :share], att[:, :, -share:])
        down, up = mlp[0].T, mlp[1]
        out, qkv = att[0], att[1:]
        qkv = jnp.transpose(qkv, (2, 0, 1))
    else:
        plane = jnp.where(s == 0, early[4], late[4])

        def scatter(value, dim):
            return lax.psum_scatter(value, "dp", scatter_dimension=dim, tiled=True).astype(F32)

        down = scatter(plane[:4].reshape(width, width), 0).T
        up = scatter(plane[4:8].reshape(width, width), 0)
        out = scatter(plane[8], 1)
        qkv = jnp.transpose(scatter(plane[9:], 2), (2, 0, 1))

    small = early[1]
    ones = jnp.where(s == 0, small[0], small[3])
    twos = jnp.where(s == 0, small[1], small[4])
    place = d * quarters + t
    span = width // (n_dp * quarters)
    ones = lax.dynamic_slice_in_dim(ones, place * span, span)
    twos = lax.dynamic_slice_in_dim(twos, place * span, span)
    routers = lax.dynamic_slice_in_dim(small[2], (s * n_dp * quarters + place) * (span // 2), span // 2)
    return (
        outputs[None], input_grads[None], qkv[None], out[None], up[None], down[None],
        ones[None], twos[None], routers,
    )


def solution(mesh):
    return jax.shard_map(
        on_device,
        mesh=mesh,
        in_specs=(
            P(None, ("dp", "tensor"), None),
            P(None, ("dp", "tensor"), None),
            P(None, "dp", None),
            P(None, "dp"),
            P("section", None, None, "tensor"),
            P("section", "tensor", None),
            P("section", None, "tensor"),
            P("section", "tensor", None),
            P("section", None),
            P("section", None),
            P(),
        ),
        out_specs=(
            P("section", None, ("dp", "tensor"), None),
            P("section", None, ("dp", "tensor"), None),
            P("section", "dp", None, "tensor"),
            P("section", "tensor", "dp"),
            P("section", "dp", "tensor"),
            P("section", "tensor", "dp"),
            P("section", ("dp", "tensor")),
            P("section", ("dp", "tensor")),
            P(("section", "dp", "tensor")),
        ),
        check_vma=False,
    )
```

```python
import functools

import jax
import jax.numpy as jnp
from jax import lax
from jax.experimental import pallas as pl
from jax.experimental.pallas import tpu as pltpu
from jax.sharding import PartitionSpec as P

HEAD_DIM = 64
LANES = 128
CUT = 197
EPS = 1e-06
NEG = -1000000000.0
ROWS = 384
TILE = 64
MESH = pl.DeviceIdType.MESH
NT = (((1,), (1,)), ((), ()))
TN = (((0,), (0,)), ((), ()))
NN = (((1,), (0,)), ((), ()))
VMEM_BYTES = 62 * 1024 * 1024
F32, BF16 = jnp.float32, jnp.bfloat16


def dot(left, right, dims=NN):
    return lax.dot_general(left, right, dims, preferred_element_type=F32)


def tiles(body, rows=ROWS, tile=TILE):
    def step(index, carry):
        body(pl.ds(pl.multiple_of(index * tile, tile), tile))
        return carry

    lax.fori_loop(0, rows // tile, step, 0)


def standardize(values):
    centre = values - jnp.mean(values, axis=-1, keepdims=True)
    spread = jnp.mean(centre * centre, axis=-1, keepdims=True)
    rstd = lax.rsqrt(spread + EPS)
    return centre * rstd, rstd


def norm_pull(xhat, rstd, gain, grad):
    grad_hat = grad * gain
    mean_grad = jnp.mean(grad_hat, axis=-1, keepdims=True)
    mean_both = jnp.mean(grad_hat * xhat, axis=-1, keepdims=True)
    return rstd * (grad_hat - mean_grad - xhat * mean_both)


def fold_rows(values):
    return jnp.sum(values.reshape(values.shape[0] // 8, 8, values.shape[1]), axis=0)


def half_masks():
    lane = lax.broadcasted_iota(jnp.int32, (1, LANES), 1)
    return [lane < HEAD_DIM, lane >= HEAD_DIM]


def softmax_parts(scores):
    expo = jnp.exp(scores - jnp.max(scores, axis=-1, keepdims=True))
    return expo, 1.0 / jnp.sum(expo, axis=-1, keepdims=True)


def valid_rows(x_half, tok_rows, row):
    held, low, _ = token_layout(tok_rows)
    rest = (row < tok_rows) | ((row >= held + CUT - low) & (row < held + tok_rows - low))
    return ((x_half == 0) & (row < CUT)) | ((x_half == 1) & rest)


def only(mask, values):
    return jnp.where(mask, values, jnp.zeros_like(values))


def token_layout(tok_rows):
    held = -(-tok_rows // 16) * 16
    low = CUT // 16 * 16
    return held, low, held - low


class Place:
    def __init__(self):
        self.s = lax.axis_index("section")
        self.d = lax.axis_index("dp")
        self.t = lax.axis_index("tensor")
        self.x = self.t % 2
        self.y = self.t // 2
        self.near = self.t + (1 - self.s) * (1 - 2 * self.x) + self.s * (2 - 4 * self.y)
        self.far = self.t + self.s * (1 - 2 * self.x) + (1 - self.s) * (2 - 4 * self.y)
        self.cross = 3 - self.t
        self.beside = self.t + 1 - 2 * self.x
        self.sibling = (1 - self.s, self.d, self.t)
        self.diagonal = (1 - self.s, self.d, self.beside)

    def at(self, tensor):
        return (self.s, self.d, tensor)


def remote(src, dst, send, recv, device):
    return pltpu.make_async_remote_copy(
        src_ref=src, dst_ref=dst, send_sem=send, recv_sem=recv, device_id=device, device_id_type=MESH
    )


def greet(peers):
    barrier = pltpu.get_barrier_semaphore()
    for peer in peers:
        pl.semaphore_signal(barrier, inc=1, device_id=peer, device_id_type=MESH)
    pl.semaphore_wait(barrier, len(peers))


class HandBack:
    def __init__(self, here, layer, tok_rows, rows_ref, main_out, back_out, sems):
        held, _, spare = token_layout(tok_rows)
        main_send, main_recv, back_send, back_recv, own = sems
        self.here, self.layer = here, layer
        main, back = rows_ref.at[pl.ds(0, held)], rows_ref.at[pl.ds(held, spare)]
        s = here.s
        self.local = pltpu.make_async_copy(main, main_out.at[s], own)
        self.away = remote(main, main_out.at[s], main_send, main_recv, here.sibling)
        self.backs = [
            remote(back, back_out.at[s], back_send, back_recv.at[s], (layer, here.d, here.beside)),
        ]
        self.landing = [
            remote(back, back_out.at[i], back_send, back_recv.at[i], here.sibling) for i in range(2)
        ]

    def start(self):
        mine = self.here.s == self.layer
        pl.when(mine)(self.local.start)
        pl.when(jnp.logical_not(mine))(self.away.start)
        pl.when(self.here.x == 1)(self.backs[0].start)

    def wait(self):
        mine = self.here.s == self.layer

        @pl.when(mine)
        def _():
            self.local.wait()
            self.away.wait_recv()

            @pl.when(self.here.x == 0)
            def _():
                for landing in self.landing:
                    landing.wait_recv()

        pl.when(jnp.logical_not(mine))(self.away.wait_send)
        pl.when(self.here.x == 1)(self.backs[0].wait_send)


def hand_back_sems():
    dma = pltpu.SemaphoreType.DMA
    return [dma, dma, dma, dma((2,)), dma]


KINDS = 4
FIRST_PLAN = [
    (0, 0, False), (0, 1, True), (1, 0, False), (2, 0, True), (2, 2, True), (3, 0, True), (3, 2, False), (3, 3, False)
]
SECOND_PLAN = [
    (0, 0, False), (0, 1, True), (1, 0, False), (2, 0, True), (2, 2, True),
    (3, 0, False), (3, 1, False), (3, 2, False), (3, 3, False),
]
PLAN = [(0, *step) for step in FIRST_PLAN] + [(1, *step) for step in SECOND_PLAN]
STARTS = (0, len(FIRST_PLAN))
WINDOW = 2


def forward_kernel(
    tok_rows,
    keep_ref, bias_ref, my_gain, router_ref, tok_ref, wq_ref, wo_ref, wu_ref, wd_ref,
    x_out, gain_out, main_out, back_out, grad_out,
    gq_out, go_out, gu_out, gd_out, norm_out, qkv_out, mixed_out, hidden_out,
    second_out, active_out, slope_out, branch_out,
    x_own, gain_ref,
    gq, go, gu, gd, normed, qkv, mixed, hidden, second, active, slope, branch, work,
    own_sem, lend_send, lend_recv, a_send, a_recv, b_send, b_recv, c_send, c_recv,
    e_send, e_recv, f_send, f_recv, out_sem, save_sem, tok_sem, tok_send, tok_recv, gain_sem, gain_send, gain_recv, x_sem,
    *back_sems,
):
    here = Place()
    held, low, spare = token_layout(tok_rows)
    part = wo_ref.shape[0]
    unit = part // 2
    shards = (wq_ref, wo_ref, wu_ref, wd_ref)

    def block(kind, layer, quarter):
        rows = pl.ds(pl.multiple_of(quarter * part, part), part)
        if kind == 0:
            return gq.at[layer, :, rows, :]
        if kind == 1:
            return go.at[layer, rows, :]
        return (gu if kind == 2 else gd).at[layer, quarter]

    parity = here.d % 2

    def chunk(step, quarter, half, other=0):
        layer, kind, piece, shared = PLAN[step]
        if shared:
            piece = piece + other + (1 - 2 * other) * parity
        if kind < 2:
            rows = pl.ds(pl.multiple_of(quarter * part + half * unit, unit), unit)
            return gq.at[layer, piece, rows, :] if kind == 0 else go.at[layer, rows, :]
        rows = pl.ds(pl.multiple_of((4 * half + piece) * unit, unit), unit)
        return (gu if kind == 2 else gd).at[layer, quarter, rows, :]

    def own_copy(kind):
        return pltpu.make_async_copy(shards[kind], block(kind, here.s, here.t), own_sem.at[kind])

    def lend(kind, layer):
        return remote(
            shards[kind], block(kind, layer, here.t), lend_send.at[kind], lend_recv.at[kind], here.sibling
        )

    def along(step, quarter, peer, send, recv):
        piece = chunk(step, quarter, here.s)
        return remote(piece, piece, send.at[step], recv.at[step], peer)

    def send_a(step):
        return along(step, here.t, here.at(here.near), a_send, a_recv)

    def send_b(step):
        return along(step, here.t, here.at(here.far), b_send, b_recv)

    def send_c(step):
        return along(step, here.near, here.at(here.far), c_send, c_recv)

    def send_e(step, which, half=None, other=0):
        piece = chunk(step, three[which], here.s if half is None else half, other)
        index = which + 3 * other
        return remote(piece, piece, e_send.at[step, index], e_recv.at[step, index], here.sibling)

    def send_f(step, which, other=0):
        piece = chunk(step, three[which], here.s, other)
        return remote(piece, piece, f_send.at[step, which], f_recv.at[step, which], z_beside)

    three = (here.near, here.far, here.cross)
    z_beside = (here.s, here.d + 1 - 2 * parity, here.t)
    total = len(PLAN)

    greet([here.sibling, here.at(here.near), here.at(here.far), here.diagonal, z_beside])

    gain_own = pltpu.make_async_copy(my_gain, gain_ref.at[here.s], gain_sem)
    gain_away = remote(my_gain, gain_ref.at[here.s], gain_send, gain_recv, here.sibling)
    tok_own, tok_away = [], []
    for which, target in enumerate((x_own.at[0], grad_out)):
        tok_own.append(
            pltpu.make_async_copy(tok_ref.at[which], target.at[pl.ds(0, held)], tok_sem.at[which])
        )
        tok_away.append(
            remote(
                tok_ref.at[which, pl.ds(low, spare)], target.at[pl.ds(held, spare)],
                tok_send.at[which], tok_recv.at[which], here.at(here.beside),
            )
        )
    tok_own[0].start()
    pl.when(here.x == 0)(tok_away[0].start)
    gain_own.start()
    gain_away.start()
    for kind in range(KINDS):
        lend(kind, here.s).start()
        own_copy(kind).start()

    def issue(step):
        if step >= total:
            return
        layer, kind, piece, _ = PLAN[step]
        if piece == 0:
            pl.when(here.s == layer)(lambda: own_copy(kind).wait())
            pl.when(here.s != layer)(lambda: lend(kind, layer).wait_recv())
        send_a(step).start()
        send_b(step).start()

    def pass_on(step, which):
        send_e(step, which).start()
        if PLAN[step][3]:
            send_f(step, which).start()

    def relay(step):
        if step >= total:
            return
        send_a(step).wait_recv()
        send_c(step).start()
        pass_on(step, 0)
        issue(step + WINDOW)

    def fetch(step):
        if step >= total:
            return
        send_b(step).wait_recv()
        pass_on(step, 1)
        send_c(step).wait_recv()
        pass_on(step, 2)

    moved = [0]

    def tick(upto):
        while moved[0] <= min(upto, total - 1):
            step = moved[0]
            if step == 0:
                relay(0)
                relay(1)
            relay(step + 2)
            fetch(step)
            moved[0] += 1

    def pump(step):
        tick(step + 2)
        shared = PLAN[step][3]
        if shared:
            for which in range(3):
                send_f(step, which, 1).wait_recv()
                send_e(step, which, None, 1).start()
        for other in range(1 + shared):
            for which in range(3):
                send_e(step, which, 1 - here.s, other).wait_recv()

    for step in range(WINDOW):
        issue(step)
    tok_own[1].start()
    pl.when(here.x == 0)(tok_away[1].start)

    tok_own[0].wait()
    pl.when(here.x == 1)(tok_away[0].wait_recv)

    def clear(rows):
        row = lax.broadcasted_iota(jnp.int32, (TILE, 1), 0) + rows.start
        valid = valid_rows(here.x, tok_rows, row)
        x_own[0, rows, :] = only(valid, x_own[0, rows, :])

    tiles(clear)
    x_save = pltpu.make_async_copy(x_own.at[0], x_out.at[0], x_sem.at[0])
    x_save.start()
    gain_own.wait()
    gain_away.wait_recv()
    gain_out[...] = gain_ref[...]
    masks = half_masks()
    saves = []
    backs = []

    def weight_save(kind, layer):
        src, dst = ((gq, gq_out), (go, go_out), (gu, gu_out), (gd, gd_out))[kind]
        return pltpu.make_async_copy(src.at[layer], dst.at[layer], out_sem.at[layer, kind])

    def keep_weight(kind, layer):
        weight_save(kind, layer).start()

    def save(index, layer, src, dst):
        copy = pltpu.make_async_copy(src, dst.at[layer], save_sem.at[index])
        copy.start()
        return copy

    for layer in range(2):
        x_now = x_own.at[layer]

        def first_norm(rows):
            xhat, _ = standardize(x_now[rows, :].astype(F32))
            normed[rows, :] = (xhat * gain_ref[layer, 0:1, :]).astype(BF16)

        for copy in saves:
            copy.wait()
        saves = []
        tiles(first_norm)
        saves.append(save(0, layer, normed, norm_out))
        base = STARTS[layer]
        pump(base)
        qkv[0] = dot(normed[...], gq[layer, 0], NT).astype(BF16)
        pump(base + 1)
        keep_weight(0, layer)

        def project(j, carry):
            qkv[j] = dot(normed[...], gq[layer, j], NT).astype(BF16)
            return carry

        lax.fori_loop(1, 3, project, 0)
        saves.append(save(1, layer, qkv, qkv_out))

        def attend(pair, carry):
            cols = pl.ds(pl.multiple_of(pair * LANES, LANES), LANES)
            key, value = qkv[1, :, cols], qkv[2, :, cols]
            query = qkv[0, :, cols] * BF16(0.125)
            outs = []
            for mask in masks:
                expo, inverse = softmax_parts(dot(only(mask, query), key, NT) + bias_ref[layer])
                outs.append(dot(expo.astype(BF16), value) * inverse)
            mixed[:, cols] = jnp.where(masks[0], outs[0], outs[1]).astype(BF16)
            return carry

        pairs = mixed.shape[1] // LANES
        for part_of in range(3):
            lax.fori_loop(pairs * part_of // 3, pairs * (part_of + 1) // 3, attend, 0)
            tick(base + 4 + part_of)
        saves.append(save(2, layer, mixed, mixed_out))
        pump(base + 2)
        keep_weight(1, layer)
        branch[...] = dot(mixed[...], go[layer])

        def second_norm(rows):
            value = x_now[rows, :].astype(F32) + branch[rows, :]
            hidden[rows, :] = value
            xhat, _ = standardize(value)
            second[rows, :] = (xhat * gain_ref[layer, 1:2, :]).astype(BF16)

        tiles(second_norm)
        saves.append(save(3, layer, hidden, hidden_out))
        saves.append(save(4, layer, second, second_out))
        pump(base + 3)
        pump(base + 4)
        keep_weight(2, layer)

        def widen(g, carry):
            work[...] = dot(second[...], gu[layer, g])

            def bend(rows):
                upper = work[rows, :]
                phi = 0.5 * (1.0 + lax.erf(upper * 0.7071067811865476))
                bell = jnp.exp(-0.5 * upper * upper) * 0.3989422804014327
                active[g, rows, :] = (upper * phi).astype(BF16)
                slope[g, rows, :] = (phi + upper * bell).astype(BF16)

            tiles(bend, tile=32)
            return carry

        for g in range(4):
            widen(g, 0)
            tick(base + 6 + g)
        saves.append(save(5, layer, active, active_out))
        saves.append(save(6, layer, slope, slope_out))
        for step in range(base + 5, (*STARTS, total)[layer + 1]):
            pump(step)
        keep_weight(3, layer)

        def narrow(g, carry):
            branch[...] += dot(active[g], gd[layer, g])
            return carry

        lax.fori_loop(0, 4, narrow, 0)
        saves.append(save(7, layer, branch, branch_out))

        def finish(rows):
            value = x_now[rows, :].astype(F32)
            change = branch[rows, :]
            if layer == 0:
                logit = jnp.sum(value * router_ref[...], axis=-1, keepdims=True)
                change = change * (keep_ref[rows, :] / (1.0 + jnp.exp(-logit)))
            x_own[layer + 1, rows, :] = (value + change).astype(BF16)

        tiles(finish)
        sems = back_sems[5 * layer : 5 * layer + 5]
        backs.append(HandBack(here, layer, tok_rows, x_own.at[layer + 1], main_out, back_out, sems))
        backs[layer].start()
        if layer == 0:
            y_save = pltpu.make_async_copy(x_own.at[1], x_out.at[1], x_sem.at[1])
            y_save.start()
    for copy in [*saves, x_save, y_save, tok_own[1]]:
        copy.wait()
    for back in backs:
        back.wait()
    gain_away.wait_send()

    @pl.when(here.x == 0)
    def _():
        for away in tok_away:
            away.wait_send()

    pl.when(here.x == 1)(tok_away[1].wait_recv)
    for layer in range(2):
        for kind in range(KINDS):
            weight_save(kind, layer).wait()
    for kind in range(KINDS):
        lend(kind, here.s).wait_send()
    for step in range(total):
        send_a(step).wait_send()
        send_b(step).wait_send()
        send_c(step).wait_send()
        shared = PLAN[step][3]
        for which in range(3):
            send_e(step, which).wait_send()
            if shared:
                send_f(step, which).wait_send()
                send_e(step, which, None, 1).wait_send()


def forward(tok_rows, keep, bias, gains, router, tokens, wq, wo, wu, wd):
    width = tokens.shape[2]
    held, _, spare = token_layout(tok_rows)
    any_spec = pl.BlockSpec(memory_space=pl.ANY)
    vmem = pl.BlockSpec(memory_space=pltpu.VMEM)

    def pair(*shape, dtype=BF16):
        return jax.ShapeDtypeStruct((2, *shape), dtype)

    shapes = [
        pair(ROWS, width), pair(8, width, dtype=F32), pair(held, width), pair(spare, width),
        jax.ShapeDtypeStruct((ROWS, width), BF16),
        pair(3, width, width), pair(width, width), pair(4, width, width), pair(4, width, width),
        pair(ROWS, width), pair(3, ROWS, width), pair(ROWS, width), pair(ROWS, width, dtype=F32),
        pair(ROWS, width), pair(4, ROWS, width), pair(4, ROWS, width), pair(ROWS, width, dtype=F32),
    ]
    dma = pltpu.SemaphoreType.DMA
    scratch = [
        pltpu.VMEM((3, ROWS, width), BF16), pltpu.VMEM((2, 8, width), F32),
        pltpu.VMEM((2, 3, width, width), BF16), pltpu.VMEM((2, width, width), BF16),
        pltpu.VMEM((2, 4, width, width), BF16), pltpu.VMEM((2, 4, width, width), BF16),
        pltpu.VMEM((ROWS, width), BF16), pltpu.VMEM((3, ROWS, width), BF16),
        pltpu.VMEM((ROWS, width), BF16), pltpu.VMEM((ROWS, width), F32),
        pltpu.VMEM((ROWS, width), BF16), pltpu.VMEM((4, ROWS, width), BF16),
        pltpu.VMEM((4, ROWS, width), BF16), pltpu.VMEM((ROWS, width), F32),
        pltpu.VMEM((ROWS, width), F32),
        dma((KINDS,)), dma((KINDS,)), dma((KINDS,)),
        *[dma((len(PLAN),))] * 6, *[dma((len(PLAN), 6))] * 2, *[dma((len(PLAN), 3))] * 2,
        dma((2, KINDS)), dma((8,)),
        dma((2,)), dma((2,)), dma((2,)), dma, dma, dma, dma((2,)),
        *hand_back_sems(), *hand_back_sems(),
    ]
    return pl.pallas_call(
        functools.partial(forward_kernel, tok_rows),
        out_shape=shapes,
        in_specs=[vmem] * 4 + [any_spec] * 5,
        out_specs=[any_spec, vmem] + [any_spec] * 15,
        scratch_shapes=scratch,
        compiler_params=pltpu.CompilerParams(
            collective_id=0, has_side_effects=True, vmem_limit_bytes=VMEM_BYTES
        ),
        cost_estimate=pl.CostEstimate(flops=24 * ROWS * width * width * 2, bytes_accessed=60_000_000, transcendentals=0),
        name="forward_layers",
    )(keep, bias, gains, router, tokens, wq, wo, wu, wd)


UNITS = 12
RING = 6
LAGS = [(1, 3, 5), (1, 3, 5), (1, 3, 5), (0, 2, 4), (0, 1, 3), (0, 0, 2), (1, 1, 2), (1, 2, 3), (1, 2, 4), (0, 1, 3)]


def backward_kernel(
    in_kernel_z, tok_rows,
    keep_ref, bias_ref, gain_ref, router_ref, grad_in, x_in,
    gq, go, gu, gd, norm_in, qkv_in, mixed_in, hidden_in, second_in, active_in, slope_in, branch_in,
    small_out, main_out, back_out, mlp_out, att_out,
    grad_ref, x_ref, dx_ref, dx_low, small_ref, tot, got,
    wq, wo, wu, wd, normed, qkv, mixed, hidden, second, active, slope, branch,
    dbranch, dfed, dfed_t, work, dup, dsecond, datt, dmixed, dqkv, stage, sib, near_in, far_in, plane,
    load_sem, wu_sem, wd_sem, slope_sem,
    sib_send, sib_recv, near_send, near_recv, far_send, far_recv,
    mlp_send, mlp_recv, att_send, att_recv, local_sem, tot_send, tot_recv, *back_sems,
):
    here = Place()
    s, d, t = here.s, here.d, here.t
    quarter_rows = stage.shape[2]
    half_rows = quarter_rows // 2
    my_rows = pl.ds(pl.multiple_of(s * half_rows, half_rows), half_rows)
    their_rows = pl.ds(pl.multiple_of((1 - s) * half_rows, half_rows), half_rows)
    n_dp = lax.axis_size("dp")

    saved = {
        "active": (active_in, active), "x": (x_in, x_ref), "second": (second_in, second),
        "hidden": (hidden_in, hidden), "mixed": (mixed_in, mixed), "wo": (go, wo), "qkv": (qkv_in, qkv),
        "normed": (norm_in, normed), "wq": (gq, wq), "branch": (branch_in, branch),
    }

    def load(name, layer):
        src, dst = saved[name]
        return pltpu.make_async_copy(src.at[layer], dst, load_sem.at[layer, list(saved).index(name)])

    def prefetch(name, layer):
        if layer == 1:
            load(name, 0).start()

    streams = ((gd, wd, wd_sem), (slope_in, slope, slope_sem), (gu, wu, wu_sem))

    def quarter_load(stream, layer, g):
        src, dst, sems = stream
        return pltpu.make_async_copy(src.at[layer, g], dst.at[g % 2], sems.at[layer, g % 2])

    load_grad = pltpu.make_async_copy(grad_in, grad_ref, load_sem.at[0, len(saved)])
    load_grad.start()
    load("active", 1).start()
    for g in range(2):
        for stream in streams:
            quarter_load(stream, 1, g).start()
    for name in saved:
        if name not in ("active", "branch"):
            load(name, 1).start()
    load("branch", 0).start()

    peers = [here.sibling, here.at(here.near), here.at(here.far), here.diagonal]
    doubled = [here.sibling, here.at(here.near), here.at(here.far)]
    bit = 1
    while bit < n_dp:
        doubled.append((s, d + bit * (1 - 2 * (d // bit % 2)), t))
        bit *= 2
    if in_kernel_z:
        for shift in range(1, n_dp):
            for section in range(2):
                peers.append((section, (d + shift) % n_dp, t))
    else:
        peers += doubled[3:]
    greet(peers)

    def total_move(step):
        return remote(tot.at[step], got.at[step], tot_send.at[step], tot_recv.at[step], doubled[step])

    def add_total(step):
        if step >= len(doubled):
            return
        total_move(step).wait_recv()
        tot[step + 1] = tot[step] + got[step]
        if step + 1 < len(doubled):
            total_move(step + 1).start()

    near_sent = [s * (2 * (1 - here.y) + i) + (1 - s) * (2 * i + 1 - here.x) for i in range(2)]
    own_slot = s * here.x + (1 - s) * here.y

    def to_sibling(u):
        return remote(
            stage.at[u % RING, :, their_rows, :], sib.at[u % UNITS], sib_send.at[u], sib_recv.at[u], here.sibling
        )

    def to_near(u, i):
        return remote(
            stage.at[u % RING, near_sent[i], my_rows, :], near_in.at[u % UNITS, i],
            near_send.at[u, i], near_recv.at[u, i], here.at(here.near),
        )

    def to_far(u):
        return remote(
            stage.at[u % RING, here.far, my_rows, :], far_in.at[u % UNITS],
            far_send.at[u], far_recv.at[u], here.at(here.far),
        )

    def give(u):
        to_sibling(u).start()

    def first(u):
        to_sibling(u).wait_recv()

        def add(q, carry):
            stage[u % RING, q, my_rows, :] = (
                stage[u % RING, q, my_rows, :].astype(F32) + sib[u % UNITS, q].astype(F32)
            ).astype(BF16)
            return carry

        lax.fori_loop(0, 4, add, 0)
        for i in range(2):
            to_near(u, i).start()

    def second_step(u):
        for i in range(2):
            to_near(u, i).wait_recv()
        stage[u % RING, here.far, my_rows, :] = (
            stage[u % RING, here.far, my_rows, :].astype(F32) + near_in[u % UNITS, 1 - own_slot].astype(F32)
        ).astype(BF16)
        to_far(u).start()

    def z_moves(u):
        layer, v = 1 - u // UNITS, u % UNITS
        moves = []
        if not in_kernel_z:
            target = mlp_out.at[v, my_rows, :]
            mine = s == layer
            moves.append((mine, pltpu.make_async_copy(plane.at[v], target, local_sem.at[u, 0]), remote(
                plane.at[v], target, mlp_send.at[u], mlp_recv.at[v, 0, s], (layer, d, t))))
        elif v < 8:
            target = mlp_out.at[v // 4, d, my_rows, :]
            mine = (s == layer) & (d == v % 4)
            moves.append((mine, pltpu.make_async_copy(plane.at[v], target, local_sem.at[u, 0]), remote(
                plane.at[v], target, mlp_send.at[u], mlp_recv.at[v // 4, d, s], (layer, v % 4, t))))
        else:
            for other in range(4):
                lanes = plane.shape[2] // 4 * other // LANES * LANES
                piece = plane.at[v, :, pl.ds(lanes, 2 * LANES)]
                target = att_out.at[v - 8, d, my_rows, :]
                mine = (s == layer) & (d == other)
                moves.append((mine, pltpu.make_async_copy(piece, target, local_sem.at[u, other]), remote(
                    piece, target, att_send.at[layer, v - 8, other], att_recv.at[v - 8, d, s], (layer, other, t))))
        return moves

    def moved_out(u):
        for mine, local, away in z_moves(u):
            pl.when(mine)(local.wait)
            pl.when(jnp.logical_not(mine))(away.wait_send)

    def third(u):
        to_far(u).wait_recv()
        if u >= UNITS:
            moved_out(u - UNITS)
        plane[u % UNITS] = (
            stage[u % RING, t, my_rows, :].astype(F32)
            + near_in[u % UNITS, own_slot].astype(F32) + far_in[u % UNITS].astype(F32)
        ).astype(BF16)
        for mine, local, away in z_moves(u):
            pl.when(mine)(local.start)
            pl.when(jnp.logical_not(mine))(away.start)
        to_sibling(u).wait_send()
        for i in range(2):
            to_near(u, i).wait_send()
        to_far(u).wait_send()

    done = [0, 0, 0]
    given = [0]

    def progress(*lags):
        for which, (step, lag) in enumerate(zip((first, second_step, third), lags)):
            while done[which] < given[0] - lag:
                step(done[which])
                done[which] += 1

    def room():
        while done[2] < given[0] + 1 - RING:
            progress(0, 0, max(given[0] - done[2] - 1, 0))

    def slot(*lags):
        give(given[0])
        given[0] += 1
        progress(*lags)

    def transpose(src, dst):
        def step(index, carry):
            cols = pl.ds(pl.multiple_of(index * LANES, LANES), LANES)
            dst[cols, :] = src[:, cols].astype(F32).T.astype(BF16)
            return carry

        lax.fori_loop(0, dst.shape[0] // LANES, step, 0)

    def rows_unit(k, left, right):
        room()
        place = given[0] % RING
        rows = pl.ds(k * quarter_rows, quarter_rows)

        def step(g, carry):
            stage[place, g] = dot(left[rows, :], right[g]).astype(BF16)
            return carry

        lax.fori_loop(0, 4, step, 0)

    def square_unit(left, right):
        room()
        place = given[0] % RING
        width = left.shape[1] // 2

        def step(c, carry):
            cols = pl.ds(pl.multiple_of(c * width, width), width)
            product = dot(left[:, cols], right[...], TN).astype(BF16)
            stage[place, pl.ds(2 * c, 2)] = product.reshape(2, quarter_rows, product.shape[1])
            return carry

        lax.fori_loop(0, 2, step, 0)

    masks = half_masks()
    backs = []

    def run_layer(layer):
        source = grad_ref if layer == 1 else dx_low.at[1]

        def prepare(rows):
            row = lax.broadcasted_iota(jnp.int32, (TILE, 1), 0) + rows.start
            grad = only(valid_rows(here.x, tok_rows, row), source[rows, :]).astype(F32)
            if layer == 0:
                value = x_ref[rows, :].astype(F32)
                logit = jnp.sum(value * router_ref[...], axis=-1, keepdims=True)
                sigma = 1.0 / (1.0 + jnp.exp(-logit))
                keep = keep_ref[rows, :]
                dlogit = jnp.sum(grad * branch[rows, :], axis=-1, keepdims=True) * keep * sigma * (1.0 - sigma)
                small_ref[2] += fold_rows(value * dlogit)
                dx_ref[rows, :] = grad + dlogit * router_ref[...]
                grad = grad * (sigma * keep)
            else:
                dx_ref[rows, :] = grad
            dbranch[rows, :] = grad
            dfed[rows, :] = grad.astype(BF16)

        small_ref[...] = jnp.zeros_like(small_ref)
        if layer == 1:
            load_grad.wait()
        else:
            load("branch", 0).wait()
            load("x", 0).wait()
        tiles(prepare)
        transpose(dfed, dfed_t)
        load("active", layer).wait()
        for k in range(4):
            g = k
            rows_unit(k, dfed_t, active)
            slot(*LAGS[0])
            if k == 3:
                prefetch("active", layer)
            for stream in streams:
                quarter_load(stream, layer, g).wait()
            work[...] = dot(dfed[...], wd[g % 2], NT)

            def bend(rows):
                dup[g, rows, :] = (work[rows, :] * slope[g % 2, rows, :].astype(F32)).astype(BF16)

            tiles(bend)
            part = dot(dup[g], wu[g % 2], NT)
            if g == 0:
                dsecond[...] = part
            else:
                dsecond[...] += part
            for stream in streams:
                if g < 2:
                    quarter_load(stream, layer, g + 2).start()
                elif layer == 1:
                    quarter_load(stream, 0, g - 2).start()

        load("second", layer).wait()
        transpose(second, dfed_t)
        prefetch("second", layer)
        for k in range(4):
            rows_unit(k, dfed_t, dup)
            slot(*LAGS[1])

        load("hidden", layer).wait()

        def second_pull(rows):
            xhat, rstd = standardize(hidden[rows, :])
            grad = dsecond[rows, :]
            small_ref[1] += fold_rows(grad * xhat)
            dhidden = norm_pull(xhat, rstd, gain_ref[layer, 1:2, :], grad)
            dx_ref[rows, :] += dhidden
            datt[rows, :] = (dbranch[rows, :] + dhidden).astype(BF16)

        tiles(second_pull)
        prefetch("hidden", layer)
        load("mixed", layer).wait()
        square_unit(mixed, datt)
        prefetch("mixed", layer)
        slot(*LAGS[2])
        load("wo", layer).wait()
        dmixed[...] = dot(datt[...], wo[...], NT).astype(BF16)
        prefetch("wo", layer)
        load("qkv", layer).wait()

        def attend(pair, carry):
            cols = pl.ds(pl.multiple_of(pair * LANES, LANES), LANES)
            key, value = qkv[1, :, cols], qkv[2, :, cols]
            scaled = key * BF16(0.125)
            query = qkv[0, :, cols] * BF16(0.125)
            grad = dmixed[:, cols]
            sums = None
            for mask in masks:
                query_head, grad_head = only(mask, query), only(mask, grad)
                expo, inverse = softmax_parts(dot(query_head, key, NT) + bias_ref[layer])
                probs = expo * inverse
                dprobs = dot(grad_head, value, NT)
                dscores = probs * (dprobs - jnp.sum(probs * dprobs, axis=-1, keepdims=True))
                dscores = dscores.astype(BF16)
                parts = [
                    dot(dscores, only(mask, scaled)),
                    dot(dscores, query_head, TN),
                    dot(probs.astype(BF16), grad_head, TN),
                ]
                sums = parts if sums is None else [left + right for left, right in zip(sums, parts)]
            for j in range(3):
                dqkv[j, :, cols] = sums[j].astype(BF16)
            return carry

        pairs = dmixed.shape[1] // LANES
        for part_of in range(3):
            lax.fori_loop(pairs * part_of // 3, pairs * (part_of + 1) // 3, attend, 0)
            progress(*LAGS[3 + part_of])
        prefetch("qkv", layer)

        load("normed", layer).wait()
        for j in range(3):
            square_unit(dqkv.at[j], normed)
            slot(*LAGS[6 + j])
        prefetch("normed", layer)
        load("wq", layer).wait()
        work[...] = dot(dqkv[0], wq[0])
        work[...] += dot(dqkv[1], wq[1])
        progress(*LAGS[9])
        work[...] += dot(dqkv[2], wq[2])
        prefetch("wq", layer)
        if layer == 1:
            load("x", 1).wait()

        def first_pull(rows):
            xhat, rstd = standardize(x_ref[rows, :].astype(F32))
            grad = work[rows, :]
            small_ref[0] += fold_rows(grad * xhat)
            total = dx_ref[rows, :] + norm_pull(xhat, rstd, gain_ref[layer, 0:1, :], grad)
            dx_low[layer, rows, :] = total.astype(BF16)

        tiles(first_pull)
        prefetch("x", layer)
        sems = back_sems[5 * layer : 5 * layer + 5]
        backs.append(HandBack(here, layer, tok_rows, dx_low.at[layer], main_out, back_out, sems))
        backs[-1].start()
        sums = jnp.sum(small_ref[...], axis=1)
        if layer == 1:
            tot[0] = jnp.zeros(tot.shape[1:], F32)
            tot[0, 3:5, :] = sums[0:2]
        else:
            tot[0, 0:3, :] = sums
            total_move(0).start()

    run_layer(1)
    run_layer(0)
    progress(0, 1, 2)
    add_total(0)
    progress(0, 0, 2)
    add_total(1)
    progress(0, 0, 1)
    add_total(2)
    progress(0, 0, 0)
    for step in range(3, len(doubled)):
        add_total(step)
    small_out[...] = tot[len(doubled)]
    for step in range(len(doubled)):
        total_move(step).wait_send()
    for back in backs:
        back.wait()
    for u in range(UNITS, 2 * UNITS):
        moved_out(u)

    if not in_kernel_z:
        for v in range(UNITS):
            remote(
                plane.at[v], mlp_out.at[v, their_rows, :], mlp_send.at[v], mlp_recv.at[v, 0, 1 - s], here.sibling
            ).wait_recv()
        return
    for source in range(4):
        for half in range(2):
            rows = pl.ds(half * half_rows, half_rows)

            def arrive():
                for kind in range(2):
                    target = mlp_out.at[kind, source, rows, :]
                    remote(target, target, mlp_send.at[0], mlp_recv.at[kind, source, half], here.sibling).wait_recv()
                for b in range(4):
                    target = att_out.at[b, source, rows, :]
                    remote(
                        target, target, att_send.at[0, 0, 0], att_recv.at[b, source, half], here.sibling
                    ).wait_recv()

            pl.when(jnp.logical_not((d == source) & (s == half)))(arrive)


def backward(n_dp, tok_rows, keep, bias, gains, router, grad, x, saved):
    width = x.shape[2]
    held, _, spare = token_layout(tok_rows)
    quarter_rows = width // 4
    half_rows = quarter_rows // 2
    in_kernel_z = n_dp == 4
    steps = 3
    while 2 ** (steps - 3) < n_dp:
        steps += 1
    any_spec = pl.BlockSpec(memory_space=pl.ANY)
    vmem = pl.BlockSpec(memory_space=pltpu.VMEM)
    dma = pltpu.SemaphoreType.DMA

    def low(*shape):
        return pltpu.VMEM(shape, BF16)

    def wide(*shape):
        return pltpu.VMEM(shape, F32)

    mlp_shape = (2, 4, quarter_rows, width) if in_kernel_z else (UNITS, quarter_rows, width)
    units = 2 * UNITS
    scratch = [
        low(ROWS, width), low(ROWS, width), wide(ROWS, width), low(2, ROWS, width), wide(3, 8, width),
        wide(steps + 1, 8, width), wide(steps, 8, width),
        low(3, width, width), low(width, width), low(2, width, width), low(2, width, width),
        low(ROWS, width), low(3, ROWS, width), low(ROWS, width), wide(ROWS, width), low(ROWS, width),
        low(4, ROWS, width), low(2, ROWS, width), wide(ROWS, width),
        wide(ROWS, width), low(ROWS, width), low(width, ROWS), wide(ROWS, width), low(4, ROWS, width),
        wide(ROWS, width), low(ROWS, width), low(ROWS, width), low(3, ROWS, width),
        low(RING, 4, quarter_rows, width), low(UNITS, 4, half_rows, width), low(UNITS, 2, half_rows, width),
        low(UNITS, half_rows, width), low(UNITS, half_rows, width),
        dma((2, 11)), dma((2, 2)), dma((2, 2)), dma((2, 2)),
        dma((units,)), dma((units,)), dma((units, 2)), dma((units, 2)), dma((units,)), dma((units,)),
        dma((units,)), dma((UNITS, 4, 2)), dma((2, 4, 4)), dma((4, 4, 2)), dma((units, 4)),
        dma((steps,)), dma((steps,)), *hand_back_sems(), *hand_back_sems(),
    ]
    return pl.pallas_call(
        functools.partial(backward_kernel, in_kernel_z, tok_rows),
        out_shape=[
            jax.ShapeDtypeStruct((8, width), F32),
            jax.ShapeDtypeStruct((2, held, width), BF16),
            jax.ShapeDtypeStruct((2, spare, width), BF16),
            jax.ShapeDtypeStruct(mlp_shape, BF16),
            jax.ShapeDtypeStruct((4, 4, quarter_rows, 2 * LANES), BF16),
        ],
        in_specs=[vmem] * 4 + [any_spec] * 14,
        out_specs=[vmem] + [any_spec] * 4,
        scratch_shapes=scratch,
        compiler_params=pltpu.CompilerParams(
            collective_id=1, has_side_effects=True, vmem_limit_bytes=VMEM_BYTES
        ),
        cost_estimate=pl.CostEstimate(flops=96 * ROWS * width * width, bytes_accessed=120_000_000, transcendentals=0),
        name="backward_layers",
    )(keep, bias, gains, router, grad, x, *saved)


def on_device(
    patches, cotangent, crop_lengths, route_mask, w_qkv, w_out, w_up, w_down, ln1_gain, ln2_gain, router
):
    micro, tok_rows, width = patches.shape
    images = crop_lengths.shape[1]
    slot_len = route_mask.shape[1] // images
    s = lax.axis_index("section")
    d = lax.axis_index("dp")
    t = lax.axis_index("tensor")
    n_dp, quarters = lax.axis_size("dp"), lax.axis_size("tensor")
    x_half, image = t % 2, t // 2
    held, low, spare = token_layout(tok_rows)

    tokens = jnp.stack([patches, cotangent])
    tokens = lax.dynamic_index_in_dim(tokens, s, 1, keepdims=False)
    tokens = jnp.pad(tokens, ((0, 0), (0, held - tok_rows), (0, 0)))
    row = jnp.arange(ROWS, dtype=jnp.int32)
    valid = valid_rows(x_half, tok_rows, row)
    position = jnp.where(
        x_half == 0, row, jnp.where(row < held, tok_rows + row, low + row - held)
    )
    lengths = crop_lengths[s, image]
    crop = jnp.sum((position[:, None] >= jnp.cumsum(lengths)[None, :]).astype(jnp.int32), axis=1)
    crop = jnp.where(valid, crop, -1)
    routes = lax.dynamic_slice(route_mask, (s, image * slot_len), (1, slot_len))[0]
    routes = jnp.pad(routes, (0, ROWS))
    routed = jnp.where(
        x_half == 0,
        routes[:ROWS],
        jnp.concatenate(
            [routes[tok_rows : tok_rows + held], routes[low:held], jnp.zeros((ROWS - held - spare,), jnp.int32)]
        ),
    )
    keep = jnp.where(valid, routed, 1)
    same = crop[:, None] == crop[None, :]
    bias = jnp.stack(
        [jnp.where(same & (keep > 0)[None, :], 0.0, NEG), jnp.where(same, 0.0, NEG)]
    ).astype(F32)
    keep_rows = jnp.where(valid, routed, 0).astype(F32)[:, None]
    my_gains = jnp.concatenate([ln1_gain, ln2_gain, jnp.zeros((6, width), F32)])
    router_row = router.astype(F32)[None, :]

    wq = jnp.transpose(w_qkv[0], (1, 2, 0))
    x, gains, y_main, y_back, grad, *saved = forward(
        tok_rows, keep_rows, bias, my_gains, router_row, tokens, wq, w_out[0], w_up[0], w_down[0]
    )
    small, dx_main, dx_back, mlp, att = backward(
        n_dp, tok_rows, keep_rows, bias, gains, router_row, grad, x, saved
    )

    def joined(main, back):
        back = jnp.pad(back, ((0, 0), (low, 0), (0, 0)))[:, :tok_rows]
        is_back = (x_half == 0) & (jnp.arange(tok_rows) >= CUT)
        return jnp.where(is_back[None, :, None], back, main[:, :tok_rows])

    outputs = joined(y_main, y_back)
    input_grads = joined(dx_main, dx_back).astype(F32)

    share = width // n_dp
    if n_dp == 4:
        mlp = mlp.astype(F32).sum(axis=1)
        att = att.astype(F32).sum(axis=1)
        att = jnp.where(d % 2 == 0, att[:, :, :share], att[:, :, -share:])
        down, up = mlp[0].T, mlp[1]
        out, qkv = att[0], att[1:]
        qkv = jnp.transpose(qkv, (2, 0, 1))
    else:

        def scatter(value, dim):
            return lax.psum_scatter(value, "dp", scatter_dimension=dim, tiled=True).astype(F32)

        down = scatter(mlp[:4].reshape(width, width), 0).T
        up = scatter(mlp[4:8].reshape(width, width), 0)
        out = scatter(mlp[8], 1)
        qkv = jnp.transpose(scatter(mlp[9:], 2), (2, 0, 1))

    ones = jnp.where(s == 0, small[0], small[3])
    twos = jnp.where(s == 0, small[1], small[4])
    place = d * quarters + t
    span = width // (n_dp * quarters)
    ones = lax.dynamic_slice_in_dim(ones, place * span, span)
    twos = lax.dynamic_slice_in_dim(twos, place * span, span)
    routers = lax.dynamic_slice_in_dim(small[2], (s * n_dp * quarters + place) * (span // 2), span // 2)
    return (
        outputs[None], input_grads[None], qkv[None], out[None], up[None], down[None],
        ones[None], twos[None], routers,
    )


def solution(mesh):
    return jax.shard_map(
        on_device,
        mesh=mesh,
        in_specs=(
            P(None, ("dp", "tensor"), None),
            P(None, ("dp", "tensor"), None),
            P(None, "dp", None),
            P(None, "dp"),
            P("section", None, None, "tensor"),
            P("section", "tensor", None),
            P("section", None, "tensor"),
            P("section", "tensor", None),
            P("section", None),
            P("section", None),
            P(),
        ),
        out_specs=(
            P("section", None, ("dp", "tensor"), None),
            P("section", None, ("dp", "tensor"), None),
            P("section", "dp", None, "tensor"),
            P("section", "tensor", "dp"),
            P("section", "dp", "tensor"),
            P("section", "tensor", "dp"),
            P("section", ("dp", "tensor")),
            P("section", ("dp", "tensor")),
            P(("section", "dp", "tensor")),
        ),
        check_vma=False,
    )
```

```python
import functools

import jax
import jax.numpy as jnp
from jax import lax
from jax.experimental import pallas as pl
from jax.experimental.pallas import tpu as pltpu
from jax.sharding import PartitionSpec as P

HEAD_DIM = 64
LANES = 128
CUT = 197
EPS = 1e-06
NEG = -1000000000.0
ROWS = 384
TILE = 64
MESH = pl.DeviceIdType.MESH
NT = (((1,), (1,)), ((), ()))
TN = (((0,), (0,)), ((), ()))
NN = (((1,), (0,)), ((), ()))
VMEM_BYTES = 62 * 1024 * 1024
F32, BF16 = jnp.float32, jnp.bfloat16


def dot(left, right, dims=NN):
    return lax.dot_general(left, right, dims, preferred_element_type=F32)


def tiles(body, rows=ROWS, tile=TILE):
    def step(index, carry):
        body(pl.ds(pl.multiple_of(index * tile, tile), tile))
        return carry

    lax.fori_loop(0, rows // tile, step, 0)


def standardize(values):
    centre = values - jnp.mean(values, axis=-1, keepdims=True)
    spread = jnp.mean(centre * centre, axis=-1, keepdims=True)
    rstd = lax.rsqrt(spread + EPS)
    return centre * rstd, rstd


def norm_pull(xhat, rstd, gain, grad):
    grad_hat = grad * gain
    mean_grad = jnp.mean(grad_hat, axis=-1, keepdims=True)
    mean_both = jnp.mean(grad_hat * xhat, axis=-1, keepdims=True)
    return rstd * (grad_hat - mean_grad - xhat * mean_both)


def fold_rows(values):
    return jnp.sum(values.reshape(values.shape[0] // 8, 8, values.shape[1]), axis=0)


def half_masks():
    lane = lax.broadcasted_iota(jnp.int32, (1, LANES), 1)
    return [lane < HEAD_DIM, lane >= HEAD_DIM]


def softmax_parts(scores):
    expo = jnp.exp(scores - jnp.max(scores, axis=-1, keepdims=True))
    return expo, 1.0 / jnp.sum(expo, axis=-1, keepdims=True)


def valid_rows(x_half, tok_rows, row):
    held, low, _ = token_layout(tok_rows)
    rest = (row < tok_rows) | ((row >= held + CUT - low) & (row < held + tok_rows - low))
    return ((x_half == 0) & (row < CUT)) | ((x_half == 1) & rest)


def only(mask, values):
    return jnp.where(mask, values, jnp.zeros_like(values))


def token_layout(tok_rows):
    held = -(-tok_rows // 16) * 16
    low = CUT // 16 * 16
    return held, low, held - low


def transpose_into(src, dst):
    def step(index, carry):
        cols = pl.ds(pl.multiple_of(index * LANES, LANES), LANES)
        dst[cols, :] = src[:, cols].astype(F32).T.astype(BF16)
        return carry

    lax.fori_loop(0, dst.shape[0] // LANES, step, 0)


class Place:
    def __init__(self):
        self.s = lax.axis_index("section")
        self.d = lax.axis_index("dp")
        self.t = lax.axis_index("tensor")
        self.x = self.t % 2
        self.y = self.t // 2
        self.near = self.t + (1 - self.s) * (1 - 2 * self.x) + self.s * (2 - 4 * self.y)
        self.far = self.t + self.s * (1 - 2 * self.x) + (1 - self.s) * (2 - 4 * self.y)
        self.cross = 3 - self.t
        self.beside = self.t + 1 - 2 * self.x
        self.above = self.t + 2 - 4 * self.y
        self.sibling = (1 - self.s, self.d, self.t)
        self.diagonal = (1 - self.s, self.d, self.beside)

    def at(self, tensor):
        return (self.s, self.d, tensor)


def remote(src, dst, send, recv, device):
    return pltpu.make_async_remote_copy(
        src_ref=src, dst_ref=dst, send_sem=send, recv_sem=recv, device_id=device, device_id_type=MESH
    )


def greet(peers):
    barrier = pltpu.get_barrier_semaphore()
    for peer in peers:
        pl.semaphore_signal(barrier, inc=1, device_id=peer, device_id_type=MESH)
    pl.semaphore_wait(barrier, len(peers))


class HandBack:
    def __init__(self, here, layer, tok_rows, rows_ref, main_out, back_out, sems):
        held, _, spare = token_layout(tok_rows)
        main_send, main_recv, back_send, back_recv, own = sems
        self.here, self.layer = here, layer
        main, back = rows_ref.at[pl.ds(0, held)], rows_ref.at[pl.ds(held, spare)]
        s = here.s
        self.local = pltpu.make_async_copy(main, main_out.at[s], own)
        self.away = remote(main, main_out.at[s], main_send, main_recv, here.sibling)
        self.backs = [
            remote(back, back_out.at[s], back_send, back_recv.at[s], (layer, here.d, here.beside)),
        ]
        self.landing = [
            remote(back, back_out.at[i], back_send, back_recv.at[i], here.sibling) for i in range(2)
        ]

    def start(self):
        mine = self.here.s == self.layer
        pl.when(mine)(self.local.start)
        pl.when(jnp.logical_not(mine))(self.away.start)
        pl.when(self.here.x == 1)(self.backs[0].start)

    def wait(self):
        mine = self.here.s == self.layer

        @pl.when(mine)
        def _():
            self.local.wait()
            self.away.wait_recv()

            @pl.when(self.here.x == 0)
            def _():
                for landing in self.landing:
                    landing.wait_recv()

        pl.when(jnp.logical_not(mine))(self.away.wait_send)
        pl.when(self.here.x == 1)(self.backs[0].wait_send)


def hand_back_sems():
    dma = pltpu.SemaphoreType.DMA
    return [dma, dma, dma, dma((2,)), dma]


KINDS = 4
FIRST_PLAN = [
    (0, 0, False), (0, 1, True), (1, 0, False), (2, 0, True), (2, 2, True), (3, 0, True), (3, 2, False), (3, 3, False)
]
SECOND_PLAN = [
    (0, 0, False), (0, 1, True), (1, 0, False), (2, 0, True), (2, 2, True),
    (3, 0, False), (3, 1, False), (3, 2, False), (3, 3, False),
]
PLAN = [(0, *step) for step in FIRST_PLAN] + [(1, *step) for step in SECOND_PLAN]
STARTS = (0, len(FIRST_PLAN))
WINDOW = 2


def forward_kernel(
    tok_rows,
    crop_ref, route_ref, one_ref, two_ref, router_in, patch_ref, cotangent_ref, wq_ref, wo_ref, wu_ref, wd_ref,
    x_out, gain_out, keep_out, router_out, bias_out, grad_out,
    gq_out, go_out, gu_out, gd_out, norm_out, qkv_out, mixed_out, hidden_out,
    second_out, active_out, slope_out, branch_out,
    x_own, gain_ref, my_gain, keep_ref, router_ref, bias_ref, tokens, spare_rows, grad_own,
    gq, go, gu, gd, normed, qkv, mixed, hidden, second, active, slope, branch, work,
    own_sem, lend_send, lend_recv, a_send, a_recv, b_send, b_recv, c_send, c_recv,
    e_send, e_recv, f_send, f_recv, out_sem, save_sem, tok_sem, tok_send, tok_recv, gain_sem, gain_send, gain_recv, x_sem, bias_sem,
):
    here = Place()
    held, low, spare = token_layout(tok_rows)
    part = wo_ref.shape[0]
    unit = part // 2
    shards = (wq_ref, wo_ref, wu_ref, wd_ref)

    def block(kind, layer, quarter):
        rows = pl.ds(pl.multiple_of(quarter * part, part), part)
        if kind == 0:
            return gq.at[layer, :, rows, :]
        if kind == 1:
            return go.at[layer, rows, :]
        return (gu if kind == 2 else gd).at[layer, quarter]

    parity = here.d % 2

    def chunk(step, quarter, half, other=0):
        layer, kind, piece, shared = PLAN[step]
        if shared:
            piece = piece + other + (1 - 2 * other) * parity
        if kind < 2:
            rows = pl.ds(pl.multiple_of(quarter * part + half * unit, unit), unit)
            return gq.at[layer, piece, rows, :] if kind == 0 else go.at[layer, rows, :]
        rows = pl.ds(pl.multiple_of((4 * half + piece) * unit, unit), unit)
        return (gu if kind == 2 else gd).at[layer, quarter, rows, :]

    def own_copy(kind):
        return pltpu.make_async_copy(shards[kind], block(kind, here.s, here.t), own_sem.at[kind])

    def lend(kind, layer):
        return remote(
            shards[kind], block(kind, layer, here.t), lend_send.at[kind], lend_recv.at[kind], here.sibling
        )

    def along(step, quarter, peer, send, recv):
        piece = chunk(step, quarter, here.s)
        return remote(piece, piece, send.at[step], recv.at[step], peer)

    def send_a(step):
        return along(step, here.t, here.at(here.near), a_send, a_recv)

    def send_b(step):
        return along(step, here.t, here.at(here.far), b_send, b_recv)

    def send_c(step):
        return along(step, here.near, here.at(here.far), c_send, c_recv)

    def send_e(step, which, half=None, other=0):
        piece = chunk(step, three[which], here.s if half is None else half, other)
        index = which + 3 * other
        return remote(piece, piece, e_send.at[step, index], e_recv.at[step, index], here.sibling)

    def send_f(step, which, other=0):
        piece = chunk(step, three[which], here.s, other)
        return remote(piece, piece, f_send.at[step, which], f_recv.at[step, which], z_beside)

    three = (here.near, here.far, here.cross)
    z_beside = (here.s, here.d + 1 - 2 * parity, here.t)
    total = len(PLAN)

    greet([here.sibling, here.at(here.near), here.at(here.far), z_beside])

    my_gain[...] = jnp.zeros_like(my_gain)
    my_gain[0:1, :] = one_ref[...]
    my_gain[1:2, :] = two_ref[...]
    gain_own = pltpu.make_async_copy(my_gain, gain_ref.at[here.s], gain_sem)
    gain_away = remote(my_gain, gain_ref.at[here.s], gain_send, gain_recv, here.sibling)
    token_loads = []
    for which, source in enumerate((patch_ref, cotangent_ref)):
        tokens[which, pl.ds(tok_rows, held - tok_rows)] = jnp.zeros((held - tok_rows, *tokens.shape[2:]), BF16)
        token_loads.append(
            pltpu.make_async_copy(source, tokens.at[which, pl.ds(0, tok_rows)], tok_sem.at[which])
        )
    tok_away = [
        remote(src, dst.at[pl.ds(held, spare)], tok_send.at[i], tok_recv.at[i], here.at(here.beside))
        for i, (src, dst) in enumerate(((spare_rows, x_own.at[0]), (grad_own.at[pl.ds(low, spare)], grad_out)))
    ]
    grad_save = pltpu.make_async_copy(grad_own, grad_out.at[pl.ds(0, held)], tok_sem.at[2])
    for copy in token_loads:
        copy.start()
    gain_own.start()
    gain_away.start()
    for kind in range(KINDS):
        lend(kind, here.s).start()
        own_copy(kind).start()

    def issue(step):
        if step >= total:
            return
        layer, kind, piece, _ = PLAN[step]
        if piece == 0:
            pl.when(here.s == layer)(lambda: own_copy(kind).wait())
            pl.when(here.s != layer)(lambda: lend(kind, layer).wait_recv())
        send_a(step).start()
        send_b(step).start()

    def pass_on(step, which):
        send_e(step, which).start()
        if PLAN[step][3]:
            send_f(step, which).start()

    def relay(step):
        if step >= total:
            return
        send_a(step).wait_recv()
        send_c(step).start()
        pass_on(step, 0)
        issue(step + WINDOW)

    def fetch(step):
        if step >= total:
            return
        send_b(step).wait_recv()
        pass_on(step, 1)
        send_c(step).wait_recv()
        pass_on(step, 2)

    moved = [0]

    def tick(upto):
        while moved[0] <= min(upto, total - 1):
            step = moved[0]
            if step == 0:
                relay(0)
                relay(1)
            relay(step + 2)
            fetch(step)
            moved[0] += 1

    def pump(step):
        tick(step + 2)
        shared = PLAN[step][3]
        if shared:
            for which in range(3):
                send_f(step, which, 1).wait_recv()
                send_e(step, which, None, 1).start()
        for other in range(1 + shared):
            for which in range(3):
                send_e(step, which, 1 - here.s, other).wait_recv()

    for step in range(WINDOW):
        issue(step)
    def take(which, dst):
        def step(rows):
            dst[rows, :] = jnp.where(here.s == 0, tokens[which, rows, 0, :], tokens[which, rows, 1, :])

        tiles(step, rows=held, tile=16)

    for copy in token_loads:
        copy.wait()
    take(0, x_own.at[0])
    spare_rows[...] = x_own[0, pl.ds(low, spare), :]
    pl.when(here.x == 0)(tok_away[0].start)
    take(1, grad_own)
    pl.when(here.x == 0)(tok_away[1].start)
    grad_save.start()
    router_ref[...] = router_in[...].astype(F32).reshape(router_ref.shape)
    router_out[...] = router_ref[...]

    image = here.t // 2
    slot_len = route_ref.shape[1] // crop_ref.shape[1]
    routes = jnp.where(here.s == 0, route_ref[0:1, :], route_ref[1:2, :]).astype(F32)
    lanes = -(-(routes.shape[1] + ROWS) // LANES) * LANES
    routes = jnp.concatenate([routes, jnp.zeros((1, lanes - routes.shape[1]), F32)], axis=1)
    routes = jnp.broadcast_to(routes, (8, lanes))

    def routed_from(start):
        return pltpu.roll(routes, (2 * lanes - start) % lanes, 1)[0:1, :ROWS]

    def rows_info(row):
        valid = valid_rows(here.x, tok_rows, row)
        position = jnp.where(row < held, here.x * tok_rows + row, low - held + row)
        position = jnp.where(here.x == 0, row, position)
        crop = jnp.zeros_like(row)
        end = 0
        for i in range(crop_ref.shape[2]):
            end = end + crop_ref[here.s, image, i]
            crop += (position >= end).astype(jnp.int32)
        return valid, jnp.where(valid, crop, -1)

    across = lax.broadcasted_iota(jnp.int32, (1, ROWS), 1)
    valid, crop_across = rows_info(across)
    routed = jnp.where(
        across < held,
        routed_from(image * slot_len + here.x * tok_rows),
        routed_from(image * slot_len + low - held),
    )
    routed = jnp.where(valid, routed, 0.0)
    keep_ref[...] = jnp.broadcast_to(routed, (LANES, ROWS)).T[:, 0:1]
    keep_out[...] = keep_ref[...]
    usable = jnp.where(valid, routed, 1.0) > 0.0

    def allow(rows):
        _, crop_down = rows_info(lax.broadcasted_iota(jnp.int32, (TILE, 1), 0) + rows.start)
        same = crop_down == crop_across
        bias_ref[0, rows, :] = jnp.where(same & usable, 0.0, NEG)
        bias_ref[1, rows, :] = jnp.where(same, 0.0, NEG)

    tiles(allow)
    bias_save = pltpu.make_async_copy(bias_ref, bias_out, bias_sem)
    bias_save.start()

    pl.when(here.x == 1)(tok_away[0].wait_recv)

    def clear(block):
        def step(rows):
            row = lax.broadcasted_iota(jnp.int32, (TILE, 1), 0) + rows.start
            block[rows, :] = only(valid_rows(here.x, tok_rows, row), block[rows, :])

        tiles(step)

    clear(x_own.at[0])
    x_saves = [pltpu.make_async_copy(x_own.at[i], x_out.at[i], x_sem.at[i]) for i in range(3)]
    x_saves[0].start()
    gain_own.wait()
    gain_away.wait_recv()
    gain_out[...] = gain_ref[...]
    masks = half_masks()
    saves = []

    def weight_save(kind, layer):
        src, dst = ((gq, gq_out), (go, go_out), (gu, gu_out), (gd, gd_out))[kind]
        return pltpu.make_async_copy(src.at[layer], dst.at[layer], out_sem.at[layer, kind])

    def keep_weight(kind, layer):
        weight_save(kind, layer).start()

    def save(index, layer, src, dst):
        copy = pltpu.make_async_copy(src, dst.at[layer], save_sem.at[index])
        copy.start()
        return copy

    for layer in range(2):
        x_now = x_own.at[layer]

        def first_norm(rows):
            xhat, _ = standardize(x_now[rows, :].astype(F32))
            normed[rows, :] = (xhat * gain_ref[layer, 0:1, :]).astype(BF16)

        for copy in saves:
            copy.wait()
        saves = []
        tiles(first_norm)
        saves.append(save(0, layer, normed, norm_out))
        base = STARTS[layer]
        pump(base)
        qkv[0] = dot(normed[...], gq[layer, 0], NT).astype(BF16)
        pump(base + 1)
        keep_weight(0, layer)

        def project(j, carry):
            qkv[j] = dot(normed[...], gq[layer, j], NT).astype(BF16)
            return carry

        lax.fori_loop(1, 3, project, 0)
        saves.append(save(1, layer, qkv, qkv_out))

        def attend(pair, carry):
            cols = pl.ds(pl.multiple_of(pair * LANES, LANES), LANES)
            key, value = qkv[1, :, cols], qkv[2, :, cols]
            query = qkv[0, :, cols] * BF16(0.125)
            outs = []
            for mask in masks:
                expo, inverse = softmax_parts(dot(only(mask, query), key, NT) + bias_ref[layer])
                outs.append(dot(expo.astype(BF16), value) * inverse)
            mixed[:, cols] = jnp.where(masks[0], outs[0], outs[1]).astype(BF16)
            return carry

        pairs = mixed.shape[1] // LANES
        for part_of in range(3):
            lax.fori_loop(pairs * part_of // 3, pairs * (part_of + 1) // 3, attend, 0)
            tick(base + 4 + part_of)
        saves.append(save(2, layer, mixed, mixed_out))
        pump(base + 2)
        keep_weight(1, layer)
        branch[...] = dot(mixed[...], go[layer])

        def second_norm(rows):
            value = x_now[rows, :].astype(F32) + branch[rows, :]
            hidden[rows, :] = value
            xhat, _ = standardize(value)
            second[rows, :] = (xhat * gain_ref[layer, 1:2, :]).astype(BF16)

        tiles(second_norm)
        saves.append(save(3, layer, hidden, hidden_out))
        saves.append(save(4, layer, second, second_out))
        pump(base + 3)
        pump(base + 4)
        keep_weight(2, layer)

        def widen(g, carry):
            work[...] = dot(second[...], gu[layer, g])

            def bend(rows):
                upper = work[rows, :]
                phi = 0.5 * (1.0 + lax.erf(upper * 0.7071067811865476))
                bell = jnp.exp(-0.5 * upper * upper) * 0.3989422804014327
                active[g, rows, :] = (upper * phi).astype(BF16)
                slope[g, rows, :] = (phi + upper * bell).astype(BF16)

            tiles(bend, tile=32)
            return carry

        for g in range(4):
            widen(g, 0)
            tick(base + 6 + g)
        saves.append(save(5, layer, active, active_out))
        saves.append(save(6, layer, slope, slope_out))
        for step in range(base + 5, (*STARTS, total)[layer + 1]):
            pump(step)
        keep_weight(3, layer)

        def narrow(g, carry):
            branch[...] += dot(active[g], gd[layer, g])
            return carry

        lax.fori_loop(0, 4, narrow, 0)
        saves.append(save(7, layer, branch, branch_out))

        def finish(rows):
            value = x_now[rows, :].astype(F32)
            change = branch[rows, :]
            if layer == 0:
                logit = jnp.sum(value * router_ref[...], axis=-1, keepdims=True)
                change = change * (keep_ref[rows, :] / (1.0 + jnp.exp(-logit)))
            x_own[layer + 1, rows, :] = (value + change).astype(BF16)

        tiles(finish)
        x_saves[layer + 1].start()

    for copy in [*saves, *x_saves, grad_save, bias_save]:
        copy.wait()
    gain_away.wait_send()

    @pl.when(here.x == 0)
    def _():
        for away in tok_away:
            away.wait_send()

    pl.when(here.x == 1)(tok_away[1].wait_recv)
    for layer in range(2):
        for kind in range(KINDS):
            weight_save(kind, layer).wait()
    for kind in range(KINDS):
        lend(kind, here.s).wait_send()
    for step in range(total):
        send_a(step).wait_send()
        send_b(step).wait_send()
        send_c(step).wait_send()
        shared = PLAN[step][3]
        for which in range(3):
            send_e(step, which).wait_send()
            if shared:
                send_f(step, which).wait_send()
                send_e(step, which, None, 1).wait_send()


def forward(crops, routes, one, two, router, patches, cotangent, wq, wo, wu, wd):
    tok_rows, _, width = patches.shape
    held, _, spare = token_layout(tok_rows)
    any_spec = pl.BlockSpec(memory_space=pl.ANY)
    vmem = pl.BlockSpec(memory_space=pltpu.VMEM)

    def pair(*shape, dtype=BF16):
        return jax.ShapeDtypeStruct((2, *shape), dtype)

    shapes = [
        jax.ShapeDtypeStruct((3, ROWS, width), BF16), pair(8, width, dtype=F32),
        jax.ShapeDtypeStruct((ROWS, 1), F32), jax.ShapeDtypeStruct((1, width), F32), pair(ROWS, ROWS, dtype=F32),
        jax.ShapeDtypeStruct((ROWS, width), BF16),
        pair(3, width, width), pair(width, width), pair(4, width, width), pair(4, width, width),
        pair(ROWS, width), pair(3, ROWS, width), pair(ROWS, width), pair(ROWS, width, dtype=F32),
        pair(ROWS, width), pair(4, ROWS, width), pair(4, ROWS, width), pair(ROWS, width, dtype=F32),
    ]
    dma = pltpu.SemaphoreType.DMA
    scratch = [
        pltpu.VMEM((3, ROWS, width), BF16), pltpu.VMEM((2, 8, width), F32), pltpu.VMEM((8, width), F32),
        pltpu.VMEM((ROWS, 1), F32), pltpu.VMEM((1, width), F32), pltpu.VMEM((2, ROWS, ROWS), F32),
        pltpu.VMEM((2, held, 2, width), BF16), pltpu.VMEM((spare, width), BF16), pltpu.VMEM((held, width), BF16),
        pltpu.VMEM((2, 3, width, width), BF16), pltpu.VMEM((2, width, width), BF16),
        pltpu.VMEM((2, 4, width, width), BF16), pltpu.VMEM((2, 4, width, width), BF16),
        pltpu.VMEM((ROWS, width), BF16), pltpu.VMEM((3, ROWS, width), BF16),
        pltpu.VMEM((ROWS, width), BF16), pltpu.VMEM((ROWS, width), F32),
        pltpu.VMEM((ROWS, width), BF16), pltpu.VMEM((4, ROWS, width), BF16),
        pltpu.VMEM((4, ROWS, width), BF16), pltpu.VMEM((ROWS, width), F32),
        pltpu.VMEM((ROWS, width), F32),
        dma((KINDS,)), dma((KINDS,)), dma((KINDS,)),
        *[dma((len(PLAN),))] * 6, *[dma((len(PLAN), 6))] * 2, *[dma((len(PLAN), 3))] * 2,
        dma((2, KINDS)), dma((8,)),
        dma((3,)), dma((2,)), dma((2,)), dma, dma, dma, dma((3,)), dma,
    ]
    return pl.pallas_call(
        functools.partial(forward_kernel, tok_rows),
        out_shape=shapes,
        in_specs=[pl.BlockSpec(memory_space=pltpu.SMEM)] + [vmem] * 4 + [any_spec] * 6,
        out_specs=[any_spec, vmem, vmem, vmem] + [any_spec] * 14,
        scratch_shapes=scratch,
        compiler_params=pltpu.CompilerParams(
            collective_id=0, has_side_effects=True, vmem_limit_bytes=VMEM_BYTES
        ),
        cost_estimate=pl.CostEstimate(flops=24 * ROWS * width * width * 2, bytes_accessed=60_000_000, transcendentals=0),
        name="forward_layers",
    )(crops, routes, one, two, router, patches, cotangent, wq, wo, wu, wd)


UNITS = 12
RING = 6
Y_FIRST = ()
SCHEDULE = [
    (0, 0, 0), (0, 0, 0), (0, 0, 0), (0, 0, 0), (0, 0, 0), (0, 0, 0), (1, 0, 0), (1, 0, 0), (2, 0, 0),
    (2, 0, 0), (2, 0, 0), (3, 1, 0), (3, 1, 0), (3, 1, 0), (4, 2, 0), (4, 2, 0), (4, 2, 0), (6, 3, 1),
    (7, 4, 2), (8, 4, 3), (8, 5, 3), (8, 5, 3), (9, 6, 3), (9, 6, 4), (9, 7, 4), (9, 8, 4), (9, 8, 5),
    (10, 8, 6), (11, 8, 6), (11, 9, 6), (12, 9, 8), (12, 9, 8), (12, 9, 8), (12, 9, 8),
    (12, 10, 8), (12, 10, 8), (12, 10, 8), (13, 11, 8), (13, 11, 9), (14, 11, 9), (14, 11, 9), (14, 12, 9),
    (15, 12, 10), (15, 12, 11), (15, 12, 11), (16, 12, 11), (16, 13, 11), (17, 14, 12), (18, 16, 14),
    (18, 16, 14), (19, 17, 14), (20, 17, 15), (20, 17, 16), (21, 18, 16), (21, 18, 17), (21, 19, 17),
    (21, 19, 17), (21, 20, 17), (23, 21, 19), (23, 21, 19), (24, 21, 20), (24, 21, 21), (24, 22, 21),
    (24, 23, 21), (24, 24, 21), (24, 24, 22), (24, 24, 23), (24, 24, 24),
]


def backward_kernel(
    in_kernel_z, tok_rows,
    keep_ref, gain_ref, router_ref, bias_in, grad_in, x_in,
    gq, go, gu, gd, norm_in, qkv_in, mixed_in, hidden_in, second_in, active_in, slope_in, branch_in,
    small_out, y_main, y_back, main_out, back_out, mlp_out, att_out,
    grad_ref, x_ref, dx_ref, dx_low, small_ref, tot, got, bias_ref,
    wq, wo, wu, wd, normed, qkv, mixed, hidden, second, active, slope, branch,
    dbranch, dfed, dfed_t, work, dup, dsecond, datt, dmixed, dqkv, stage, sib, near_in, far_in, plane,
    load_sem, wu_sem, wd_sem, slope_sem,
    sib_send, sib_recv, near_send, near_recv, far_send, far_recv,
    mlp_send, mlp_recv, att_send, att_recv, local_sem, tot_send, tot_recv, *back_sems,
):
    here = Place()
    s, d, t = here.s, here.d, here.t
    quarter_rows = stage.shape[2]
    half_rows = quarter_rows // 2
    my_rows = pl.ds(pl.multiple_of(s * half_rows, half_rows), half_rows)
    their_rows = pl.ds(pl.multiple_of((1 - s) * half_rows, half_rows), half_rows)
    n_dp = lax.axis_size("dp")

    saved = {
        "active": (active_in, active), "x": (x_in, x_ref), "second": (second_in, second),
        "hidden": (hidden_in, hidden), "mixed": (mixed_in, mixed), "wo": (go, wo), "qkv": (qkv_in, qkv),
        "normed": (norm_in, normed), "wq": (gq, wq), "branch": (branch_in, branch),
    }

    def load(name, layer):
        src, dst = saved[name]
        return pltpu.make_async_copy(src.at[layer], dst, load_sem.at[layer, list(saved).index(name)])

    def prefetch(name, layer):
        if layer == 1:
            load(name, 0).start()

    streams = ((gd, wd, wd_sem), (slope_in, slope, slope_sem), (gu, wu, wu_sem))

    def quarter_load(stream, layer, g):
        src, dst, sems = stream
        return pltpu.make_async_copy(src.at[layer, g], dst.at[g % 2], sems.at[layer, g % 2])

    load_grad = pltpu.make_async_copy(grad_in, grad_ref, load_sem.at[0, len(saved)])
    load_bias = pltpu.make_async_copy(bias_in, bias_ref, load_sem.at[1, len(saved)])
    load_grad.start()

    load("active", 1).start()
    for g in range(2):
        for stream in streams:
            quarter_load(stream, 1, g).start()
    for name in saved:
        if name not in ("active", "branch"):
            load(name, 1).start()
    load("branch", 0).start()
    load_bias.start()

    peers = [here.sibling, here.at(here.near), here.at(here.far), here.diagonal]
    doubled = [here.sibling, here.at(here.near), here.at(here.far)]
    bit = 1
    while bit < n_dp:
        doubled.append((s, d + bit * (1 - 2 * (d // bit % 2)), t))
        bit *= 2
    if in_kernel_z:
        for shift in range(1, n_dp):
            for section in range(2):
                peers.append((section, (d + shift) % n_dp, t))
    else:
        peers += doubled[3:]
    greet(peers)

    backs = []

    def hand_back(layer, rows_ref, main, back):
        sems = back_sems[5 * len(backs) : 5 * len(backs) + 5]
        backs.append(HandBack(here, layer, tok_rows, rows_ref, main, back, sems))
        backs[-1].start()

    for layer in range(2):
        hand_back(layer, x_in.at[layer + 1], y_main, y_back)

    def total_move(step):
        return remote(tot.at[step], got.at[step], tot_send.at[step], tot_recv.at[step], doubled[step])

    def add_total(step):
        if step >= len(doubled):
            return
        total_move(step).wait_recv()
        tot[step + 1] = tot[step] + got[step]
        if step + 1 < len(doubled):
            total_move(step + 1).start()

    class Way:
        def __init__(self, u):
            first_y = 1 if u in Y_FIRST else s
            self.near = here.near if u not in Y_FIRST else here.above
            self.far = here.far if u not in Y_FIRST else here.beside
            self.sent = [first_y * (2 * (1 - here.y) + i) + (1 - first_y) * (2 * i + 1 - here.x) for i in range(2)]
            self.own_slot = first_y * here.x + (1 - first_y) * here.y


    def to_sibling(u):
        return remote(
            stage.at[u % RING, :, their_rows, :], sib.at[u % UNITS], sib_send.at[u], sib_recv.at[u], here.sibling
        )

    def to_near(u, i):
        way = Way(u)
        return remote(
            stage.at[u % RING, way.sent[i], my_rows, :], near_in.at[u % UNITS, i],
            near_send.at[u, i], near_recv.at[u, i], here.at(way.near),
        )

    def to_far(u):
        way = Way(u)
        return remote(
            stage.at[u % RING, way.far, my_rows, :], far_in.at[u % UNITS],
            far_send.at[u], far_recv.at[u], here.at(way.far),
        )

    def give(u):
        to_sibling(u).start()

    def first(u):
        to_sibling(u).wait_recv()

        def add(q, carry):
            stage[u % RING, q, my_rows, :] += sib[u % UNITS, q]
            return carry

        lax.fori_loop(0, 4, add, 0)
        for i in range(2):
            to_near(u, i).start()

    def second_step(u):
        for i in range(2):
            to_near(u, i).wait_recv()
        way = Way(u)
        stage[u % RING, way.far, my_rows, :] += near_in[u % UNITS, 1 - way.own_slot]
        to_far(u).start()

    def z_moves(u):
        layer, v = 1 - u // UNITS, u % UNITS
        moves = []
        if not in_kernel_z:
            target = mlp_out.at[v, my_rows, :]
            mine = s == layer
            moves.append((mine, pltpu.make_async_copy(plane.at[v], target, local_sem.at[u, 0]), remote(
                plane.at[v], target, mlp_send.at[u], mlp_recv.at[v, 0, s], (layer, d, t))))
        elif v < 8:
            target = mlp_out.at[v // 4, d, my_rows, :]
            mine = (s == layer) & (d == v % 4)
            moves.append((mine, pltpu.make_async_copy(plane.at[v], target, local_sem.at[u, 0]), remote(
                plane.at[v], target, mlp_send.at[u], mlp_recv.at[v // 4, d, s], (layer, v % 4, t))))
        else:
            for other in range(4):
                lanes = plane.shape[2] // 4 * other // LANES * LANES
                piece = plane.at[v, :, pl.ds(lanes, 2 * LANES)]
                target = att_out.at[v - 8, d, my_rows, :]
                mine = (s == layer) & (d == other)
                moves.append((mine, pltpu.make_async_copy(piece, target, local_sem.at[u, other]), remote(
                    piece, target, att_send.at[layer, v - 8, other], att_recv.at[v - 8, d, s], (layer, other, t))))
        return moves

    def moved_out(u):
        for mine, local, away in z_moves(u):
            pl.when(mine)(local.wait)
            pl.when(jnp.logical_not(mine))(away.wait_send)

    def third(u):
        to_far(u).wait_recv()
        if u >= UNITS:
            moved_out(u - UNITS)
        plane[u % UNITS] = (
            stage[u % RING, t, my_rows, :].astype(F32)
            + near_in[u % UNITS, Way(u).own_slot].astype(F32) + far_in[u % UNITS].astype(F32)
        ).astype(BF16)
        for mine, local, away in z_moves(u):
            pl.when(mine)(local.start)
            pl.when(jnp.logical_not(mine))(away.start)
        to_sibling(u).wait_send()
        for i in range(2):
            to_near(u, i).wait_send()
        to_far(u).wait_send()

    done = [0, 0, 0]
    given = [0]

    steps = (first, second_step, third)

    def reach(*targets):
        while any(now < target for now, target in zip(done, targets)):
            for which in (1, 0, 2):
                if done[which] < targets[which] and (which == 0 or done[which] < done[which - 1]):
                    steps[which](done[which])
                    done[which] += 1

    points = iter(SCHEDULE)

    def point():
        reach(*next(points))

    def room():
        need = given[0] + 1 - RING
        reach(*[max(need, now) for now in done])

    def slot():
        give(given[0])
        given[0] += 1
        point()

    def rows_unit(k, left, right):
        room()
        place = given[0] % RING
        rows = pl.ds(k * quarter_rows, quarter_rows)

        def step(g, carry):
            stage[place, g] = dot(left[rows, :], right[g]).astype(BF16)
            return carry

        lax.fori_loop(0, 4, step, 0)

    def square_unit(left, right):
        room()
        place = given[0] % RING
        width = left.shape[1] // 2

        def step(c, carry):
            cols = pl.ds(pl.multiple_of(c * width, width), width)
            product = dot(left[:, cols], right[...], TN).astype(BF16)
            stage[place, pl.ds(2 * c, 2)] = product.reshape(2, quarter_rows, product.shape[1])
            return carry

        lax.fori_loop(0, 2, step, 0)

    masks = half_masks()

    def run_layer(layer):
        source = grad_ref if layer == 1 else dx_low.at[1]

        def prepare(rows):
            row = lax.broadcasted_iota(jnp.int32, (TILE, 1), 0) + rows.start
            grad = only(valid_rows(here.x, tok_rows, row), source[rows, :]).astype(F32)
            if layer == 0:
                value = x_ref[rows, :].astype(F32)
                logit = jnp.sum(value * router_ref[...], axis=-1, keepdims=True)
                sigma = 1.0 / (1.0 + jnp.exp(-logit))
                keep = keep_ref[rows, :]
                dlogit = jnp.sum(grad * branch[rows, :], axis=-1, keepdims=True) * keep * sigma * (1.0 - sigma)
                small_ref[2] += fold_rows(value * dlogit)
                dx_ref[rows, :] = grad + dlogit * router_ref[...]
                grad = grad * (sigma * keep)
            else:
                dx_ref[rows, :] = grad
            dbranch[rows, :] = grad
            dfed[rows, :] = grad.astype(BF16)

        small_ref[...] = jnp.zeros_like(small_ref)
        if layer == 1:
            load_grad.wait()
        else:
            load("branch", 0).wait()
            load("x", 0).wait()
        tiles(prepare)
        point()
        transpose_into(dfed, dfed_t)
        point()
        load("active", layer).wait()
        for k in range(4):
            g = k
            rows_unit(k, dfed_t, active)
            slot()
            if k == 3:
                prefetch("active", layer)
            for stream in streams:
                quarter_load(stream, layer, g).wait()
            work[...] = dot(dfed[...], wd[g % 2], NT)

            def bend(rows):
                dup[g, rows, :] = (work[rows, :] * slope[g % 2, rows, :].astype(F32)).astype(BF16)

            tiles(bend)
            point()
            part = dot(dup[g], wu[g % 2], NT)
            if g == 0:
                dsecond[...] = part
            else:
                dsecond[...] += part
            for stream in streams:
                if g < 2:
                    quarter_load(stream, layer, g + 2).start()
                elif layer == 1:
                    quarter_load(stream, 0, g - 2).start()
            point()

        load("second", layer).wait()
        transpose_into(second, dfed_t)
        point()
        prefetch("second", layer)
        for k in range(4):
            rows_unit(k, dfed_t, dup)
            slot()

        load("hidden", layer).wait()

        def second_pull(rows):
            xhat, rstd = standardize(hidden[rows, :])
            grad = dsecond[rows, :]
            small_ref[1] += fold_rows(grad * xhat)
            dhidden = norm_pull(xhat, rstd, gain_ref[layer, 1:2, :], grad)
            dx_ref[rows, :] += dhidden
            datt[rows, :] = (dbranch[rows, :] + dhidden).astype(BF16)

        tiles(second_pull)
        point()
        prefetch("hidden", layer)
        load("mixed", layer).wait()
        square_unit(mixed, datt)
        prefetch("mixed", layer)
        slot()
        load("wo", layer).wait()
        dmixed[...] = dot(datt[...], wo[...], NT).astype(BF16)
        prefetch("wo", layer)
        point()
        load("qkv", layer).wait()
        if layer == 1:
            load_bias.wait()

        def attend(pair, carry):
            cols = pl.ds(pl.multiple_of(pair * LANES, LANES), LANES)
            key, value = qkv[1, :, cols], qkv[2, :, cols]
            scaled = key * BF16(0.125)
            query = qkv[0, :, cols] * BF16(0.125)
            grad = dmixed[:, cols]
            sums = None
            for mask in masks:
                query_head, grad_head = only(mask, query), only(mask, grad)
                expo, inverse = softmax_parts(dot(query_head, key, NT) + bias_ref[layer])
                probs = expo * inverse
                dprobs = dot(grad_head, value, NT)
                dscores = probs * (dprobs - jnp.sum(probs * dprobs, axis=-1, keepdims=True))
                dscores = dscores.astype(BF16)
                parts = [
                    dot(dscores, only(mask, scaled)),
                    dot(dscores, query_head, TN),
                    dot(probs.astype(BF16), grad_head, TN),
                ]
                sums = parts if sums is None else [left + right for left, right in zip(sums, parts)]
            for j in range(3):
                dqkv[j, :, cols] = sums[j].astype(BF16)
            return carry

        pairs = dmixed.shape[1] // LANES
        for part_of in range(3):
            lax.fori_loop(pairs * part_of // 3, pairs * (part_of + 1) // 3, attend, 0)
            point()
        prefetch("qkv", layer)

        load("normed", layer).wait()
        for j in range(3):
            square_unit(dqkv.at[j], normed)
            slot()
        prefetch("normed", layer)
        load("wq", layer).wait()
        work[...] = dot(dqkv[0], wq[0])
        work[...] += dot(dqkv[1], wq[1])
        point()
        work[...] += dot(dqkv[2], wq[2])
        point()
        prefetch("wq", layer)
        if layer == 1:
            load("x", 1).wait()

        def first_pull(rows):
            xhat, rstd = standardize(x_ref[rows, :].astype(F32))
            grad = work[rows, :]
            small_ref[0] += fold_rows(grad * xhat)
            total = dx_ref[rows, :] + norm_pull(xhat, rstd, gain_ref[layer, 0:1, :], grad)
            dx_low[layer, rows, :] = total.astype(BF16)

        tiles(first_pull)
        point()
        prefetch("x", layer)
        hand_back(layer, dx_low.at[layer], main_out, back_out)
        sums = jnp.sum(small_ref[...], axis=1)
        if layer == 1:
            tot[0] = jnp.zeros(tot.shape[1:], F32)
            tot[0, 3:5, :] = sums[0:2]
        else:
            tot[0, 0:3, :] = sums
            total_move(0).start()

    run_layer(1)
    run_layer(0)
    added = 0
    for targets in points:
        reach(*targets)
        add_total(added)
        added += 1
    reach(2 * UNITS, 2 * UNITS, 2 * UNITS)
    for step in range(added, len(doubled)):
        add_total(step)
    small_out[...] = tot[len(doubled)]
    for step in range(len(doubled)):
        total_move(step).wait_send()
    for back in backs:
        back.wait()
    for u in range(UNITS, 2 * UNITS):
        moved_out(u)

    if not in_kernel_z:
        for v in range(UNITS):
            remote(
                plane.at[v], mlp_out.at[v, their_rows, :], mlp_send.at[v], mlp_recv.at[v, 0, 1 - s], here.sibling
            ).wait_recv()
        return
    for source in range(4):
        for half in range(2):
            rows = pl.ds(half * half_rows, half_rows)

            def arrive():
                for kind in range(2):
                    target = mlp_out.at[kind, source, rows, :]
                    remote(target, target, mlp_send.at[0], mlp_recv.at[kind, source, half], here.sibling).wait_recv()
                for b in range(4):
                    target = att_out.at[b, source, rows, :]
                    remote(
                        target, target, att_send.at[0, 0, 0], att_recv.at[b, source, half], here.sibling
                    ).wait_recv()

            pl.when(jnp.logical_not((d == source) & (s == half)))(arrive)


def backward(n_dp, tok_rows, keep, gains, router, bias, grad, x, saved):
    width = x.shape[2]
    held, _, spare = token_layout(tok_rows)
    quarter_rows = width // 4
    half_rows = quarter_rows // 2
    in_kernel_z = n_dp == 4
    steps = 3
    while 2 ** (steps - 3) < n_dp:
        steps += 1
    any_spec = pl.BlockSpec(memory_space=pl.ANY)
    vmem = pl.BlockSpec(memory_space=pltpu.VMEM)
    dma = pltpu.SemaphoreType.DMA

    def low(*shape):
        return pltpu.VMEM(shape, BF16)

    def wide(*shape):
        return pltpu.VMEM(shape, F32)

    mlp_shape = (2, 4, quarter_rows, width) if in_kernel_z else (UNITS, quarter_rows, width)
    units = 2 * UNITS
    scratch = [
        low(ROWS, width), low(ROWS, width), wide(ROWS, width), low(2, ROWS, width), wide(3, 8, width),
        wide(steps + 1, 8, width), wide(steps, 8, width), wide(2, ROWS, ROWS),
        low(3, width, width), low(width, width), low(2, width, width), low(2, width, width),
        low(ROWS, width), low(3, ROWS, width), low(ROWS, width), wide(ROWS, width), low(ROWS, width),
        low(4, ROWS, width), low(2, ROWS, width), wide(ROWS, width),
        wide(ROWS, width), low(ROWS, width), low(width, ROWS), wide(ROWS, width), low(4, ROWS, width),
        wide(ROWS, width), low(ROWS, width), low(ROWS, width), low(3, ROWS, width),
        low(RING, 4, quarter_rows, width), low(UNITS, 4, half_rows, width), low(UNITS, 2, half_rows, width),
        low(UNITS, half_rows, width), low(UNITS, half_rows, width),
        dma((2, 11)), dma((2, 2)), dma((2, 2)), dma((2, 2)),
        dma((units,)), dma((units,)), dma((units, 2)), dma((units, 2)), dma((units,)), dma((units,)),
        dma((units,)), dma((UNITS, 4, 2)), dma((2, 4, 4)), dma((4, 4, 2)), dma((units, 4)),
        dma((steps,)), dma((steps,)), *[sem for _ in range(4) for sem in hand_back_sems()],
    ]
    return pl.pallas_call(
        functools.partial(backward_kernel, in_kernel_z, tok_rows),
        out_shape=[
            jax.ShapeDtypeStruct((8, width), F32),
            jax.ShapeDtypeStruct((2, held, width), BF16),
            jax.ShapeDtypeStruct((2, spare, width), BF16),
            jax.ShapeDtypeStruct((2, held, width), BF16),
            jax.ShapeDtypeStruct((2, spare, width), BF16),
            jax.ShapeDtypeStruct(mlp_shape, BF16),
            jax.ShapeDtypeStruct((4, 4, quarter_rows, 2 * LANES), BF16),
        ],
        in_specs=[vmem] * 3 + [any_spec] * 15,
        out_specs=[vmem] + [any_spec] * 6,
        scratch_shapes=scratch,
        compiler_params=pltpu.CompilerParams(
            collective_id=1, has_side_effects=True, vmem_limit_bytes=VMEM_BYTES
        ),
        cost_estimate=pl.CostEstimate(flops=96 * ROWS * width * width, bytes_accessed=120_000_000, transcendentals=0),
        name="backward_layers",
    )(keep, gains, router, bias, grad, x, *saved)


def finish_kernel(
    tok_rows, sums,
    small_ref, y_main, y_back, dx_main, dx_back, mlp_in, att_in,
    y_out, dx_out, ones_out, twos_out, router_out, *rest,
):
    if sums:
        (down_out, up_out, out_out, qkv_out, *rest) = rest
    y_rows, y_tail, dx_rows, dx_tail, y_buf, dx_buf, mlp, att, mlp_sum, att_sum, in_sem, out_sem = rest
    held, low, spare = token_layout(tok_rows)
    section, d, t = lax.axis_index("section"), lax.axis_index("dp"), lax.axis_index("tensor")
    n_dp, quarters = lax.axis_size("dp"), lax.axis_size("tensor")
    x_half = t % 2
    moves = [(dx_main, dx_rows), (dx_back, dx_tail), (y_main, y_rows), (y_back, y_tail)]
    if sums:
        moves += [(mlp_in.at[0], mlp.at[0]), (mlp_in.at[1], mlp.at[1]), (att_in, att)]
    copies = [pltpu.make_async_copy(src, dst, in_sem.at[i]) for i, (src, dst) in enumerate(moves)]
    for copy in copies:
        copy.start()
    results = []

    def give(src, dst):
        copy = pltpu.make_async_copy(src, dst, out_sem.at[len(results)])
        copy.start()
        results.append(copy)

    def join(main, back, buffer, out):
        def plain(i, carry):
            rows = pl.ds(pl.multiple_of(i * 16, 16), 16)
            for m in range(2):
                buffer[rows, m, :] = main[m, rows, :].astype(buffer.dtype)
            return carry

        def mixed_rows(i, carry):
            rows = pl.ds(pl.multiple_of(i * 16, 16), 16)
            from_back = pl.ds(pl.multiple_of(i * 16 - low, 16), 16)
            row = lax.broadcasted_iota(jnp.int32, (16, 1), 0) + i * 16
            is_back = (x_half == 0) & (row >= CUT)
            for m in range(2):
                value = jnp.where(is_back, back[m, from_back, :], main[m, rows, :])
                buffer[rows, m, :] = value.astype(buffer.dtype)
            return carry

        lax.fori_loop(0, low // 16, plain, 0)
        lax.fori_loop(low // 16, held // 16, mixed_rows, 0)
        give(buffer.at[pl.ds(0, tok_rows)], out)

    for i, pieces in enumerate(((dx_rows, dx_tail, dx_buf, dx_out), (y_rows, y_tail, y_buf, y_out))):
        copies[2 * i].wait()
        copies[2 * i + 1].wait()
        join(*pieces)
    if sums:
        width = mlp_sum.shape[1]
        for kind in range(2):
            copies[4 + kind].wait()

            def add(rows):
                parts = [mlp[kind, source, rows, :].astype(F32) for source in range(4)]
                mlp_sum[kind, rows, :] = parts[0] + parts[1] + parts[2] + parts[3]

            tiles(add, rows=width, tile=32)
            give(mlp_sum.at[kind], (down_out, up_out)[kind])
        copies[6].wait()
        for b in range(4):
            total = att[b, 0].astype(F32) + att[b, 1].astype(F32) + att[b, 2].astype(F32) + att[b, 3].astype(F32)
            total = jnp.where(d % 2 == 0, total[:, :width], total[:, -width:])
            att_sum[b] = total if b == 0 else total.T
            give(att_sum.at[b], out_out if b == 0 else qkv_out.at[b - 1])

    columns = small_ref[...].T
    place = d * quarters + t

    def pick(values, start, count):
        row = lax.broadcasted_iota(jnp.int32, (columns.shape[0], count), 0)
        lane = lax.broadcasted_iota(jnp.int32, (columns.shape[0], count), 1)
        return jnp.sum(jnp.where(row == start + lane, values, 0.0), axis=0, keepdims=True)

    span = ones_out.shape[1]
    ones_out[...] = pick(jnp.where(section == 0, columns[:, 0:1], columns[:, 3:4]), place * span, span)
    twos_out[...] = pick(jnp.where(section == 0, columns[:, 1:2], columns[:, 4:5]), place * span, span)
    span = router_out.shape[1]
    router_out[...] = pick(columns[:, 2:3], (section * n_dp * quarters + place) * span, span)
    for copy in results:
        copy.wait()


def finish(tok_rows, n_dp, quarters, small, y_main, y_back, dx_main, dx_back, mlp, att):
    width = small.shape[1]
    held, _, spare = token_layout(tok_rows)
    part = width // 4
    span = width // (n_dp * quarters)
    sums = n_dp == 4
    any_spec = pl.BlockSpec(memory_space=pl.ANY)
    vmem = pl.BlockSpec(memory_space=pltpu.VMEM)
    shapes = [
        jax.ShapeDtypeStruct((tok_rows, 2, width), BF16), jax.ShapeDtypeStruct((tok_rows, 2, width), F32),
        jax.ShapeDtypeStruct((1, span), F32), jax.ShapeDtypeStruct((1, span), F32),
        jax.ShapeDtypeStruct((1, span // 2), F32),
    ]
    specs = [any_spec, any_spec, vmem, vmem, vmem]
    if sums:
        shapes += [jax.ShapeDtypeStruct(shape, F32) for shape in ((part, width), (part, width), (part, part), (3, part, part))]
        specs += [any_spec] * 4
    dma = pltpu.SemaphoreType.DMA
    return pl.pallas_call(
        functools.partial(finish_kernel, tok_rows, sums),
        out_shape=shapes,
        in_specs=[vmem] + [any_spec] * 6,
        out_specs=specs,
        scratch_shapes=[
            pltpu.VMEM((2, held, width), BF16), pltpu.VMEM((2, spare, width), BF16),
            pltpu.VMEM((2, held, width), BF16), pltpu.VMEM((2, spare, width), BF16),
            pltpu.VMEM((held, 2, width), BF16), pltpu.VMEM((held, 2, width), F32),
            pltpu.VMEM((2, 4, part, width), BF16), pltpu.VMEM((4, 4, part, 2 * LANES), BF16),
            pltpu.VMEM((2, part, width), F32), pltpu.VMEM((4, part, part), F32), dma((7,)), dma((8,)),
        ],
        compiler_params=pltpu.CompilerParams(vmem_limit_bytes=VMEM_BYTES),
        cost_estimate=pl.CostEstimate(flops=4_000_000, bytes_accessed=12_000_000, transcendentals=0),
        name="finish",
    )(small, y_main, y_back, dx_main, dx_back, mlp, att)


def on_device(
    patches, cotangent, crop_lengths, route_mask, w_qkv, w_out, w_up, w_down, ln1_gain, ln2_gain, router
):
    tok_rows, width = patches.shape[1:]
    n_dp, quarters = lax.axis_size("dp"), lax.axis_size("tensor")
    wq = jnp.transpose(w_qkv[0], (1, 2, 0))
    x, gains, keep_rows, router_row, bias, grad, *saved = forward(
        crop_lengths, route_mask, ln1_gain, ln2_gain, router, jnp.transpose(patches, (1, 0, 2)),
        jnp.transpose(cotangent, (1, 0, 2)), wq, w_out[0], w_up[0], w_down[0],
    )
    small, y_main, y_back, dx_main, dx_back, mlp, att = backward(
        n_dp, tok_rows, keep_rows, gains, router_row, bias, grad, x, saved
    )

    y_out, dx_out, ones, twos, routers, *grads = finish(
        tok_rows, n_dp, quarters, small, y_main, y_back, dx_main, dx_back, mlp, att
    )
    outputs = jnp.transpose(y_out, (1, 0, 2))
    input_grads = jnp.transpose(dx_out, (1, 0, 2))
    if n_dp == 4:
        down, up, out, qkv = grads
    else:

        def scatter(value, dim):
            return lax.psum_scatter(value, "dp", scatter_dimension=dim, tiled=True).astype(F32)

        down = scatter(mlp[:4].reshape(width, width), 0)
        up = scatter(mlp[4:8].reshape(width, width), 0)
        out = scatter(mlp[8], 1)
        qkv = jnp.transpose(scatter(mlp[9:], 2), (0, 2, 1))
    qkv = jnp.transpose(qkv, (1, 0, 2))
    return (
        outputs[None], input_grads[None], qkv[None], out[None], up[None], down.T[None], ones, twos, routers[0],
    )


def solution(mesh):
    return jax.shard_map(
        on_device,
        mesh=mesh,
        in_specs=(
            P(None, ("dp", "tensor"), None),
            P(None, ("dp", "tensor"), None),
            P(None, "dp", None),
            P(None, "dp"),
            P("section", None, None, "tensor"),
            P("section", "tensor", None),
            P("section", None, "tensor"),
            P("section", "tensor", None),
            P("section", None),
            P("section", None),
            P(),
        ),
        out_specs=(
            P("section", None, ("dp", "tensor"), None),
            P("section", None, ("dp", "tensor"), None),
            P("section", "dp", None, "tensor"),
            P("section", "tensor", "dp"),
            P("section", "dp", "tensor"),
            P("section", "tensor", "dp"),
            P("section", ("dp", "tensor")),
            P("section", ("dp", "tensor")),
            P(("section", "dp", "tensor")),
        ),
        check_vma=False,
    )
```

```python
import functools

import jax
import jax.numpy as jnp
from jax import lax
from jax.experimental import pallas as pl
from jax.experimental.pallas import tpu as pltpu
from jax.sharding import PartitionSpec as P

HEAD_DIM = 64
LANES = 128
CUT = 197
EPS = 1e-06
NEG = -1000000000.0
ROWS = 384
TILE = 64
MESH = pl.DeviceIdType.MESH
NT = (((1,), (1,)), ((), ()))
TN = (((0,), (0,)), ((), ()))
NN = (((1,), (0,)), ((), ()))
VMEM_BYTES = 62 * 1024 * 1024
F32, BF16 = jnp.float32, jnp.bfloat16


def dot(left, right, dims=NN):
    return lax.dot_general(left, right, dims, preferred_element_type=F32)


def tiles(body, rows=ROWS, tile=TILE):
    def step(index, carry):
        body(pl.ds(pl.multiple_of(index * tile, tile), tile))
        return carry

    lax.fori_loop(0, rows // tile, step, 0)


def standardize(values):
    centre = values - jnp.mean(values, axis=-1, keepdims=True)
    spread = jnp.mean(centre * centre, axis=-1, keepdims=True)
    rstd = lax.rsqrt(spread + EPS)
    return centre * rstd, rstd


def norm_pull(xhat, rstd, gain, grad):
    grad_hat = grad * gain
    mean_grad = jnp.mean(grad_hat, axis=-1, keepdims=True)
    mean_both = jnp.mean(grad_hat * xhat, axis=-1, keepdims=True)
    return rstd * (grad_hat - mean_grad - xhat * mean_both)


def fold_rows(values):
    return jnp.sum(values.reshape(values.shape[0] // 8, 8, values.shape[1]), axis=0)


def half_masks():
    lane = lax.broadcasted_iota(jnp.int32, (1, LANES), 1)
    return [lane < HEAD_DIM, lane >= HEAD_DIM]


def softmax_parts(scores):
    expo = jnp.exp(scores - jnp.max(scores, axis=-1, keepdims=True))
    return expo, 1.0 / jnp.sum(expo, axis=-1, keepdims=True)


def valid_rows(x_half, tok_rows, row):
    held, low, _ = token_layout(tok_rows)
    rest = (row < tok_rows) | ((row >= held + CUT - low) & (row < held + tok_rows - low))
    return ((x_half == 0) & (row < CUT)) | ((x_half == 1) & rest)


def only(mask, values):
    return jnp.where(mask, values, jnp.zeros_like(values))


def token_layout(tok_rows):
    held = -(-tok_rows // 16) * 16
    low = CUT // 16 * 16
    return held, low, held - low


def transpose_into(src, dst):
    def step(index, carry):
        cols = pl.ds(pl.multiple_of(index * LANES, LANES), LANES)
        dst[cols, :] = src[:, cols].astype(F32).T.astype(BF16)
        return carry

    lax.fori_loop(0, dst.shape[0] // LANES, step, 0)


class Place:
    def __init__(self):
        self.s = lax.axis_index("section")
        self.d = lax.axis_index("dp")
        self.t = lax.axis_index("tensor")
        self.x = self.t % 2
        self.y = self.t // 2
        self.near = self.t + (1 - self.s) * (1 - 2 * self.x) + self.s * (2 - 4 * self.y)
        self.far = self.t + self.s * (1 - 2 * self.x) + (1 - self.s) * (2 - 4 * self.y)
        self.cross = 3 - self.t
        self.beside = self.t + 1 - 2 * self.x
        self.above = self.t + 2 - 4 * self.y
        self.sibling = (1 - self.s, self.d, self.t)
        self.diagonal = (1 - self.s, self.d, self.beside)

    def at(self, tensor):
        return (self.s, self.d, tensor)


def remote(src, dst, send, recv, device):
    return pltpu.make_async_remote_copy(
        src_ref=src, dst_ref=dst, send_sem=send, recv_sem=recv, device_id=device, device_id_type=MESH
    )


def greet(peers):
    barrier = pltpu.get_barrier_semaphore()
    for peer in peers:
        pl.semaphore_signal(barrier, inc=1, device_id=peer, device_id_type=MESH)
    pl.semaphore_wait(barrier, len(peers))


class HandBack:
    def __init__(self, here, layer, tok_rows, rows_ref, main_out, back_out, sems):
        held, _, spare = token_layout(tok_rows)
        main_send, main_recv, back_send, back_recv, own = sems
        self.here, self.layer = here, layer
        main, back = rows_ref.at[pl.ds(0, held)], rows_ref.at[pl.ds(held, spare)]
        s = here.s
        self.local = pltpu.make_async_copy(main, main_out.at[s], own)
        self.away = remote(main, main_out.at[s], main_send, main_recv, here.sibling)
        self.backs = [
            remote(back, back_out.at[s], back_send, back_recv.at[s], (layer, here.d, here.beside)),
        ]
        self.landing = [
            remote(back, back_out.at[i], back_send, back_recv.at[i], here.sibling) for i in range(2)
        ]

    def start(self):
        mine = self.here.s == self.layer
        pl.when(mine)(self.local.start)
        pl.when(jnp.logical_not(mine))(self.away.start)
        pl.when(self.here.x == 1)(self.backs[0].start)

    def wait(self):
        mine = self.here.s == self.layer

        @pl.when(mine)
        def _():
            self.local.wait()
            self.away.wait_recv()

            @pl.when(self.here.x == 0)
            def _():
                for landing in self.landing:
                    landing.wait_recv()

        pl.when(jnp.logical_not(mine))(self.away.wait_send)
        pl.when(self.here.x == 1)(self.backs[0].wait_send)


def hand_back_sems():
    dma = pltpu.SemaphoreType.DMA
    return [dma, dma, dma, dma((2,)), dma]


KINDS = 4
FIRST_PLAN = [
    (0, 0, False), (0, 1, True), (1, 0, False), (2, 0, True), (2, 2, True), (3, 0, True), (3, 2, False), (3, 3, False)
]
SECOND_PLAN = [
    (0, 0, False), (0, 1, True), (1, 0, False), (2, 0, True), (2, 2, True),
    (3, 0, False), (3, 1, False), (3, 2, False), (3, 3, False),
]
PLAN = [(0, *step) for step in FIRST_PLAN] + [(1, *step) for step in SECOND_PLAN]
STARTS = (0, len(FIRST_PLAN))
WINDOW = 2


def forward_kernel(
    tok_rows,
    crop_ref, route_ref, one_ref, two_ref, router_in, patch_ref, cotangent_ref, wq_ref, wo_ref, wu_ref, wd_ref,
    x_out, gain_out, keep_out, router_out, bias_out, grad_out,
    gq_out, go_out, gu_out, gd_out, norm_out, qkv_out, mixed_out, hidden_out,
    second_out, active_out, slope_out, branch_out,
    x_own, gain_ref, my_gain, keep_ref, router_ref, bias_ref, tokens, spare_rows, grad_own,
    gq, go, gu, gd, normed, qkv, mixed, hidden, second, active, slope, branch, work,
    own_sem, lend_send, lend_recv, a_send, a_recv, b_send, b_recv, c_send, c_recv,
    e_send, e_recv, f_send, f_recv, out_sem, save_sem, tok_sem, tok_send, tok_recv, gain_sem, gain_send, gain_recv, x_sem, bias_sem,
):
    here = Place()
    held, low, spare = token_layout(tok_rows)
    part = wo_ref.shape[0]
    unit = part // 2
    shards = (wq_ref, wo_ref, wu_ref, wd_ref)

    def block(kind, layer, quarter):
        rows = pl.ds(pl.multiple_of(quarter * part, part), part)
        if kind == 0:
            return gq.at[layer, :, rows, :]
        if kind == 1:
            return go.at[layer, rows, :]
        return (gu if kind == 2 else gd).at[layer, quarter]

    parity = here.d % 2

    def chunk(step, quarter, half, other=0):
        layer, kind, piece, shared = PLAN[step]
        if shared:
            piece = piece + other + (1 - 2 * other) * parity
        if kind < 2:
            rows = pl.ds(pl.multiple_of(quarter * part + half * unit, unit), unit)
            return gq.at[layer, piece, rows, :] if kind == 0 else go.at[layer, rows, :]
        rows = pl.ds(pl.multiple_of((4 * half + piece) * unit, unit), unit)
        return (gu if kind == 2 else gd).at[layer, quarter, rows, :]

    def own_copy(kind):
        return pltpu.make_async_copy(shards[kind], block(kind, here.s, here.t), own_sem.at[kind])

    def lend(kind, layer):
        return remote(
            shards[kind], block(kind, layer, here.t), lend_send.at[kind], lend_recv.at[kind], here.sibling
        )

    def along(step, quarter, peer, send, recv):
        piece = chunk(step, quarter, here.s)
        return remote(piece, piece, send.at[step], recv.at[step], peer)

    def send_a(step):
        return along(step, here.t, here.at(here.near), a_send, a_recv)

    def send_b(step):
        return along(step, here.t, here.at(here.far), b_send, b_recv)

    def send_c(step):
        return along(step, here.near, here.at(here.far), c_send, c_recv)

    def send_e(step, which, half=None, other=0):
        piece = chunk(step, three[which], here.s if half is None else half, other)
        index = which + 3 * other
        return remote(piece, piece, e_send.at[step, index], e_recv.at[step, index], here.sibling)

    def send_f(step, which, other=0):
        piece = chunk(step, three[which], here.s, other)
        return remote(piece, piece, f_send.at[step, which], f_recv.at[step, which], z_beside)

    three = (here.near, here.far, here.cross)
    z_beside = (here.s, here.d + 1 - 2 * parity, here.t)
    total = len(PLAN)

    greet([here.sibling, here.at(here.near), here.at(here.far), z_beside])

    my_gain[...] = jnp.zeros_like(my_gain)
    my_gain[0:1, :] = one_ref[...]
    my_gain[1:2, :] = two_ref[...]
    gain_own = pltpu.make_async_copy(my_gain, gain_ref.at[here.s], gain_sem)
    gain_away = remote(my_gain, gain_ref.at[here.s], gain_send, gain_recv, here.sibling)
    token_loads = []
    for which, source in enumerate((patch_ref, cotangent_ref)):
        tokens[which, pl.ds(tok_rows, held - tok_rows)] = jnp.zeros((held - tok_rows, *tokens.shape[2:]), BF16)
        token_loads.append(
            pltpu.make_async_copy(source, tokens.at[which, pl.ds(0, tok_rows)], tok_sem.at[which])
        )
    tok_away = [
        remote(src, dst.at[pl.ds(held, spare)], tok_send.at[i], tok_recv.at[i], here.at(here.beside))
        for i, (src, dst) in enumerate(((spare_rows, x_own.at[0]), (grad_own.at[pl.ds(low, spare)], grad_out)))
    ]
    grad_save = pltpu.make_async_copy(grad_own, grad_out.at[pl.ds(0, held)], tok_sem.at[2])
    for copy in token_loads:
        copy.start()
    gain_own.start()
    gain_away.start()
    for kind in range(KINDS):
        lend(kind, here.s).start()
        own_copy(kind).start()

    def issue(step):
        if step >= total:
            return
        layer, kind, piece, _ = PLAN[step]
        if piece == 0:
            pl.when(here.s == layer)(lambda: own_copy(kind).wait())
            pl.when(here.s != layer)(lambda: lend(kind, layer).wait_recv())
        send_a(step).start()
        send_b(step).start()

    def pass_on(step, which):
        send_e(step, which).start()
        if PLAN[step][3]:
            send_f(step, which).start()

    def relay(step):
        if step >= total:
            return
        send_a(step).wait_recv()
        send_c(step).start()
        pass_on(step, 0)
        issue(step + WINDOW)

    def fetch(step):
        if step >= total:
            return
        send_b(step).wait_recv()
        pass_on(step, 1)
        send_c(step).wait_recv()
        pass_on(step, 2)

    moved = [0]
    relayed = [0]

    def relays(upto):
        while relayed[0] < min(upto, total):
            relay(relayed[0])
            relayed[0] += 1

    def tick(upto):
        while moved[0] <= min(upto, total - 1):
            relays(moved[0] + 3)
            fetch(moved[0])
            moved[0] += 1

    def pump(step):
        tick(step + 2)
        shared = PLAN[step][3]
        if shared:
            for which in range(3):
                send_f(step, which, 1).wait_recv()
                send_e(step, which, None, 1).start()
        for other in range(1 + shared):
            for which in range(3):
                send_e(step, which, 1 - here.s, other).wait_recv()

    for step in range(WINDOW):
        issue(step)
    def take(which, dst):
        def step(rows):
            dst[rows, :] = jnp.where(here.s == 0, tokens[which, rows, 0, :], tokens[which, rows, 1, :])

        tiles(step, rows=held, tile=16)

    for copy in token_loads:
        copy.wait()
    take(0, x_own.at[0])
    spare_rows[...] = x_own[0, pl.ds(low, spare), :]
    pl.when(here.x == 0)(tok_away[0].start)
    take(1, grad_own)
    pl.when(here.x == 0)(tok_away[1].start)
    grad_save.start()
    router_ref[...] = router_in[...].astype(F32).reshape(router_ref.shape)
    router_out[...] = router_ref[...]

    relays(1)

    image = here.t // 2
    slot_len = route_ref.shape[1] // crop_ref.shape[1]
    routes = jnp.where(here.s == 0, route_ref[0:1, :], route_ref[1:2, :]).astype(F32)
    lanes = -(-(routes.shape[1] + ROWS) // LANES) * LANES
    routes = jnp.concatenate([routes, jnp.zeros((1, lanes - routes.shape[1]), F32)], axis=1)
    routes = jnp.broadcast_to(routes, (8, lanes))

    def routed_from(start):
        return pltpu.roll(routes, (2 * lanes - start) % lanes, 1)[0:1, :ROWS]

    def rows_info(row):
        valid = valid_rows(here.x, tok_rows, row)
        position = jnp.where(row < held, here.x * tok_rows + row, low - held + row)
        position = jnp.where(here.x == 0, row, position)
        crop = jnp.zeros_like(row)
        end = 0
        for i in range(crop_ref.shape[2]):
            end = end + crop_ref[here.s, image, i]
            crop += (position >= end).astype(jnp.int32)
        return valid, jnp.where(valid, crop, -1)

    across = lax.broadcasted_iota(jnp.int32, (1, ROWS), 1)
    valid, crop_across = rows_info(across)
    routed = jnp.where(
        across < held,
        routed_from(image * slot_len + here.x * tok_rows),
        routed_from(image * slot_len + low - held),
    )
    routed = jnp.where(valid, routed, 0.0)
    keep_ref[...] = jnp.broadcast_to(routed, (LANES, ROWS)).T[:, 0:1]
    keep_out[...] = keep_ref[...]
    usable = jnp.where(valid, routed, 1.0) > 0.0

    def allow(rows):
        _, crop_down = rows_info(lax.broadcasted_iota(jnp.int32, (TILE, 1), 0) + rows.start)
        same = crop_down == crop_across
        bias_ref[0, rows, :] = jnp.where(same & usable, 0.0, NEG)
        bias_ref[1, rows, :] = jnp.where(same, 0.0, NEG)

    tiles(allow)
    bias_save = pltpu.make_async_copy(bias_ref, bias_out, bias_sem)
    bias_save.start()
    relays(2)

    pl.when(here.x == 1)(tok_away[0].wait_recv)

    def clear(block):
        def step(rows):
            row = lax.broadcasted_iota(jnp.int32, (TILE, 1), 0) + rows.start
            block[rows, :] = only(valid_rows(here.x, tok_rows, row), block[rows, :])

        tiles(step)

    clear(x_own.at[0])
    x_saves = [pltpu.make_async_copy(x_own.at[i], x_out.at[i], x_sem.at[i]) for i in range(3)]
    x_saves[0].start()
    gain_own.wait()
    gain_away.wait_recv()
    gain_out[...] = gain_ref[...]
    masks = half_masks()
    saves = []

    def weight_save(kind, layer):
        src, dst = ((gq, gq_out), (go, go_out), (gu, gu_out), (gd, gd_out))[kind]
        return pltpu.make_async_copy(src.at[layer], dst.at[layer], out_sem.at[layer, kind])

    def keep_weight(kind, layer):
        weight_save(kind, layer).start()

    def save(index, layer, src, dst):
        copy = pltpu.make_async_copy(src, dst.at[layer], save_sem.at[index])
        copy.start()
        return copy

    for layer in range(2):
        x_now = x_own.at[layer]

        def first_norm(rows):
            xhat, _ = standardize(x_now[rows, :].astype(F32))
            normed[rows, :] = (xhat * gain_ref[layer, 0:1, :]).astype(BF16)

        for copy in saves:
            copy.wait()
        saves = []
        tiles(first_norm)
        saves.append(save(0, layer, normed, norm_out))
        base = STARTS[layer]
        pump(base)
        qkv[0] = dot(normed[...], gq[layer, 0], NT).astype(BF16)
        pump(base + 1)
        keep_weight(0, layer)

        def project(j, carry):
            qkv[j] = dot(normed[...], gq[layer, j], NT).astype(BF16)
            return carry

        lax.fori_loop(1, 3, project, 0)
        saves.append(save(1, layer, qkv, qkv_out))

        def attend(pair, carry):
            cols = pl.ds(pl.multiple_of(pair * LANES, LANES), LANES)
            key, value = qkv[1, :, cols], qkv[2, :, cols]
            query = qkv[0, :, cols] * BF16(0.125)
            outs = []
            for mask in masks:
                expo, inverse = softmax_parts(dot(only(mask, query), key, NT) + bias_ref[layer])
                outs.append(dot(expo.astype(BF16), value) * inverse)
            mixed[:, cols] = jnp.where(masks[0], outs[0], outs[1]).astype(BF16)
            return carry

        pairs = mixed.shape[1] // LANES
        for part_of in range(3):
            lax.fori_loop(pairs * part_of // 3, pairs * (part_of + 1) // 3, attend, 0)
            tick(base + 4 + part_of)
        saves.append(save(2, layer, mixed, mixed_out))
        pump(base + 2)
        keep_weight(1, layer)
        branch[...] = dot(mixed[...], go[layer])

        def second_norm(rows):
            value = x_now[rows, :].astype(F32) + branch[rows, :]
            hidden[rows, :] = value
            xhat, _ = standardize(value)
            second[rows, :] = (xhat * gain_ref[layer, 1:2, :]).astype(BF16)

        tiles(second_norm)
        saves.append(save(3, layer, hidden, hidden_out))
        saves.append(save(4, layer, second, second_out))
        pump(base + 3)
        pump(base + 4)
        keep_weight(2, layer)

        def widen(g, carry):
            work[...] = dot(second[...], gu[layer, g])

            def bend(rows):
                upper = work[rows, :]
                phi = 0.5 * (1.0 + lax.erf(upper * 0.7071067811865476))
                bell = jnp.exp(-0.5 * upper * upper) * 0.3989422804014327
                active[g, rows, :] = (upper * phi).astype(BF16)
                slope[g, rows, :] = (phi + upper * bell).astype(BF16)

            tiles(bend, tile=32)
            return carry

        for g in range(4):
            widen(g, 0)
            tick(base + 6 + g)
        saves.append(save(5, layer, active, active_out))
        saves.append(save(6, layer, slope, slope_out))
        for step in range(base + 5, (*STARTS, total)[layer + 1]):
            pump(step)
        keep_weight(3, layer)

        def narrow(g, carry):
            branch[...] += dot(active[g], gd[layer, g])
            return carry

        lax.fori_loop(0, 4, narrow, 0)
        if layer == 0:
            saves.append(save(7, layer, branch, branch_out))

        def finish(rows):
            value = x_now[rows, :].astype(F32)
            change = branch[rows, :]
            if layer == 0:
                logit = jnp.sum(value * router_ref[...], axis=-1, keepdims=True)
                change = change * (keep_ref[rows, :] / (1.0 + jnp.exp(-logit)))
            x_own[layer + 1, rows, :] = (value + change).astype(BF16)

        tiles(finish)
        x_saves[layer + 1].start()

    for copy in [*saves, *x_saves, grad_save, bias_save]:
        copy.wait()
    gain_away.wait_send()

    @pl.when(here.x == 0)
    def _():
        for away in tok_away:
            away.wait_send()

    pl.when(here.x == 1)(tok_away[1].wait_recv)
    for layer in range(2):
        for kind in range(KINDS):
            weight_save(kind, layer).wait()
    for kind in range(KINDS):
        lend(kind, here.s).wait_send()
    for step in range(total):
        send_a(step).wait_send()
        send_b(step).wait_send()
        send_c(step).wait_send()
        shared = PLAN[step][3]
        for which in range(3):
            send_e(step, which).wait_send()
            if shared:
                send_f(step, which).wait_send()
                send_e(step, which, None, 1).wait_send()


def forward(crops, routes, one, two, router, patches, cotangent, wq, wo, wu, wd):
    tok_rows, _, width = patches.shape
    held, _, spare = token_layout(tok_rows)
    any_spec = pl.BlockSpec(memory_space=pl.ANY)
    vmem = pl.BlockSpec(memory_space=pltpu.VMEM)

    def pair(*shape, dtype=BF16):
        return jax.ShapeDtypeStruct((2, *shape), dtype)

    shapes = [
        jax.ShapeDtypeStruct((3, ROWS, width), BF16), pair(8, width, dtype=F32),
        jax.ShapeDtypeStruct((ROWS, 1), F32), jax.ShapeDtypeStruct((1, width), F32), pair(ROWS, ROWS, dtype=F32),
        jax.ShapeDtypeStruct((ROWS, width), BF16),
        pair(3, width, width), pair(width, width), pair(4, width, width), pair(4, width, width),
        pair(ROWS, width), pair(3, ROWS, width), pair(ROWS, width), pair(ROWS, width, dtype=F32),
        pair(ROWS, width), pair(4, ROWS, width), pair(4, ROWS, width), pair(ROWS, width, dtype=F32),
    ]
    dma = pltpu.SemaphoreType.DMA
    scratch = [
        pltpu.VMEM((3, ROWS, width), BF16), pltpu.VMEM((2, 8, width), F32), pltpu.VMEM((8, width), F32),
        pltpu.VMEM((ROWS, 1), F32), pltpu.VMEM((1, width), F32), pltpu.VMEM((2, ROWS, ROWS), F32),
        pltpu.VMEM((2, held, 2, width), BF16), pltpu.VMEM((spare, width), BF16), pltpu.VMEM((held, width), BF16),
        pltpu.VMEM((2, 3, width, width), BF16), pltpu.VMEM((2, width, width), BF16),
        pltpu.VMEM((2, 4, width, width), BF16), pltpu.VMEM((2, 4, width, width), BF16),
        pltpu.VMEM((ROWS, width), BF16), pltpu.VMEM((3, ROWS, width), BF16),
        pltpu.VMEM((ROWS, width), BF16), pltpu.VMEM((ROWS, width), F32),
        pltpu.VMEM((ROWS, width), BF16), pltpu.VMEM((4, ROWS, width), BF16),
        pltpu.VMEM((4, ROWS, width), BF16), pltpu.VMEM((ROWS, width), F32),
        pltpu.VMEM((ROWS, width), F32),
        dma((KINDS,)), dma((KINDS,)), dma((KINDS,)),
        *[dma((len(PLAN),))] * 6, *[dma((len(PLAN), 6))] * 2, *[dma((len(PLAN), 3))] * 2,
        dma((2, KINDS)), dma((8,)),
        dma((3,)), dma((2,)), dma((2,)), dma, dma, dma, dma((3,)), dma,
    ]
    return pl.pallas_call(
        functools.partial(forward_kernel, tok_rows),
        out_shape=shapes,
        in_specs=[pl.BlockSpec(memory_space=pltpu.SMEM)] + [vmem] * 4 + [any_spec] * 6,
        out_specs=[any_spec, vmem, vmem, vmem] + [any_spec] * 14,
        scratch_shapes=scratch,
        compiler_params=pltpu.CompilerParams(
            collective_id=0, has_side_effects=True, vmem_limit_bytes=VMEM_BYTES
        ),
        cost_estimate=pl.CostEstimate(flops=24 * ROWS * width * width * 2, bytes_accessed=60_000_000, transcendentals=0),
        name="forward_layers",
    )(crops, routes, one, two, router, patches, cotangent, wq, wo, wu, wd)


UNITS = 12
RING = 6
TOTALS = (3, 6, 9)
Y_FIRST = (20,)
SCHEDULE = [
    (0, 0, 0), (0, 0, 0), (0, 0, 0), (0, 0, 0), (0, 0, 0), (0, 0, 0), (1, 0, 0), (1, 0, 0), (2, 0, 0),
    (2, 0, 0), (2, 0, 0), (3, 1, 0), (3, 1, 0), (3, 1, 0), (4, 2, 0), (4, 2, 0), (4, 2, 0), (6, 3, 1),
    (7, 4, 2), (8, 4, 3), (8, 5, 3), (8, 5, 3), (9, 6, 3), (9, 6, 4), (9, 7, 4), (9, 8, 4), (9, 8, 5),
    (10, 8, 6), (11, 8, 6), (11, 9, 6), (12, 9, 8), (12, 9, 8), (12, 9, 8), (12, 9, 8),
    (12, 10, 8), (12, 10, 8), (12, 10, 8), (13, 11, 8), (13, 11, 9), (14, 11, 9), (14, 11, 9), (14, 12, 9),
    (15, 12, 10), (15, 12, 11), (15, 12, 11), (16, 12, 11), (16, 13, 11), (17, 14, 12), (18, 16, 14),
    (18, 16, 14), (19, 17, 14), (20, 17, 15), (20, 17, 16), (21, 18, 16), (21, 18, 17), (21, 19, 17),
    (21, 19, 17), (21, 20, 17), (23, 21, 19), (23, 21, 19), (24, 21, 20), (24, 21, 21), (24, 22, 21),
    (24, 23, 21), (24, 24, 21), (24, 24, 22), (24, 24, 23), (24, 24, 24),
]


def backward_kernel(
    in_kernel_z, tok_rows,
    keep_ref, gain_ref, router_ref, bias_in, grad_in, x_in,
    gq, go, gu, gd, norm_in, qkv_in, mixed_in, hidden_in, second_in, active_in, slope_in, branch_in,
    small_out, y_main, y_back, main_out, back_out, mlp_out, att_out,
    grad_ref, x_ref, dx_ref, dx_low, small_ref, tot, got, bias_ref,
    wq, wo, wu, wd, normed, qkv, mixed, hidden, second, active, slope, branch,
    dbranch, dfed, dfed_t, work, dup, dsecond, datt, dmixed, dqkv, stage, sib, near_in, far_in, plane,
    load_sem, wu_sem, wd_sem, slope_sem,
    sib_send, sib_recv, near_send, near_recv, far_send, far_recv,
    mlp_send, mlp_recv, att_send, att_recv, local_sem, tot_send, tot_recv, *back_sems,
):
    here = Place()
    s, d, t = here.s, here.d, here.t
    quarter_rows = stage.shape[2]
    half_rows = quarter_rows // 2
    my_rows = pl.ds(pl.multiple_of(s * half_rows, half_rows), half_rows)
    their_rows = pl.ds(pl.multiple_of((1 - s) * half_rows, half_rows), half_rows)
    n_dp = lax.axis_size("dp")

    saved = {
        "active": (active_in, active), "x": (x_in, x_ref), "second": (second_in, second),
        "hidden": (hidden_in, hidden), "mixed": (mixed_in, mixed), "wo": (go, wo), "qkv": (qkv_in, qkv),
        "normed": (norm_in, normed), "wq": (gq, wq), "branch": (branch_in, branch),
    }

    def load(name, layer):
        src, dst = saved[name]
        return pltpu.make_async_copy(src.at[layer], dst, load_sem.at[layer, list(saved).index(name)])

    def prefetch(name, layer):
        if layer == 1:
            load(name, 0).start()

    streams = ((gd, wd, wd_sem), (slope_in, slope, slope_sem), (gu, wu, wu_sem))

    def quarter_load(stream, layer, g):
        src, dst, sems = stream
        return pltpu.make_async_copy(src.at[layer, g], dst.at[g % 2], sems.at[layer, g % 2])

    load_grad = pltpu.make_async_copy(grad_in, grad_ref, load_sem.at[0, len(saved)])
    load_bias = pltpu.make_async_copy(bias_in, bias_ref, load_sem.at[1, len(saved)])
    load_grad.start()

    load("active", 1).start()
    for g in range(2):
        for stream in streams:
            quarter_load(stream, 1, g).start()
    for name in saved:
        if name not in ("active", "branch"):
            load(name, 1).start()
    load("branch", 0).start()
    load_bias.start()

    peers = [here.sibling, here.at(here.near), here.at(here.far), here.diagonal]
    doubled = [here.sibling, here.at(here.near), here.at(here.far)]
    along_z = [(s, (d + shift) % n_dp, t) for shift in range(1, n_dp)]
    peers += along_z
    if in_kernel_z:
        peers += [(1 - s, z, t) for _, z, _ in along_z]
    greet(peers)

    backs = []

    def hand_back(layer, rows_ref, main, back):
        sems = back_sems[5 * len(backs) : 5 * len(backs) + 5]
        backs.append(HandBack(here, layer, tok_rows, rows_ref, main, back, sems))
        backs[-1].start()

    for layer in range(2):
        hand_back(layer, x_in.at[layer + 1], y_main, y_back)

    def total_move(step):
        last = len(doubled)
        return remote(
            tot.at[min(step, last)], got.at[step], tot_send.at[step], tot_recv.at[step], (doubled + along_z)[step]
        )

    def add_total(step):
        total_move(step).wait_recv()
        tot[step + 1] = tot[step] + got[step]
        if step + 1 < len(doubled):
            total_move(step + 1).start()
        else:
            for shift in range(len(along_z)):
                total_move(step + 1 + shift).start()

    class Way:
        def __init__(self, u):
            first_y = 1 if u in Y_FIRST else s
            self.near = here.near if u not in Y_FIRST else here.above
            self.far = here.far if u not in Y_FIRST else here.beside
            self.sent = [first_y * (2 * (1 - here.y) + i) + (1 - first_y) * (2 * i + 1 - here.x) for i in range(2)]
            self.own_slot = first_y * here.x + (1 - first_y) * here.y


    def to_sibling(u):
        return remote(
            stage.at[u % RING, :, their_rows, :], sib.at[u % UNITS], sib_send.at[u], sib_recv.at[u], here.sibling
        )

    def to_near(u, i):
        way = Way(u)
        return remote(
            stage.at[u % RING, way.sent[i], my_rows, :], near_in.at[u % UNITS, i],
            near_send.at[u, i], near_recv.at[u, i], here.at(way.near),
        )

    def to_far(u):
        way = Way(u)
        return remote(
            stage.at[u % RING, way.far, my_rows, :], far_in.at[u % UNITS],
            far_send.at[u], far_recv.at[u], here.at(way.far),
        )

    def give(u):
        to_sibling(u).start()

    def first(u):
        to_sibling(u).wait_recv()

        def add(q, carry):
            stage[u % RING, q, my_rows, :] += sib[u % UNITS, q]
            return carry

        lax.fori_loop(0, 4, add, 0)
        for i in range(2):
            to_near(u, i).start()

    def second_step(u):
        for i in range(2):
            to_near(u, i).wait_recv()
        way = Way(u)
        stage[u % RING, way.far, my_rows, :] += near_in[u % UNITS, 1 - way.own_slot]
        to_far(u).start()

    def z_moves(u):
        layer, v = 1 - u // UNITS, u % UNITS
        moves = []
        if not in_kernel_z:
            target = mlp_out.at[v, my_rows, :]
            mine = s == layer
            moves.append((mine, pltpu.make_async_copy(plane.at[v], target, local_sem.at[u, 0]), remote(
                plane.at[v], target, mlp_send.at[u], mlp_recv.at[v, 0, s], (layer, d, t))))
        elif v < 8:
            target = mlp_out.at[v // 4, d, my_rows, :]
            mine = (s == layer) & (d == v % 4)
            moves.append((mine, pltpu.make_async_copy(plane.at[v], target, local_sem.at[u, 0]), remote(
                plane.at[v], target, mlp_send.at[u], mlp_recv.at[v // 4, d, s], (layer, v % 4, t))))
        else:
            for other in range(4):
                lanes = plane.shape[2] // 4 * other // LANES * LANES
                piece = plane.at[v, :, pl.ds(lanes, 2 * LANES)]
                target = att_out.at[v - 8, d, my_rows, :]
                mine = (s == layer) & (d == other)
                moves.append((mine, pltpu.make_async_copy(piece, target, local_sem.at[u, other]), remote(
                    piece, target, att_send.at[layer, v - 8, other], att_recv.at[v - 8, d, s], (layer, other, t))))
        return moves

    def moved_out(u):
        for mine, local, away in z_moves(u):
            pl.when(mine)(local.wait)
            pl.when(jnp.logical_not(mine))(away.wait_send)

    def third(u):
        to_far(u).wait_recv()
        if u >= UNITS:
            moved_out(u - UNITS)
        plane[u % UNITS] = (
            stage[u % RING, t, my_rows, :].astype(F32)
            + near_in[u % UNITS, Way(u).own_slot].astype(F32) + far_in[u % UNITS].astype(F32)
        ).astype(BF16)
        for mine, local, away in z_moves(u):
            pl.when(mine)(local.start)
            pl.when(jnp.logical_not(mine))(away.start)
        to_sibling(u).wait_send()
        for i in range(2):
            to_near(u, i).wait_send()
        to_far(u).wait_send()

    done = [0, 0, 0]
    given = [0]

    steps = (first, second_step, third)

    def reach(*targets):
        while any(now < target for now, target in zip(done, targets)):
            for which in (1, 0, 2):
                if done[which] < targets[which] and (which == 0 or done[which] < done[which - 1]):
                    steps[which](done[which])
                    done[which] += 1

    points = iter(SCHEDULE)

    def point():
        reach(*next(points))

    def room():
        need = given[0] + 1 - RING
        reach(*[max(need, now) for now in done])

    def slot():
        give(given[0])
        given[0] += 1
        point()

    def rows_unit(k, left, right):
        room()
        place = given[0] % RING
        rows = pl.ds(k * quarter_rows, quarter_rows)

        def step(g, carry):
            stage[place, g] = dot(left[rows, :], right[g]).astype(BF16)
            return carry

        lax.fori_loop(0, 4, step, 0)

    def square_unit(left, right):
        room()
        place = given[0] % RING
        width = left.shape[1] // 2

        def step(c, carry):
            cols = pl.ds(pl.multiple_of(c * width, width), width)
            product = dot(left[:, cols], right[...], TN).astype(BF16)
            stage[place, pl.ds(2 * c, 2)] = product.reshape(2, quarter_rows, product.shape[1])
            return carry

        lax.fori_loop(0, 2, step, 0)

    masks = half_masks()

    def run_layer(layer):
        source = grad_ref if layer == 1 else dx_low.at[1]

        def prepare(rows):
            row = lax.broadcasted_iota(jnp.int32, (TILE, 1), 0) + rows.start
            grad = only(valid_rows(here.x, tok_rows, row), source[rows, :]).astype(F32)
            if layer == 0:
                value = x_ref[rows, :].astype(F32)
                logit = jnp.sum(value * router_ref[...], axis=-1, keepdims=True)
                sigma = 1.0 / (1.0 + jnp.exp(-logit))
                keep = keep_ref[rows, :]
                dlogit = jnp.sum(grad * branch[rows, :], axis=-1, keepdims=True) * keep * sigma * (1.0 - sigma)
                small_ref[2] += fold_rows(value * dlogit)
                dx_ref[rows, :] = grad + dlogit * router_ref[...]
                grad = grad * (sigma * keep)
            else:
                dx_ref[rows, :] = grad
            dbranch[rows, :] = grad
            dfed[rows, :] = grad.astype(BF16)

        small_ref[...] = jnp.zeros_like(small_ref)
        if layer == 1:
            load_grad.wait()
        else:
            load("branch", 0).wait()
            load("x", 0).wait()
        tiles(prepare)
        point()
        transpose_into(dfed, dfed_t)
        point()
        load("active", layer).wait()
        for k in range(4):
            g = k
            rows_unit(k, dfed_t, active)
            slot()
            if k == 3:
                prefetch("active", layer)
            for stream in streams:
                quarter_load(stream, layer, g).wait()
            work[...] = dot(dfed[...], wd[g % 2], NT)

            def bend(rows):
                dup[g, rows, :] = (work[rows, :] * slope[g % 2, rows, :].astype(F32)).astype(BF16)

            tiles(bend)
            point()
            part = dot(dup[g], wu[g % 2], NT)
            if g == 0:
                dsecond[...] = part
            else:
                dsecond[...] += part
            for stream in streams:
                if g < 2:
                    quarter_load(stream, layer, g + 2).start()
                elif layer == 1:
                    quarter_load(stream, 0, g - 2).start()
            point()

        load("second", layer).wait()
        transpose_into(second, dfed_t)
        point()
        prefetch("second", layer)
        for k in range(4):
            rows_unit(k, dfed_t, dup)
            slot()

        load("hidden", layer).wait()

        def second_pull(rows):
            xhat, rstd = standardize(hidden[rows, :])
            grad = dsecond[rows, :]
            small_ref[1] += fold_rows(grad * xhat)
            dhidden = norm_pull(xhat, rstd, gain_ref[layer, 1:2, :], grad)
            dx_ref[rows, :] += dhidden
            datt[rows, :] = (dbranch[rows, :] + dhidden).astype(BF16)

        tiles(second_pull)
        point()
        prefetch("hidden", layer)
        load("mixed", layer).wait()
        square_unit(mixed, datt)
        prefetch("mixed", layer)
        slot()
        load("wo", layer).wait()
        dmixed[...] = dot(datt[...], wo[...], NT).astype(BF16)
        prefetch("wo", layer)
        point()
        load("qkv", layer).wait()
        if layer == 1:
            load_bias.wait()

        def attend(pair, carry):
            cols = pl.ds(pl.multiple_of(pair * LANES, LANES), LANES)
            key, value = qkv[1, :, cols], qkv[2, :, cols]
            scaled = key * BF16(0.125)
            query = qkv[0, :, cols] * BF16(0.125)
            grad = dmixed[:, cols]
            sums = None
            for mask in masks:
                query_head, grad_head = only(mask, query), only(mask, grad)
                expo, inverse = softmax_parts(dot(query_head, key, NT) + bias_ref[layer])
                probs = expo * inverse
                dprobs = dot(grad_head, value, NT)
                dscores = probs * (dprobs - jnp.sum(probs * dprobs, axis=-1, keepdims=True))
                dscores = dscores.astype(BF16)
                parts = [
                    dot(dscores, only(mask, scaled)),
                    dot(dscores, query_head, TN),
                    dot(probs.astype(BF16), grad_head, TN),
                ]
                sums = parts if sums is None else [left + right for left, right in zip(sums, parts)]
            for j in range(3):
                dqkv[j, :, cols] = sums[j].astype(BF16)
            return carry

        pairs = dmixed.shape[1] // LANES
        for part_of in range(3):
            lax.fori_loop(pairs * part_of // 3, pairs * (part_of + 1) // 3, attend, 0)
            point()
        prefetch("qkv", layer)

        load("normed", layer).wait()
        for j in range(3):
            square_unit(dqkv.at[j], normed)
            slot()
        prefetch("normed", layer)
        load("wq", layer).wait()
        work[...] = dot(dqkv[0], wq[0])
        work[...] += dot(dqkv[1], wq[1])
        point()
        work[...] += dot(dqkv[2], wq[2])
        point()
        prefetch("wq", layer)
        if layer == 1:
            load("x", 1).wait()

        def first_pull(rows):
            xhat, rstd = standardize(x_ref[rows, :].astype(F32))
            grad = work[rows, :]
            small_ref[0] += fold_rows(grad * xhat)
            total = dx_ref[rows, :] + norm_pull(xhat, rstd, gain_ref[layer, 0:1, :], grad)
            dx_low[layer, rows, :] = total.astype(BF16)

        tiles(first_pull)
        point()
        prefetch("x", layer)
        hand_back(layer, dx_low.at[layer], main_out, back_out)
        sums = jnp.sum(small_ref[...], axis=1)
        if layer == 1:
            tot[0] = jnp.zeros(tot.shape[1:], F32)
            tot[0, 3:5, :] = sums[0:2]
        else:
            tot[0, 0:3, :] = sums
            total_move(0).start()

    run_layer(1)
    run_layer(0)
    added = 0
    for index, targets in enumerate(points):
        reach(*targets)
        if index in TOTALS:
            add_total(added)
            added += 1
    reach(2 * UNITS, 2 * UNITS, 2 * UNITS)
    for step in range(added, len(doubled)):
        add_total(step)
    moves = [total_move(step) for step in range(len(doubled) + len(along_z))]
    for move in moves[len(doubled) :]:
        move.wait_recv()
    total = jnp.zeros_like(small_out)
    for z in range(n_dp):
        shift = (z - d + n_dp) % n_dp
        total += jnp.where(shift == 0, tot[len(doubled)], got[len(doubled) - 1 + jnp.maximum(shift, 1)])
    small_out[...] = total
    for move in moves:
        move.wait_send()
    for back in backs:
        back.wait()
    for u in range(UNITS, 2 * UNITS):
        moved_out(u)

    if not in_kernel_z:
        for v in range(UNITS):
            remote(
                plane.at[v], mlp_out.at[v, their_rows, :], mlp_send.at[v], mlp_recv.at[v, 0, 1 - s], here.sibling
            ).wait_recv()
        return
    for source in range(4):
        for half in range(2):
            rows = pl.ds(half * half_rows, half_rows)

            def arrive():
                for kind in range(2):
                    target = mlp_out.at[kind, source, rows, :]
                    remote(target, target, mlp_send.at[0], mlp_recv.at[kind, source, half], here.sibling).wait_recv()
                for b in range(4):
                    target = att_out.at[b, source, rows, :]
                    remote(
                        target, target, att_send.at[0, 0, 0], att_recv.at[b, source, half], here.sibling
                    ).wait_recv()

            pl.when(jnp.logical_not((d == source) & (s == half)))(arrive)


def backward(n_dp, tok_rows, keep, gains, router, bias, grad, x, saved):
    width = x.shape[2]
    held, _, spare = token_layout(tok_rows)
    quarter_rows = width // 4
    half_rows = quarter_rows // 2
    in_kernel_z = n_dp == 4
    steps = 3 + n_dp - 1
    any_spec = pl.BlockSpec(memory_space=pl.ANY)
    vmem = pl.BlockSpec(memory_space=pltpu.VMEM)
    dma = pltpu.SemaphoreType.DMA

    def low(*shape):
        return pltpu.VMEM(shape, BF16)

    def wide(*shape):
        return pltpu.VMEM(shape, F32)

    mlp_shape = (2, 4, quarter_rows, width) if in_kernel_z else (UNITS, quarter_rows, width)
    units = 2 * UNITS
    scratch = [
        low(ROWS, width), low(ROWS, width), wide(ROWS, width), low(2, ROWS, width), wide(3, 8, width),
        wide(4, 8, width), wide(steps, 8, width), wide(2, ROWS, ROWS),
        low(3, width, width), low(width, width), low(2, width, width), low(2, width, width),
        low(ROWS, width), low(3, ROWS, width), low(ROWS, width), wide(ROWS, width), low(ROWS, width),
        low(4, ROWS, width), low(2, ROWS, width), wide(ROWS, width),
        wide(ROWS, width), low(ROWS, width), low(width, ROWS), wide(ROWS, width), low(4, ROWS, width),
        wide(ROWS, width), low(ROWS, width), low(ROWS, width), low(3, ROWS, width),
        low(RING, 4, quarter_rows, width), low(UNITS, 4, half_rows, width), low(UNITS, 2, half_rows, width),
        low(UNITS, half_rows, width), low(UNITS, half_rows, width),
        dma((2, 11)), dma((2, 2)), dma((2, 2)), dma((2, 2)),
        dma((units,)), dma((units,)), dma((units, 2)), dma((units, 2)), dma((units,)), dma((units,)),
        dma((units,)), dma((UNITS, 4, 2)), dma((2, 4, 4)), dma((4, 4, 2)), dma((units, 4)),
        dma((steps,)), dma((steps,)), *[sem for _ in range(4) for sem in hand_back_sems()],
    ]
    return pl.pallas_call(
        functools.partial(backward_kernel, in_kernel_z, tok_rows),
        out_shape=[
            jax.ShapeDtypeStruct((8, width), F32),
            jax.ShapeDtypeStruct((2, held, width), BF16),
            jax.ShapeDtypeStruct((2, spare, width), BF16),
            jax.ShapeDtypeStruct((2, held, width), BF16),
            jax.ShapeDtypeStruct((2, spare, width), BF16),
            jax.ShapeDtypeStruct(mlp_shape, BF16),
            jax.ShapeDtypeStruct((4, 4, quarter_rows, 2 * LANES), BF16),
        ],
        in_specs=[vmem] * 3 + [any_spec] * 15,
        out_specs=[vmem] + [any_spec] * 6,
        scratch_shapes=scratch,
        compiler_params=pltpu.CompilerParams(
            collective_id=1, has_side_effects=True, vmem_limit_bytes=VMEM_BYTES
        ),
        cost_estimate=pl.CostEstimate(flops=96 * ROWS * width * width, bytes_accessed=120_000_000, transcendentals=0),
        name="backward_layers",
    )(keep, gains, router, bias, grad, x, *saved)


def finish_kernel(
    tok_rows, sums,
    small_ref, y_main, y_back, dx_main, dx_back, mlp_in, att_in,
    y_out, dx_out, ones_out, twos_out, router_out, *rest,
):
    if sums:
        (down_out, up_out, out_out, qkv_out, *rest) = rest
    y_rows, y_tail, dx_rows, dx_tail, y_buf, dx_buf, mlp, att, mlp_sum, att_sum, in_sem, out_sem = rest
    held, low, spare = token_layout(tok_rows)
    section, d, t = lax.axis_index("section"), lax.axis_index("dp"), lax.axis_index("tensor")
    n_dp, quarters = lax.axis_size("dp"), lax.axis_size("tensor")
    x_half = t % 2
    moves = [(dx_main, dx_rows), (dx_back, dx_tail), (y_main, y_rows), (y_back, y_tail)]
    if sums:
        moves += [(mlp_in.at[0], mlp.at[0]), (mlp_in.at[1], mlp.at[1]), (att_in, att)]
    copies = [pltpu.make_async_copy(src, dst, in_sem.at[i]) for i, (src, dst) in enumerate(moves)]
    for copy in copies:
        copy.start()
    results = []

    def give(src, dst):
        copy = pltpu.make_async_copy(src, dst, out_sem.at[len(results)])
        copy.start()
        results.append(copy)

    def join(main, back, buffer, out):
        def plain(i, carry):
            rows = pl.ds(pl.multiple_of(i * 16, 16), 16)
            for m in range(2):
                buffer[rows, m, :] = main[m, rows, :].astype(buffer.dtype)
            return carry

        def mixed_rows(i, carry):
            rows = pl.ds(pl.multiple_of(i * 16, 16), 16)
            from_back = pl.ds(pl.multiple_of(i * 16 - low, 16), 16)
            row = lax.broadcasted_iota(jnp.int32, (16, 1), 0) + i * 16
            is_back = (x_half == 0) & (row >= CUT)
            for m in range(2):
                value = jnp.where(is_back, back[m, from_back, :], main[m, rows, :])
                buffer[rows, m, :] = value.astype(buffer.dtype)
            return carry

        lax.fori_loop(0, low // 16, plain, 0)
        lax.fori_loop(low // 16, held // 16, mixed_rows, 0)
        give(buffer.at[pl.ds(0, tok_rows)], out)

    for i, pieces in enumerate(((dx_rows, dx_tail, dx_buf, dx_out), (y_rows, y_tail, y_buf, y_out))):
        copies[2 * i].wait()
        copies[2 * i + 1].wait()
        join(*pieces)
    if sums:
        width = mlp_sum.shape[1]
        for kind in range(2):
            copies[4 + kind].wait()

            def add(rows):
                parts = [mlp[kind, source, rows, :].astype(F32) for source in range(4)]
                mlp_sum[kind, rows, :] = parts[0] + parts[1] + parts[2] + parts[3]

            tiles(add, rows=width, tile=32)
            give(mlp_sum.at[kind], (down_out, up_out)[kind])
        copies[6].wait()
        for b in range(4):
            total = att[b, 0].astype(F32) + att[b, 1].astype(F32) + att[b, 2].astype(F32) + att[b, 3].astype(F32)
            total = jnp.where(d % 2 == 0, total[:, :width], total[:, -width:])
            att_sum[b] = total if b == 0 else total.T
            give(att_sum.at[b], out_out if b == 0 else qkv_out.at[b - 1])

    columns = small_ref[...].T
    place = d * quarters + t

    def pick(values, start, count):
        row = lax.broadcasted_iota(jnp.int32, (columns.shape[0], count), 0)
        lane = lax.broadcasted_iota(jnp.int32, (columns.shape[0], count), 1)
        return jnp.sum(jnp.where(row == start + lane, values, 0.0), axis=0, keepdims=True)

    span = ones_out.shape[1]
    ones_out[...] = pick(jnp.where(section == 0, columns[:, 0:1], columns[:, 3:4]), place * span, span)
    twos_out[...] = pick(jnp.where(section == 0, columns[:, 1:2], columns[:, 4:5]), place * span, span)
    span = router_out.shape[1]
    router_out[...] = pick(columns[:, 2:3], (section * n_dp * quarters + place) * span, span)
    for copy in results:
        copy.wait()


def finish(tok_rows, n_dp, quarters, small, y_main, y_back, dx_main, dx_back, mlp, att):
    width = small.shape[1]
    held, _, spare = token_layout(tok_rows)
    part = width // 4
    span = width // (n_dp * quarters)
    sums = n_dp == 4
    any_spec = pl.BlockSpec(memory_space=pl.ANY)
    vmem = pl.BlockSpec(memory_space=pltpu.VMEM)
    shapes = [
        jax.ShapeDtypeStruct((tok_rows, 2, width), BF16), jax.ShapeDtypeStruct((tok_rows, 2, width), F32),
        jax.ShapeDtypeStruct((1, span), F32), jax.ShapeDtypeStruct((1, span), F32),
        jax.ShapeDtypeStruct((1, span // 2), F32),
    ]
    specs = [any_spec, any_spec, vmem, vmem, vmem]
    if sums:
        shapes += [jax.ShapeDtypeStruct(shape, F32) for shape in ((part, width), (part, width), (part, part), (3, part, part))]
        specs += [any_spec] * 4
    dma = pltpu.SemaphoreType.DMA
    return pl.pallas_call(
        functools.partial(finish_kernel, tok_rows, sums),
        out_shape=shapes,
        in_specs=[vmem] + [any_spec] * 6,
        out_specs=specs,
        scratch_shapes=[
            pltpu.VMEM((2, held, width), BF16), pltpu.VMEM((2, spare, width), BF16),
            pltpu.VMEM((2, held, width), BF16), pltpu.VMEM((2, spare, width), BF16),
            pltpu.VMEM((held, 2, width), BF16), pltpu.VMEM((held, 2, width), F32),
            pltpu.VMEM((2, 4, part, width), BF16), pltpu.VMEM((4, 4, part, 2 * LANES), BF16),
            pltpu.VMEM((2, part, width), F32), pltpu.VMEM((4, part, part), F32), dma((7,)), dma((8,)),
        ],
        compiler_params=pltpu.CompilerParams(vmem_limit_bytes=VMEM_BYTES),
        cost_estimate=pl.CostEstimate(flops=4_000_000, bytes_accessed=12_000_000, transcendentals=0),
        name="finish",
    )(small, y_main, y_back, dx_main, dx_back, mlp, att)


def on_device(
    patches, cotangent, crop_lengths, route_mask, w_qkv, w_out, w_up, w_down, ln1_gain, ln2_gain, router
):
    tok_rows, width = patches.shape[1:]
    n_dp, quarters = lax.axis_size("dp"), lax.axis_size("tensor")
    wq = jnp.transpose(w_qkv[0], (1, 2, 0))
    x, gains, keep_rows, router_row, bias, grad, *saved = forward(
        crop_lengths, route_mask, ln1_gain, ln2_gain, router, jnp.transpose(patches, (1, 0, 2)),
        jnp.transpose(cotangent, (1, 0, 2)), wq, w_out[0], w_up[0], w_down[0],
    )
    small, y_main, y_back, dx_main, dx_back, mlp, att = backward(
        n_dp, tok_rows, keep_rows, gains, router_row, bias, grad, x, saved
    )

    y_out, dx_out, ones, twos, routers, *grads = finish(
        tok_rows, n_dp, quarters, small, y_main, y_back, dx_main, dx_back, mlp, att
    )
    outputs = jnp.transpose(y_out, (1, 0, 2))
    input_grads = jnp.transpose(dx_out, (1, 0, 2))
    if n_dp == 4:
        down, up, out, qkv = grads
    else:

        def scatter(value, dim):
            return lax.psum_scatter(value, "dp", scatter_dimension=dim, tiled=True).astype(F32)

        down = scatter(mlp[:4].reshape(width, width), 0)
        up = scatter(mlp[4:8].reshape(width, width), 0)
        out = scatter(mlp[8], 1)
        qkv = jnp.transpose(scatter(mlp[9:], 2), (0, 2, 1))
    qkv = jnp.transpose(qkv, (1, 0, 2))
    return (
        outputs[None], input_grads[None], qkv[None], out[None], up[None], down.T[None], ones, twos, routers[0],
    )


def solution(mesh):
    return jax.shard_map(
        on_device,
        mesh=mesh,
        in_specs=(
            P(None, ("dp", "tensor"), None),
            P(None, ("dp", "tensor"), None),
            P(None, "dp", None),
            P(None, "dp"),
            P("section", None, None, "tensor"),
            P("section", "tensor", None),
            P("section", None, "tensor"),
            P("section", "tensor", None),
            P("section", None),
            P("section", None),
            P(),
        ),
        out_specs=(
            P("section", None, ("dp", "tensor"), None),
            P("section", None, ("dp", "tensor"), None),
            P("section", "dp", None, "tensor"),
            P("section", "tensor", "dp"),
            P("section", "dp", "tensor"),
            P("section", "tensor", "dp"),
            P("section", ("dp", "tensor")),
            P("section", ("dp", "tensor")),
            P(("section", "dp", "tensor")),
        ),
        check_vma=False,
    )
```

```python
import functools

import jax
import jax.numpy as jnp
from jax import lax
from jax.experimental import pallas as pl
from jax.experimental.pallas import tpu as pltpu
from jax.sharding import PartitionSpec as P

HEAD_DIM = 64
LANES = 128
CUT = 197
EPS = 1e-06
NEG = -1000000000.0
ROWS = 384
TILE = 64
MESH = pl.DeviceIdType.MESH
NT = (((1,), (1,)), ((), ()))
TN = (((0,), (0,)), ((), ()))
NN = (((1,), (0,)), ((), ()))
VMEM_BYTES = 62 * 1024 * 1024
F32, BF16 = jnp.float32, jnp.bfloat16


def dot(left, right, dims=NN):
    return lax.dot_general(left, right, dims, preferred_element_type=F32)


def tiles(body, rows=ROWS, tile=TILE):
    def step(index, carry):
        body(pl.ds(pl.multiple_of(index * tile, tile), tile))
        return carry

    lax.fori_loop(0, rows // tile, step, 0)


def standardize(values):
    centre = values - jnp.mean(values, axis=-1, keepdims=True)
    spread = jnp.mean(centre * centre, axis=-1, keepdims=True)
    rstd = lax.rsqrt(spread + EPS)
    return centre * rstd, rstd


def norm_pull(xhat, rstd, gain, grad):
    grad_hat = grad * gain
    mean_grad = jnp.mean(grad_hat, axis=-1, keepdims=True)
    mean_both = jnp.mean(grad_hat * xhat, axis=-1, keepdims=True)
    return rstd * (grad_hat - mean_grad - xhat * mean_both)


def fold_rows(values):
    return jnp.sum(values.reshape(values.shape[0] // 8, 8, values.shape[1]), axis=0)


def half_masks():
    lane = lax.broadcasted_iota(jnp.int32, (1, LANES), 1)
    return [lane < HEAD_DIM, lane >= HEAD_DIM]


def softmax_parts(scores):
    expo = jnp.exp(scores - jnp.max(scores, axis=-1, keepdims=True))
    return expo, 1.0 / jnp.sum(expo, axis=-1, keepdims=True)


def valid_rows(x_half, tok_rows, row):
    held, low, _ = token_layout(tok_rows)
    rest = (row < tok_rows) | ((row >= held + CUT - low) & (row < held + tok_rows - low))
    return ((x_half == 0) & (row < CUT)) | ((x_half == 1) & rest)


def only(mask, values):
    return jnp.where(mask, values, jnp.zeros_like(values))


def token_layout(tok_rows):
    held = -(-tok_rows // 16) * 16
    low = CUT // 16 * 16
    return held, low, held - low


def transpose_into(src, dst):
    def step(index, carry):
        cols = pl.ds(pl.multiple_of(index * LANES, LANES), LANES)
        dst[cols, :] = src[:, cols].astype(F32).T.astype(BF16)
        return carry

    lax.fori_loop(0, dst.shape[0] // LANES, step, 0)


class Place:
    def __init__(self):
        self.s = lax.axis_index("section")
        self.d = lax.axis_index("dp")
        self.t = lax.axis_index("tensor")
        self.x = self.t % 2
        self.y = self.t // 2
        self.near = self.t + (1 - self.s) * (1 - 2 * self.x) + self.s * (2 - 4 * self.y)
        self.far = self.t + self.s * (1 - 2 * self.x) + (1 - self.s) * (2 - 4 * self.y)
        self.cross = 3 - self.t
        self.beside = self.t + 1 - 2 * self.x
        self.above = self.t + 2 - 4 * self.y
        self.sibling = (1 - self.s, self.d, self.t)
        self.diagonal = (1 - self.s, self.d, self.beside)

    def at(self, tensor):
        return (self.s, self.d, tensor)


def remote(src, dst, send, recv, device):
    return pltpu.make_async_remote_copy(
        src_ref=src, dst_ref=dst, send_sem=send, recv_sem=recv, device_id=device, device_id_type=MESH
    )


def greet(peers):
    barrier = pltpu.get_barrier_semaphore()
    for peer in peers:
        pl.semaphore_signal(barrier, inc=1, device_id=peer, device_id_type=MESH)
    pl.semaphore_wait(barrier, len(peers))


class HandBack:
    def __init__(self, here, layer, tok_rows, rows_ref, main_out, back_out, sems):
        held, _, spare = token_layout(tok_rows)
        main_send, main_recv, back_send, back_recv, own = sems
        self.here, self.layer = here, layer
        main, back = rows_ref.at[pl.ds(0, held)], rows_ref.at[pl.ds(held, spare)]
        s = here.s
        self.local = pltpu.make_async_copy(main, main_out.at[s], own)
        self.away = remote(main, main_out.at[s], main_send, main_recv, here.sibling)
        self.backs = [
            remote(back, back_out.at[s], back_send, back_recv.at[s], (layer, here.d, here.beside)),
        ]
        self.landing = [
            remote(back, back_out.at[i], back_send, back_recv.at[i], here.sibling) for i in range(2)
        ]

    def start(self):
        mine = self.here.s == self.layer
        pl.when(mine)(self.local.start)
        pl.when(jnp.logical_not(mine))(self.away.start)
        pl.when(self.here.x == 1)(self.backs[0].start)

    def wait(self):
        mine = self.here.s == self.layer

        @pl.when(mine)
        def _():
            self.local.wait()
            self.away.wait_recv()

            @pl.when(self.here.x == 0)
            def _():
                for landing in self.landing:
                    landing.wait_recv()

        pl.when(jnp.logical_not(mine))(self.away.wait_send)
        pl.when(self.here.x == 1)(self.backs[0].wait_send)


def hand_back_sems():
    dma = pltpu.SemaphoreType.DMA
    return [dma, dma, dma, dma((2,)), dma]


KINDS = 4
FIRST_PLAN = [
    (0, 0, False), (0, 1, True), (1, 0, False), (2, 0, True), (2, 2, True), (3, 0, True), (3, 2, False), (3, 3, False)
]
SECOND_PLAN = [
    (0, 0, False), (0, 1, True), (1, 0, False), (2, 0, True), (2, 2, True),
    (3, 0, False), (3, 1, False), (3, 2, False), (3, 3, False),
]
PLAN = [(0, *step) for step in FIRST_PLAN] + [(1, *step) for step in SECOND_PLAN]
STARTS = (0, len(FIRST_PLAN))
WINDOW = 2


def forward_kernel(
    tok_rows,
    crop_ref, route_ref, one_ref, two_ref, router_in, patch_ref, cotangent_ref, wq_ref, wo_ref, wu_ref, wd_ref,
    x_out, gain_out, keep_out, router_out, bias_out, grad_out,
    gq_out, go_out, gu_out, gd_out, norm_out, qkv_out, mixed_out, hidden_out,
    second_out, active_out, slope_out, branch_out,
    x_own, gain_ref, my_gain, keep_ref, router_ref, bias_ref, tokens, spare_rows, grad_own,
    gq, go, gu, gd, normed, qkv, mixed, hidden, second, active, slope, branch, work,
    own_sem, lend_send, lend_recv, a_send, a_recv, b_send, b_recv, c_send, c_recv,
    e_send, e_recv, f_send, f_recv, out_sem, save_sem, tok_sem, tok_send, tok_recv, gain_sem, gain_send, gain_recv, x_sem, bias_sem,
):
    here = Place()
    held, low, spare = token_layout(tok_rows)
    part = wo_ref.shape[0]
    unit = part // 2
    shards = (wq_ref, wo_ref, wu_ref, wd_ref)

    def block(kind, layer, quarter):
        rows = pl.ds(pl.multiple_of(quarter * part, part), part)
        if kind == 0:
            return gq.at[layer, :, rows, :]
        if kind == 1:
            return go.at[layer, rows, :]
        return (gu if kind == 2 else gd).at[layer, quarter]

    parity = here.d % 2

    def chunk(step, quarter, half, other=0):
        layer, kind, piece, shared = PLAN[step]
        if shared:
            piece = piece + other + (1 - 2 * other) * parity
        if kind < 2:
            rows = pl.ds(pl.multiple_of(quarter * part + half * unit, unit), unit)
            return gq.at[layer, piece, rows, :] if kind == 0 else go.at[layer, rows, :]
        rows = pl.ds(pl.multiple_of((4 * half + piece) * unit, unit), unit)
        return (gu if kind == 2 else gd).at[layer, quarter, rows, :]

    def own_copy(kind):
        return pltpu.make_async_copy(shards[kind], block(kind, here.s, here.t), own_sem.at[kind])

    def lend(kind, layer):
        return remote(
            shards[kind], block(kind, layer, here.t), lend_send.at[kind], lend_recv.at[kind], here.sibling
        )

    def along(step, quarter, peer, send, recv):
        piece = chunk(step, quarter, here.s)
        return remote(piece, piece, send.at[step], recv.at[step], peer)

    def send_a(step):
        return along(step, here.t, here.at(here.near), a_send, a_recv)

    def send_b(step):
        return along(step, here.t, here.at(here.far), b_send, b_recv)

    def send_c(step):
        return along(step, here.near, here.at(here.far), c_send, c_recv)

    def send_e(step, which, half=None, other=0):
        piece = chunk(step, three[which], here.s if half is None else half, other)
        index = which + 3 * other
        return remote(piece, piece, e_send.at[step, index], e_recv.at[step, index], here.sibling)

    def send_f(step, which, other=0):
        piece = chunk(step, three[which], here.s, other)
        return remote(piece, piece, f_send.at[step, which], f_recv.at[step, which], z_beside)

    three = (here.near, here.far, here.cross)
    z_beside = (here.s, here.d + 1 - 2 * parity, here.t)
    total = len(PLAN)

    greet([here.sibling, here.at(here.near), here.at(here.far), z_beside])

    lend(0, here.s).start()
    own_copy(0).start()
    my_gain[...] = jnp.zeros_like(my_gain)
    my_gain[0:1, :] = one_ref[...]
    my_gain[1:2, :] = two_ref[...]
    gain_own = pltpu.make_async_copy(my_gain, gain_ref.at[here.s], gain_sem)
    gain_away = remote(my_gain, gain_ref.at[here.s], gain_send, gain_recv, here.sibling)
    token_loads = []
    for which, source in enumerate((patch_ref, cotangent_ref)):
        tokens[which, pl.ds(tok_rows, held - tok_rows)] = jnp.zeros((held - tok_rows, *tokens.shape[2:]), BF16)
        token_loads.append(
            pltpu.make_async_copy(source, tokens.at[which, pl.ds(0, tok_rows)], tok_sem.at[which])
        )
    tok_away = [
        remote(src, dst.at[pl.ds(held, spare)], tok_send.at[i], tok_recv.at[i], here.at(here.beside))
        for i, (src, dst) in enumerate(((spare_rows, x_own.at[0]), (grad_own.at[pl.ds(low, spare)], grad_out)))
    ]
    grad_save = pltpu.make_async_copy(grad_own, grad_out.at[pl.ds(0, held)], tok_sem.at[2])
    for copy in token_loads:
        copy.start()
    gain_own.start()
    gain_away.start()

    def issue(step):
        if step >= total:
            return
        layer, kind, piece, _ = PLAN[step]
        if piece == 0:
            pl.when(here.s == layer)(lambda: own_copy(kind).wait())
            pl.when(here.s != layer)(lambda: lend(kind, layer).wait_recv())
        send_a(step).start()
        send_b(step).start()

    def pass_on(step, which):
        send_e(step, which).start()
        if PLAN[step][3]:
            send_f(step, which).start()

    def relay(step):
        if step >= total:
            return
        send_a(step).wait_recv()
        send_c(step).start()
        pass_on(step, 0)
        issue(step + WINDOW)

    def fetch(step):
        if step >= total:
            return
        send_b(step).wait_recv()
        pass_on(step, 1)
        send_c(step).wait_recv()
        pass_on(step, 2)

    moved = [0]
    relayed = [0]

    def relays(upto):
        while relayed[0] < min(upto, total):
            relay(relayed[0])
            relayed[0] += 1

    def tick(upto):
        while moved[0] <= min(upto, total - 1):
            relays(moved[0] + 3)
            fetch(moved[0])
            moved[0] += 1

    def pump(step):
        tick(step + 2)
        shared = PLAN[step][3]
        if shared:
            for which in range(3):
                send_f(step, which, 1).wait_recv()
                send_e(step, which, None, 1).start()
        for other in range(1 + shared):
            for which in range(3):
                send_e(step, which, 1 - here.s, other).wait_recv()

    for step in range(WINDOW):
        issue(step)
    for kind in range(1, KINDS):
        lend(kind, here.s).start()
        own_copy(kind).start()
    def take(which, dst):
        def step(rows):
            dst[rows, :] = jnp.where(here.s == 0, tokens[which, rows, 0, :], tokens[which, rows, 1, :])

        tiles(step, rows=held, tile=16)

    for copy in token_loads:
        copy.wait()
    take(0, x_own.at[0])
    spare_rows[...] = x_own[0, pl.ds(low, spare), :]
    pl.when(here.x == 0)(tok_away[0].start)
    take(1, grad_own)
    pl.when(here.x == 0)(tok_away[1].start)
    grad_save.start()
    router_ref[...] = router_in[...].astype(F32).reshape(router_ref.shape)
    router_out[...] = router_ref[...]

    relays(1)

    image = here.t // 2
    slot_len = route_ref.shape[1] // crop_ref.shape[1]
    routes = jnp.where(here.s == 0, route_ref[0:1, :], route_ref[1:2, :]).astype(F32)
    lanes = -(-(routes.shape[1] + ROWS) // LANES) * LANES
    routes = jnp.concatenate([routes, jnp.zeros((1, lanes - routes.shape[1]), F32)], axis=1)
    routes = jnp.broadcast_to(routes, (8, lanes))

    def routed_from(start):
        return pltpu.roll(routes, (2 * lanes - start) % lanes, 1)[0:1, :ROWS]

    def rows_info(row):
        valid = valid_rows(here.x, tok_rows, row)
        position = jnp.where(row < held, here.x * tok_rows + row, low - held + row)
        position = jnp.where(here.x == 0, row, position)
        crop = jnp.zeros_like(row)
        end = 0
        for i in range(crop_ref.shape[2]):
            end = end + crop_ref[here.s, image, i]
            crop += (position >= end).astype(jnp.int32)
        return valid, jnp.where(valid, crop, -1)

    across = lax.broadcasted_iota(jnp.int32, (1, ROWS), 1)
    valid, crop_across = rows_info(across)
    routed = jnp.where(
        across < held,
        routed_from(image * slot_len + here.x * tok_rows),
        routed_from(image * slot_len + low - held),
    )
    routed = jnp.where(valid, routed, 0.0)
    keep_ref[...] = jnp.broadcast_to(routed, (LANES, ROWS)).T[:, 0:1]
    keep_out[...] = keep_ref[...]
    usable = jnp.where(valid, routed, 1.0) > 0.0

    def allow(rows):
        _, crop_down = rows_info(lax.broadcasted_iota(jnp.int32, (TILE, 1), 0) + rows.start)
        same = crop_down == crop_across
        bias_ref[0, rows, :] = jnp.where(same & usable, 0.0, NEG)
        bias_ref[1, rows, :] = jnp.where(same, 0.0, NEG)

    tiles(allow)
    bias_save = pltpu.make_async_copy(bias_ref, bias_out, bias_sem)
    bias_save.start()
    relays(2)

    pl.when(here.x == 1)(tok_away[0].wait_recv)

    def clear(block):
        def step(rows):
            row = lax.broadcasted_iota(jnp.int32, (TILE, 1), 0) + rows.start
            block[rows, :] = only(valid_rows(here.x, tok_rows, row), block[rows, :])

        tiles(step)

    clear(x_own.at[0])
    x_saves = [pltpu.make_async_copy(x_own.at[i], x_out.at[i], x_sem.at[i]) for i in range(3)]
    x_saves[0].start()
    gain_own.wait()
    gain_away.wait_recv()
    gain_out[...] = gain_ref[...]
    masks = half_masks()
    saves = []

    def weight_save(kind, layer):
        src, dst = ((gq, gq_out), (go, go_out), (gu, gu_out), (gd, gd_out))[kind]
        return pltpu.make_async_copy(src.at[layer], dst.at[layer], out_sem.at[layer, kind])

    def keep_weight(kind, layer):
        weight_save(kind, layer).start()

    def save(index, layer, src, dst):
        copy = pltpu.make_async_copy(src, dst.at[layer], save_sem.at[index])
        copy.start()
        return copy

    for layer in range(2):
        x_now = x_own.at[layer]

        def first_norm(rows):
            xhat, _ = standardize(x_now[rows, :].astype(F32))
            normed[rows, :] = (xhat * gain_ref[layer, 0:1, :]).astype(BF16)

        for copy in saves:
            copy.wait()
        saves = []
        tiles(first_norm)
        saves.append(save(0, layer, normed, norm_out))
        base = STARTS[layer]
        pump(base)
        qkv[0] = dot(normed[...], gq[layer, 0], NT).astype(BF16)
        pump(base + 1)
        keep_weight(0, layer)

        def project(j, carry):
            qkv[j] = dot(normed[...], gq[layer, j], NT).astype(BF16)
            return carry

        lax.fori_loop(1, 3, project, 0)
        saves.append(save(1, layer, qkv, qkv_out))

        def attend(pair, carry):
            cols = pl.ds(pl.multiple_of(pair * LANES, LANES), LANES)
            key, value = qkv[1, :, cols], qkv[2, :, cols]
            query = qkv[0, :, cols] * BF16(0.125)
            outs = []
            for mask in masks:
                expo, inverse = softmax_parts(dot(only(mask, query), key, NT) + bias_ref[layer])
                outs.append(dot(expo.astype(BF16), value) * inverse)
            mixed[:, cols] = jnp.where(masks[0], outs[0], outs[1]).astype(BF16)
            return carry

        pairs = mixed.shape[1] // LANES
        for part_of in range(3):
            lax.fori_loop(pairs * part_of // 3, pairs * (part_of + 1) // 3, attend, 0)
            tick(base + 3 + part_of)
        saves.append(save(2, layer, mixed, mixed_out))
        pump(base + 2)
        keep_weight(1, layer)
        branch[...] = dot(mixed[...], go[layer])

        def second_norm(rows):
            value = x_now[rows, :].astype(F32) + branch[rows, :]
            hidden[rows, :] = value
            xhat, _ = standardize(value)
            second[rows, :] = (xhat * gain_ref[layer, 1:2, :]).astype(BF16)

        tiles(second_norm)
        saves.append(save(3, layer, hidden, hidden_out))
        saves.append(save(4, layer, second, second_out))
        pump(base + 3)
        pump(base + 4)
        keep_weight(2, layer)

        def widen(g, carry):
            work[...] = dot(second[...], gu[layer, g])

            def bend(rows):
                upper = work[rows, :]
                phi = 0.5 * (1.0 + lax.erf(upper * 0.7071067811865476))
                bell = jnp.exp(-0.5 * upper * upper) * 0.3989422804014327
                active[g, rows, :] = (upper * phi).astype(BF16)
                slope[g, rows, :] = (phi + upper * bell).astype(BF16)

            tiles(bend, tile=32)
            return carry

        for g in range(4):
            widen(g, 0)
            tick(base + 6 + g)
        saves.append(save(5, layer, active, active_out))
        saves.append(save(6, layer, slope, slope_out))
        for step in range(base + 5, (*STARTS, total)[layer + 1]):
            pump(step)
        keep_weight(3, layer)

        def narrow(g, carry):
            branch[...] += dot(active[g], gd[layer, g])
            return carry

        for g in range(4):
            narrow(g, 0)
            tick((*STARTS, total)[layer + 1] + g // 2)
        if layer == 0:
            saves.append(save(7, layer, branch, branch_out))

        def finish(rows):
            value = x_now[rows, :].astype(F32)
            change = branch[rows, :]
            if layer == 0:
                logit = jnp.sum(value * router_ref[...], axis=-1, keepdims=True)
                change = change * (keep_ref[rows, :] / (1.0 + jnp.exp(-logit)))
            x_own[layer + 1, rows, :] = (value + change).astype(BF16)

        tiles(finish)
        x_saves[layer + 1].start()

    for copy in [*saves, *x_saves, grad_save, bias_save]:
        copy.wait()
    gain_away.wait_send()

    @pl.when(here.x == 0)
    def _():
        for away in tok_away:
            away.wait_send()

    pl.when(here.x == 1)(tok_away[1].wait_recv)
    for layer in range(2):
        for kind in range(KINDS):
            weight_save(kind, layer).wait()
    for kind in range(KINDS):
        lend(kind, here.s).wait_send()
    for step in range(total):
        send_a(step).wait_send()
        send_b(step).wait_send()
        send_c(step).wait_send()
        shared = PLAN[step][3]
        for which in range(3):
            send_e(step, which).wait_send()
            if shared:
                send_f(step, which).wait_send()
                send_e(step, which, None, 1).wait_send()


def forward(crops, routes, one, two, router, patches, cotangent, wq, wo, wu, wd):
    tok_rows, _, width = patches.shape
    held, _, spare = token_layout(tok_rows)
    any_spec = pl.BlockSpec(memory_space=pl.ANY)
    vmem = pl.BlockSpec(memory_space=pltpu.VMEM)

    def pair(*shape, dtype=BF16):
        return jax.ShapeDtypeStruct((2, *shape), dtype)

    shapes = [
        jax.ShapeDtypeStruct((3, ROWS, width), BF16), pair(8, width, dtype=F32),
        jax.ShapeDtypeStruct((ROWS, 1), F32), jax.ShapeDtypeStruct((1, width), F32), pair(ROWS, ROWS, dtype=F32),
        jax.ShapeDtypeStruct((ROWS, width), BF16),
        pair(3, width, width), pair(width, width), pair(4, width, width), pair(4, width, width),
        pair(ROWS, width), pair(3, ROWS, width), pair(ROWS, width), pair(ROWS, width, dtype=F32),
        pair(ROWS, width), pair(4, ROWS, width), pair(4, ROWS, width), pair(ROWS, width, dtype=F32),
    ]
    dma = pltpu.SemaphoreType.DMA
    scratch = [
        pltpu.VMEM((3, ROWS, width), BF16), pltpu.VMEM((2, 8, width), F32), pltpu.VMEM((8, width), F32),
        pltpu.VMEM((ROWS, 1), F32), pltpu.VMEM((1, width), F32), pltpu.VMEM((2, ROWS, ROWS), F32),
        pltpu.VMEM((2, held, 2, width), BF16), pltpu.VMEM((spare, width), BF16), pltpu.VMEM((held, width), BF16),
        pltpu.VMEM((2, 3, width, width), BF16), pltpu.VMEM((2, width, width), BF16),
        pltpu.VMEM((2, 4, width, width), BF16), pltpu.VMEM((2, 4, width, width), BF16),
        pltpu.VMEM((ROWS, width), BF16), pltpu.VMEM((3, ROWS, width), BF16),
        pltpu.VMEM((ROWS, width), BF16), pltpu.VMEM((ROWS, width), F32),
        pltpu.VMEM((ROWS, width), BF16), pltpu.VMEM((4, ROWS, width), BF16),
        pltpu.VMEM((4, ROWS, width), BF16), pltpu.VMEM((ROWS, width), F32),
        pltpu.VMEM((ROWS, width), F32),
        dma((KINDS,)), dma((KINDS,)), dma((KINDS,)),
        *[dma((len(PLAN),))] * 6, *[dma((len(PLAN), 6))] * 2, *[dma((len(PLAN), 3))] * 2,
        dma((2, KINDS)), dma((8,)),
        dma((3,)), dma((2,)), dma((2,)), dma, dma, dma, dma((3,)), dma,
    ]
    return pl.pallas_call(
        functools.partial(forward_kernel, tok_rows),
        out_shape=shapes,
        in_specs=[pl.BlockSpec(memory_space=pltpu.SMEM)] + [vmem] * 4 + [any_spec] * 6,
        out_specs=[any_spec, vmem, vmem, vmem] + [any_spec] * 14,
        scratch_shapes=scratch,
        compiler_params=pltpu.CompilerParams(
            collective_id=0, has_side_effects=True, vmem_limit_bytes=VMEM_BYTES
        ),
        cost_estimate=pl.CostEstimate(flops=24 * ROWS * width * width * 2, bytes_accessed=60_000_000, transcendentals=0),
        name="forward_layers",
    )(crops, routes, one, two, router, patches, cotangent, wq, wo, wu, wd)


UNITS = 12
RING = 6
TOTALS = (3, 6, 9)
Y_FIRST = (20,)
SCHEDULE = [
    (0, 0, 0), (0, 0, 0), (0, 0, 0), (0, 0, 0), (0, 0, 0), (0, 0, 0), (1, 0, 0), (1, 0, 0), (2, 0, 0),
    (2, 0, 0), (2, 0, 0), (3, 1, 0), (3, 1, 0), (3, 1, 0), (4, 2, 0), (4, 2, 0), (4, 2, 0), (6, 3, 1),
    (7, 4, 2), (8, 4, 3), (8, 5, 3), (8, 5, 3), (9, 6, 3), (9, 6, 4), (9, 7, 4), (9, 8, 4), (9, 8, 5),
    (10, 8, 6), (11, 8, 6), (11, 9, 6), (12, 9, 8), (12, 9, 8), (12, 9, 8), (12, 9, 8),
    (12, 10, 8), (12, 10, 8), (12, 10, 8), (13, 11, 8), (13, 11, 9), (14, 11, 9), (14, 11, 9), (14, 12, 9),
    (15, 12, 10), (15, 12, 11), (15, 12, 11), (16, 12, 11), (16, 13, 11), (17, 14, 12), (18, 16, 14),
    (18, 16, 14), (19, 17, 14), (20, 17, 15), (20, 17, 16), (21, 18, 16), (21, 18, 17), (21, 19, 17),
    (21, 19, 17), (21, 20, 17), (23, 21, 19), (23, 21, 19), (24, 21, 20), (24, 21, 21), (24, 22, 21),
    (24, 23, 21), (24, 24, 21), (24, 24, 22), (24, 24, 23), (24, 24, 24),
]


def backward_kernel(
    in_kernel_z, tok_rows,
    keep_ref, gain_ref, router_ref, bias_in, grad_in, x_in,
    gq, go, gu, gd, norm_in, qkv_in, mixed_in, hidden_in, second_in, active_in, slope_in, branch_in,
    small_out, y_main, y_back, main_out, back_out, mlp_out, att_out,
    grad_ref, x_ref, dx_ref, dx_low, small_ref, tot, got, bias_ref,
    wq, wo, wu, wd, normed, qkv, mixed, hidden, second, active, slope, branch,
    dbranch, dfed, dfed_t, work, dup, dsecond, datt, dmixed, dqkv, stage, sib, near_in, far_in, plane,
    load_sem, wu_sem, wd_sem, slope_sem,
    sib_send, sib_recv, near_send, near_recv, far_send, far_recv,
    mlp_send, mlp_recv, att_send, att_recv, local_sem, tot_send, tot_recv, *back_sems,
):
    here = Place()
    s, d, t = here.s, here.d, here.t
    quarter_rows = stage.shape[2]
    half_rows = quarter_rows // 2
    my_rows = pl.ds(pl.multiple_of(s * half_rows, half_rows), half_rows)
    their_rows = pl.ds(pl.multiple_of((1 - s) * half_rows, half_rows), half_rows)
    n_dp = lax.axis_size("dp")

    saved = {
        "active": (active_in, active), "x": (x_in, x_ref), "second": (second_in, second),
        "hidden": (hidden_in, hidden), "mixed": (mixed_in, mixed), "wo": (go, wo), "qkv": (qkv_in, qkv),
        "normed": (norm_in, normed), "wq": (gq, wq), "branch": (branch_in, branch),
    }

    def load(name, layer):
        src, dst = saved[name]
        return pltpu.make_async_copy(src.at[layer], dst, load_sem.at[layer, list(saved).index(name)])

    def prefetch(name, layer):
        if layer == 1:
            load(name, 0).start()

    streams = ((gd, wd, wd_sem), (slope_in, slope, slope_sem), (gu, wu, wu_sem))

    def quarter_load(stream, layer, g):
        src, dst, sems = stream
        return pltpu.make_async_copy(src.at[layer, g], dst.at[g % 2], sems.at[layer, g % 2])

    load_grad = pltpu.make_async_copy(grad_in, grad_ref, load_sem.at[0, len(saved)])
    load_bias = pltpu.make_async_copy(bias_in, bias_ref, load_sem.at[1, len(saved)])
    load_grad.start()

    load("active", 1).start()
    for g in range(2):
        for stream in streams:
            quarter_load(stream, 1, g).start()
    for name in saved:
        if name not in ("active", "branch"):
            load(name, 1).start()
    load("branch", 0).start()
    load_bias.start()

    peers = [here.sibling, here.at(here.near), here.at(here.far), here.diagonal]
    doubled = [here.sibling, here.at(here.near), here.at(here.far)]
    along_z = [(s, (d + shift) % n_dp, t) for shift in range(1, n_dp)]
    peers += along_z
    if in_kernel_z:
        peers += [(1 - s, z, t) for _, z, _ in along_z]
    greet(peers)

    backs = []

    def hand_back(layer, rows_ref, main, back):
        sems = back_sems[5 * len(backs) : 5 * len(backs) + 5]
        backs.append(HandBack(here, layer, tok_rows, rows_ref, main, back, sems))
        backs[-1].start()

    for layer in range(2):
        hand_back(layer, x_in.at[layer + 1], y_main, y_back)

    def total_move(step):
        last = len(doubled)
        return remote(
            tot.at[min(step, last)], got.at[step], tot_send.at[step], tot_recv.at[step], (doubled + along_z)[step]
        )

    def add_total(step):
        total_move(step).wait_recv()
        tot[step + 1] = tot[step] + got[step]
        if step + 1 < len(doubled):
            total_move(step + 1).start()
        else:
            for shift in range(len(along_z)):
                total_move(step + 1 + shift).start()

    class Way:
        def __init__(self, u):
            first_y = 1 if u in Y_FIRST else s
            self.near = here.near if u not in Y_FIRST else here.above
            self.far = here.far if u not in Y_FIRST else here.beside
            self.sent = [first_y * (2 * (1 - here.y) + i) + (1 - first_y) * (2 * i + 1 - here.x) for i in range(2)]
            self.own_slot = first_y * here.x + (1 - first_y) * here.y


    def to_sibling(u):
        return remote(
            stage.at[u % RING, :, their_rows, :], sib.at[u % UNITS], sib_send.at[u], sib_recv.at[u], here.sibling
        )

    def to_near(u, i):
        way = Way(u)
        return remote(
            stage.at[u % RING, way.sent[i], my_rows, :], near_in.at[u % UNITS, i],
            near_send.at[u, i], near_recv.at[u, i], here.at(way.near),
        )

    def to_far(u):
        way = Way(u)
        return remote(
            stage.at[u % RING, way.far, my_rows, :], far_in.at[u % UNITS],
            far_send.at[u], far_recv.at[u], here.at(way.far),
        )

    def give(u):
        to_sibling(u).start()

    def first(u):
        to_sibling(u).wait_recv()

        def add(q, carry):
            stage[u % RING, q, my_rows, :] += sib[u % UNITS, q]
            return carry

        lax.fori_loop(0, 4, add, 0)
        for i in range(2):
            to_near(u, i).start()

    def second_step(u):
        for i in range(2):
            to_near(u, i).wait_recv()
        way = Way(u)
        stage[u % RING, way.far, my_rows, :] += near_in[u % UNITS, 1 - way.own_slot]
        to_far(u).start()

    def z_moves(u):
        layer, v = 1 - u // UNITS, u % UNITS
        moves = []
        if not in_kernel_z:
            target = mlp_out.at[v, my_rows, :]
            mine = s == layer
            moves.append((mine, pltpu.make_async_copy(plane.at[v], target, local_sem.at[u, 0]), remote(
                plane.at[v], target, mlp_send.at[u], mlp_recv.at[v, 0, s], (layer, d, t))))
        elif v < 8:
            target = mlp_out.at[v // 4, d, my_rows, :]
            mine = (s == layer) & (d == v % 4)
            moves.append((mine, pltpu.make_async_copy(plane.at[v], target, local_sem.at[u, 0]), remote(
                plane.at[v], target, mlp_send.at[u], mlp_recv.at[v // 4, d, s], (layer, v % 4, t))))
        else:
            for other in range(4):
                lanes = plane.shape[2] // 4 * other // LANES * LANES
                piece = plane.at[v, :, pl.ds(lanes, 2 * LANES)]
                target = att_out.at[v - 8, d, my_rows, :]
                mine = (s == layer) & (d == other)
                moves.append((mine, pltpu.make_async_copy(piece, target, local_sem.at[u, other]), remote(
                    piece, target, att_send.at[layer, v - 8, other], att_recv.at[v - 8, d, s], (layer, other, t))))
        return moves

    def moved_out(u):
        for mine, local, away in z_moves(u):
            pl.when(mine)(local.wait)
            pl.when(jnp.logical_not(mine))(away.wait_send)

    def third(u):
        to_far(u).wait_recv()
        if u >= UNITS:
            moved_out(u - UNITS)
        plane[u % UNITS] = (
            stage[u % RING, t, my_rows, :].astype(F32)
            + near_in[u % UNITS, Way(u).own_slot].astype(F32) + far_in[u % UNITS].astype(F32)
        ).astype(BF16)
        for mine, local, away in z_moves(u):
            pl.when(mine)(local.start)
            pl.when(jnp.logical_not(mine))(away.start)
        to_sibling(u).wait_send()
        for i in range(2):
            to_near(u, i).wait_send()
        to_far(u).wait_send()

    done = [0, 0, 0]
    given = [0]

    steps = (first, second_step, third)

    def reach(*targets):
        while any(now < target for now, target in zip(done, targets)):
            for which in (1, 0, 2):
                if done[which] < targets[which] and (which == 0 or done[which] < done[which - 1]):
                    steps[which](done[which])
                    done[which] += 1

    points = iter(SCHEDULE)

    def point():
        reach(*next(points))

    def room():
        need = given[0] + 1 - RING
        reach(*[max(need, now) for now in done])

    def slot():
        give(given[0])
        given[0] += 1
        point()

    def rows_unit(k, left, right):
        room()
        place = given[0] % RING
        rows = pl.ds(k * quarter_rows, quarter_rows)

        def step(g, carry):
            stage[place, g] = dot(left[rows, :], right[g]).astype(BF16)
            return carry

        lax.fori_loop(0, 4, step, 0)

    def square_unit(left, right):
        room()
        place = given[0] % RING
        width = left.shape[1] // 2

        def step(c, carry):
            cols = pl.ds(pl.multiple_of(c * width, width), width)
            product = dot(left[:, cols], right[...], TN).astype(BF16)
            stage[place, pl.ds(2 * c, 2)] = product.reshape(2, quarter_rows, product.shape[1])
            return carry

        lax.fori_loop(0, 2, step, 0)

    masks = half_masks()

    def run_layer(layer):
        source = grad_ref if layer == 1 else dx_low.at[1]

        def prepare(rows):
            row = lax.broadcasted_iota(jnp.int32, (TILE, 1), 0) + rows.start
            grad = only(valid_rows(here.x, tok_rows, row), source[rows, :]).astype(F32)
            if layer == 0:
                value = x_ref[rows, :].astype(F32)
                logit = jnp.sum(value * router_ref[...], axis=-1, keepdims=True)
                sigma = 1.0 / (1.0 + jnp.exp(-logit))
                keep = keep_ref[rows, :]
                dlogit = jnp.sum(grad * branch[rows, :], axis=-1, keepdims=True) * keep * sigma * (1.0 - sigma)
                small_ref[2] += fold_rows(value * dlogit)
                dx_ref[rows, :] = grad + dlogit * router_ref[...]
                grad = grad * (sigma * keep)
            else:
                dx_ref[rows, :] = grad
            dbranch[rows, :] = grad
            dfed[rows, :] = grad.astype(BF16)

        small_ref[...] = jnp.zeros_like(small_ref)
        if layer == 1:
            load_grad.wait()
        else:
            load("branch", 0).wait()
            load("x", 0).wait()
        tiles(prepare)
        point()
        transpose_into(dfed, dfed_t)
        point()
        load("active", layer).wait()
        for k in range(4):
            g = k
            rows_unit(k, dfed_t, active)
            slot()
            if k == 3:
                prefetch("active", layer)
            for stream in streams:
                quarter_load(stream, layer, g).wait()
            work[...] = dot(dfed[...], wd[g % 2], NT)

            def bend(rows):
                dup[g, rows, :] = (work[rows, :] * slope[g % 2, rows, :].astype(F32)).astype(BF16)

            tiles(bend)
            point()
            part = dot(dup[g], wu[g % 2], NT)
            if g == 0:
                dsecond[...] = part
            else:
                dsecond[...] += part
            for stream in streams:
                if g < 2:
                    quarter_load(stream, layer, g + 2).start()
                elif layer == 1:
                    quarter_load(stream, 0, g - 2).start()
            point()

        load("second", layer).wait()
        transpose_into(second, dfed_t)
        point()
        prefetch("second", layer)
        for k in range(4):
            rows_unit(k, dfed_t, dup)
            slot()

        load("hidden", layer).wait()

        def second_pull(rows):
            xhat, rstd = standardize(hidden[rows, :])
            grad = dsecond[rows, :]
            small_ref[1] += fold_rows(grad * xhat)
            dhidden = norm_pull(xhat, rstd, gain_ref[layer, 1:2, :], grad)
            dx_ref[rows, :] += dhidden
            datt[rows, :] = (dbranch[rows, :] + dhidden).astype(BF16)

        tiles(second_pull)
        point()
        prefetch("hidden", layer)
        load("mixed", layer).wait()
        square_unit(mixed, datt)
        prefetch("mixed", layer)
        slot()
        load("wo", layer).wait()
        dmixed[...] = dot(datt[...], wo[...], NT).astype(BF16)
        prefetch("wo", layer)
        point()
        load("qkv", layer).wait()
        if layer == 1:
            load_bias.wait()

        def attend(pair, carry):
            cols = pl.ds(pl.multiple_of(pair * LANES, LANES), LANES)
            key, value = qkv[1, :, cols], qkv[2, :, cols]
            scaled = key * BF16(0.125)
            query = qkv[0, :, cols] * BF16(0.125)
            grad = dmixed[:, cols]
            sums = None
            for mask in masks:
                query_head, grad_head = only(mask, query), only(mask, grad)
                expo, inverse = softmax_parts(dot(query_head, key, NT) + bias_ref[layer])
                probs = expo * inverse
                dprobs = dot(grad_head, value, NT)
                dscores = probs * (dprobs - jnp.sum(probs * dprobs, axis=-1, keepdims=True))
                dscores = dscores.astype(BF16)
                parts = [
                    dot(dscores, only(mask, scaled)),
                    dot(dscores, query_head, TN),
                    dot(probs.astype(BF16), grad_head, TN),
                ]
                sums = parts if sums is None else [left + right for left, right in zip(sums, parts)]
            for j in range(3):
                dqkv[j, :, cols] = sums[j].astype(BF16)
            return carry

        pairs = dmixed.shape[1] // LANES
        for part_of in range(3):
            lax.fori_loop(pairs * part_of // 3, pairs * (part_of + 1) // 3, attend, 0)
            point()
        prefetch("qkv", layer)

        load("normed", layer).wait()
        for j in range(3):
            square_unit(dqkv.at[j], normed)
            slot()
        prefetch("normed", layer)
        load("wq", layer).wait()
        work[...] = dot(dqkv[0], wq[0])
        work[...] += dot(dqkv[1], wq[1])
        point()
        work[...] += dot(dqkv[2], wq[2])
        point()
        prefetch("wq", layer)
        if layer == 1:
            load("x", 1).wait()

        def first_pull(rows):
            xhat, rstd = standardize(x_ref[rows, :].astype(F32))
            grad = work[rows, :]
            small_ref[0] += fold_rows(grad * xhat)
            total = dx_ref[rows, :] + norm_pull(xhat, rstd, gain_ref[layer, 0:1, :], grad)
            dx_low[layer, rows, :] = total.astype(BF16)

        tiles(first_pull)
        point()
        prefetch("x", layer)
        hand_back(layer, dx_low.at[layer], main_out, back_out)
        sums = jnp.sum(small_ref[...], axis=1)
        if layer == 1:
            tot[0] = jnp.zeros(tot.shape[1:], F32)
            tot[0, 3:5, :] = sums[0:2]
        else:
            tot[0, 0:3, :] = sums
            total_move(0).start()

    run_layer(1)
    run_layer(0)
    added = 0
    for index, targets in enumerate(points):
        reach(*targets)
        if index in TOTALS:
            add_total(added)
            added += 1
    reach(2 * UNITS, 2 * UNITS, 2 * UNITS)
    for step in range(added, len(doubled)):
        add_total(step)
    moves = [total_move(step) for step in range(len(doubled) + len(along_z))]
    for move in moves[len(doubled) :]:
        move.wait_recv()
    total = jnp.zeros_like(small_out)
    for z in range(n_dp):
        shift = (z - d + n_dp) % n_dp
        total += jnp.where(shift == 0, tot[len(doubled)], got[len(doubled) - 1 + jnp.maximum(shift, 1)])
    small_out[...] = total
    for move in moves:
        move.wait_send()
    for back in backs:
        back.wait()
    for u in range(UNITS, 2 * UNITS):
        moved_out(u)

    if not in_kernel_z:
        for v in range(UNITS):
            remote(
                plane.at[v], mlp_out.at[v, their_rows, :], mlp_send.at[v], mlp_recv.at[v, 0, 1 - s], here.sibling
            ).wait_recv()
        return
    for source in range(4):
        for half in range(2):
            rows = pl.ds(half * half_rows, half_rows)

            def arrive():
                for kind in range(2):
                    target = mlp_out.at[kind, source, rows, :]
                    remote(target, target, mlp_send.at[0], mlp_recv.at[kind, source, half], here.sibling).wait_recv()
                for b in range(4):
                    target = att_out.at[b, source, rows, :]
                    remote(
                        target, target, att_send.at[0, 0, 0], att_recv.at[b, source, half], here.sibling
                    ).wait_recv()

            pl.when(jnp.logical_not((d == source) & (s == half)))(arrive)


def backward(n_dp, tok_rows, keep, gains, router, bias, grad, x, saved):
    width = x.shape[2]
    held, _, spare = token_layout(tok_rows)
    quarter_rows = width // 4
    half_rows = quarter_rows // 2
    in_kernel_z = n_dp == 4
    steps = 3 + n_dp - 1
    any_spec = pl.BlockSpec(memory_space=pl.ANY)
    vmem = pl.BlockSpec(memory_space=pltpu.VMEM)
    dma = pltpu.SemaphoreType.DMA

    def low(*shape):
        return pltpu.VMEM(shape, BF16)

    def wide(*shape):
        return pltpu.VMEM(shape, F32)

    mlp_shape = (2, 4, quarter_rows, width) if in_kernel_z else (UNITS, quarter_rows, width)
    units = 2 * UNITS
    scratch = [
        low(ROWS, width), low(ROWS, width), wide(ROWS, width), low(2, ROWS, width), wide(3, 8, width),
        wide(4, 8, width), wide(steps, 8, width), wide(2, ROWS, ROWS),
        low(3, width, width), low(width, width), low(2, width, width), low(2, width, width),
        low(ROWS, width), low(3, ROWS, width), low(ROWS, width), wide(ROWS, width), low(ROWS, width),
        low(4, ROWS, width), low(2, ROWS, width), wide(ROWS, width),
        wide(ROWS, width), low(ROWS, width), low(width, ROWS), wide(ROWS, width), low(4, ROWS, width),
        wide(ROWS, width), low(ROWS, width), low(ROWS, width), low(3, ROWS, width),
        low(RING, 4, quarter_rows, width), low(UNITS, 4, half_rows, width), low(UNITS, 2, half_rows, width),
        low(UNITS, half_rows, width), low(UNITS, half_rows, width),
        dma((2, 11)), dma((2, 2)), dma((2, 2)), dma((2, 2)),
        dma((units,)), dma((units,)), dma((units, 2)), dma((units, 2)), dma((units,)), dma((units,)),
        dma((units,)), dma((UNITS, 4, 2)), dma((2, 4, 4)), dma((4, 4, 2)), dma((units, 4)),
        dma((steps,)), dma((steps,)), *[sem for _ in range(4) for sem in hand_back_sems()],
    ]
    return pl.pallas_call(
        functools.partial(backward_kernel, in_kernel_z, tok_rows),
        out_shape=[
            jax.ShapeDtypeStruct((8, width), F32),
            jax.ShapeDtypeStruct((2, held, width), BF16),
            jax.ShapeDtypeStruct((2, spare, width), BF16),
            jax.ShapeDtypeStruct((2, held, width), BF16),
            jax.ShapeDtypeStruct((2, spare, width), BF16),
            jax.ShapeDtypeStruct(mlp_shape, BF16),
            jax.ShapeDtypeStruct((4, 4, quarter_rows, 2 * LANES), BF16),
        ],
        in_specs=[vmem] * 3 + [any_spec] * 15,
        out_specs=[vmem] + [any_spec] * 6,
        scratch_shapes=scratch,
        compiler_params=pltpu.CompilerParams(
            collective_id=1, has_side_effects=True, vmem_limit_bytes=VMEM_BYTES
        ),
        cost_estimate=pl.CostEstimate(flops=96 * ROWS * width * width, bytes_accessed=120_000_000, transcendentals=0),
        name="backward_layers",
    )(keep, gains, router, bias, grad, x, *saved)


def finish_kernel(
    tok_rows, sums,
    small_ref, y_main, y_back, dx_main, dx_back, mlp_in, att_in,
    y_out, dx_out, ones_out, twos_out, router_out, *rest,
):
    if sums:
        (down_out, up_out, out_out, qkv_out, *rest) = rest
    y_rows, y_tail, dx_rows, dx_tail, y_buf, dx_buf, mlp, att, mlp_sum, att_sum, in_sem, out_sem = rest
    held, low, spare = token_layout(tok_rows)
    section, d, t = lax.axis_index("section"), lax.axis_index("dp"), lax.axis_index("tensor")
    n_dp, quarters = lax.axis_size("dp"), lax.axis_size("tensor")
    x_half = t % 2
    moves = [(dx_main, dx_rows), (dx_back, dx_tail), (y_main, y_rows), (y_back, y_tail)]
    if sums:
        moves += [(mlp_in.at[0], mlp.at[0]), (mlp_in.at[1], mlp.at[1]), (att_in, att)]
    copies = [pltpu.make_async_copy(src, dst, in_sem.at[i]) for i, (src, dst) in enumerate(moves)]
    for copy in copies:
        copy.start()
    results = []

    def give(src, dst):
        copy = pltpu.make_async_copy(src, dst, out_sem.at[len(results)])
        copy.start()
        results.append(copy)

    def join(main, back, buffer, out):
        def plain(i, carry):
            rows = pl.ds(pl.multiple_of(i * 16, 16), 16)
            for m in range(2):
                buffer[rows, m, :] = main[m, rows, :].astype(buffer.dtype)
            return carry

        def mixed_rows(i, carry):
            rows = pl.ds(pl.multiple_of(i * 16, 16), 16)
            from_back = pl.ds(pl.multiple_of(i * 16 - low, 16), 16)
            row = lax.broadcasted_iota(jnp.int32, (16, 1), 0) + i * 16
            is_back = (x_half == 0) & (row >= CUT)
            for m in range(2):
                value = jnp.where(is_back, back[m, from_back, :], main[m, rows, :])
                buffer[rows, m, :] = value.astype(buffer.dtype)
            return carry

        lax.fori_loop(0, low // 16, plain, 0)
        lax.fori_loop(low // 16, held // 16, mixed_rows, 0)
        give(buffer.at[pl.ds(0, tok_rows)], out)

    for i, pieces in enumerate(((dx_rows, dx_tail, dx_buf, dx_out), (y_rows, y_tail, y_buf, y_out))):
        copies[2 * i].wait()
        copies[2 * i + 1].wait()
        join(*pieces)
    if sums:
        width = mlp_sum.shape[1]
        for kind in range(2):
            copies[4 + kind].wait()

            def add(rows):
                parts = [mlp[kind, source, rows, :].astype(F32) for source in range(4)]
                mlp_sum[kind, rows, :] = parts[0] + parts[1] + parts[2] + parts[3]

            tiles(add, rows=width, tile=32)
            give(mlp_sum.at[kind], (down_out, up_out)[kind])
        copies[6].wait()
        for b in range(4):
            total = att[b, 0].astype(F32) + att[b, 1].astype(F32) + att[b, 2].astype(F32) + att[b, 3].astype(F32)
            total = jnp.where(d % 2 == 0, total[:, :width], total[:, -width:])
            att_sum[b] = total if b == 0 else total.T
            give(att_sum.at[b], out_out if b == 0 else qkv_out.at[b - 1])

    columns = small_ref[...].T
    place = d * quarters + t

    def pick(values, start, count):
        row = lax.broadcasted_iota(jnp.int32, (columns.shape[0], count), 0)
        lane = lax.broadcasted_iota(jnp.int32, (columns.shape[0], count), 1)
        return jnp.sum(jnp.where(row == start + lane, values, 0.0), axis=0, keepdims=True)

    span = ones_out.shape[1]
    ones_out[...] = pick(jnp.where(section == 0, columns[:, 0:1], columns[:, 3:4]), place * span, span)
    twos_out[...] = pick(jnp.where(section == 0, columns[:, 1:2], columns[:, 4:5]), place * span, span)
    span = router_out.shape[1]
    router_out[...] = pick(columns[:, 2:3], (section * n_dp * quarters + place) * span, span)
    for copy in results:
        copy.wait()


def finish(tok_rows, n_dp, quarters, small, y_main, y_back, dx_main, dx_back, mlp, att):
    width = small.shape[1]
    held, _, spare = token_layout(tok_rows)
    part = width // 4
    span = width // (n_dp * quarters)
    sums = n_dp == 4
    any_spec = pl.BlockSpec(memory_space=pl.ANY)
    vmem = pl.BlockSpec(memory_space=pltpu.VMEM)
    shapes = [
        jax.ShapeDtypeStruct((tok_rows, 2, width), BF16), jax.ShapeDtypeStruct((tok_rows, 2, width), F32),
        jax.ShapeDtypeStruct((1, span), F32), jax.ShapeDtypeStruct((1, span), F32),
        jax.ShapeDtypeStruct((1, span // 2), F32),
    ]
    specs = [any_spec, any_spec, vmem, vmem, vmem]
    if sums:
        shapes += [jax.ShapeDtypeStruct(shape, F32) for shape in ((part, width), (part, width), (part, part), (3, part, part))]
        specs += [any_spec] * 4
    dma = pltpu.SemaphoreType.DMA
    return pl.pallas_call(
        functools.partial(finish_kernel, tok_rows, sums),
        out_shape=shapes,
        in_specs=[vmem] + [any_spec] * 6,
        out_specs=specs,
        scratch_shapes=[
            pltpu.VMEM((2, held, width), BF16), pltpu.VMEM((2, spare, width), BF16),
            pltpu.VMEM((2, held, width), BF16), pltpu.VMEM((2, spare, width), BF16),
            pltpu.VMEM((held, 2, width), BF16), pltpu.VMEM((held, 2, width), F32),
            pltpu.VMEM((2, 4, part, width), BF16), pltpu.VMEM((4, 4, part, 2 * LANES), BF16),
            pltpu.VMEM((2, part, width), F32), pltpu.VMEM((4, part, part), F32), dma((7,)), dma((8,)),
        ],
        compiler_params=pltpu.CompilerParams(vmem_limit_bytes=VMEM_BYTES),
        cost_estimate=pl.CostEstimate(flops=4_000_000, bytes_accessed=12_000_000, transcendentals=0),
        name="finish",
    )(small, y_main, y_back, dx_main, dx_back, mlp, att)


def on_device(
    patches, cotangent, crop_lengths, route_mask, w_qkv, w_out, w_up, w_down, ln1_gain, ln2_gain, router
):
    tok_rows, width = patches.shape[1:]
    n_dp, quarters = lax.axis_size("dp"), lax.axis_size("tensor")
    wq = jnp.transpose(w_qkv[0], (1, 2, 0))
    x, gains, keep_rows, router_row, bias, grad, *saved = forward(
        crop_lengths, route_mask, ln1_gain, ln2_gain, router, jnp.transpose(patches, (1, 0, 2)),
        jnp.transpose(cotangent, (1, 0, 2)), wq, w_out[0], w_up[0], w_down[0],
    )
    small, y_main, y_back, dx_main, dx_back, mlp, att = backward(
        n_dp, tok_rows, keep_rows, gains, router_row, bias, grad, x, saved
    )

    y_out, dx_out, ones, twos, routers, *grads = finish(
        tok_rows, n_dp, quarters, small, y_main, y_back, dx_main, dx_back, mlp, att
    )
    outputs = jnp.transpose(y_out, (1, 0, 2))
    input_grads = jnp.transpose(dx_out, (1, 0, 2))
    if n_dp == 4:
        down, up, out, qkv = grads
    else:

        def scatter(value, dim):
            return lax.psum_scatter(value, "dp", scatter_dimension=dim, tiled=True).astype(F32)

        down = scatter(mlp[:4].reshape(width, width), 0)
        up = scatter(mlp[4:8].reshape(width, width), 0)
        out = scatter(mlp[8], 1)
        qkv = jnp.transpose(scatter(mlp[9:], 2), (0, 2, 1))
    qkv = jnp.transpose(qkv, (1, 0, 2))
    return (
        outputs[None], input_grads[None], qkv[None], out[None], up[None], down.T[None], ones, twos, routers[0],
    )


def solution(mesh):
    return jax.shard_map(
        on_device,
        mesh=mesh,
        in_specs=(
            P(None, ("dp", "tensor"), None),
            P(None, ("dp", "tensor"), None),
            P(None, "dp", None),
            P(None, "dp"),
            P("section", None, None, "tensor"),
            P("section", "tensor", None),
            P("section", None, "tensor"),
            P("section", "tensor", None),
            P("section", None),
            P("section", None),
            P(),
        ),
        out_specs=(
            P("section", None, ("dp", "tensor"), None),
            P("section", None, ("dp", "tensor"), None),
            P("section", "dp", None, "tensor"),
            P("section", "tensor", "dp"),
            P("section", "dp", "tensor"),
            P("section", "tensor", "dp"),
            P("section", ("dp", "tensor")),
            P("section", ("dp", "tensor")),
            P(("section", "dp", "tensor")),
        ),
        check_vma=False,
    )
```

```python
import functools

import jax
import jax.numpy as jnp
from jax import lax
from jax.experimental import pallas as pl
from jax.experimental.pallas import tpu as pltpu
from jax.sharding import PartitionSpec as P

HEAD_DIM = 64
LANES = 128
CUT = 197
EPS = 1e-06
NEG = -1000000000.0
ROWS = 384
TILE = 64
MESH = pl.DeviceIdType.MESH
NT = (((1,), (1,)), ((), ()))
TN = (((0,), (0,)), ((), ()))
NN = (((1,), (0,)), ((), ()))
VMEM_BYTES = 62 * 1024 * 1024
F32, BF16 = jnp.float32, jnp.bfloat16


def dot(left, right, dims=NN):
    return lax.dot_general(left, right, dims, preferred_element_type=F32)


def tiles(body, rows=ROWS, tile=TILE):
    def step(index, carry):
        body(pl.ds(pl.multiple_of(index * tile, tile), tile))
        return carry

    lax.fori_loop(0, rows // tile, step, 0)


def standardize(values):
    centre = values - jnp.mean(values, axis=-1, keepdims=True)
    spread = jnp.mean(centre * centre, axis=-1, keepdims=True)
    rstd = lax.rsqrt(spread + EPS)
    return centre * rstd, rstd


def norm_pull(xhat, rstd, gain, grad):
    grad_hat = grad * gain
    mean_grad = jnp.mean(grad_hat, axis=-1, keepdims=True)
    mean_both = jnp.mean(grad_hat * xhat, axis=-1, keepdims=True)
    return rstd * (grad_hat - mean_grad - xhat * mean_both)


def fold_rows(values):
    return jnp.sum(values.reshape(values.shape[0] // 8, 8, values.shape[1]), axis=0)


def half_masks():
    lane = lax.broadcasted_iota(jnp.int32, (1, LANES), 1)
    return [lane < HEAD_DIM, lane >= HEAD_DIM]


def softmax_parts(scores):
    expo = jnp.exp(scores - jnp.max(scores, axis=-1, keepdims=True))
    return expo, 1.0 / jnp.sum(expo, axis=-1, keepdims=True)


def valid_rows(x_half, tok_rows, row):
    held, low, _ = token_layout(tok_rows)
    rest = (row < tok_rows) | ((row >= held + CUT - low) & (row < held + tok_rows - low))
    return ((x_half == 0) & (row < CUT)) | ((x_half == 1) & rest)


def only(mask, values):
    return jnp.where(mask, values, jnp.zeros_like(values))


def token_layout(tok_rows):
    held = -(-tok_rows // 16) * 16
    low = CUT // 16 * 16
    return held, low, held - low


def transpose_into(src, dst):
    def step(index, carry):
        cols = pl.ds(pl.multiple_of(index * LANES, LANES), LANES)
        dst[cols, :] = src[:, cols].astype(F32).T.astype(BF16)
        return carry

    lax.fori_loop(0, dst.shape[0] // LANES, step, 0)


class Place:
    def __init__(self):
        self.s = lax.axis_index("section")
        self.d = lax.axis_index("dp")
        self.t = lax.axis_index("tensor")
        self.x = self.t % 2
        self.y = self.t // 2
        self.near = self.t + (1 - self.s) * (1 - 2 * self.x) + self.s * (2 - 4 * self.y)
        self.far = self.t + self.s * (1 - 2 * self.x) + (1 - self.s) * (2 - 4 * self.y)
        self.cross = 3 - self.t
        self.beside = self.t + 1 - 2 * self.x
        self.above = self.t + 2 - 4 * self.y
        self.sibling = (1 - self.s, self.d, self.t)
        self.diagonal = (1 - self.s, self.d, self.beside)

    def at(self, tensor):
        return (self.s, self.d, tensor)


def remote(src, dst, send, recv, device):
    return pltpu.make_async_remote_copy(
        src_ref=src, dst_ref=dst, send_sem=send, recv_sem=recv, device_id=device, device_id_type=MESH
    )


def greet(peers):
    barrier = pltpu.get_barrier_semaphore()
    for peer in peers:
        pl.semaphore_signal(barrier, inc=1, device_id=peer, device_id_type=MESH)
    pl.semaphore_wait(barrier, len(peers))


class HandBack:
    def __init__(self, here, layer, tok_rows, rows_ref, main_out, back_out, sems):
        held, _, spare = token_layout(tok_rows)
        main_send, main_recv, back_send, back_recv, own = sems
        self.here, self.layer = here, layer
        main, back = rows_ref.at[pl.ds(0, held)], rows_ref.at[pl.ds(held, spare)]
        s = here.s
        self.local = pltpu.make_async_copy(main, main_out.at[s], own)
        self.away = remote(main, main_out.at[s], main_send, main_recv, here.sibling)
        self.backs = [
            remote(back, back_out.at[s], back_send, back_recv.at[s], (layer, here.d, here.beside)),
        ]
        self.landing = [
            remote(back, back_out.at[i], back_send, back_recv.at[i], here.sibling) for i in range(2)
        ]

    def start(self):
        mine = self.here.s == self.layer
        pl.when(mine)(self.local.start)
        pl.when(jnp.logical_not(mine))(self.away.start)

    def start_back(self):
        pl.when(self.here.x == 1)(self.backs[0].start)

    def wait(self):
        mine = self.here.s == self.layer

        @pl.when(mine)
        def _():
            self.local.wait()
            self.away.wait_recv()

            @pl.when(self.here.x == 0)
            def _():
                for landing in self.landing:
                    landing.wait_recv()

        pl.when(jnp.logical_not(mine))(self.away.wait_send)
        pl.when(self.here.x == 1)(self.backs[0].wait_send)


def hand_back_sems():
    dma = pltpu.SemaphoreType.DMA
    return [dma, dma, dma, dma((2,)), dma]


KINDS = 4
FIRST_PLAN = [
    (0, 0, False), (0, 1, True), (1, 0, False), (2, 0, True), (2, 2, True), (3, 0, True), (3, 2, False), (3, 3, False)
]
SECOND_PLAN = [
    (0, 0, False), (0, 1, True), (1, 0, False), (2, 0, True), (2, 2, True),
    (3, 0, False), (3, 1, False), (3, 2, False), (3, 3, False),
]
PLAN = [(0, *step) for step in FIRST_PLAN] + [(1, *step) for step in SECOND_PLAN]
STARTS = (0, len(FIRST_PLAN))
WINDOW = 2


def forward_kernel(
    tok_rows,
    crop_ref, route_ref, one_ref, two_ref, router_in, patch_ref, cotangent_ref, wq_ref, wo_ref, wu_ref, wd_ref,
    x_out, gain_out, keep_out, router_out, bias_out, grad_out,
    gq_out, go_out, gu_out, gd_out, norm_out, qkv_out, mixed_out, hidden_out,
    second_out, active_out, slope_out, branch_out,
    x_own, gain_ref, my_gain, keep_ref, router_ref, bias_ref, tokens, spare_rows, grad_own,
    gq, go, gu, gd, normed, qkv, mixed, hidden, second, active, slope, branch, work,
    own_sem, lend_send, lend_recv, a_send, a_recv, b_send, b_recv, c_send, c_recv,
    e_send, e_recv, f_send, f_recv, out_sem, save_sem, tok_sem, tok_send, tok_recv, gain_sem, gain_send, gain_recv, x_sem, bias_sem,
):
    here = Place()
    held, low, spare = token_layout(tok_rows)
    part = wo_ref.shape[0]
    unit = part // 2
    shards = (wq_ref, wo_ref, wu_ref, wd_ref)

    def block(kind, layer, quarter):
        rows = pl.ds(pl.multiple_of(quarter * part, part), part)
        if kind == 0:
            return gq.at[layer, :, rows, :]
        if kind == 1:
            return go.at[layer, rows, :]
        return (gu if kind == 2 else gd).at[layer, quarter]

    parity = here.d % 2

    def chunk(step, quarter, half, other=0):
        layer, kind, piece, shared = PLAN[step]
        if shared:
            piece = piece + other + (1 - 2 * other) * parity
        if kind < 2:
            rows = pl.ds(pl.multiple_of(quarter * part + half * unit, unit), unit)
            return gq.at[layer, piece, rows, :] if kind == 0 else go.at[layer, rows, :]
        rows = pl.ds(pl.multiple_of((4 * half + piece) * unit, unit), unit)
        return (gu if kind == 2 else gd).at[layer, quarter, rows, :]

    def own_copy(kind):
        return pltpu.make_async_copy(shards[kind], block(kind, here.s, here.t), own_sem.at[kind])

    def lend(kind, layer):
        return remote(
            shards[kind], block(kind, layer, here.t), lend_send.at[kind], lend_recv.at[kind], here.sibling
        )

    def along(step, quarter, peer, send, recv):
        piece = chunk(step, quarter, here.s)
        return remote(piece, piece, send.at[step], recv.at[step], peer)

    def send_a(step):
        return along(step, here.t, here.at(here.near), a_send, a_recv)

    def send_b(step):
        return along(step, here.t, here.at(here.far), b_send, b_recv)

    def send_c(step):
        return along(step, here.near, here.at(here.far), c_send, c_recv)

    def send_e(step, which, half=None, other=0):
        piece = chunk(step, three[which], here.s if half is None else half, other)
        index = which + 3 * other
        return remote(piece, piece, e_send.at[step, index], e_recv.at[step, index], here.sibling)

    def send_f(step, which, other=0):
        piece = chunk(step, three[which], here.s, other)
        return remote(piece, piece, f_send.at[step, which], f_recv.at[step, which], z_beside)

    three = (here.near, here.far, here.cross)
    z_beside = (here.s, here.d + 1 - 2 * parity, here.t)
    total = len(PLAN)

    greet([here.sibling, here.at(here.near), here.at(here.far), z_beside])

    lend(0, here.s).start()
    own_copy(0).start()
    my_gain[...] = jnp.zeros_like(my_gain)
    my_gain[0:1, :] = one_ref[...]
    my_gain[1:2, :] = two_ref[...]
    gain_own = pltpu.make_async_copy(my_gain, gain_ref.at[here.s], gain_sem)
    gain_away = remote(my_gain, gain_ref.at[here.s], gain_send, gain_recv, here.sibling)
    token_loads = []
    for which, source in enumerate((patch_ref, cotangent_ref)):
        tokens[which, pl.ds(tok_rows, held - tok_rows)] = jnp.zeros((held - tok_rows, *tokens.shape[2:]), BF16)
        token_loads.append(
            pltpu.make_async_copy(source, tokens.at[which, pl.ds(0, tok_rows)], tok_sem.at[which])
        )
    tok_away = [
        remote(src, dst.at[pl.ds(held, spare)], tok_send.at[i], tok_recv.at[i], here.at(here.beside))
        for i, (src, dst) in enumerate(((spare_rows, x_own.at[0]), (grad_own.at[pl.ds(low, spare)], grad_out)))
    ]
    grad_save = pltpu.make_async_copy(grad_own, grad_out.at[pl.ds(0, held)], tok_sem.at[2])
    for copy in token_loads:
        copy.start()
    gain_own.start()
    gain_away.start()

    def issue(step):
        if step >= total:
            return
        layer, kind, piece, _ = PLAN[step]
        if piece == 0:
            pl.when(here.s == layer)(lambda: own_copy(kind).wait())
            pl.when(here.s != layer)(lambda: lend(kind, layer).wait_recv())
        send_a(step).start()
        send_b(step).start()

    def pass_on(step, which):
        send_e(step, which).start()
        if PLAN[step][3]:
            send_f(step, which).start()

    def relay(step):
        if step >= total:
            return
        send_a(step).wait_recv()
        send_c(step).start()
        pass_on(step, 0)
        issue(step + WINDOW)

    def fetch(step):
        if step >= total:
            return
        send_b(step).wait_recv()
        pass_on(step, 1)
        send_c(step).wait_recv()
        pass_on(step, 2)

    moved = [0]
    relayed = [0]

    def relays(upto):
        while relayed[0] < min(upto, total):
            relay(relayed[0])
            relayed[0] += 1

    def tick(upto):
        while moved[0] <= min(upto, total - 1):
            relays(moved[0] + 3)
            fetch(moved[0])
            moved[0] += 1

    def pump(step):
        tick(step + 2)
        shared = PLAN[step][3]
        if shared:
            for which in range(3):
                send_f(step, which, 1).wait_recv()
                send_e(step, which, None, 1).start()
        for other in range(1 + shared):
            for which in range(3):
                send_e(step, which, 1 - here.s, other).wait_recv()

    for step in range(WINDOW):
        issue(step)
    for kind in range(1, KINDS):
        lend(kind, here.s).start()
        own_copy(kind).start()
    def take(which, dst):
        def step(rows):
            dst[rows, :] = jnp.where(here.s == 0, tokens[which, rows, 0, :], tokens[which, rows, 1, :])

        tiles(step, rows=held, tile=16)

    for copy in token_loads:
        copy.wait()
    take(0, x_own.at[0])
    spare_rows[...] = x_own[0, pl.ds(low, spare), :]
    pl.when(here.x == 0)(tok_away[0].start)
    take(1, grad_own)
    pl.when(here.x == 0)(tok_away[1].start)
    grad_save.start()
    router_ref[...] = router_in[...].astype(F32).reshape(router_ref.shape)
    router_out[...] = router_ref[...]

    relays(1)

    image = here.t // 2
    slot_len = route_ref.shape[1] // crop_ref.shape[1]
    routes = jnp.where(here.s == 0, route_ref[0:1, :], route_ref[1:2, :]).astype(F32)
    lanes = -(-(routes.shape[1] + ROWS) // LANES) * LANES
    routes = jnp.concatenate([routes, jnp.zeros((1, lanes - routes.shape[1]), F32)], axis=1)
    routes = jnp.broadcast_to(routes, (8, lanes))

    def routed_from(start):
        return pltpu.roll(routes, (2 * lanes - start) % lanes, 1)[0:1, :ROWS]

    def rows_info(row):
        valid = valid_rows(here.x, tok_rows, row)
        position = jnp.where(row < held, here.x * tok_rows + row, low - held + row)
        position = jnp.where(here.x == 0, row, position)
        crop = jnp.zeros_like(row)
        end = 0
        for i in range(crop_ref.shape[2]):
            end = end + crop_ref[here.s, image, i]
            crop += (position >= end).astype(jnp.int32)
        return valid, jnp.where(valid, crop, -1)

    across = lax.broadcasted_iota(jnp.int32, (1, ROWS), 1)
    valid, crop_across = rows_info(across)
    routed = jnp.where(
        across < held,
        routed_from(image * slot_len + here.x * tok_rows),
        routed_from(image * slot_len + low - held),
    )
    routed = jnp.where(valid, routed, 0.0)
    keep_ref[...] = jnp.broadcast_to(routed, (LANES, ROWS)).T[:, 0:1]
    keep_out[...] = keep_ref[...]
    usable = jnp.where(valid, routed, 1.0) > 0.0

    def allow(rows):
        _, crop_down = rows_info(lax.broadcasted_iota(jnp.int32, (TILE, 1), 0) + rows.start)
        same = crop_down == crop_across
        bias_ref[0, rows, :] = jnp.where(same & usable, 0.0, NEG)
        bias_ref[1, rows, :] = jnp.where(same, 0.0, NEG)

    tiles(allow)
    bias_save = pltpu.make_async_copy(bias_ref, bias_out, bias_sem)
    bias_save.start()
    relays(2)

    pl.when(here.x == 1)(tok_away[0].wait_recv)

    def clear(block):
        def step(rows):
            row = lax.broadcasted_iota(jnp.int32, (TILE, 1), 0) + rows.start
            block[rows, :] = only(valid_rows(here.x, tok_rows, row), block[rows, :])

        tiles(step)

    clear(x_own.at[0])
    x_saves = [pltpu.make_async_copy(x_own.at[i], x_out.at[i], x_sem.at[i]) for i in range(3)]
    x_saves[0].start()
    gain_own.wait()
    gain_away.wait_recv()
    gain_out[...] = gain_ref[...]
    masks = half_masks()
    saves = []

    def weight_save(kind, layer):
        src, dst = ((gq, gq_out), (go, go_out), (gu, gu_out), (gd, gd_out))[kind]
        return pltpu.make_async_copy(src.at[layer], dst.at[layer], out_sem.at[layer, kind])

    def keep_weight(kind, layer):
        weight_save(kind, layer).start()

    def save(index, layer, src, dst):
        copy = pltpu.make_async_copy(src, dst.at[layer], save_sem.at[index])
        copy.start()
        return copy

    for layer in range(2):
        x_now = x_own.at[layer]

        def first_norm(rows):
            xhat, _ = standardize(x_now[rows, :].astype(F32))
            normed[rows, :] = (xhat * gain_ref[layer, 0:1, :]).astype(BF16)

        for copy in saves:
            copy.wait()
        saves = []
        tiles(first_norm)
        saves.append(save(0, layer, normed, norm_out))
        base = STARTS[layer]
        pump(base)
        qkv[0] = dot(normed[...], gq[layer, 0], NT).astype(BF16)
        pump(base + 1)
        keep_weight(0, layer)

        def project(j, carry):
            qkv[j] = dot(normed[...], gq[layer, j], NT).astype(BF16)
            return carry

        lax.fori_loop(1, 3, project, 0)
        saves.append(save(1, layer, qkv, qkv_out))

        def attend(pair, carry):
            cols = pl.ds(pl.multiple_of(pair * LANES, LANES), LANES)
            key, value = qkv[1, :, cols], qkv[2, :, cols]
            query = qkv[0, :, cols] * BF16(0.125)
            outs = []
            for mask in masks:
                expo, inverse = softmax_parts(dot(only(mask, query), key, NT) + bias_ref[layer])
                outs.append(dot(expo.astype(BF16), value) * inverse)
            mixed[:, cols] = jnp.where(masks[0], outs[0], outs[1]).astype(BF16)
            return carry

        pairs = mixed.shape[1] // LANES
        for part_of in range(3):
            lax.fori_loop(pairs * part_of // 3, pairs * (part_of + 1) // 3, attend, 0)
            tick(base + 3 + part_of)
        saves.append(save(2, layer, mixed, mixed_out))
        pump(base + 2)
        keep_weight(1, layer)
        branch[...] = dot(mixed[...], go[layer])

        def second_norm(rows):
            value = x_now[rows, :].astype(F32) + branch[rows, :]
            hidden[rows, :] = value
            xhat, _ = standardize(value)
            second[rows, :] = (xhat * gain_ref[layer, 1:2, :]).astype(BF16)

        tiles(second_norm)
        saves.append(save(3, layer, hidden, hidden_out))
        saves.append(save(4, layer, second, second_out))
        pump(base + 3)
        pump(base + 4)
        keep_weight(2, layer)

        def widen(g, carry):
            work[...] = dot(second[...], gu[layer, g])

            def bend(rows):
                upper = work[rows, :]
                phi = 0.5 * (1.0 + lax.erf(upper * 0.7071067811865476))
                bell = jnp.exp(-0.5 * upper * upper) * 0.3989422804014327
                active[g, rows, :] = (upper * phi).astype(BF16)
                slope[g, rows, :] = (phi + upper * bell).astype(BF16)

            tiles(bend, tile=32)
            return carry

        for g in range(4):
            widen(g, 0)
            tick(base + 6 + g)
        saves.append(save(5, layer, active, active_out))
        saves.append(save(6, layer, slope, slope_out))
        for step in range(base + 5, (*STARTS, total)[layer + 1]):
            pump(step)
        keep_weight(3, layer)

        def narrow(g, carry):
            branch[...] += dot(active[g], gd[layer, g])
            return carry

        for g in range(4):
            narrow(g, 0)
            tick((*STARTS, total)[layer + 1] + g // 2)
        if layer == 0:
            saves.append(save(7, layer, branch, branch_out))

        def finish(rows):
            value = x_now[rows, :].astype(F32)
            change = branch[rows, :]
            if layer == 0:
                logit = jnp.sum(value * router_ref[...], axis=-1, keepdims=True)
                change = change * (keep_ref[rows, :] / (1.0 + jnp.exp(-logit)))
            x_own[layer + 1, rows, :] = (value + change).astype(BF16)

        tiles(finish)
        x_saves[layer + 1].start()

    for copy in [*saves, *x_saves, grad_save, bias_save]:
        copy.wait()
    gain_away.wait_send()

    @pl.when(here.x == 0)
    def _():
        for away in tok_away:
            away.wait_send()

    pl.when(here.x == 1)(tok_away[1].wait_recv)
    for layer in range(2):
        for kind in range(KINDS):
            weight_save(kind, layer).wait()
    for kind in range(KINDS):
        lend(kind, here.s).wait_send()
    for step in range(total):
        send_a(step).wait_send()
        send_b(step).wait_send()
        send_c(step).wait_send()
        shared = PLAN[step][3]
        for which in range(3):
            send_e(step, which).wait_send()
            if shared:
                send_f(step, which).wait_send()
                send_e(step, which, None, 1).wait_send()


def forward(crops, routes, one, two, router, patches, cotangent, wq, wo, wu, wd):
    tok_rows, _, width = patches.shape
    held, _, spare = token_layout(tok_rows)
    any_spec = pl.BlockSpec(memory_space=pl.ANY)
    vmem = pl.BlockSpec(memory_space=pltpu.VMEM)

    def pair(*shape, dtype=BF16):
        return jax.ShapeDtypeStruct((2, *shape), dtype)

    shapes = [
        jax.ShapeDtypeStruct((3, ROWS, width), BF16), pair(8, width, dtype=F32),
        jax.ShapeDtypeStruct((ROWS, 1), F32), jax.ShapeDtypeStruct((1, width), F32), pair(ROWS, ROWS, dtype=F32),
        jax.ShapeDtypeStruct((ROWS, width), BF16),
        pair(3, width, width), pair(width, width), pair(4, width, width), pair(4, width, width),
        pair(ROWS, width), pair(3, ROWS, width), pair(ROWS, width), pair(ROWS, width, dtype=F32),
        pair(ROWS, width), pair(4, ROWS, width), pair(4, ROWS, width), pair(ROWS, width, dtype=F32),
    ]
    dma = pltpu.SemaphoreType.DMA
    scratch = [
        pltpu.VMEM((3, ROWS, width), BF16), pltpu.VMEM((2, 8, width), F32), pltpu.VMEM((8, width), F32),
        pltpu.VMEM((ROWS, 1), F32), pltpu.VMEM((1, width), F32), pltpu.VMEM((2, ROWS, ROWS), F32),
        pltpu.VMEM((2, held, 2, width), BF16), pltpu.VMEM((spare, width), BF16), pltpu.VMEM((held, width), BF16),
        pltpu.VMEM((2, 3, width, width), BF16), pltpu.VMEM((2, width, width), BF16),
        pltpu.VMEM((2, 4, width, width), BF16), pltpu.VMEM((2, 4, width, width), BF16),
        pltpu.VMEM((ROWS, width), BF16), pltpu.VMEM((3, ROWS, width), BF16),
        pltpu.VMEM((ROWS, width), BF16), pltpu.VMEM((ROWS, width), F32),
        pltpu.VMEM((ROWS, width), BF16), pltpu.VMEM((4, ROWS, width), BF16),
        pltpu.VMEM((4, ROWS, width), BF16), pltpu.VMEM((ROWS, width), F32),
        pltpu.VMEM((ROWS, width), F32),
        dma((KINDS,)), dma((KINDS,)), dma((KINDS,)),
        *[dma((len(PLAN),))] * 6, *[dma((len(PLAN), 6))] * 2, *[dma((len(PLAN), 3))] * 2,
        dma((2, KINDS)), dma((8,)),
        dma((3,)), dma((2,)), dma((2,)), dma, dma, dma, dma((3,)), dma,
    ]
    return pl.pallas_call(
        functools.partial(forward_kernel, tok_rows),
        out_shape=shapes,
        in_specs=[pl.BlockSpec(memory_space=pltpu.SMEM)] + [vmem] * 4 + [any_spec] * 6,
        out_specs=[any_spec, vmem, vmem, vmem] + [any_spec] * 14,
        scratch_shapes=scratch,
        compiler_params=pltpu.CompilerParams(
            collective_id=0, has_side_effects=True, vmem_limit_bytes=VMEM_BYTES
        ),
        cost_estimate=pl.CostEstimate(flops=24 * ROWS * width * width * 2, bytes_accessed=60_000_000, transcendentals=0),
        name="forward_layers",
    )(crops, routes, one, two, router, patches, cotangent, wq, wo, wu, wd)


UNITS = 12
RING = 7
EARLY_BACKS = 2
TOTALS = (3, 6, 9)
SIBS, NEARS, FARS, PLANES = 8, 12, 10, 8
Z_FIRST = (3,15)
ORDER = sorted(range(2 * UNITS), key=lambda u: u + 2.5 if u in Z_FIRST else u)
SCHEDULE = [
    (0, 0, 0, 0), (0, 0, 0, 0), (0, 0, 0, 0), (0, 0, 0, 0), (0, 0, 0, 0), (0, 0, 0, 0), (1, 0, 0, 0),
    (1, 0, 0, 0), (2, 0, 0, 0), (2, 0, 0, 0), (2, 0, 0, 0), (3, 0, 1, 0), (3, 0, 1, 0), (3, 0, 1, 0),
    (4, 0, 2, 0), (4, 0, 2, 0), (4, 0, 2, 0), (4, 0, 3, 0), (6, 0, 3, 2), (7, 1, 3, 3), (7, 1, 3, 3),
    (7, 1, 4, 3), (8, 1, 5, 3), (8, 1, 6, 3), (8, 1, 7, 3), (9, 1, 7, 4), (10, 1, 8, 6), (10, 1, 8, 7),
    (11, 1, 8, 7), (11, 1, 9, 7), (11, 1, 9, 8), (12, 1, 9, 8), (12, 1, 10, 8), (12, 1, 10, 8),
    (12, 1, 10, 8),
    (12, 1, 10, 8), (12, 1, 11, 8), (13, 1, 11, 9), (13, 1, 11, 9), (13, 1, 11, 9), (13, 1, 12, 9),
    (13, 1, 12, 9), (14, 1, 12, 10), (14, 1, 12, 11), (15, 1, 12, 11), (15, 1, 12, 11), (15, 1, 13, 11),
    (15, 1, 13, 12), (17, 1, 13, 12), (18, 1, 15, 13), (18, 1, 16, 13), (19, 1, 16, 14), (19, 1, 16, 15),
    (19, 2, 17, 15), (20, 2, 17, 16), (20, 2, 19, 16), (21, 2, 19, 17), (22, 2, 20, 18), (22, 2, 20, 19),
    (23, 2, 20, 19), (23, 2, 21, 19), (23, 2, 21, 20), (24, 2, 21, 20), (24, 2, 22, 20), (24, 2, 23, 20),
    (24, 2, 23, 21), (24, 2, 24, 21), (24, 2, 24, 22), (24, 2, 24, 23), (24, 2, 24, 24),
]


def comes_first_z(section, d, kind):
    units = [u for u in Z_FIRST if u % UNITS // 4 == kind]
    return functools.reduce(
        jnp.logical_or, [(section == 1 - u // UNITS) & (d == u % UNITS % 4) for u in units], section < 0
    )


def backward_kernel(
    in_kernel_z, tok_rows,
    keep_ref, gain_ref, router_ref, bias_in, grad_in, x_in,
    gq, go, gu, gd, norm_in, qkv_in, mixed_in, hidden_in, second_in, active_in, slope_in, branch_in,
    small_out, y_main, y_back, main_out, back_out, mlp_out, att_out,
    grad_ref, x_ref, dx_ref, dx_low, small_ref, tot, got, bias_ref,
    wq, wo, wu, wd, normed, qkv, mixed, hidden, second, active, slope,
    dbranch, dfed, dfed_t, work, dup, dsecond, datt, dmixed, dqkv, stage, sib, near_in, far_in, plane, mate_in,
    load_sem, wu_sem, wd_sem, slope_sem,
    sib_send, sib_recv, near_send, near_recv, far_send, far_recv,
    mlp_send, mlp_recv, att_send, att_recv, local_sem, tot_send, tot_recv, mate_send, mate_recv, *back_sems,
):
    here = Place()
    s, d, t = here.s, here.d, here.t
    quarter_rows = stage.shape[2]
    half_rows = quarter_rows // 2
    my_rows = pl.ds(pl.multiple_of(s * half_rows, half_rows), half_rows)
    their_rows = pl.ds(pl.multiple_of((1 - s) * half_rows, half_rows), half_rows)
    n_dp = lax.axis_size("dp")
    branch = dsecond

    saved = {
        "active": (active_in, active), "x": (x_in, x_ref), "second": (second_in, second),
        "hidden": (hidden_in, hidden), "mixed": (mixed_in, mixed), "wo": (go, wo), "qkv": (qkv_in, qkv),
        "normed": (norm_in, normed), "wq": (gq, wq), "branch": (branch_in, branch),
    }

    def load(name, layer):
        src, dst = saved[name]
        return pltpu.make_async_copy(src.at[layer], dst, load_sem.at[layer, list(saved).index(name)])

    def prefetch(name, layer):
        if layer == 1:
            load(name, 0).start()

    streams = ((gd, wd, wd_sem), (slope_in, slope, slope_sem), (gu, wu, wu_sem))

    def quarter_load(stream, layer, g):
        src, dst, sems = stream
        return pltpu.make_async_copy(src.at[layer, g], dst.at[g % 2], sems.at[layer, g % 2])

    load_grad = pltpu.make_async_copy(grad_in, grad_ref, load_sem.at[0, len(saved)])
    load_bias = pltpu.make_async_copy(bias_in, bias_ref, load_sem.at[1, len(saved)])
    load_grad.start()

    load("active", 1).start()
    for g in range(2):
        for stream in streams:
            quarter_load(stream, 1, g).start()
    for name in saved:
        if name not in ("active", "branch"):
            load(name, 1).start()
    load_bias.start()

    peers = [here.sibling, here.at(here.near), here.at(here.far), here.diagonal]
    doubled = [here.sibling, here.at(here.near), here.at(here.far)]
    along_z = [(s, (d + shift) % n_dp, t) for shift in range(1, n_dp)]
    peers += along_z
    if in_kernel_z:
        peers += [(1 - s, z, t) for _, z, _ in along_z]
    greet(peers)

    backs = []

    def hand_back(layer, rows_ref, main, back):
        sems = back_sems[5 * len(backs) : 5 * len(backs) + 5]
        backs.append(HandBack(here, layer, tok_rows, rows_ref, main, back, sems))
        backs[-1].start()
        if len(backs) <= EARLY_BACKS:
            backs[-1].start_back()

    for layer in range(2):
        hand_back(layer, x_in.at[layer + 1], y_main, y_back)

    def total_move(step):
        last = len(doubled)
        return remote(
            tot.at[min(step, last)], got.at[step], tot_send.at[step], tot_recv.at[step], (doubled + along_z)[step]
        )

    def add_total(step):
        total_move(step).wait_recv()
        tot[step + 1] = tot[step] + got[step]
        if step + 1 < len(doubled):
            total_move(step + 1).start()
        else:
            for shift in range(len(along_z)):
                total_move(step + 1 + shift).start()

    near_sent = [s * (2 * (1 - here.y) + i) + (1 - s) * (2 * i + 1 - here.x) for i in range(2)]
    own_slot = s * here.x + (1 - s) * here.y
    z_first = Z_FIRST if in_kernel_z else ()
    fewer = half_rows // 2
    parity = d % 2
    z_mate = (s, d + 1 - 2 * parity, t)

    def rows_of(u):
        if u not in z_first:
            return my_rows, half_rows
        return pl.ds(pl.multiple_of(s * half_rows + parity * fewer, fewer), fewer), fewer

    def to_mate(u):
        rows = pl.ds(pl.multiple_of(s * half_rows + (1 - parity) * fewer, fewer), fewer)
        i = z_first.index(u)
        return remote(stage.at[u % RING, :, rows, :], mate_in.at[i], mate_send.at[i], mate_recv.at[i], z_mate)

    def to_sibling(u):
        return remote(
            stage.at[u % RING, :, their_rows, :], sib.at[u % SIBS], sib_send.at[u], sib_recv.at[u], here.sibling
        )

    def to_near(u, i):
        rows, count = rows_of(u)
        return remote(
            stage.at[u % RING, near_sent[i], rows, :], near_in.at[u % NEARS, i, pl.ds(0, count)],
            near_send.at[u, i], near_recv.at[u, i], here.at(here.near),
        )

    def to_far(u):
        rows, count = rows_of(u)
        return remote(
            stage.at[u % RING, here.far, rows, :], far_in.at[u % FARS, pl.ds(0, count)],
            far_send.at[u], far_recv.at[u], here.at(here.far),
        )

    def give(u):
        to_sibling(u).start()

    def first(u):
        to_sibling(u).wait_recv()

        def add(q, carry):
            stage[u % RING, q, my_rows, :] += sib[u % SIBS, q]
            return carry

        lax.fori_loop(0, 4, add, 0)
        if u in z_first:
            to_mate(u).start()
            return
        for i in range(2):
            to_near(u, i).start()

    def middle(index):
        u = z_first[index]
        to_mate(u).wait_recv()
        rows, _ = rows_of(u)

        def add(q, carry):
            stage[u % RING, q, rows, :] += mate_in[index, q]
            return carry

        lax.fori_loop(0, 4, add, 0)
        for i in range(2):
            to_near(u, i).start()

    def second_step(place):
        u = ORDER[place]
        for i in range(2):
            to_near(u, i).wait_recv()
        rows, count = rows_of(u)
        stage[u % RING, here.far, rows, :] += near_in[u % NEARS, 1 - own_slot, pl.ds(0, count)]
        to_far(u).start()

    def z_moves(u):
        layer, v = 1 - u // UNITS, u % UNITS
        kept = ORDER.index(u) % PLANES
        moves = []
        if not in_kernel_z:
            target = mlp_out.at[v, my_rows, :]
            mine = s == layer
            moves.append((mine, pltpu.make_async_copy(plane.at[kept], target, local_sem.at[u, 0]), remote(
                plane.at[kept], target, mlp_send.at[u], mlp_recv.at[v, 0, s], (layer, d, t))))
        elif v < 8:
            rows, count = rows_of(u)
            piece = plane.at[kept, pl.ds(0, count)]
            target = mlp_out.at[v // 4, d, rows, :]
            mine = (s == layer) & (d == v % 4)
            moves.append((mine, pltpu.make_async_copy(piece, target, local_sem.at[u, 0]), remote(
                piece, target, mlp_send.at[u], mlp_recv.at[v // 4, d, s], (layer, v % 4, t))))
        else:
            for other in range(4):
                lanes = plane.shape[2] // 4 * other // LANES * LANES
                piece = plane.at[kept, :, pl.ds(lanes, 2 * LANES)]
                target = att_out.at[v - 8, d, my_rows, :]
                mine = (s == layer) & (d == other)
                moves.append((mine, pltpu.make_async_copy(piece, target, local_sem.at[u, other]), remote(
                    piece, target, att_send.at[layer, v - 8, other], att_recv.at[v - 8, d, s], (layer, other, t))))
        return moves

    def moved_out(u):
        for mine, local, away in z_moves(u):
            pl.when(mine)(local.wait)
            pl.when(jnp.logical_not(mine))(away.wait_send)

    def third(place):
        u = ORDER[place]
        to_far(u).wait_recv()
        if place >= PLANES:
            moved_out(ORDER[place - PLANES])
        rows, count = rows_of(u)
        some = pl.ds(0, count)
        plane[place % PLANES, some] = (
            stage[u % RING, t, rows, :].astype(F32)
            + near_in[u % NEARS, own_slot, some].astype(F32) + far_in[u % FARS, some].astype(F32)
        ).astype(BF16)
        for mine, local, away in z_moves(u):
            pl.when(mine)(local.start)
            pl.when(jnp.logical_not(mine))(away.start)
        to_sibling(u).wait_send()
        if u in z_first:
            to_mate(u).wait_send()
        for i in range(2):
            to_near(u, i).wait_send()
        to_far(u).wait_send()

    done = [0, 0, 0, 0]
    given = [0]
    steps = (first, middle, second_step, third)

    def ready(which):
        place = done[which]
        if which == 0:
            return place < given[0]
        if which == 1:
            return place < len(z_first) and z_first[place] < done[0]
        if which == 3:
            return place < done[2]
        u = ORDER[place]
        return u < done[0] and (u not in z_first or z_first.index(u) < done[1])

    def reach(*targets):
        targets = [targets[0], min(targets[1], len(z_first)), *targets[2:]]
        while any(now < target for now, target in zip(done, targets)):
            before = list(done)
            for which in (2, 0, 1, 3):
                if done[which] < targets[which] and ready(which):
                    steps[which](done[which])
                    done[which] += 1
            if done == before:
                which = next(which for which in (2, 1, 0) if ready(which))
                steps[which](done[which])
                done[which] += 1

    points = iter(SCHEDULE)

    def point():
        reach(*next(points))

    def room():
        old = given[0] - RING
        if old >= 0:
            last = max(ORDER.index(u) for u in range(old + 1))
            while done[3] <= last:
                for which in (3, 2, 1, 0):
                    if ready(which):
                        steps[which](done[which])
                        done[which] += 1
                        break

    def slot():
        give(given[0])
        given[0] += 1
        point()

    def rows_unit(k, left, right):
        room()
        place = given[0] % RING
        rows = pl.ds(k * quarter_rows, quarter_rows)

        def step(g, carry):
            stage[place, g] = dot(left[rows, :], right[g]).astype(BF16)
            return carry

        lax.fori_loop(0, 4, step, 0)

    def square_unit(left, right):
        room()
        place = given[0] % RING
        width = left.shape[1] // 2

        def step(c, carry):
            cols = pl.ds(pl.multiple_of(c * width, width), width)
            product = dot(left[:, cols], right[...], TN).astype(BF16)
            stage[place, pl.ds(2 * c, 2)] = product.reshape(2, quarter_rows, product.shape[1])
            return carry

        lax.fori_loop(0, 2, step, 0)

    masks = half_masks()

    def run_layer(layer):
        source = grad_ref if layer == 1 else dx_low.at[1]

        def prepare(rows):
            row = lax.broadcasted_iota(jnp.int32, (TILE, 1), 0) + rows.start
            grad = only(valid_rows(here.x, tok_rows, row), source[rows, :]).astype(F32)
            if layer == 0:
                value = x_ref[rows, :].astype(F32)
                logit = jnp.sum(value * router_ref[...], axis=-1, keepdims=True)
                sigma = 1.0 / (1.0 + jnp.exp(-logit))
                keep = keep_ref[rows, :]
                dlogit = jnp.sum(grad * branch[rows, :], axis=-1, keepdims=True) * keep * sigma * (1.0 - sigma)
                small_ref[2] += fold_rows(value * dlogit)
                dx_ref[rows, :] = grad + dlogit * router_ref[...]
                grad = grad * (sigma * keep)
            else:
                dx_ref[rows, :] = grad
            dbranch[rows, :] = grad
            dfed[rows, :] = grad.astype(BF16)

        small_ref[...] = jnp.zeros_like(small_ref)
        if layer == 1:
            load_grad.wait()
        else:
            load("branch", 0).wait()
            load("x", 0).wait()
        tiles(prepare)
        point()
        transpose_into(dfed, dfed_t)
        point()
        load("active", layer).wait()
        for k in range(4):
            g = k
            rows_unit(k, dfed_t, active)
            slot()
            if k == 3:
                prefetch("active", layer)
            for stream in streams:
                quarter_load(stream, layer, g).wait()
            work[...] = dot(dfed[...], wd[g % 2], NT)

            def bend(rows):
                dup[g, rows, :] = (work[rows, :] * slope[g % 2, rows, :].astype(F32)).astype(BF16)

            tiles(bend)
            point()
            part = dot(dup[g], wu[g % 2], NT)
            if g == 0:
                dsecond[...] = part
            else:
                dsecond[...] += part
            for stream in streams:
                if g < 2:
                    quarter_load(stream, layer, g + 2).start()
                elif layer == 1:
                    quarter_load(stream, 0, g - 2).start()
            point()

        load("second", layer).wait()
        transpose_into(second, dfed_t)
        point()
        prefetch("second", layer)
        for k in range(4):
            rows_unit(k, dfed_t, dup)
            slot()

        load("hidden", layer).wait()

        def second_pull(rows):
            xhat, rstd = standardize(hidden[rows, :])
            grad = dsecond[rows, :]
            small_ref[1] += fold_rows(grad * xhat)
            dhidden = norm_pull(xhat, rstd, gain_ref[layer, 1:2, :], grad)
            dx_ref[rows, :] += dhidden
            datt[rows, :] = (dbranch[rows, :] + dhidden).astype(BF16)

        tiles(second_pull)
        point()
        prefetch("hidden", layer)
        prefetch("branch", layer)
        load("mixed", layer).wait()
        square_unit(mixed, datt)
        prefetch("mixed", layer)
        slot()
        load("wo", layer).wait()
        dmixed[...] = dot(datt[...], wo[...], NT).astype(BF16)
        prefetch("wo", layer)
        point()
        load("qkv", layer).wait()
        if layer == 1:
            load_bias.wait()

        def attend(pair, carry):
            cols = pl.ds(pl.multiple_of(pair * LANES, LANES), LANES)
            key, value = qkv[1, :, cols], qkv[2, :, cols]
            scaled = key * BF16(0.125)
            query = qkv[0, :, cols] * BF16(0.125)
            grad = dmixed[:, cols]
            sums = None
            for mask in masks:
                query_head, grad_head = only(mask, query), only(mask, grad)
                expo, inverse = softmax_parts(dot(query_head, key, NT) + bias_ref[layer])
                probs = expo * inverse
                dprobs = dot(grad_head, value, NT)
                dscores = probs * (dprobs - jnp.sum(probs * dprobs, axis=-1, keepdims=True))
                dscores = dscores.astype(BF16)
                parts = [
                    dot(dscores, only(mask, scaled)),
                    dot(dscores, query_head, TN),
                    dot(probs.astype(BF16), grad_head, TN),
                ]
                sums = parts if sums is None else [left + right for left, right in zip(sums, parts)]
            for j in range(3):
                dqkv[j, :, cols] = sums[j].astype(BF16)
            return carry

        pairs = dmixed.shape[1] // LANES
        for part_of in range(3):
            lax.fori_loop(pairs * part_of // 3, pairs * (part_of + 1) // 3, attend, 0)
            point()
        prefetch("qkv", layer)

        load("normed", layer).wait()
        for j in range(3):
            square_unit(dqkv.at[j], normed)
            slot()
        prefetch("normed", layer)
        load("wq", layer).wait()
        work[...] = dot(dqkv[0], wq[0])
        work[...] += dot(dqkv[1], wq[1])
        point()
        work[...] += dot(dqkv[2], wq[2])
        point()
        prefetch("wq", layer)
        if layer == 1:
            load("x", 1).wait()

        def first_pull(rows):
            xhat, rstd = standardize(x_ref[rows, :].astype(F32))
            grad = work[rows, :]
            small_ref[0] += fold_rows(grad * xhat)
            total = dx_ref[rows, :] + norm_pull(xhat, rstd, gain_ref[layer, 0:1, :], grad)
            dx_low[layer, rows, :] = total.astype(BF16)

        tiles(first_pull)
        point()
        prefetch("x", layer)
        hand_back(layer, dx_low.at[layer], main_out, back_out)
        sums = jnp.sum(small_ref[...], axis=1)
        if layer == 1:
            tot[0] = jnp.zeros(tot.shape[1:], F32)
            tot[0, 3:5, :] = sums[0:2]
        else:
            tot[0, 0:3, :] = sums
            total_move(0).start()

    run_layer(1)
    run_layer(0)
    added = 0
    late_backs = backs[EARLY_BACKS:]
    for index, targets in enumerate(points):
        reach(*targets)
        if done[2] == 2 * UNITS and late_backs:
            for back in late_backs:
                back.start_back()
            late_backs = []
        if index in TOTALS:
            add_total(added)
            added += 1
    reach(2 * UNITS, len(z_first), 2 * UNITS, 2 * UNITS)
    for step in range(added, len(doubled)):
        add_total(step)
    for back in late_backs:
        back.start_back()
    moves = [total_move(step) for step in range(len(doubled) + len(along_z))]
    for move in moves[len(doubled) :]:
        move.wait_recv()
    total = jnp.zeros_like(small_out)
    for z in range(n_dp):
        shift = (z - d + n_dp) % n_dp
        total += jnp.where(shift == 0, tot[len(doubled)], got[len(doubled) - 1 + jnp.maximum(shift, 1)])
    small_out[...] = total
    for move in moves:
        move.wait_send()
    for back in backs:
        back.wait()
    for u in ORDER[-PLANES:]:
        moved_out(u)

    if not in_kernel_z:
        for v in range(UNITS):
            remote(
                plane.at[0], mlp_out.at[v, their_rows, :], mlp_send.at[v], mlp_recv.at[v, 0, 1 - s], here.sibling
            ).wait_recv()
        return
    for source in range(4):
        for half in range(2):
            rows = pl.ds(half * half_rows, half_rows)

            def arrive():
                for kind in range(2):
                    sent = mlp_recv.at[kind, source, half]
                    first_z = comes_first_z(s, d, kind)
                    for count, now in ((fewer, first_z), (half_rows, jnp.logical_not(first_z))):
                        target = mlp_out.at[kind, source, pl.ds(half * half_rows, count), :]
                        pl.when(now)(remote(target, target, mlp_send.at[0], sent, here.sibling).wait_recv)
                for b in range(4):
                    target = att_out.at[b, source, rows, :]
                    remote(
                        target, target, att_send.at[0, 0, 0], att_recv.at[b, source, half], here.sibling
                    ).wait_recv()

            pl.when(jnp.logical_not((d == source) & (s == half)))(arrive)


def backward(n_dp, tok_rows, keep, gains, router, bias, grad, x, saved):
    width = x.shape[2]
    held, _, spare = token_layout(tok_rows)
    quarter_rows = width // 4
    half_rows = quarter_rows // 2
    in_kernel_z = n_dp == 4
    steps = 3 + n_dp - 1
    any_spec = pl.BlockSpec(memory_space=pl.ANY)
    vmem = pl.BlockSpec(memory_space=pltpu.VMEM)
    dma = pltpu.SemaphoreType.DMA

    def low(*shape):
        return pltpu.VMEM(shape, BF16)

    def wide(*shape):
        return pltpu.VMEM(shape, F32)

    mlp_shape = (2, 4, quarter_rows, width) if in_kernel_z else (UNITS, quarter_rows, width)
    units = 2 * UNITS
    scratch = [
        low(ROWS, width), low(ROWS, width), wide(ROWS, width), low(2, ROWS, width), wide(3, 8, width),
        wide(4, 8, width), wide(steps, 8, width), wide(2, ROWS, ROWS),
        low(3, width, width), low(width, width), low(2, width, width), low(2, width, width),
        low(ROWS, width), low(3, ROWS, width), low(ROWS, width), wide(ROWS, width), low(ROWS, width),
        low(4, ROWS, width), low(2, ROWS, width),
        wide(ROWS, width), low(ROWS, width), low(width, ROWS), wide(ROWS, width), low(4, ROWS, width),
        wide(ROWS, width), low(ROWS, width), low(ROWS, width), low(3, ROWS, width),
        low(RING, 4, quarter_rows, width), low(SIBS, 4, half_rows, width), low(NEARS, 2, half_rows, width),
        low(FARS, half_rows, width), low(PLANES, half_rows, width),
        low(len(Z_FIRST), 4, half_rows // 2, width),
        dma((2, 11)), dma((2, 2)), dma((2, 2)), dma((2, 2)),
        dma((units,)), dma((units,)), dma((units, 2)), dma((units, 2)), dma((units,)), dma((units,)),
        dma((units,)), dma((UNITS, 4, 2)), dma((2, 4, 4)), dma((4, 4, 2)), dma((units, 4)),
        dma((steps,)), dma((steps,)), dma((len(Z_FIRST),)), dma((len(Z_FIRST),)), *[sem for _ in range(4) for sem in hand_back_sems()],
    ]
    return pl.pallas_call(
        functools.partial(backward_kernel, in_kernel_z, tok_rows),
        out_shape=[
            jax.ShapeDtypeStruct((8, width), F32),
            jax.ShapeDtypeStruct((2, held, width), BF16),
            jax.ShapeDtypeStruct((2, spare, width), BF16),
            jax.ShapeDtypeStruct((2, held, width), BF16),
            jax.ShapeDtypeStruct((2, spare, width), BF16),
            jax.ShapeDtypeStruct(mlp_shape, BF16),
            jax.ShapeDtypeStruct((4, 4, quarter_rows, 2 * LANES), BF16),
        ],
        in_specs=[vmem] * 3 + [any_spec] * 15,
        out_specs=[vmem] + [any_spec] * 6,
        scratch_shapes=scratch,
        compiler_params=pltpu.CompilerParams(
            collective_id=1, has_side_effects=True, vmem_limit_bytes=VMEM_BYTES
        ),
        cost_estimate=pl.CostEstimate(flops=96 * ROWS * width * width, bytes_accessed=120_000_000, transcendentals=0),
        name="backward_layers",
    )(keep, gains, router, bias, grad, x, *saved)


def finish_kernel(
    tok_rows, sums,
    small_ref, y_main, y_back, dx_main, dx_back, mlp_in, att_in,
    y_out, dx_out, ones_out, twos_out, router_out, *rest,
):
    if sums:
        (down_out, up_out, out_out, qkv_out, *rest) = rest
    y_rows, y_tail, dx_rows, dx_tail, y_buf, dx_buf, mlp, att, mlp_sum, att_sum, in_sem, out_sem = rest
    held, low, spare = token_layout(tok_rows)
    section, d, t = lax.axis_index("section"), lax.axis_index("dp"), lax.axis_index("tensor")
    n_dp, quarters = lax.axis_size("dp"), lax.axis_size("tensor")
    x_half = t % 2
    moves = [(dx_main, dx_rows), (dx_back, dx_tail), (y_main, y_rows), (y_back, y_tail)]
    if sums:
        moves += [(mlp_in.at[0], mlp.at[0]), (mlp_in.at[1], mlp.at[1]), (att_in, att)]
    copies = [pltpu.make_async_copy(src, dst, in_sem.at[i]) for i, (src, dst) in enumerate(moves)]
    for copy in copies:
        copy.start()
    results = []

    def give(src, dst):
        copy = pltpu.make_async_copy(src, dst, out_sem.at[len(results)])
        copy.start()
        results.append(copy)

    def join(main, back, buffer, out):
        def plain(i, carry):
            rows = pl.ds(pl.multiple_of(i * 16, 16), 16)
            for m in range(2):
                buffer[rows, m, :] = main[m, rows, :].astype(buffer.dtype)
            return carry

        def mixed_rows(i, carry):
            rows = pl.ds(pl.multiple_of(i * 16, 16), 16)
            from_back = pl.ds(pl.multiple_of(i * 16 - low, 16), 16)
            row = lax.broadcasted_iota(jnp.int32, (16, 1), 0) + i * 16
            is_back = (x_half == 0) & (row >= CUT)
            for m in range(2):
                value = jnp.where(is_back, back[m, from_back, :], main[m, rows, :])
                buffer[rows, m, :] = value.astype(buffer.dtype)
            return carry

        lax.fori_loop(0, low // 16, plain, 0)
        lax.fori_loop(low // 16, held // 16, mixed_rows, 0)
        give(buffer.at[pl.ds(0, tok_rows)], out)

    for i, pieces in enumerate(((dx_rows, dx_tail, dx_buf, dx_out), (y_rows, y_tail, y_buf, y_out))):
        copies[2 * i].wait()
        copies[2 * i + 1].wait()
        join(*pieces)
    if sums:
        width = mlp_sum.shape[1]
        for kind in range(2):
            copies[4 + kind].wait()

            first_z = comes_first_z(section, d, kind)

            def add(rows):
                odd = rows.start // (width // 4) % 2
                parts = [
                    only(jnp.logical_not(first_z) | (odd == source % 2), mlp[kind, source, rows, :]).astype(F32)
                    for source in range(4)
                ]
                mlp_sum[kind, rows, :] = parts[0] + parts[1] + parts[2] + parts[3]

            tiles(add, rows=width, tile=16)
            give(mlp_sum.at[kind], (down_out, up_out)[kind])
        copies[6].wait()
        for b in range(4):
            total = att[b, 0].astype(F32) + att[b, 1].astype(F32) + att[b, 2].astype(F32) + att[b, 3].astype(F32)
            total = jnp.where(d % 2 == 0, total[:, :width], total[:, -width:])
            att_sum[b] = total if b == 0 else total.T
            give(att_sum.at[b], out_out if b == 0 else qkv_out.at[b - 1])

    columns = small_ref[...].T
    place = d * quarters + t

    def pick(values, start, count):
        row = lax.broadcasted_iota(jnp.int32, (columns.shape[0], count), 0)
        lane = lax.broadcasted_iota(jnp.int32, (columns.shape[0], count), 1)
        return jnp.sum(jnp.where(row == start + lane, values, 0.0), axis=0, keepdims=True)

    span = ones_out.shape[1]
    ones_out[...] = pick(jnp.where(section == 0, columns[:, 0:1], columns[:, 3:4]), place * span, span)
    twos_out[...] = pick(jnp.where(section == 0, columns[:, 1:2], columns[:, 4:5]), place * span, span)
    span = router_out.shape[1]
    router_out[...] = pick(columns[:, 2:3], (section * n_dp * quarters + place) * span, span)
    for copy in results:
        copy.wait()


def finish(tok_rows, n_dp, quarters, small, y_main, y_back, dx_main, dx_back, mlp, att):
    width = small.shape[1]
    held, _, spare = token_layout(tok_rows)
    part = width // 4
    span = width // (n_dp * quarters)
    sums = n_dp == 4
    any_spec = pl.BlockSpec(memory_space=pl.ANY)
    vmem = pl.BlockSpec(memory_space=pltpu.VMEM)
    shapes = [
        jax.ShapeDtypeStruct((tok_rows, 2, width), BF16), jax.ShapeDtypeStruct((tok_rows, 2, width), F32),
        jax.ShapeDtypeStruct((1, span), F32), jax.ShapeDtypeStruct((1, span), F32),
        jax.ShapeDtypeStruct((1, span // 2), F32),
    ]
    specs = [any_spec, any_spec, vmem, vmem, vmem]
    if sums:
        shapes += [jax.ShapeDtypeStruct(shape, F32) for shape in ((part, width), (part, width), (part, part), (3, part, part))]
        specs += [any_spec] * 4
    dma = pltpu.SemaphoreType.DMA
    return pl.pallas_call(
        functools.partial(finish_kernel, tok_rows, sums),
        out_shape=shapes,
        in_specs=[vmem] + [any_spec] * 6,
        out_specs=specs,
        scratch_shapes=[
            pltpu.VMEM((2, held, width), BF16), pltpu.VMEM((2, spare, width), BF16),
            pltpu.VMEM((2, held, width), BF16), pltpu.VMEM((2, spare, width), BF16),
            pltpu.VMEM((held, 2, width), BF16), pltpu.VMEM((held, 2, width), F32),
            pltpu.VMEM((2, 4, part, width), BF16), pltpu.VMEM((4, 4, part, 2 * LANES), BF16),
            pltpu.VMEM((2, part, width), F32), pltpu.VMEM((4, part, part), F32), dma((7,)), dma((8,)),
        ],
        compiler_params=pltpu.CompilerParams(vmem_limit_bytes=VMEM_BYTES),
        cost_estimate=pl.CostEstimate(flops=4_000_000, bytes_accessed=12_000_000, transcendentals=0),
        name="finish",
    )(small, y_main, y_back, dx_main, dx_back, mlp, att)


def on_device(
    patches, cotangent, crop_lengths, route_mask, w_qkv, w_out, w_up, w_down, ln1_gain, ln2_gain, router
):
    tok_rows, width = patches.shape[1:]
    n_dp, quarters = lax.axis_size("dp"), lax.axis_size("tensor")
    wq = jnp.transpose(w_qkv[0], (1, 2, 0))
    x, gains, keep_rows, router_row, bias, grad, *saved = forward(
        crop_lengths, route_mask, ln1_gain, ln2_gain, router, jnp.transpose(patches, (1, 0, 2)),
        jnp.transpose(cotangent, (1, 0, 2)), wq, w_out[0], w_up[0], w_down[0],
    )
    small, y_main, y_back, dx_main, dx_back, mlp, att = backward(
        n_dp, tok_rows, keep_rows, gains, router_row, bias, grad, x, saved
    )

    y_out, dx_out, ones, twos, routers, *grads = finish(
        tok_rows, n_dp, quarters, small, y_main, y_back, dx_main, dx_back, mlp, att
    )
    outputs = jnp.transpose(y_out, (1, 0, 2))
    input_grads = jnp.transpose(dx_out, (1, 0, 2))
    if n_dp == 4:
        down, up, out, qkv = grads
    else:

        def scatter(value, dim):
            return lax.psum_scatter(value, "dp", scatter_dimension=dim, tiled=True).astype(F32)

        down = scatter(mlp[:4].reshape(width, width), 0)
        up = scatter(mlp[4:8].reshape(width, width), 0)
        out = scatter(mlp[8], 1)
        qkv = jnp.transpose(scatter(mlp[9:], 2), (0, 2, 1))
    qkv = jnp.transpose(qkv, (1, 0, 2))
    return (
        outputs[None], input_grads[None], qkv[None], out[None], up[None], down.T[None], ones, twos, routers[0],
    )


def solution(mesh):
    return jax.shard_map(
        on_device,
        mesh=mesh,
        in_specs=(
            P(None, ("dp", "tensor"), None),
            P(None, ("dp", "tensor"), None),
            P(None, "dp", None),
            P(None, "dp"),
            P("section", None, None, "tensor"),
            P("section", "tensor", None),
            P("section", None, "tensor"),
            P("section", "tensor", None),
            P("section", None),
            P("section", None),
            P(),
        ),
        out_specs=(
            P("section", None, ("dp", "tensor"), None),
            P("section", None, ("dp", "tensor"), None),
            P("section", "dp", None, "tensor"),
            P("section", "tensor", "dp"),
            P("section", "dp", "tensor"),
            P("section", "tensor", "dp"),
            P("section", ("dp", "tensor")),
            P("section", ("dp", "tensor")),
            P(("section", "dp", "tensor")),
        ),
        check_vma=False,
    )
```

```python
import functools

import jax
import jax.numpy as jnp
from jax import lax
from jax.experimental import pallas as pl
from jax.experimental.pallas import tpu as pltpu
from jax.sharding import PartitionSpec as P

HEAD_DIM = 64
LANES = 128
CUT = 197
EPS = 1e-06
NEG = -1000000000.0
ROWS = 384
TILE = 64
MESH = pl.DeviceIdType.MESH
NT = (((1,), (1,)), ((), ()))
TN = (((0,), (0,)), ((), ()))
NN = (((1,), (0,)), ((), ()))
VMEM_BYTES = 62 * 1024 * 1024
F32, BF16 = jnp.float32, jnp.bfloat16


def dot(left, right, dims=NN):
    return lax.dot_general(left, right, dims, preferred_element_type=F32)


def tiles(body, rows=ROWS, tile=TILE):
    def step(index, carry):
        body(pl.ds(pl.multiple_of(index * tile, tile), tile))
        return carry

    lax.fori_loop(0, rows // tile, step, 0)


def standardize(values):
    centre = values - jnp.mean(values, axis=-1, keepdims=True)
    spread = jnp.mean(centre * centre, axis=-1, keepdims=True)
    rstd = lax.rsqrt(spread + EPS)
    return centre * rstd, rstd


def norm_pull(xhat, rstd, gain, grad):
    grad_hat = grad * gain
    mean_grad = jnp.mean(grad_hat, axis=-1, keepdims=True)
    mean_both = jnp.mean(grad_hat * xhat, axis=-1, keepdims=True)
    return rstd * (grad_hat - mean_grad - xhat * mean_both)


def fold_rows(values):
    return jnp.sum(values.reshape(values.shape[0] // 8, 8, values.shape[1]), axis=0)


def half_masks():
    lane = lax.broadcasted_iota(jnp.int32, (1, LANES), 1)
    return [lane < HEAD_DIM, lane >= HEAD_DIM]


def softmax_parts(scores):
    expo = jnp.exp(scores - jnp.max(scores, axis=-1, keepdims=True))
    return expo, 1.0 / jnp.sum(expo, axis=-1, keepdims=True)


def valid_rows(x_half, tok_rows, row):
    held, low, _ = token_layout(tok_rows)
    rest = (row < tok_rows) | ((row >= held + CUT - low) & (row < held + tok_rows - low))
    return ((x_half == 0) & (row < CUT)) | ((x_half == 1) & rest)


def only(mask, values):
    return jnp.where(mask, values, jnp.zeros_like(values))


def token_layout(tok_rows):
    held = -(-tok_rows // 16) * 16
    low = CUT // 16 * 16
    return held, low, held - low


def transpose_into(src, dst):
    def step(index, carry):
        cols = pl.ds(pl.multiple_of(index * LANES, LANES), LANES)
        dst[cols, :] = src[:, cols].astype(F32).T.astype(BF16)
        return carry

    lax.fori_loop(0, dst.shape[0] // LANES, step, 0)


class Place:
    def __init__(self):
        self.s = lax.axis_index("section")
        self.d = lax.axis_index("dp")
        self.t = lax.axis_index("tensor")
        self.x = self.t % 2
        self.y = self.t // 2
        self.near = self.t + (1 - self.s) * (1 - 2 * self.x) + self.s * (2 - 4 * self.y)
        self.far = self.t + self.s * (1 - 2 * self.x) + (1 - self.s) * (2 - 4 * self.y)
        self.cross = 3 - self.t
        self.beside = self.t + 1 - 2 * self.x
        self.above = self.t + 2 - 4 * self.y
        self.sibling = (1 - self.s, self.d, self.t)
        self.diagonal = (1 - self.s, self.d, self.beside)

    def at(self, tensor):
        return (self.s, self.d, tensor)


def remote(src, dst, send, recv, device):
    return pltpu.make_async_remote_copy(
        src_ref=src, dst_ref=dst, send_sem=send, recv_sem=recv, device_id=device, device_id_type=MESH
    )


def greet(peers):
    barrier = pltpu.get_barrier_semaphore()
    for peer in peers:
        pl.semaphore_signal(barrier, inc=1, device_id=peer, device_id_type=MESH)
    pl.semaphore_wait(barrier, len(peers))


class HandBack:
    def __init__(self, here, layer, tok_rows, rows_ref, main_out, back_out, sems):
        held, _, spare = token_layout(tok_rows)
        main_send, main_recv, back_send, back_recv, own = sems
        self.here, self.layer = here, layer
        main, back = rows_ref.at[pl.ds(0, held)], rows_ref.at[pl.ds(held, spare)]
        s = here.s
        self.local = pltpu.make_async_copy(main, main_out.at[s], own)
        self.away = remote(main, main_out.at[s], main_send, main_recv, here.sibling)
        self.backs = [
            remote(back, back_out.at[s], back_send, back_recv.at[s], (layer, here.d, here.beside)),
        ]
        self.landing = [
            remote(back, back_out.at[i], back_send, back_recv.at[i], here.sibling) for i in range(2)
        ]

    def start(self):
        mine = self.here.s == self.layer
        pl.when(mine)(self.local.start)
        pl.when(jnp.logical_not(mine))(self.away.start)

    def start_back(self):
        pl.when(self.here.x == 1)(self.backs[0].start)

    def wait(self):
        mine = self.here.s == self.layer

        @pl.when(mine)
        def _():
            self.local.wait()
            self.away.wait_recv()

            @pl.when(self.here.x == 0)
            def _():
                for landing in self.landing:
                    landing.wait_recv()

        pl.when(jnp.logical_not(mine))(self.away.wait_send)
        pl.when(self.here.x == 1)(self.backs[0].wait_send)


def hand_back_sems():
    dma = pltpu.SemaphoreType.DMA
    return [dma, dma, dma, dma((2,)), dma]


KINDS = 4
FIRST_PLAN = [
    (0, 0, False), (0, 1, True), (1, 0, False), (2, 0, True), (2, 2, True), (3, 0, True), (3, 2, False), (3, 3, False)
]
SECOND_PLAN = [
    (0, 0, False), (0, 1, True), (1, 0, False), (2, 0, True), (2, 2, True),
    (3, 0, False), (3, 1, False), (3, 2, False), (3, 3, False),
]
PLAN = [(0, *step) for step in FIRST_PLAN] + [(1, *step) for step in SECOND_PLAN]
STARTS = (0, len(FIRST_PLAN))
WINDOW = 2


def forward_kernel(
    tok_rows,
    crop_ref, route_ref, one_ref, two_ref, router_in, patch_ref, cotangent_ref, wq_ref, wo_ref, wu_ref, wd_ref,
    x_out, gain_out, keep_out, router_out, bias_out, grad_out,
    gq_out, go_out, gu_out, gd_out, norm_out, qkv_out, mixed_out, hidden_out,
    second_out, active_out, slope_out, branch_out,
    x_own, gain_ref, my_gain, keep_ref, router_ref, bias_ref, tokens, spare_rows, grad_own,
    gq, go, gu, gd, normed, qkv, mixed, hidden, second, active, slope, branch, work,
    own_sem, lend_send, lend_recv, a_send, a_recv, b_send, b_recv, c_send, c_recv,
    e_send, e_recv, f_send, f_recv, out_sem, save_sem, tok_sem, tok_send, tok_recv, gain_sem, gain_send, gain_recv, x_sem, bias_sem,
):
    here = Place()
    held, low, spare = token_layout(tok_rows)
    part = wo_ref.shape[0]
    unit = part // 2
    shards = (wq_ref, wo_ref, wu_ref, wd_ref)

    def block(kind, layer, quarter):
        rows = pl.ds(pl.multiple_of(quarter * part, part), part)
        if kind == 0:
            return gq.at[layer, :, rows, :]
        if kind == 1:
            return go.at[layer, rows, :]
        return (gu if kind == 2 else gd).at[layer, quarter]

    parity = here.d % 2

    def chunk(step, quarter, half, other=0):
        layer, kind, piece, shared = PLAN[step]
        if shared:
            piece = piece + other + (1 - 2 * other) * parity
        if kind < 2:
            rows = pl.ds(pl.multiple_of(quarter * part + half * unit, unit), unit)
            return gq.at[layer, piece, rows, :] if kind == 0 else go.at[layer, rows, :]
        rows = pl.ds(pl.multiple_of((4 * half + piece) * unit, unit), unit)
        return (gu if kind == 2 else gd).at[layer, quarter, rows, :]

    def own_copy(kind):
        return pltpu.make_async_copy(shards[kind], block(kind, here.s, here.t), own_sem.at[kind])

    def lend(kind, layer):
        return remote(
            shards[kind], block(kind, layer, here.t), lend_send.at[kind], lend_recv.at[kind], here.sibling
        )

    def along(step, quarter, peer, send, recv):
        piece = chunk(step, quarter, here.s)
        return remote(piece, piece, send.at[step], recv.at[step], peer)

    def send_a(step):
        return along(step, here.t, here.at(here.near), a_send, a_recv)

    def send_b(step):
        return along(step, here.t, here.at(here.far), b_send, b_recv)

    def send_c(step):
        return along(step, here.near, here.at(here.far), c_send, c_recv)

    def send_e(step, which, half=None, other=0):
        piece = chunk(step, three[which], here.s if half is None else half, other)
        index = which + 3 * other
        return remote(piece, piece, e_send.at[step, index], e_recv.at[step, index], here.sibling)

    def send_f(step, which, other=0):
        piece = chunk(step, three[which], here.s, other)
        return remote(piece, piece, f_send.at[step, which], f_recv.at[step, which], z_beside)

    three = (here.near, here.far, here.cross)
    z_beside = (here.s, here.d + 1 - 2 * parity, here.t)
    total = len(PLAN)

    greet([here.sibling, here.at(here.near), here.at(here.far), z_beside])

    lend(0, here.s).start()
    own_copy(0).start()
    my_gain[...] = jnp.zeros_like(my_gain)
    my_gain[0:1, :] = one_ref[...]
    my_gain[1:2, :] = two_ref[...]
    gain_own = pltpu.make_async_copy(my_gain, gain_ref.at[here.s], gain_sem)
    gain_away = remote(my_gain, gain_ref.at[here.s], gain_send, gain_recv, here.sibling)
    token_loads = []
    for which, source in enumerate((patch_ref, cotangent_ref)):
        tokens[which, pl.ds(tok_rows, held - tok_rows)] = jnp.zeros((held - tok_rows, *tokens.shape[2:]), BF16)
        token_loads.append(
            pltpu.make_async_copy(source, tokens.at[which, pl.ds(0, tok_rows)], tok_sem.at[which])
        )
    tok_away = [
        remote(src, dst.at[pl.ds(held, spare)], tok_send.at[i], tok_recv.at[i], here.at(here.beside))
        for i, (src, dst) in enumerate(((spare_rows, x_own.at[0]), (grad_own.at[pl.ds(low, spare)], grad_out)))
    ]
    grad_save = pltpu.make_async_copy(grad_own, grad_out.at[pl.ds(0, held)], tok_sem.at[2])
    for copy in token_loads:
        copy.start()
    gain_own.start()
    gain_away.start()

    def issue(step):
        if step >= total:
            return
        layer, kind, piece, _ = PLAN[step]
        if piece == 0:
            pl.when(here.s == layer)(lambda: own_copy(kind).wait())
            pl.when(here.s != layer)(lambda: lend(kind, layer).wait_recv())
        send_a(step).start()
        send_b(step).start()

    def pass_on(step, which):
        send_e(step, which).start()
        if PLAN[step][3]:
            send_f(step, which).start()

    def relay(step):
        if step >= total:
            return
        send_a(step).wait_recv()
        send_c(step).start()
        pass_on(step, 0)
        issue(step + WINDOW)

    def fetch(step):
        if step >= total:
            return
        send_b(step).wait_recv()
        pass_on(step, 1)
        send_c(step).wait_recv()
        pass_on(step, 2)

    moved = [0]
    relayed = [0]

    def relays(upto):
        while relayed[0] < min(upto, total):
            relay(relayed[0])
            relayed[0] += 1

    def tick(upto):
        while moved[0] <= min(upto, total - 1):
            relays(moved[0] + 3)
            fetch(moved[0])
            moved[0] += 1

    def pump(step):
        tick(step + 2)
        shared = PLAN[step][3]
        if shared:
            for which in range(3):
                send_f(step, which, 1).wait_recv()
                send_e(step, which, None, 1).start()
        for other in range(1 + shared):
            for which in range(3):
                send_e(step, which, 1 - here.s, other).wait_recv()

    for step in range(WINDOW):
        issue(step)
    for kind in range(1, KINDS):
        lend(kind, here.s).start()
        own_copy(kind).start()
    def take(which, dst):
        def step(rows):
            dst[rows, :] = jnp.where(here.s == 0, tokens[which, rows, 0, :], tokens[which, rows, 1, :])

        tiles(step, rows=held, tile=16)

    for copy in token_loads:
        copy.wait()
    take(0, x_own.at[0])
    spare_rows[...] = x_own[0, pl.ds(low, spare), :]
    pl.when(here.x == 0)(tok_away[0].start)
    take(1, grad_own)
    pl.when(here.x == 0)(tok_away[1].start)
    grad_save.start()
    router_ref[...] = router_in[...].astype(F32).reshape(router_ref.shape)
    router_out[...] = router_ref[...]

    relays(1)

    image = here.t // 2
    slot_len = route_ref.shape[1] // crop_ref.shape[1]
    routes = jnp.where(here.s == 0, route_ref[0:1, :], route_ref[1:2, :]).astype(F32)
    lanes = -(-(routes.shape[1] + ROWS) // LANES) * LANES
    routes = jnp.concatenate([routes, jnp.zeros((1, lanes - routes.shape[1]), F32)], axis=1)
    routes = jnp.broadcast_to(routes, (8, lanes))

    def routed_from(start):
        return pltpu.roll(routes, (2 * lanes - start) % lanes, 1)[0:1, :ROWS]

    def rows_info(row):
        valid = valid_rows(here.x, tok_rows, row)
        position = jnp.where(row < held, here.x * tok_rows + row, low - held + row)
        position = jnp.where(here.x == 0, row, position)
        crop = jnp.zeros_like(row)
        end = 0
        for i in range(crop_ref.shape[2]):
            end = end + crop_ref[here.s, image, i]
            crop += (position >= end).astype(jnp.int32)
        return valid, jnp.where(valid, crop, -1)

    across = lax.broadcasted_iota(jnp.int32, (1, ROWS), 1)
    valid, crop_across = rows_info(across)
    routed = jnp.where(
        across < held,
        routed_from(image * slot_len + here.x * tok_rows),
        routed_from(image * slot_len + low - held),
    )
    routed = jnp.where(valid, routed, 0.0)
    keep_ref[...] = jnp.broadcast_to(routed, (LANES, ROWS)).T[:, 0:1]
    keep_out[...] = keep_ref[...]
    usable = jnp.where(valid, routed, 1.0) > 0.0

    def allow(rows):
        _, crop_down = rows_info(lax.broadcasted_iota(jnp.int32, (TILE, 1), 0) + rows.start)
        same = crop_down == crop_across
        bias_ref[0, rows, :] = jnp.where(same & usable, 0.0, NEG)
        bias_ref[1, rows, :] = jnp.where(same, 0.0, NEG)

    tiles(allow)
    bias_save = pltpu.make_async_copy(bias_ref, bias_out, bias_sem)
    bias_save.start()
    relays(2)

    pl.when(here.x == 1)(tok_away[0].wait_recv)

    def clear(block):
        def step(rows):
            row = lax.broadcasted_iota(jnp.int32, (TILE, 1), 0) + rows.start
            block[rows, :] = only(valid_rows(here.x, tok_rows, row), block[rows, :])

        tiles(step)

    clear(x_own.at[0])
    x_saves = [pltpu.make_async_copy(x_own.at[i], x_out.at[i], x_sem.at[i]) for i in range(3)]
    x_saves[0].start()
    gain_own.wait()
    gain_away.wait_recv()
    gain_out[...] = gain_ref[...]
    masks = half_masks()
    saves = []

    def weight_save(kind, layer):
        src, dst = ((gq, gq_out), (go, go_out), (gu, gu_out), (gd, gd_out))[kind]
        return pltpu.make_async_copy(src.at[layer], dst.at[layer], out_sem.at[layer, kind])

    def keep_weight(kind, layer):
        weight_save(kind, layer).start()

    def save(index, layer, src, dst):
        copy = pltpu.make_async_copy(src, dst.at[layer], save_sem.at[index])
        copy.start()
        return copy

    for layer in range(2):
        x_now = x_own.at[layer]

        def first_norm(rows):
            xhat, _ = standardize(x_now[rows, :].astype(F32))
            normed[rows, :] = (xhat * gain_ref[layer, 0:1, :]).astype(BF16)

        for copy in saves:
            copy.wait()
        saves = []
        tiles(first_norm)
        saves.append(save(0, layer, normed, norm_out))
        base = STARTS[layer]
        pump(base)
        qkv[0] = dot(normed[...], gq[layer, 0], NT).astype(BF16)
        pump(base + 1)
        keep_weight(0, layer)

        def project(j, carry):
            qkv[j] = dot(normed[...], gq[layer, j], NT).astype(BF16)
            return carry

        lax.fori_loop(1, 3, project, 0)
        saves.append(save(1, layer, qkv, qkv_out))

        def attend(pair, carry):
            cols = pl.ds(pl.multiple_of(pair * LANES, LANES), LANES)
            key, value = qkv[1, :, cols], qkv[2, :, cols]
            query = qkv[0, :, cols] * BF16(0.125)
            outs = []
            for mask in masks:
                expo, inverse = softmax_parts(dot(only(mask, query), key, NT) + bias_ref[layer])
                outs.append(dot(expo.astype(BF16), value) * inverse)
            mixed[:, cols] = jnp.where(masks[0], outs[0], outs[1]).astype(BF16)
            return carry

        pairs = mixed.shape[1] // LANES
        for part_of in range(3):
            lax.fori_loop(pairs * part_of // 3, pairs * (part_of + 1) // 3, attend, 0)
            tick(base + 3 + part_of)
        saves.append(save(2, layer, mixed, mixed_out))
        pump(base + 2)
        keep_weight(1, layer)
        branch[...] = dot(mixed[...], go[layer])

        def second_norm(rows):
            value = x_now[rows, :].astype(F32) + branch[rows, :]
            hidden[rows, :] = value
            xhat, _ = standardize(value)
            second[rows, :] = (xhat * gain_ref[layer, 1:2, :]).astype(BF16)

        tiles(second_norm)
        saves.append(save(3, layer, hidden, hidden_out))
        saves.append(save(4, layer, second, second_out))
        pump(base + 3)
        pump(base + 4)
        keep_weight(2, layer)

        def widen(g, carry):
            work[...] = dot(second[...], gu[layer, g])

            def bend(rows):
                upper = work[rows, :]
                phi = 0.5 * (1.0 + lax.erf(upper * 0.7071067811865476))
                bell = jnp.exp(-0.5 * upper * upper) * 0.3989422804014327
                active[g, rows, :] = (upper * phi).astype(BF16)
                slope[g, rows, :] = (phi + upper * bell).astype(BF16)

            tiles(bend, tile=32)
            return carry

        for g in range(4):
            widen(g, 0)
            tick(base + 6 + g)
        saves.append(save(5, layer, active, active_out))
        saves.append(save(6, layer, slope, slope_out))
        for step in range(base + 5, (*STARTS, total)[layer + 1]):
            pump(step)
        keep_weight(3, layer)

        def narrow(g, carry):
            branch[...] += dot(active[g], gd[layer, g])
            return carry

        for g in range(4):
            narrow(g, 0)
            tick((*STARTS, total)[layer + 1] + g // 2)
        if layer == 0:
            saves.append(save(7, layer, branch, branch_out))

        def finish(rows):
            value = x_now[rows, :].astype(F32)
            change = branch[rows, :]
            if layer == 0:
                logit = jnp.sum(value * router_ref[...], axis=-1, keepdims=True)
                change = change * (keep_ref[rows, :] / (1.0 + jnp.exp(-logit)))
            x_own[layer + 1, rows, :] = (value + change).astype(BF16)

        tiles(finish)
        x_saves[layer + 1].start()

    for copy in [*saves, *x_saves, grad_save, bias_save]:
        copy.wait()
    gain_away.wait_send()

    @pl.when(here.x == 0)
    def _():
        for away in tok_away:
            away.wait_send()

    pl.when(here.x == 1)(tok_away[1].wait_recv)
    for layer in range(2):
        for kind in range(KINDS):
            weight_save(kind, layer).wait()
    for kind in range(KINDS):
        lend(kind, here.s).wait_send()
    for step in range(total):
        send_a(step).wait_send()
        send_b(step).wait_send()
        send_c(step).wait_send()
        shared = PLAN[step][3]
        for which in range(3):
            send_e(step, which).wait_send()
            if shared:
                send_f(step, which).wait_send()
                send_e(step, which, None, 1).wait_send()


def forward(crops, routes, one, two, router, patches, cotangent, wq, wo, wu, wd):
    tok_rows, _, width = patches.shape
    held, _, spare = token_layout(tok_rows)
    any_spec = pl.BlockSpec(memory_space=pl.ANY)
    vmem = pl.BlockSpec(memory_space=pltpu.VMEM)

    def pair(*shape, dtype=BF16):
        return jax.ShapeDtypeStruct((2, *shape), dtype)

    shapes = [
        jax.ShapeDtypeStruct((3, ROWS, width), BF16), pair(8, width, dtype=F32),
        jax.ShapeDtypeStruct((ROWS, 1), F32), jax.ShapeDtypeStruct((1, width), F32), pair(ROWS, ROWS, dtype=F32),
        jax.ShapeDtypeStruct((ROWS, width), BF16),
        pair(3, width, width), pair(width, width), pair(4, width, width), pair(4, width, width),
        pair(ROWS, width), pair(3, ROWS, width), pair(ROWS, width), pair(ROWS, width, dtype=F32),
        pair(ROWS, width), pair(4, ROWS, width), pair(4, ROWS, width), pair(ROWS, width, dtype=F32),
    ]
    dma = pltpu.SemaphoreType.DMA
    scratch = [
        pltpu.VMEM((3, ROWS, width), BF16), pltpu.VMEM((2, 8, width), F32), pltpu.VMEM((8, width), F32),
        pltpu.VMEM((ROWS, 1), F32), pltpu.VMEM((1, width), F32), pltpu.VMEM((2, ROWS, ROWS), F32),
        pltpu.VMEM((2, held, 2, width), BF16), pltpu.VMEM((spare, width), BF16), pltpu.VMEM((held, width), BF16),
        pltpu.VMEM((2, 3, width, width), BF16), pltpu.VMEM((2, width, width), BF16),
        pltpu.VMEM((2, 4, width, width), BF16), pltpu.VMEM((2, 4, width, width), BF16),
        pltpu.VMEM((ROWS, width), BF16), pltpu.VMEM((3, ROWS, width), BF16),
        pltpu.VMEM((ROWS, width), BF16), pltpu.VMEM((ROWS, width), F32),
        pltpu.VMEM((ROWS, width), BF16), pltpu.VMEM((4, ROWS, width), BF16),
        pltpu.VMEM((4, ROWS, width), BF16), pltpu.VMEM((ROWS, width), F32),
        pltpu.VMEM((ROWS, width), F32),
        dma((KINDS,)), dma((KINDS,)), dma((KINDS,)),
        *[dma((len(PLAN),))] * 6, *[dma((len(PLAN), 6))] * 2, *[dma((len(PLAN), 3))] * 2,
        dma((2, KINDS)), dma((8,)),
        dma((3,)), dma((2,)), dma((2,)), dma, dma, dma, dma((3,)), dma,
    ]
    return pl.pallas_call(
        functools.partial(forward_kernel, tok_rows),
        out_shape=shapes,
        in_specs=[pl.BlockSpec(memory_space=pltpu.SMEM)] + [vmem] * 4 + [any_spec] * 6,
        out_specs=[any_spec, vmem, vmem, vmem] + [any_spec] * 14,
        scratch_shapes=scratch,
        compiler_params=pltpu.CompilerParams(
            collective_id=0, has_side_effects=True, vmem_limit_bytes=VMEM_BYTES
        ),
        cost_estimate=pl.CostEstimate(flops=24 * ROWS * width * width * 2, bytes_accessed=60_000_000, transcendentals=0),
        name="forward_layers",
    )(crops, routes, one, two, router, patches, cotangent, wq, wo, wu, wd)


UNITS = 12
RING = 7
EARLY_BACKS = 2
TOTALS = (3, 6, 9)
SIBS, NEARS, FARS, PLANES = 8, 12, 10, 8
Z_FIRST = (5,17)
ORDER = sorted(range(2 * UNITS), key=lambda u: u + 2.5 if u in Z_FIRST else u)
SCHEDULE = [
    (0, 0, 0, 0), (0, 0, 0, 0), (0, 0, 0, 0), (0, 0, 0, 0), (0, 0, 0, 0), (0, 0, 0, 0), (1, 0, 0, 0),
    (1, 0, 0, 0), (2, 0, 0, 0), (2, 0, 0, 0), (2, 0, 0, 0), (3, 0, 1, 0), (3, 0, 1, 0), (3, 0, 1, 0),
    (4, 0, 2, 0), (4, 0, 2, 0), (4, 0, 2, 0), (4, 0, 3, 0), (5, 0, 3, 1), (5, 0, 4, 1), (7, 0, 4, 3),
    (7, 0, 4, 3), (8, 0, 5, 3), (9, 0, 5, 4), (9, 1, 6, 5), (9, 1, 6, 5), (9, 1, 7, 5), (9, 1, 7, 5),
    (10, 1, 7, 5), (10, 1, 7, 5), (11, 1, 9, 6), (11, 1, 9, 6), (11, 1, 9, 7), (12, 1, 11, 9),
    (12, 1, 11, 9), (12, 1, 11, 9),
    (13, 1, 11, 10), (13, 1, 11, 10), (13, 1, 11, 11), (14, 1, 11, 11), (14, 1, 12, 11), (14, 1, 12, 11),
    (15, 1, 12, 11), (15, 1, 13, 11), (15, 1, 13, 11), (15, 1, 13, 11), (16, 1, 14, 11), (16, 1, 14, 11),
    (16, 1, 14, 12), (17, 1, 15, 13), (17, 1, 16, 13), (19, 1, 16, 15), (19, 1, 16, 15), (20, 1, 17, 15),
    (21, 1, 17, 16), (21, 2, 18, 17), (21, 2, 18, 17), (21, 2, 19, 17), (21, 2, 19, 17), (22, 2, 19, 17),
    (22, 2, 19, 17), (23, 2, 21, 18), (24, 2, 21, 18), (24, 2, 21, 19), (24, 2, 22, 19), (24, 2, 23, 19),
    (24, 2, 23, 20), (24, 2, 23, 21), (24, 2, 24, 21), (24, 2, 24, 22), (24, 2, 24, 23), (24, 2, 24, 24),
]


def comes_first_z(section, d, kind):
    units = [u for u in Z_FIRST if u % UNITS // 4 == kind]
    return functools.reduce(
        jnp.logical_or, [(section == 1 - u // UNITS) & (d == u % UNITS % 4) for u in units], section < 0
    )


def backward_kernel(
    in_kernel_z, tok_rows,
    keep_ref, gain_ref, router_ref, bias_in, grad_in, x_in,
    gq, go, gu, gd, norm_in, qkv_in, mixed_in, hidden_in, second_in, active_in, slope_in, branch_in,
    small_out, y_main, y_back, main_out, back_out, mlp_out, att_out,
    grad_ref, x_ref, dx_ref, dx_low, small_ref, tot, got, bias_ref,
    wq, wo, wu, wd, normed, qkv, mixed, hidden, second, active, slope,
    dbranch, dfed, dfed_t, work, dup, dsecond, datt, dmixed, dqkv, stage, sib, near_in, far_in, plane, mate_in,
    load_sem, wu_sem, wd_sem, slope_sem,
    sib_send, sib_recv, near_send, near_recv, far_send, far_recv,
    mlp_send, mlp_recv, att_send, att_recv, local_sem, tot_send, tot_recv, mate_send, mate_recv, *back_sems,
):
    here = Place()
    s, d, t = here.s, here.d, here.t
    quarter_rows = stage.shape[2]
    half_rows = quarter_rows // 2
    my_rows = pl.ds(pl.multiple_of(s * half_rows, half_rows), half_rows)
    their_rows = pl.ds(pl.multiple_of((1 - s) * half_rows, half_rows), half_rows)
    n_dp = lax.axis_size("dp")
    branch = dsecond

    saved = {
        "active": (active_in, active), "x": (x_in, x_ref), "second": (second_in, second),
        "hidden": (hidden_in, hidden), "mixed": (mixed_in, mixed), "wo": (go, wo), "qkv": (qkv_in, qkv),
        "normed": (norm_in, normed), "wq": (gq, wq), "branch": (branch_in, branch),
    }

    def load(name, layer):
        src, dst = saved[name]
        return pltpu.make_async_copy(src.at[layer], dst, load_sem.at[layer, list(saved).index(name)])

    def prefetch(name, layer):
        if layer == 1:
            load(name, 0).start()

    streams = ((gd, wd, wd_sem), (slope_in, slope, slope_sem), (gu, wu, wu_sem))

    def quarter_load(stream, layer, g):
        src, dst, sems = stream
        return pltpu.make_async_copy(src.at[layer, g], dst.at[g % 2], sems.at[layer, g % 2])

    load_grad = pltpu.make_async_copy(grad_in, grad_ref, load_sem.at[0, len(saved)])
    load_bias = pltpu.make_async_copy(bias_in, bias_ref, load_sem.at[1, len(saved)])
    load_grad.start()

    load("active", 1).start()
    for g in range(2):
        for stream in streams:
            quarter_load(stream, 1, g).start()
    for name in saved:
        if name not in ("active", "branch"):
            load(name, 1).start()
    load_bias.start()

    peers = [here.sibling, here.at(here.near), here.at(here.far), here.diagonal]
    doubled = [here.sibling, here.at(here.near), here.at(here.far)]
    along_z = [(s, (d + shift) % n_dp, t) for shift in range(1, n_dp)]
    peers += along_z
    if in_kernel_z:
        peers += [(1 - s, z, t) for _, z, _ in along_z]
    greet(peers)

    backs = []

    def hand_back(layer, rows_ref, main, back):
        sems = back_sems[5 * len(backs) : 5 * len(backs) + 5]
        backs.append(HandBack(here, layer, tok_rows, rows_ref, main, back, sems))
        backs[-1].start()
        if len(backs) <= EARLY_BACKS:
            backs[-1].start_back()

    for layer in range(2):
        hand_back(layer, x_in.at[layer + 1], y_main, y_back)

    def total_move(step):
        last = len(doubled)
        return remote(
            tot.at[min(step, last)], got.at[step], tot_send.at[step], tot_recv.at[step], (doubled + along_z)[step]
        )

    def add_total(step):
        total_move(step).wait_recv()
        tot[step + 1] = tot[step] + got[step]
        if step + 1 < len(doubled):
            total_move(step + 1).start()
        else:
            for shift in range(len(along_z)):
                total_move(step + 1 + shift).start()

    near_sent = [s * (2 * (1 - here.y) + i) + (1 - s) * (2 * i + 1 - here.x) for i in range(2)]
    own_slot = s * here.x + (1 - s) * here.y
    z_first = Z_FIRST if in_kernel_z else ()
    fewer = half_rows // 2
    parity = d % 2
    z_mate = (s, d + 1 - 2 * parity, t)

    def rows_of(u):
        if u not in z_first:
            return my_rows, half_rows
        return pl.ds(pl.multiple_of(s * half_rows + parity * fewer, fewer), fewer), fewer

    def to_mate(u):
        rows = pl.ds(pl.multiple_of(s * half_rows + (1 - parity) * fewer, fewer), fewer)
        i = z_first.index(u)
        return remote(stage.at[u % RING, :, rows, :], mate_in.at[i], mate_send.at[i], mate_recv.at[i], z_mate)

    def to_sibling(u):
        return remote(
            stage.at[u % RING, :, their_rows, :], sib.at[u % SIBS], sib_send.at[u], sib_recv.at[u], here.sibling
        )

    def to_near(u, i):
        rows, count = rows_of(u)
        return remote(
            stage.at[u % RING, near_sent[i], rows, :], near_in.at[u % NEARS, i, pl.ds(0, count)],
            near_send.at[u, i], near_recv.at[u, i], here.at(here.near),
        )

    def to_far(u):
        rows, count = rows_of(u)
        return remote(
            stage.at[u % RING, here.far, rows, :], far_in.at[u % FARS, pl.ds(0, count)],
            far_send.at[u], far_recv.at[u], here.at(here.far),
        )

    def give(u):
        to_sibling(u).start()

    def first(u):
        to_sibling(u).wait_recv()

        def add(q, carry):
            stage[u % RING, q, my_rows, :] += sib[u % SIBS, q]
            return carry

        lax.fori_loop(0, 4, add, 0)
        if u in z_first:
            to_mate(u).start()
            return
        for i in range(2):
            to_near(u, i).start()

    def middle(index):
        u = z_first[index]
        to_mate(u).wait_recv()
        rows, _ = rows_of(u)

        def add(q, carry):
            stage[u % RING, q, rows, :] += mate_in[index, q]
            return carry

        lax.fori_loop(0, 4, add, 0)
        for i in range(2):
            to_near(u, i).start()

    def second_step(place):
        u = ORDER[place]
        for i in range(2):
            to_near(u, i).wait_recv()
        rows, count = rows_of(u)
        stage[u % RING, here.far, rows, :] += near_in[u % NEARS, 1 - own_slot, pl.ds(0, count)]
        to_far(u).start()

    def z_moves(u):
        layer, v = 1 - u // UNITS, u % UNITS
        kept = ORDER.index(u) % PLANES
        moves = []
        if not in_kernel_z:
            target = mlp_out.at[v, my_rows, :]
            mine = s == layer
            moves.append((mine, pltpu.make_async_copy(plane.at[kept], target, local_sem.at[u, 0]), remote(
                plane.at[kept], target, mlp_send.at[u], mlp_recv.at[v, 0, s], (layer, d, t))))
        elif v < 8:
            rows, count = rows_of(u)
            piece = plane.at[kept, pl.ds(0, count)]
            target = mlp_out.at[v // 4, d, rows, :]
            mine = (s == layer) & (d == v % 4)
            moves.append((mine, pltpu.make_async_copy(piece, target, local_sem.at[u, 0]), remote(
                piece, target, mlp_send.at[u], mlp_recv.at[v // 4, d, s], (layer, v % 4, t))))
        else:
            for other in range(4):
                lanes = plane.shape[2] // 4 * other // LANES * LANES
                piece = plane.at[kept, :, pl.ds(lanes, 2 * LANES)]
                target = att_out.at[v - 8, d, my_rows, :]
                mine = (s == layer) & (d == other)
                moves.append((mine, pltpu.make_async_copy(piece, target, local_sem.at[u, other]), remote(
                    piece, target, att_send.at[layer, v - 8, other], att_recv.at[v - 8, d, s], (layer, other, t))))
        return moves

    def moved_out(u):
        for mine, local, away in z_moves(u):
            pl.when(mine)(local.wait)
            pl.when(jnp.logical_not(mine))(away.wait_send)

    def third(place):
        u = ORDER[place]
        to_far(u).wait_recv()
        if place >= PLANES:
            moved_out(ORDER[place - PLANES])
        rows, count = rows_of(u)
        some = pl.ds(0, count)
        plane[place % PLANES, some] = (
            stage[u % RING, t, rows, :].astype(F32)
            + near_in[u % NEARS, own_slot, some].astype(F32) + far_in[u % FARS, some].astype(F32)
        ).astype(BF16)
        for mine, local, away in z_moves(u):
            pl.when(mine)(local.start)
            pl.when(jnp.logical_not(mine))(away.start)
        to_sibling(u).wait_send()
        if u in z_first:
            to_mate(u).wait_send()
        for i in range(2):
            to_near(u, i).wait_send()
        to_far(u).wait_send()

    done = [0, 0, 0, 0]
    given = [0]
    steps = (first, middle, second_step, third)

    def ready(which):
        place = done[which]
        if which == 0:
            return place < given[0]
        if which == 1:
            return place < len(z_first) and z_first[place] < done[0]
        if which == 3:
            return place < done[2]
        u = ORDER[place]
        return u < done[0] and (u not in z_first or z_first.index(u) < done[1])

    def reach(*targets):
        targets = [targets[0], min(targets[1], len(z_first)), *targets[2:]]
        while any(now < target for now, target in zip(done, targets)):
            before = list(done)
            for which in (2, 0, 1, 3):
                if done[which] < targets[which] and ready(which):
                    steps[which](done[which])
                    done[which] += 1
            if done == before:
                which = next(which for which in (2, 1, 0) if ready(which))
                steps[which](done[which])
                done[which] += 1

    points = iter(SCHEDULE)

    def point():
        reach(*next(points))

    def room():
        old = given[0] - RING
        if old >= 0:
            last = max(ORDER.index(u) for u in range(old + 1))
            while done[3] <= last:
                for which in (3, 2, 1, 0):
                    if ready(which):
                        steps[which](done[which])
                        done[which] += 1
                        break

    def slot():
        give(given[0])
        given[0] += 1
        point()

    def rows_unit(k, left, right):
        room()
        place = given[0] % RING
        rows = pl.ds(k * quarter_rows, quarter_rows)

        def step(g, carry):
            stage[place, g] = dot(left[rows, :], right[g]).astype(BF16)
            return carry

        lax.fori_loop(0, 4, step, 0)

    def square_unit(left, right):
        room()
        place = given[0] % RING
        width = left.shape[1] // 2

        def step(c, carry):
            cols = pl.ds(pl.multiple_of(c * width, width), width)
            product = dot(left[:, cols], right[...], TN).astype(BF16)
            stage[place, pl.ds(2 * c, 2)] = product.reshape(2, quarter_rows, product.shape[1])
            return carry

        lax.fori_loop(0, 2, step, 0)

    masks = half_masks()

    def run_layer(layer):
        source = grad_ref if layer == 1 else dx_low.at[1]

        def prepare(rows):
            row = lax.broadcasted_iota(jnp.int32, (TILE, 1), 0) + rows.start
            grad = only(valid_rows(here.x, tok_rows, row), source[rows, :]).astype(F32)
            if layer == 0:
                value = x_ref[rows, :].astype(F32)
                logit = jnp.sum(value * router_ref[...], axis=-1, keepdims=True)
                sigma = 1.0 / (1.0 + jnp.exp(-logit))
                keep = keep_ref[rows, :]
                dlogit = jnp.sum(grad * branch[rows, :], axis=-1, keepdims=True) * keep * sigma * (1.0 - sigma)
                small_ref[2] += fold_rows(value * dlogit)
                dx_ref[rows, :] = grad + dlogit * router_ref[...]
                grad = grad * (sigma * keep)
            else:
                dx_ref[rows, :] = grad
            dbranch[rows, :] = grad
            dfed[rows, :] = grad.astype(BF16)

        small_ref[...] = jnp.zeros_like(small_ref)
        if layer == 1:
            load_grad.wait()
        else:
            load("branch", 0).wait()
            load("x", 0).wait()
        tiles(prepare)
        point()
        transpose_into(dfed, dfed_t)
        point()
        load("active", layer).wait()
        for k in range(4):
            g = k
            rows_unit(k, dfed_t, active)
            slot()
            if k == 3:
                prefetch("active", layer)
            for stream in streams:
                quarter_load(stream, layer, g).wait()
            work[...] = dot(dfed[...], wd[g % 2], NT)

            def bend(rows):
                dup[g, rows, :] = (work[rows, :] * slope[g % 2, rows, :].astype(F32)).astype(BF16)

            tiles(bend)
            point()
            part = dot(dup[g], wu[g % 2], NT)
            if g == 0:
                dsecond[...] = part
            else:
                dsecond[...] += part
            for stream in streams:
                if g < 2:
                    quarter_load(stream, layer, g + 2).start()
                elif layer == 1:
                    quarter_load(stream, 0, g - 2).start()
            point()

        load("second", layer).wait()
        transpose_into(second, dfed_t)
        point()
        prefetch("second", layer)
        for k in range(4):
            rows_unit(k, dfed_t, dup)
            slot()

        load("hidden", layer).wait()

        def second_pull(rows):
            xhat, rstd = standardize(hidden[rows, :])
            grad = dsecond[rows, :]
            small_ref[1] += fold_rows(grad * xhat)
            dhidden = norm_pull(xhat, rstd, gain_ref[layer, 1:2, :], grad)
            dx_ref[rows, :] += dhidden
            datt[rows, :] = (dbranch[rows, :] + dhidden).astype(BF16)

        tiles(second_pull)
        point()
        prefetch("hidden", layer)
        prefetch("branch", layer)
        load("mixed", layer).wait()
        square_unit(mixed, datt)
        prefetch("mixed", layer)
        slot()
        load("wo", layer).wait()
        dmixed[...] = dot(datt[...], wo[...], NT).astype(BF16)
        prefetch("wo", layer)
        point()
        load("qkv", layer).wait()
        if layer == 1:
            load_bias.wait()

        def attend(pair, carry):
            cols = pl.ds(pl.multiple_of(pair * LANES, LANES), LANES)
            key, value = qkv[1, :, cols], qkv[2, :, cols]
            scaled = key * BF16(0.125)
            query = qkv[0, :, cols] * BF16(0.125)
            grad = dmixed[:, cols]
            sums = None
            for mask in masks:
                query_head, grad_head = only(mask, query), only(mask, grad)
                expo, inverse = softmax_parts(dot(query_head, key, NT) + bias_ref[layer])
                probs = expo * inverse
                dprobs = dot(grad_head, value, NT)
                dscores = probs * (dprobs - jnp.sum(probs * dprobs, axis=-1, keepdims=True))
                dscores = dscores.astype(BF16)
                parts = [
                    dot(dscores, only(mask, scaled)),
                    dot(dscores, query_head, TN),
                    dot(probs.astype(BF16), grad_head, TN),
                ]
                sums = parts if sums is None else [left + right for left, right in zip(sums, parts)]
            for j in range(3):
                dqkv[j, :, cols] = sums[j].astype(BF16)
            return carry

        pairs = dmixed.shape[1] // LANES
        for part_of in range(3):
            lax.fori_loop(pairs * part_of // 3, pairs * (part_of + 1) // 3, attend, 0)
            point()
        prefetch("qkv", layer)

        load("normed", layer).wait()
        for j in range(3):
            square_unit(dqkv.at[j], normed)
            slot()
        prefetch("normed", layer)
        load("wq", layer).wait()
        work[...] = dot(dqkv[0], wq[0])
        work[...] += dot(dqkv[1], wq[1])
        point()
        work[...] += dot(dqkv[2], wq[2])
        point()
        prefetch("wq", layer)
        if layer == 1:
            load("x", 1).wait()

        def first_pull(rows):
            xhat, rstd = standardize(x_ref[rows, :].astype(F32))
            grad = work[rows, :]
            small_ref[0] += fold_rows(grad * xhat)
            total = dx_ref[rows, :] + norm_pull(xhat, rstd, gain_ref[layer, 0:1, :], grad)
            dx_low[layer, rows, :] = total.astype(BF16)

        tiles(first_pull)
        point()
        prefetch("x", layer)
        hand_back(layer, dx_low.at[layer], main_out, back_out)
        sums = jnp.sum(small_ref[...], axis=1)
        if layer == 1:
            tot[0] = jnp.zeros(tot.shape[1:], F32)
            tot[0, 3:5, :] = sums[0:2]
        else:
            tot[0, 0:3, :] = sums
            total_move(0).start()

    run_layer(1)
    run_layer(0)
    added = 0
    late_backs = backs[EARLY_BACKS:]
    for index, targets in enumerate(points):
        reach(*targets)
        if done[2] == 2 * UNITS and late_backs:
            for back in late_backs:
                back.start_back()
            late_backs = []
        if index in TOTALS:
            add_total(added)
            added += 1
    reach(2 * UNITS, len(z_first), 2 * UNITS, 2 * UNITS)
    for step in range(added, len(doubled)):
        add_total(step)
    for back in late_backs:
        back.start_back()
    moves = [total_move(step) for step in range(len(doubled) + len(along_z))]
    for move in moves[len(doubled) :]:
        move.wait_recv()
    total = jnp.zeros_like(small_out)
    for z in range(n_dp):
        shift = (z - d + n_dp) % n_dp
        total += jnp.where(shift == 0, tot[len(doubled)], got[len(doubled) - 1 + jnp.maximum(shift, 1)])
    small_out[...] = total
    for move in moves:
        move.wait_send()
    for back in backs:
        back.wait()
    for u in ORDER[-PLANES:]:
        moved_out(u)

    if not in_kernel_z:
        for v in range(UNITS):
            remote(
                plane.at[0], mlp_out.at[v, their_rows, :], mlp_send.at[v], mlp_recv.at[v, 0, 1 - s], here.sibling
            ).wait_recv()
        return
    for source in range(4):
        for half in range(2):
            rows = pl.ds(half * half_rows, half_rows)

            def arrive():
                for kind in range(2):
                    sent = mlp_recv.at[kind, source, half]
                    first_z = comes_first_z(s, d, kind)
                    for count, now in ((fewer, first_z), (half_rows, jnp.logical_not(first_z))):
                        target = mlp_out.at[kind, source, pl.ds(half * half_rows, count), :]
                        pl.when(now)(remote(target, target, mlp_send.at[0], sent, here.sibling).wait_recv)
                for b in range(4):
                    target = att_out.at[b, source, rows, :]
                    remote(
                        target, target, att_send.at[0, 0, 0], att_recv.at[b, source, half], here.sibling
                    ).wait_recv()

            pl.when(jnp.logical_not((d == source) & (s == half)))(arrive)


def backward(n_dp, tok_rows, keep, gains, router, bias, grad, x, saved):
    width = x.shape[2]
    held, _, spare = token_layout(tok_rows)
    quarter_rows = width // 4
    half_rows = quarter_rows // 2
    in_kernel_z = n_dp == 4
    steps = 3 + n_dp - 1
    any_spec = pl.BlockSpec(memory_space=pl.ANY)
    vmem = pl.BlockSpec(memory_space=pltpu.VMEM)
    dma = pltpu.SemaphoreType.DMA

    def low(*shape):
        return pltpu.VMEM(shape, BF16)

    def wide(*shape):
        return pltpu.VMEM(shape, F32)

    mlp_shape = (2, 4, quarter_rows, width) if in_kernel_z else (UNITS, quarter_rows, width)
    units = 2 * UNITS
    scratch = [
        low(ROWS, width), low(ROWS, width), wide(ROWS, width), low(2, ROWS, width), wide(3, 8, width),
        wide(4, 8, width), wide(steps, 8, width), wide(2, ROWS, ROWS),
        low(3, width, width), low(width, width), low(2, width, width), low(2, width, width),
        low(ROWS, width), low(3, ROWS, width), low(ROWS, width), wide(ROWS, width), low(ROWS, width),
        low(4, ROWS, width), low(2, ROWS, width),
        wide(ROWS, width), low(ROWS, width), low(width, ROWS), wide(ROWS, width), low(4, ROWS, width),
        wide(ROWS, width), low(ROWS, width), low(ROWS, width), low(3, ROWS, width),
        low(RING, 4, quarter_rows, width), low(SIBS, 4, half_rows, width), low(NEARS, 2, half_rows, width),
        low(FARS, half_rows, width), low(PLANES, half_rows, width),
        low(len(Z_FIRST), 4, half_rows // 2, width),
        dma((2, 11)), dma((2, 2)), dma((2, 2)), dma((2, 2)),
        dma((units,)), dma((units,)), dma((units, 2)), dma((units, 2)), dma((units,)), dma((units,)),
        dma((units,)), dma((UNITS, 4, 2)), dma((2, 4, 4)), dma((4, 4, 2)), dma((units, 4)),
        dma((steps,)), dma((steps,)), dma((len(Z_FIRST),)), dma((len(Z_FIRST),)), *[sem for _ in range(4) for sem in hand_back_sems()],
    ]
    return pl.pallas_call(
        functools.partial(backward_kernel, in_kernel_z, tok_rows),
        out_shape=[
            jax.ShapeDtypeStruct((8, width), F32),
            jax.ShapeDtypeStruct((2, held, width), BF16),
            jax.ShapeDtypeStruct((2, spare, width), BF16),
            jax.ShapeDtypeStruct((2, held, width), BF16),
            jax.ShapeDtypeStruct((2, spare, width), BF16),
            jax.ShapeDtypeStruct(mlp_shape, BF16),
            jax.ShapeDtypeStruct((4, 4, quarter_rows, 2 * LANES), BF16),
        ],
        in_specs=[vmem] * 3 + [any_spec] * 15,
        out_specs=[vmem] + [any_spec] * 6,
        scratch_shapes=scratch,
        compiler_params=pltpu.CompilerParams(
            collective_id=1, has_side_effects=True, vmem_limit_bytes=VMEM_BYTES
        ),
        cost_estimate=pl.CostEstimate(flops=96 * ROWS * width * width, bytes_accessed=120_000_000, transcendentals=0),
        name="backward_layers",
    )(keep, gains, router, bias, grad, x, *saved)


def finish_kernel(
    tok_rows, sums,
    small_ref, y_main, y_back, dx_main, dx_back, mlp_in, att_in,
    y_out, dx_out, ones_out, twos_out, router_out, *rest,
):
    if sums:
        (down_out, up_out, out_out, qkv_out, *rest) = rest
    y_rows, y_tail, dx_rows, dx_tail, y_buf, dx_buf, mlp, att, mlp_sum, att_sum, in_sem, out_sem = rest
    held, low, spare = token_layout(tok_rows)
    section, d, t = lax.axis_index("section"), lax.axis_index("dp"), lax.axis_index("tensor")
    n_dp, quarters = lax.axis_size("dp"), lax.axis_size("tensor")
    x_half = t % 2
    moves = [(dx_main, dx_rows), (dx_back, dx_tail), (y_main, y_rows), (y_back, y_tail)]
    if sums:
        moves += [(mlp_in.at[0], mlp.at[0]), (mlp_in.at[1], mlp.at[1]), (att_in, att)]
    copies = [pltpu.make_async_copy(src, dst, in_sem.at[i]) for i, (src, dst) in enumerate(moves)]
    for copy in copies:
        copy.start()
    results = []

    def give(src, dst):
        copy = pltpu.make_async_copy(src, dst, out_sem.at[len(results)])
        copy.start()
        results.append(copy)

    def join(main, back, buffer, out):
        def plain(i, carry):
            rows = pl.ds(pl.multiple_of(i * 16, 16), 16)
            for m in range(2):
                buffer[rows, m, :] = main[m, rows, :].astype(buffer.dtype)
            return carry

        def mixed_rows(i, carry):
            rows = pl.ds(pl.multiple_of(i * 16, 16), 16)
            from_back = pl.ds(pl.multiple_of(i * 16 - low, 16), 16)
            row = lax.broadcasted_iota(jnp.int32, (16, 1), 0) + i * 16
            is_back = (x_half == 0) & (row >= CUT)
            for m in range(2):
                value = jnp.where(is_back, back[m, from_back, :], main[m, rows, :])
                buffer[rows, m, :] = value.astype(buffer.dtype)
            return carry

        lax.fori_loop(0, low // 16, plain, 0)
        lax.fori_loop(low // 16, held // 16, mixed_rows, 0)
        give(buffer.at[pl.ds(0, tok_rows)], out)

    for i, pieces in enumerate(((dx_rows, dx_tail, dx_buf, dx_out), (y_rows, y_tail, y_buf, y_out))):
        copies[2 * i].wait()
        copies[2 * i + 1].wait()
        join(*pieces)
    if sums:
        width = mlp_sum.shape[1]
        for kind in range(2):
            copies[4 + kind].wait()

            first_z = comes_first_z(section, d, kind)

            def add(rows):
                odd = rows.start // (width // 4) % 2
                parts = [
                    only(jnp.logical_not(first_z) | (odd == source % 2), mlp[kind, source, rows, :]).astype(F32)
                    for source in range(4)
                ]
                mlp_sum[kind, rows, :] = parts[0] + parts[1] + parts[2] + parts[3]

            tiles(add, rows=width, tile=16)
            give(mlp_sum.at[kind], (down_out, up_out)[kind])
        copies[6].wait()
        for b in range(4):
            total = att[b, 0].astype(F32) + att[b, 1].astype(F32) + att[b, 2].astype(F32) + att[b, 3].astype(F32)
            total = jnp.where(d % 2 == 0, total[:, :width], total[:, -width:])
            att_sum[b] = total if b == 0 else total.T
            give(att_sum.at[b], out_out if b == 0 else qkv_out.at[b - 1])

    columns = small_ref[...].T
    place = d * quarters + t

    def pick(values, start, count):
        row = lax.broadcasted_iota(jnp.int32, (columns.shape[0], count), 0)
        lane = lax.broadcasted_iota(jnp.int32, (columns.shape[0], count), 1)
        return jnp.sum(jnp.where(row == start + lane, values, 0.0), axis=0, keepdims=True)

    span = ones_out.shape[1]
    ones_out[...] = pick(jnp.where(section == 0, columns[:, 0:1], columns[:, 3:4]), place * span, span)
    twos_out[...] = pick(jnp.where(section == 0, columns[:, 1:2], columns[:, 4:5]), place * span, span)
    span = router_out.shape[1]
    router_out[...] = pick(columns[:, 2:3], (section * n_dp * quarters + place) * span, span)
    for copy in results:
        copy.wait()


def finish(tok_rows, n_dp, quarters, small, y_main, y_back, dx_main, dx_back, mlp, att):
    width = small.shape[1]
    held, _, spare = token_layout(tok_rows)
    part = width // 4
    span = width // (n_dp * quarters)
    sums = n_dp == 4
    any_spec = pl.BlockSpec(memory_space=pl.ANY)
    vmem = pl.BlockSpec(memory_space=pltpu.VMEM)
    shapes = [
        jax.ShapeDtypeStruct((tok_rows, 2, width), BF16), jax.ShapeDtypeStruct((tok_rows, 2, width), F32),
        jax.ShapeDtypeStruct((1, span), F32), jax.ShapeDtypeStruct((1, span), F32),
        jax.ShapeDtypeStruct((1, span // 2), F32),
    ]
    specs = [any_spec, any_spec, vmem, vmem, vmem]
    if sums:
        shapes += [jax.ShapeDtypeStruct(shape, F32) for shape in ((part, width), (part, width), (part, part), (3, part, part))]
        specs += [any_spec] * 4
    dma = pltpu.SemaphoreType.DMA
    return pl.pallas_call(
        functools.partial(finish_kernel, tok_rows, sums),
        out_shape=shapes,
        in_specs=[vmem] + [any_spec] * 6,
        out_specs=specs,
        scratch_shapes=[
            pltpu.VMEM((2, held, width), BF16), pltpu.VMEM((2, spare, width), BF16),
            pltpu.VMEM((2, held, width), BF16), pltpu.VMEM((2, spare, width), BF16),
            pltpu.VMEM((held, 2, width), BF16), pltpu.VMEM((held, 2, width), F32),
            pltpu.VMEM((2, 4, part, width), BF16), pltpu.VMEM((4, 4, part, 2 * LANES), BF16),
            pltpu.VMEM((2, part, width), F32), pltpu.VMEM((4, part, part), F32), dma((7,)), dma((8,)),
        ],
        compiler_params=pltpu.CompilerParams(vmem_limit_bytes=VMEM_BYTES),
        cost_estimate=pl.CostEstimate(flops=4_000_000, bytes_accessed=12_000_000, transcendentals=0),
        name="finish",
    )(small, y_main, y_back, dx_main, dx_back, mlp, att)


def on_device(
    patches, cotangent, crop_lengths, route_mask, w_qkv, w_out, w_up, w_down, ln1_gain, ln2_gain, router
):
    tok_rows, width = patches.shape[1:]
    n_dp, quarters = lax.axis_size("dp"), lax.axis_size("tensor")
    wq = jnp.transpose(w_qkv[0], (1, 2, 0))
    x, gains, keep_rows, router_row, bias, grad, *saved = forward(
        crop_lengths, route_mask, ln1_gain, ln2_gain, router, jnp.transpose(patches, (1, 0, 2)),
        jnp.transpose(cotangent, (1, 0, 2)), wq, w_out[0], w_up[0], w_down[0],
    )
    small, y_main, y_back, dx_main, dx_back, mlp, att = backward(
        n_dp, tok_rows, keep_rows, gains, router_row, bias, grad, x, saved
    )

    y_out, dx_out, ones, twos, routers, *grads = finish(
        tok_rows, n_dp, quarters, small, y_main, y_back, dx_main, dx_back, mlp, att
    )
    outputs = jnp.transpose(y_out, (1, 0, 2))
    input_grads = jnp.transpose(dx_out, (1, 0, 2))
    if n_dp == 4:
        down, up, out, qkv = grads
    else:

        def scatter(value, dim):
            return lax.psum_scatter(value, "dp", scatter_dimension=dim, tiled=True).astype(F32)

        down = scatter(mlp[:4].reshape(width, width), 0)
        up = scatter(mlp[4:8].reshape(width, width), 0)
        out = scatter(mlp[8], 1)
        qkv = jnp.transpose(scatter(mlp[9:], 2), (0, 2, 1))
    qkv = jnp.transpose(qkv, (1, 0, 2))
    return (
        outputs[None], input_grads[None], qkv[None], out[None], up[None], down.T[None], ones, twos, routers[0],
    )


def solution(mesh):
    return jax.shard_map(
        on_device,
        mesh=mesh,
        in_specs=(
            P(None, ("dp", "tensor"), None),
            P(None, ("dp", "tensor"), None),
            P(None, "dp", None),
            P(None, "dp"),
            P("section", None, None, "tensor"),
            P("section", "tensor", None),
            P("section", None, "tensor"),
            P("section", "tensor", None),
            P("section", None),
            P("section", None),
            P(),
        ),
        out_specs=(
            P("section", None, ("dp", "tensor"), None),
            P("section", None, ("dp", "tensor"), None),
            P("section", "dp", None, "tensor"),
            P("section", "tensor", "dp"),
            P("section", "dp", "tensor"),
            P("section", "tensor", "dp"),
            P("section", ("dp", "tensor")),
            P("section", ("dp", "tensor")),
            P(("section", "dp", "tensor")),
        ),
        check_vma=False,
    )
```
